32 devices in a mesh: blk: 4 (over y, x), dp: 8 (over z, core).
Axes of the slice: x: 2, y: 2, z: 4, core: 2. Of those that a mesh axis runs over, the one named last changes fastest.
Arguments:
- inputs: bfloat16 [8, 1024, 768], P('dp', 'blk'), may hold values from -6 to 6
- condition: float32 [8, 128], P('dp'), may hold values from -6 to 6
- prefix: int32 [8], P('dp'), may hold values from 1 to 1023
- mask_embed: bfloat16 [768], replicated, may hold values from -6 to 6
- adaptive_weight: bfloat16 [2, 128, 4608], replicated, may hold values from -0.25 to 0.25
- adaptive_bias: bfloat16 [2, 4608], replicated, may hold values from -3 to 3
- triple_weight: bfloat16 [2, 768, 2304], replicated, may hold values from -0.21875 to 0.21875
- triple_bias: bfloat16 [2, 2304], replicated, may hold values from -3 to 3
- output_weight: bfloat16 [2, 768, 768], replicated, may hold values from -3.5 to 3.5
- output_bias: bfloat16 [2, 768], replicated, may hold values from -3 to 3
- expand_weight: bfloat16 [2, 768, 3072], replicated, may hold values from -0.21875 to 0.21875
- expand_bias: bfloat16 [2, 3072], replicated, may hold values from -3 to 3
- shrink_weight: bfloat16 [2, 3072, 768], replicated, may hold values from -0.109375 to 0.109375
- shrink_bias: bfloat16 [2, 768], replicated, may hold values from -3 to 3
- cotangent: bfloat16 [8, 1024, 768], P('dp', 'blk'), may hold values from -6 to 6
Outputs:
- outputs: bfloat16 [8, 1024, 768], P('dp', 'blk')
- input_gradient: float32 [8, 1024, 768], P('dp', 'blk')
- condition_gradient: float32 [8, 128], P('dp')
- mask_gradient: float32 [768], P(('blk', 'dp'))
- adaptive_weight_gradient: float32 [2, 128, 4608], P(None, ('blk', 'dp'))
- adaptive_bias_gradient: float32 [2, 4608], P(None, ('blk', 'dp'))
- triple_weight_gradient: float32 [2, 768, 2304], P(None, ('blk', 'dp'))
- triple_bias_gradient: float32 [2, 2304], P(None, ('blk', 'dp'))
- output_weight_gradient: float32 [2, 768, 768], P(None, ('blk', 'dp'))
- output_bias_gradient: float32 [2, 768], P(None, ('blk', 'dp'))
- expand_weight_gradient: float32 [2, 768, 3072], P(None, ('blk', 'dp'))
- expand_bias_gradient: float32 [2, 3072], P(None, ('blk', 'dp'))
- shrink_weight_gradient: float32 [2, 3072, 768], P(None, ('blk', 'dp'))
- shrink_bias_gradient: float32 [2, 768], P(None, ('blk', 'dp'))
The draws below stay inside these ranges and needn't reach their ends.
All inputs are finite; a program needn't handle non-finite values.
Results may differ from the reference program's by a relative error of at most 0.025.
Values may be sent and summed in bfloat16 or wider, within the bound.
No kernel may reach another device: no remote copies, remote signals or barrier semaphores. Data moves between devices by JAX's collectives and lax.ppermute only.
A program may use at most 256 MiB of HBM per device.

```python
import math
import jax
import jax.numpy as jnp
from jax import lax

WIDTH = 768
HEADS = 12
HEAD_DIM = 64
HIDDEN_SIZE = 3072
TIME_DIM = 128
LAYERS = 2
LENGTH = 1024
SEQS = 8


def touch_ends(drawn, stream_key, least, largest):
    longest = drawn.shape.index(max(drawn.shape))
    spots = []
    for shift in (0, 1):
        where = [jax.random.randint(jax.random.fold_in(stream_key, axis), (), 0, length) for axis, length in enumerate(drawn.shape)]
        where[longest] = (where[longest] + shift) % drawn.shape[longest]
        spots.append(tuple(where))
    return drawn.at[spots[0]].set(least).at[spots[1]].set(largest)


def block_scale(rng, shape, cuts, low, high):
    loudness, own = 1.0, jax.random.fold_in(rng, 6)
    for dim, parts in cuts:
        draws = jnp.exp(jax.random.uniform(jax.random.fold_in(own, dim), (parts,), jnp.float32, low / len(cuts), high / len(cuts)))
        loudness = loudness * jnp.repeat(draws, shape[dim] // parts).reshape([-1 if axis == dim else 1 for axis in range(len(shape))])
    return loudness


def normal_values(own_key, shape, spread, limit, split=(), held_as=jnp.bfloat16):
    values = spread * jax.random.normal(own_key, shape, jnp.float32)
    if split:
        values = values * block_scale(own_key, shape, split, -0.22, 0.18)
    return jnp.clip(values, -limit, limit).astype(held_as)


def setup_inputs(seed: int = 0) -> dict:
    splits = jax.random.split(jax.random.key(seed), 16)
    return {
        "inputs": normal_values(splits[0], (SEQS, LENGTH, WIDTH), 1.0, 6.0, ((0, 8), (1, 4))),
        "condition": normal_values(splits[1], (SEQS, TIME_DIM), 1.0, 6.0, ((0, 8),), jnp.float32),
        "prefix": touch_ends(jax.random.randint(splits[2], (SEQS,), 1, LENGTH), jax.random.fold_in(splits[2], 1), 1, LENGTH - 1).astype(jnp.int32),
        "mask_embed": normal_values(splits[3], (WIDTH,), 1.0, 6.0),
        "adaptive_weight": normal_values(splits[4], (LAYERS, TIME_DIM, 6 * WIDTH), (4 * TIME_DIM) ** -0.5, 0.25),
        "adaptive_bias": normal_values(splits[5], (LAYERS, 6 * WIDTH), 0.5, 3.0),
        "triple_weight": normal_values(splits[6], (LAYERS, WIDTH, 3 * WIDTH), WIDTH ** -0.5, 0.21875),
        "triple_bias": normal_values(splits[7], (LAYERS, 3 * WIDTH), 0.5, 3.0),
        "output_weight": normal_values(splits[8], (LAYERS, WIDTH, WIDTH), (max(1, WIDTH // 256)) ** -0.5, 3.5),
        "output_bias": normal_values(splits[9], (LAYERS, WIDTH), 0.5, 3.0),
        "expand_weight": normal_values(splits[10], (LAYERS, WIDTH, HIDDEN_SIZE), WIDTH ** -0.5, 0.21875),
        "expand_bias": normal_values(splits[11], (LAYERS, HIDDEN_SIZE), 0.5, 3.0),
        "shrink_weight": normal_values(splits[12], (LAYERS, HIDDEN_SIZE, WIDTH), HIDDEN_SIZE ** -0.5, 0.109375),
        "shrink_bias": normal_values(splits[13], (LAYERS, WIDTH), 0.5, 3.0),
        "cotangent": normal_values(splits[14], (SEQS, LENGTH, WIDTH), 1.0, 6.0, ((0, 8), (1, 4))),
    }


@jax.custom_vjp
def low(v):
    return lax.optimization_barrier(v.astype(jnp.bfloat16)).astype(jnp.float32)

@jax.custom_vjp
def low_back(v):
    return v

def low_keep(v):
    return (low(v), None)

def low_pass(kept, grad):
    return (grad,)

def back_keep(v):
    return (v, None)

def back_low(kept, grad):
    return (low(grad),)
low.defvjp(low_keep, low_pass)
low_back.defvjp(back_keep, back_low)
HIGHEST = lax.Precision.HIGHEST
EPSILON = 1e-06

def modulate(residual, shift, scaling):
    average = lax.optimization_barrier(jnp.mean(residual, -1, keepdims=True))
    centered = residual - average
    variance = lax.optimization_barrier(jnp.mean(centered * centered, -1, keepdims=True))
    return centered * lax.rsqrt(variance + EPSILON) * (1.0 + scaling) + shift

def tables(offset, row_count, head_dim):
    half_dim = head_dim // 2
    position = (offset + jnp.arange(row_count, dtype=jnp.int32)).astype(jnp.float32)
    frequency = jnp.exp(jnp.arange(half_dim, dtype=jnp.float32) * (-2.0 * math.log(10000.0) / head_dim))
    angles = position[:, None] * frequency[None, :]
    return (jnp.cos(angles)[:, None, :], jnp.sin(angles)[:, None, :])

def rotate(vectors, cosine, sine_table):
    half_dim = vectors.shape[-1] // 2
    front_half = vectors[..., :half_dim]
    back_half = vectors[..., half_dim:]
    return jnp.concatenate([front_half * cosine - back_half * sine_table, back_half * cosine + front_half * sine_table], -1)

def product(left, right):
    return jnp.matmul(left, right, precision=HIGHEST)

def attention(queries, key_rows, values):
    seq_len = queries.shape[1]
    block_rows = math.gcd(seq_len, 512)
    scaling = 1.0 / math.sqrt(queries.shape[-1])

    def one_sequence(triple):
        seq_query, seq_key, seq_value = triple
        blocks = seq_query.reshape(seq_len // block_rows, block_rows, seq_query.shape[1], seq_query.shape[2])

        def one_block(block_query):
            scores = low_back(jnp.einsum('qhd,khd->hqk', block_query, seq_key, precision=HIGHEST) * scaling)
            peak = lax.optimization_barrier(jnp.max(scores, -1, keepdims=True))
            weights = jnp.exp(scores - peak)
            probs = weights / lax.optimization_barrier(jnp.sum(weights, -1, keepdims=True))
            return jnp.einsum('hqk,khd->qhd', probs, seq_value, precision=HIGHEST)
        return lax.map(jax.checkpoint(one_block), blocks).reshape(seq_len, seq_query.shape[1], seq_query.shape[2])
    return lax.map(one_sequence, (queries, key_rows, values))

def forward(inputs, condition, mask_embed, adaptive_weight, adaptive_bias, triple_weight, triple_bias, output_weight, output_bias, expand_weight, expand_bias, shrink_weight, shrink_bias, prefix):
    seq_count, seq_len, width = inputs.shape
    position = jnp.arange(seq_len, dtype=jnp.int32)
    masked = position[None, :] >= prefix[:, None]
    residual = jnp.where(masked[:, :, None], mask_embed[None, None, :], inputs)
    cosine, sine_table = tables(0, seq_len, HEAD_DIM)
    for layer_index in range(LAYERS):
        modulation = product(condition, adaptive_weight[layer_index]) + adaptive_bias[layer_index]
        pieces = [modulation[:, None, number * width:(number + 1) * width] for number in range(6)]
        shift_attn, scale_attn, gate_attn, shift_mlp, scale_mlp, gate_mlp = pieces
        normed = low(modulate(residual, shift_attn, scale_attn))
        mixed = low_back(product(normed, triple_weight[layer_index]) + triple_bias[layer_index])
        head_shape = (seq_count, seq_len, HEADS, HEAD_DIM)
        queries = low(rotate(mixed[..., :width].reshape(head_shape), cosine, sine_table))
        key_rows = low(rotate(mixed[..., width:2 * width].reshape(head_shape), cosine, sine_table))
        values = low(mixed[..., 2 * width:].reshape(head_shape))
        attended = attention(queries, key_rows, values).reshape(seq_count, seq_len, width)
        attended = low(low_back(attended))
        branch = low_back(product(attended, output_weight[layer_index]) + output_bias[layer_index])
        middle = residual + gate_attn * branch
        normed_mlp = low(modulate(middle, shift_mlp, scale_mlp))
        up_proj = low_back(product(normed_mlp, expand_weight[layer_index]) + expand_bias[layer_index])
        active = low(jax.nn.gelu(up_proj, approximate=True))
        lowered = low_back(product(active, shrink_weight[layer_index]) + shrink_bias[layer_index])
        residual = middle + gate_mlp * lowered
    return residual

def reference(inputs, condition, prefix, mask_embed, adaptive_weight, adaptive_bias, triple_weight, triple_bias, output_weight, output_bias, expand_weight, expand_bias, shrink_weight, shrink_bias, cotangent):

    def wrapped(*arrays):
        return forward(*arrays, prefix)
    result, pullback = jax.vjp(wrapped, inputs.astype(jnp.float32), condition, mask_embed.astype(jnp.float32), adaptive_weight.astype(jnp.float32), adaptive_bias.astype(jnp.float32), triple_weight.astype(jnp.float32), triple_bias.astype(jnp.float32), output_weight.astype(jnp.float32), output_bias.astype(jnp.float32), expand_weight.astype(jnp.float32), expand_bias.astype(jnp.float32), shrink_weight.astype(jnp.float32), shrink_bias.astype(jnp.float32))
    grads = pullback(cotangent.astype(jnp.float32))
    return (result.astype(jnp.bfloat16), grads[0], grads[1], grads[2], grads[3], grads[4], grads[5], grads[6], grads[7], grads[8], grads[9], grads[10], grads[11], grads[12])
```

```python
import functools
import math

import jax
import jax.numpy as jnp
from jax import lax
from jax.experimental import pallas as pl
from jax.experimental.pallas import tpu as pltpu
from jax.sharding import PartitionSpec as P

HEADS = 12
HEAD_DIM = 64
LAYERS = 2


HIGHEST = lax.Precision.HIGHEST
EPSILON = 1e-06


def modulate(residual, shift, scaling):
    average = jnp.mean(residual, -1, keepdims=True)
    centered = residual - average
    variance = jnp.mean(centered * centered, -1, keepdims=True)
    return centered * lax.rsqrt(variance + EPSILON) * (1.0 + scaling) + shift


def gelu_tanh(values):
    return jax.nn.gelu(values, approximate=True)


def tables(offset, row_count, head_dim):
    half_dim = head_dim // 2
    position = (offset + jnp.arange(row_count, dtype=jnp.int32)).astype(jnp.float32)
    frequency = jnp.exp(
        jnp.arange(half_dim, dtype=jnp.float32) * (-2.0 * math.log(10000.0) / head_dim)
    )
    angles = position[:, None] * frequency[None, :]
    return (jnp.cos(angles)[:, None, :], jnp.sin(angles)[:, None, :])


def rotate(vectors, cosine, sine_table):
    half_dim = vectors.shape[-1] // 2
    front_half = vectors[..., :half_dim]
    back_half = vectors[..., half_dim:]
    return jnp.concatenate(
        [
            front_half * cosine - back_half * sine_table,
            back_half * cosine + front_half * sine_table,
        ],
        -1,
    )


def unrotate(gradient, cosine, sine_table):
    half_dim = gradient.shape[-1] // 2
    front_half = gradient[..., :half_dim]
    back_half = gradient[..., half_dim:]
    return jnp.concatenate(
        [
            front_half * cosine + back_half * sine_table,
            back_half * cosine - front_half * sine_table,
        ],
        -1,
    )


def split_einsum(form, float_left, low_right):
    upper = float_left.astype(jnp.bfloat16)
    lower = (float_left - upper.astype(jnp.float32)).astype(jnp.bfloat16)
    first = jnp.einsum(form, upper, low_right, preferred_element_type=jnp.float32)
    return first + jnp.einsum(form, lower, low_right, preferred_element_type=jnp.float32)


def fold_keys(queries, scaling):

    def absorb(carried, key_piece, offset):
        key_flat, value_flat = key_piece
        piece_rows = key_flat.shape[0]
        block_rows = math.gcd(piece_rows, 512)
        key_blocks = key_flat.reshape(piece_rows // block_rows, block_rows, HEADS, HEAD_DIM)
        value_blocks = value_flat.reshape(piece_rows // block_rows, block_rows, HEADS, HEAD_DIM)

        def absorb_inner(running, block_pair):
            running_max, running_sum, weighted = running
            key_block, value_block = block_pair
            scores = (
                jnp.einsum("qhd,khd->hqk", queries, key_block, preferred_element_type=jnp.float32)
                * scaling
            )
            new_max = jnp.maximum(running_max, jnp.max(scores, -1))
            weights = jnp.exp(scores - new_max[..., None])
            factor = jnp.exp(running_max - new_max)
            running_sum = running_sum * factor + jnp.sum(weights, -1)
            weighted = weighted * factor[..., None] + split_einsum(
                "hqk,khd->hqd", weights, value_block
            )
            return ((new_max, running_sum, weighted), None)

        carried, _ = lax.scan(absorb_inner, carried, (key_blocks, value_blocks))
        return carried

    return absorb


def attend_back(queries, key_all, value_all, out_gradient, attended_f, log_total, scaling):
    row_count = queries.shape[0]
    all_rows = key_all.shape[0]
    block_rows = math.gcd(all_rows, 512)
    key_blocks = key_all.reshape(all_rows // block_rows, block_rows, HEADS, HEAD_DIM)
    value_blocks = value_all.reshape(all_rows // block_rows, block_rows, HEADS, HEAD_DIM)
    out_float = out_gradient.astype(jnp.float32)
    row_delta = jnp.transpose(jnp.sum(out_float * attended_f, -1), (1, 0))

    def attend_inner(query_grad, block_pair):
        key_block, value_block = block_pair
        scores = (
            jnp.einsum("qhd,khd->hqk", queries, key_block, preferred_element_type=jnp.float32)
            * scaling
        )
        probs = jnp.exp(scores - log_total[..., None])
        prob_grad = jnp.einsum(
            "qhd,khd->hqk", out_gradient, value_block, preferred_element_type=jnp.float32
        )
        score_grad = (probs * (prob_grad - row_delta[..., None])).astype(jnp.bfloat16)
        query_grad = query_grad + jnp.einsum(
            "hqk,khd->qhd", score_grad, key_block, preferred_element_type=jnp.float32
        )
        key_grad = (
            jnp.einsum("hqk,qhd->khd", score_grad, queries, preferred_element_type=jnp.float32)
            * scaling
        )
        value_grad = split_einsum("hqk,qhd->khd", probs, out_gradient)
        return (query_grad, (key_grad, value_grad))

    start_grad = jnp.zeros((row_count, HEADS, HEAD_DIM), jnp.float32)
    query_grad, (key_grads, value_grads) = lax.scan(
        attend_inner, start_grad, (key_blocks, value_blocks)
    )
    width = HEADS * HEAD_DIM
    return (
        query_grad * scaling,
        key_grads.reshape(all_rows, width),
        value_grads.reshape(all_rows, width),
    )


def forward_layer(residual, modulation, layer_index, weights, cosine, sine_table, scaling):
    (
        adaptive_weight,
        adaptive_bias,
        triple_weight,
        triple_bias,
        output_weight,
        output_bias,
        expand_weight,
        expand_bias,
        shrink_weight,
        shrink_bias,
    ) = weights
    row_count, width = residual.shape
    pieces = [modulation[number * width : (number + 1) * width] for number in range(6)]
    shift_attn, scale_attn, gate_attn, shift_mlp, scale_mlp, gate_mlp = pieces
    normed = modulate(residual, shift_attn, scale_attn).astype(jnp.bfloat16)
    mixed = jnp.dot(
        normed, triple_weight[layer_index], preferred_element_type=jnp.float32
    ) + triple_bias[layer_index].astype(jnp.float32)
    head_shape = (row_count, HEADS, HEAD_DIM)
    queries = rotate(mixed[:, :width].reshape(head_shape), cosine, sine_table).astype(jnp.bfloat16)
    key_flat = (
        rotate(mixed[:, width : 2 * width].reshape(head_shape), cosine, sine_table)
        .astype(jnp.bfloat16)
        .reshape(row_count, width)
    )
    value_flat = mixed[:, 2 * width :].astype(jnp.bfloat16)
    start_state = (
        jnp.full((HEADS, row_count), -1e30, jnp.float32),
        jnp.zeros((HEADS, row_count), jnp.float32),
        jnp.zeros((HEADS, row_count, HEAD_DIM), jnp.float32),
    )
    absorb = fold_keys(queries, scaling)
    final_state = absorb(
        start_state,
        (
            lax.all_gather(key_flat, "blk", axis=0, tiled=True),
            lax.all_gather(value_flat, "blk", axis=0, tiled=True),
        ),
        jnp.int32(0),
    )
    running_max, running_sum, weighted = final_state
    log_total = running_max + jnp.log(running_sum)
    attended_f = jnp.transpose(weighted / running_sum[..., None], (1, 0, 2))
    attended = attended_f.reshape(row_count, width).astype(jnp.bfloat16)
    branch = jnp.dot(
        attended, output_weight[layer_index], preferred_element_type=jnp.float32
    ) + output_bias[layer_index].astype(jnp.float32)
    middle = residual + gate_attn * branch
    normed_mlp = modulate(middle, shift_mlp, scale_mlp).astype(jnp.bfloat16)
    up_proj = jnp.dot(
        normed_mlp, expand_weight[layer_index], preferred_element_type=jnp.float32
    ) + expand_bias[layer_index].astype(jnp.float32)
    active = gelu_tanh(up_proj).astype(jnp.bfloat16)
    lowered = jnp.dot(
        active, shrink_weight[layer_index], preferred_element_type=jnp.float32
    ) + shrink_bias[layer_index].astype(jnp.float32)
    result = middle + gate_mlp * lowered
    saved = (
        residual,
        normed,
        queries,
        key_flat,
        value_flat,
        None,
        attended_f,
        attended,
        log_total,
        branch,
        middle,
        normed_mlp,
        up_proj,
        active,
        lowered,
    )
    return (result, saved)


def backward_layer(
    gradient, modulation, layer_index, weights, saved, cosine, sine_table, scaling, condition
):
    (
        adaptive_weight,
        adaptive_bias,
        triple_weight,
        triple_bias,
        output_weight,
        output_bias,
        expand_weight,
        expand_bias,
        shrink_weight,
        shrink_bias,
    ) = weights
    (
        residual,
        normed,
        queries,
        key_flat,
        value_flat,
        gathered,
        attended_f,
        attended,
        log_total,
        branch,
        middle,
        normed_mlp,
        up_proj,
        active,
        lowered,
    ) = saved
    row_count, width = residual.shape
    pieces = [modulation[number * width : (number + 1) * width] for number in range(6)]
    shift_attn, scale_attn, gate_attn, shift_mlp, scale_mlp, gate_mlp = pieces
    gate_mlp_grad = jnp.sum(gradient * lowered, 0)
    lowered_grad = (gradient * gate_mlp).astype(jnp.bfloat16)
    shrink_w_grad = jnp.einsum(
        "tf,td->fd", active, lowered_grad, preferred_element_type=jnp.float32
    )
    shrink_b_grad = jnp.sum(lowered_grad.astype(jnp.float32), 0)
    active_grad = jnp.einsum(
        "td,fd->tf", lowered_grad, shrink_weight[layer_index], preferred_element_type=jnp.float32
    )
    _, gelu_pull = jax.vjp(gelu_tanh, up_proj)
    up_grad = gelu_pull(active_grad)[0].astype(jnp.bfloat16)
    expand_w_grad = jnp.einsum("td,tf->df", normed_mlp, up_grad, preferred_element_type=jnp.float32)
    expand_b_grad = jnp.sum(up_grad.astype(jnp.float32), 0)
    normed_mlp_grad = jnp.einsum(
        "tf,df->td", up_grad, expand_weight[layer_index], preferred_element_type=jnp.float32
    )
    _, mlp_pull = jax.vjp(modulate, middle, shift_mlp, scale_mlp)
    middle_grad, shift_mlp_grad, scale_mlp_grad = mlp_pull(normed_mlp_grad)
    middle_grad = middle_grad + gradient
    gate_attn_grad = jnp.sum(middle_grad * branch, 0)
    branch_grad = (middle_grad * gate_attn).astype(jnp.bfloat16)
    output_w_grad = jnp.einsum(
        "tc,td->cd", attended, branch_grad, preferred_element_type=jnp.float32
    )
    output_b_grad = jnp.sum(branch_grad.astype(jnp.float32), 0)
    attended_grad = jnp.einsum(
        "td,cd->tc", branch_grad, output_weight[layer_index], preferred_element_type=jnp.float32
    )
    attended_grad = attended_grad.astype(jnp.bfloat16).reshape(row_count, HEADS, HEAD_DIM)
    key_all, value_all = (
        lax.all_gather(key_flat, "blk", axis=0, tiled=True),
        lax.all_gather(value_flat, "blk", axis=0, tiled=True),
    )
    query_grad, key_all_grad, value_all_grad = attend_back(
        queries, key_all, value_all, attended_grad, attended_f, log_total, scaling
    )
    key_grad, value_grad = (
        lax.psum_scatter(
            key_all_grad.astype(jnp.bfloat16), "blk", scatter_dimension=0, tiled=True
        ).astype(jnp.float32),
        lax.psum_scatter(
            value_all_grad.astype(jnp.bfloat16), "blk", scatter_dimension=0, tiled=True
        ).astype(jnp.float32),
    )
    mixed_grad = jnp.concatenate(
        [
            unrotate(query_grad, cosine, sine_table).reshape(row_count, width),
            unrotate(key_grad.reshape(row_count, HEADS, HEAD_DIM), cosine, sine_table).reshape(
                row_count, width
            ),
            value_grad,
        ],
        -1,
    ).astype(jnp.bfloat16)
    triple_w_grad = jnp.einsum("td,tc->dc", normed, mixed_grad, preferred_element_type=jnp.float32)
    triple_b_grad = jnp.sum(mixed_grad.astype(jnp.float32), 0)
    normed_grad = jnp.einsum(
        "tc,dc->td", mixed_grad, triple_weight[layer_index], preferred_element_type=jnp.float32
    )
    _, attn_pull = jax.vjp(modulate, residual, shift_attn, scale_attn)
    residual_grad, shift_attn_grad, scale_attn_grad = attn_pull(normed_grad)
    residual_grad = residual_grad + middle_grad
    modulation_grad = jnp.concatenate(
        [
            shift_attn_grad,
            scale_attn_grad,
            gate_attn_grad,
            shift_mlp_grad,
            scale_mlp_grad,
            gate_mlp_grad,
        ],
        0,
    )
    adaptive_w_grad = condition[0][:, None] * modulation_grad[None, :]
    condition_term = jnp.dot(
        adaptive_weight[layer_index].astype(jnp.float32), modulation_grad, precision=HIGHEST
    )
    grad_terms = (
        adaptive_w_grad,
        modulation_grad,
        triple_w_grad,
        triple_b_grad,
        output_w_grad,
        output_b_grad,
        expand_w_grad,
        expand_b_grad,
        shrink_w_grad,
        shrink_b_grad,
    )
    return (residual_grad, grad_terms, condition_term)


def local(
    inputs,
    condition,
    prefix,
    mask_embed,
    adaptive_weight,
    adaptive_bias,
    triple_weight,
    triple_bias,
    output_weight,
    output_bias,
    expand_weight,
    expand_bias,
    shrink_weight,
    shrink_bias,
    cotangent,
):
    weights = (
        adaptive_weight,
        adaptive_bias,
        triple_weight,
        triple_bias,
        output_weight,
        output_bias,
        expand_weight,
        expand_bias,
        shrink_weight,
        shrink_bias,
    )
    row_count = inputs.shape[1]
    offset = lax.axis_index("blk") * row_count
    position = offset + jnp.arange(row_count, dtype=jnp.int32)
    masked = position >= prefix[0]
    residual = jnp.where(
        masked[:, None], mask_embed.astype(jnp.float32)[None, :], inputs[0].astype(jnp.float32)
    )
    cosine, sine_table = tables(offset, row_count, HEAD_DIM)
    scaling = 1.0 / math.sqrt(HEAD_DIM)
    modulations = []
    saved_layers = []
    for layer_index in range(LAYERS):
        modulation = jnp.dot(
            condition, adaptive_weight[layer_index].astype(jnp.float32), precision=HIGHEST
        )[0] + adaptive_bias[layer_index].astype(jnp.float32)
        residual, saved = forward_layer(
            residual, modulation, layer_index, weights, cosine, sine_table, scaling
        )
        modulations.append(modulation)
        saved_layers.append(saved)
    outputs = residual.astype(jnp.bfloat16)[None]
    gradient = cotangent[0].astype(jnp.float32)
    condition_total = jnp.zeros((condition.shape[1],), jnp.float32)
    collected = [None] * LAYERS
    mask_sum = None
    for layer_index in reversed(range(LAYERS)):
        gradient, grad_terms, condition_term = backward_layer(
            gradient,
            modulations[layer_index],
            layer_index,
            weights,
            saved_layers[layer_index],
            cosine,
            sine_table,
            scaling,
            condition,
        )
        condition_total = condition_total + condition_term
        collected[layer_index] = grad_terms
    mask_term = jnp.sum(jnp.where(masked[:, None], gradient, 0.0), 0)
    flat_terms = ()
    for layer_index in range(LAYERS):
        flat_terms = flat_terms + tuple(collected[layer_index])
    summed = lax.psum_scatter(
        flat_terms + (mask_term,), ("blk", "dp"), scatter_dimension=0, tiled=True
    )
    collected = [summed[layer_index * 10 : (layer_index + 1) * 10] for layer_index in range(LAYERS)]
    mask_sum = summed[LAYERS * 10]
    condition_grad = lax.psum(condition_total, "blk")[None, :]
    input_grad = jnp.where(masked[:, None], 0.0, gradient)[None]
    stacked = [
        jnp.stack([collected[layer_index][number] for layer_index in range(LAYERS)], 0)
        for number in range(10)
    ]
    return (
        outputs,
        input_grad,
        condition_grad,
        mask_sum,
        stacked[0],
        stacked[1],
        stacked[2],
        stacked[3],
        stacked[4],
        stacked[5],
        stacked[6],
        stacked[7],
        stacked[8],
        stacked[9],
    )


BF = jnp.bfloat16
F32 = jnp.float32
WIDTH = HEADS * HEAD_DIM
GROUP = WIDTH // 4
VM = pl.BlockSpec(memory_space=pltpu.VMEM)
ANY = pl.BlockSpec(memory_space=pl.ANY)
SM = pl.BlockSpec(memory_space=pltpu.SMEM)
VMEM_LIMIT = 58 * 1024 * 1024
ROOT_TWO_PI = math.sqrt(2.0 / math.pi)
CUBIC = 0.044715


def dot_nn(left, right):
    return jnp.dot(left, right, preferred_element_type=F32)


def dot_nt(left, right):
    return lax.dot_general(left, right, (((1,), (1,)), ((), ())), preferred_element_type=F32)


def dot_tn(left, right):
    return lax.dot_general(left, right, (((0,), (0,)), ((), ())), preferred_element_type=F32)


def normalise(values):
    centered = values - jnp.mean(values, -1, keepdims=True)
    rstd = lax.rsqrt(jnp.mean(centered * centered, -1, keepdims=True) + EPSILON)
    return centered * rstd, rstd


def normalise_back(upstream, unit, rstd):
    first = jnp.mean(upstream, -1, keepdims=True)
    second = jnp.mean(upstream * unit, -1, keepdims=True)
    return rstd * (upstream - first - unit * second)


def column_sum(values):
    return jnp.sum(values, 0, keepdims=True)


def turn(values, cosine, signed_sine):
    lane = lax.broadcasted_iota(jnp.int32, (values.shape[0], 128), 1)
    front = (lane % HEAD_DIM) < HEAD_DIM // 2
    pieces = []
    for start in range(0, values.shape[1], 128):
        piece = values[:, start : start + 128]
        swapped = jnp.where(front, pltpu.roll(piece, 96, 1), pltpu.roll(piece, 32, 1))
        pieces.append(piece * cosine + swapped * signed_sine)
    return jnp.concatenate(pieces, 1)


def piece_of(row, number):
    return row[:, number * WIDTH : (number + 1) * WIDTH]


BIAS_AT = {"triple": (0, 2304), "output": (2304, 3072), "expand": (3072, 6144), "shrink": (6144, 6912)}


def bias_of(bias_ref, layer, name):
    low, high = BIAS_AT[name]
    return bias_ref[layer][:, low:high]


def pack_rows(values):
    half = values.shape[0] // 2
    return jnp.concatenate([values[:half], values[half:]], 1)


def qkv_stage(x, layer, mod_row, bias_ref, triple, cos_ref, sin_ref, me, h_ref, chunk_refs, hold):
    unit, _ = normalise(x)
    h = (unit * (1.0 + piece_of(mod_row, 1)) + piece_of(mod_row, 0)).astype(BF)
    h_ref[...] = h
    bias = bias_of(bias_ref, layer, "triple")
    cosine, sine = cos_ref[0], sin_ref[0]
    parts = []
    for number in range(3):
        columns = slice(number * WIDTH, (number + 1) * WIDTH)
        mixed = dot_nn(h, triple[:, columns]) + bias[:, columns]
        if number < 2:
            mixed = turn(mixed, cosine, sine)
        if number == 0:
            mixed = mixed * HEAD_DIM**-0.5
        parts.append(mixed)
    rows = x.shape[0]
    for group in range(4):
        columns = slice(group * GROUP, (group + 1) * GROUP)
        pair = jnp.concatenate([parts[0][:, columns], parts[1][:, columns]], 1)
        hold[group, 0:rows, :] = pair.astype(BF)
        hold[group, rows : rows + rows // 2, :] = pack_rows(parts[2][:, columns]).astype(BF)
    for place in range(4):
        chunk_refs[place][...] = hold[place ^ me]


def first_kernel(
    scal, inputs, mask_embed, condition, adaptive_weight, adaptive_bias, bias_ref, cos_ref, sin_ref, triple_any,
    x_ref, mod_ref, h_ref, c0, c1, c2, c3,
    triple, hold, sems,
):
    copy = pltpu.make_async_copy(triple_any.at[0], triple, sems.at[0])
    copy.start()
    me = scal[0]
    cond = condition[...]
    upper = cond.astype(BF).astype(F32)
    rest = cond - upper
    mid = rest.astype(BF).astype(F32)
    low = rest - mid
    row = lax.broadcasted_iota(jnp.int32, (8, cond.shape[1]), 0)
    stack = jnp.where(row == 0, upper, jnp.where(row == 1, mid, jnp.where(row == 2, low, 0.0))).astype(BF)
    for layer in range(LAYERS):
        total = column_sum(dot_nn(stack, adaptive_weight[layer]))
        mod_ref[layer] = total + adaptive_bias[layer].astype(F32)
    rows = inputs.shape[1]
    position = me * rows + lax.broadcasted_iota(jnp.int32, (rows, WIDTH), 0)
    x = jnp.where(position >= scal[3], mask_embed[...].astype(F32), inputs[0].astype(F32))
    x_ref[...] = x
    copy.wait()
    qkv_stage(x, 0, mod_ref[0], bias_ref, triple, cos_ref, sin_ref, me, h_ref, (c0, c1, c2, c3), hold)


def attend_kernel(
    c0, c1, c2, c3,
    o0, o1, o2, o3, lse_ref, ot_ref,
    q_all, k_all, v_turned,
):
    rows = c0.shape[1] * 2 // 3
    rows = 256
    for place, chunk in enumerate((c0, c1, c2, c3)):
        span = slice(place * rows, (place + 1) * rows)
        q_all[place] = chunk[0:rows, 0:GROUP]
        k_all[span, :] = chunk[0:rows, GROUP : 2 * GROUP]
        tail = chunk[rows : rows + rows // 2, :]
        v_block = jnp.concatenate([tail[:, 0:GROUP], tail[:, GROUP : 2 * GROUP]], 0)
        v_turned[:, span] = v_block.T
    head = lax.broadcasted_iota(jnp.int32, (rows, GROUP), 1) // HEAD_DIM

    def step(block, carry):
        q = q_all[block]
        for number in range(3):
            masked = jnp.where(head == number, q, jnp.zeros_like(q))
            scores = dot_nt(k_all[...], masked)
            peak = jnp.max(scores, 0, keepdims=True)
            weights = jnp.exp(scores - peak)
            total = jnp.sum(weights, 0, keepdims=True)
            span = slice(number * HEAD_DIM, (number + 1) * HEAD_DIM)
            ot_ref[block, span, :] = dot_nn(v_turned[span, :], weights.astype(BF)) / total
            lse_ref[block, number : number + 1, :] = peak + jnp.log(total)
        return carry

    lax.fori_loop(0, 4, step, 0)
    for place, out in enumerate((o0, o1, o2, o3)):
        out[...] = pack_rows(ot_ref[place].T).astype(BF)


def gather_chunks(refs, hold):
    for place in range(4):
        hold[place] = refs[place][...]


def mlp_forward(
    layer, x, mod_row, bias_ref, me, o_refs, output, expand, shrink, waits, hold, o_ref, aout_ref, m_ref, h2_ref,
    z_ref, slope_ref, f_ref,
):
    gather_chunks(o_refs, hold)
    rows = x.shape[0]
    half = rows // 2
    for group in range(4):
        chunk = hold[group ^ me]
        columns = slice(group * GROUP, (group + 1) * GROUP)
        o_ref[0:half, columns] = chunk[:, 0:GROUP]
        o_ref[half:rows, columns] = chunk[:, GROUP : 2 * GROUP]
    waits[0].wait()
    a_out = dot_nn(o_ref[...], output[...]) + bias_of(bias_ref, layer, "output")
    aout_ref[...] = a_out.astype(BF)
    m = x + piece_of(mod_row, 2) * a_out
    m_ref[...] = m
    unit, _ = normalise(m)
    h2 = (unit * (1.0 + piece_of(mod_row, 4)) + piece_of(mod_row, 3)).astype(BF)
    h2_ref[...] = h2
    waits[1].wait()
    bias = bias_of(bias_ref, layer, "expand")
    f = bias_of(bias_ref, layer, "shrink")
    hidden = expand.shape[1]
    for start in range(0, hidden, 768):
        if start == 0:
            waited = False
        columns = slice(start, start + 768)
        u = dot_nn(h2, expand[:, columns]) + bias[:, columns]
        square = u * u
        gate = 0.5 + 0.5 * jnp.tanh(u * (ROOT_TWO_PI + ROOT_TWO_PI * CUBIC * square))
        active = u * gate
        slope = gate + 2.0 * active * (1.0 - gate) * (ROOT_TWO_PI + 3.0 * ROOT_TWO_PI * CUBIC * square)
        z = active.astype(BF)
        z_ref[:, columns] = z
        slope_ref[:, columns] = slope.astype(BF)
        if not waited:
            waits[2].wait()
            waited = True
        f = f + dot_nn(z, shrink[columns, :])
    f_ref[...] = f.astype(BF)
    return m + piece_of(mod_row, 5) * f


def share(values, hold, core, mine_ref, theirs_ref):
    half = values.shape[1] // 2
    hold[0] = values[:, 0:half]
    hold[1] = values[:, half : 2 * half]
    mine_ref[...] = hold[core]
    theirs_ref[...] = hold[1 - core]


def mlp_backward(
    dy, mod_row, me, core, m_ref, f_ref, slope_ref, aout_ref, output, expand, shrink, waits, hold, holds,
    df_refs, du_refs, da_refs, do_refs, dm_ref, vec_ref,
):
    def put(place, row):
        vec_ref[:, place : place + row.shape[1]] = row

    put(0, column_sum(dy * f_ref[...].astype(F32)))
    df = (dy * piece_of(mod_row, 5)).astype(BF)
    put(3072, column_sum(df.astype(F32)))
    share(df, holds[0], core, *df_refs)
    hidden = expand.shape[1]
    dh2 = jnp.zeros(dy.shape, F32)
    waits[2].wait()
    for start in range(0, hidden, 768):
        columns = slice(start, start + 768)
        dz = dot_nt(df, shrink[columns, :])
        du = (slope_ref[:, columns].astype(F32) * dz).astype(BF)
        put(3840 + start, column_sum(du.astype(F32)))
        half = hidden // 2
        holds[1][start // half, :, start % half : start % half + 768] = du
        if start == 0:
            waits[1].wait()
        dh2 = dh2 + dot_nt(du, expand[:, columns])
    du_refs[0][...] = holds[1][core]
    du_refs[1][...] = holds[1][1 - core]
    unit, rstd = normalise(m_ref[...])
    put(768, column_sum(dh2))
    put(1536, column_sum(dh2 * unit))
    dm = dy + normalise_back(dh2 * (1.0 + piece_of(mod_row, 4)), unit, rstd)
    dm_ref[...] = dm
    put(2304, column_sum(dm * aout_ref[...].astype(F32)))
    da = (dm * piece_of(mod_row, 2)).astype(BF)
    put(6912, column_sum(da.astype(F32)))
    share(da, holds[2], core, *da_refs)
    waits[0].wait()
    do = dot_nt(da, output[...])
    for group in range(4):
        hold[group] = pack_rows(do[:, group * GROUP : (group + 1) * GROUP]).astype(BF)
    for place in range(4):
        do_refs[place][...] = hold[place ^ me]


def attend_back_kernel(
    c0, c1, c2, c3, d0, d1, d2, d3, lse_ref, ot_ref, cos_ref, sin_ref,
    g0, g1, g2, g3,
    q_masked, do_masked, k_all, v_all, k_turned, lse_rows, delta_rows, dq_turned, dk_all, dv_all,
):
    rows = 256
    head = lax.broadcasted_iota(jnp.int32, (rows, GROUP), 1) // HEAD_DIM
    for place in range(4):
        chunk = (c0, c1, c2, c3)[place]
        given = (d0, d1, d2, d3)[place][...]
        span = slice(place * rows, (place + 1) * rows)
        q = chunk[0:rows, 0:GROUP]
        k = chunk[0:rows, GROUP : 2 * GROUP]
        tail = chunk[rows : rows + rows // 2, :]
        v_all[place] = jnp.concatenate([tail[:, 0:GROUP], tail[:, GROUP : 2 * GROUP]], 0)
        k_all[place] = k
        k_turned[place] = k.T
        do = jnp.concatenate([given[:, 0:GROUP], given[:, GROUP : 2 * GROUP]], 0)
        product = do.astype(F32).T * ot_ref[place]
        for number in range(3):
            q_masked[number, span, :] = jnp.where(head == number, q, jnp.zeros_like(q))
            do_masked[number, span, :] = jnp.where(head == number, do, jnp.zeros_like(do))
            part = product[number * HEAD_DIM : (number + 1) * HEAD_DIM, :]
            delta_rows[number : number + 1, span] = jnp.sum(part, 0, keepdims=True)
            lse_rows[number : number + 1, span] = lse_ref[place, number : number + 1, :]
    dq_turned[...] = jnp.zeros(dq_turned.shape, F32)

    def step(block, carry):
        k = k_all[block]
        v = v_all[block]
        dk = jnp.zeros((rows, GROUP), F32)
        dv = jnp.zeros((rows, GROUP), F32)
        for number in range(3):
            span = slice(number * HEAD_DIM, (number + 1) * HEAD_DIM)
            scores = dot_nt(k, q_masked[number])
            probs = jnp.exp(scores - lse_rows[number : number + 1, :])
            prob_grad = dot_nt(v, do_masked[number])
            score_grad = (probs * (prob_grad - delta_rows[number : number + 1, :])).astype(BF)
            dv = dv + dot_nn(probs.astype(BF), do_masked[number])
            dk = dk + dot_nn(score_grad, q_masked[number])
            dq_turned[span, :] += dot_nn(k_turned[block, span, :], score_grad)
        dk_all[block] = dk
        dv_all[block] = dv
        return carry

    lax.fori_loop(0, 4, step, 0)
    for place, out in enumerate((g0, g1, g2, g3)):
        span = slice(place * rows, (place + 1) * rows)
        dq = dq_turned[:, span].T * HEAD_DIM**-0.5
        pair = jnp.concatenate([dq, dk_all[place]], 1)
        out[0:rows, :] = turn(pair, cos_ref[place], -sin_ref[place]).astype(BF)
        out[rows : rows + rows // 2, :] = pack_rows(dv_all[place]).astype(BF)


def qkv_backward(x, dm, mod_row, me, core, g_refs, triple, wait, hold, share_hold, full, dqkv_refs, vec_ref):
    gather_chunks(g_refs, hold)
    rows = x.shape[0]
    half = rows // 2
    for group in range(4):
        chunk = hold[group ^ me]
        low = group * GROUP
        full[:, low : low + GROUP] = chunk[0:rows, 0:GROUP]
        full[:, WIDTH + low : WIDTH + low + GROUP] = chunk[0:rows, GROUP : 2 * GROUP]
        full[0:half, 2 * WIDTH + low : 2 * WIDTH + low + GROUP] = chunk[rows : rows + half, 0:GROUP]
        full[half:rows, 2 * WIDTH + low : 2 * WIDTH + low + GROUP] = chunk[rows : rows + half, GROUP : 2 * GROUP]
    dqkv = full[...]
    share(dqkv, share_hold, core, *dqkv_refs)
    vec_ref[:, 1536:3840] = column_sum(dqkv.astype(F32))
    wait.wait()
    dh = dot_nt(dqkv, triple[...])
    unit, rstd = normalise(x)
    vec_ref[:, 0:768] = column_sum(dh)
    vec_ref[:, 768:1536] = column_sum(dh * unit)
    return dm + normalise_back(dh * (1.0 + piece_of(mod_row, 1)), unit, rstd)


def fetch(pairs, sems):
    copies = []
    for number, (source, target) in enumerate(pairs):
        copy = pltpu.make_async_copy(source, target, sems.at[number])
        copy.start()
        copies.append(copy)
    return copies


class Done:
    def wait(self):
        pass


def middle_kernel(
    scal, x_ref, mod_ref, bias_ref, cos_ref, sin_ref, o0, o1, o2, o3, output_any, expand_any, shrink_any, triple_any,
    o_ref, aout_ref, m_ref, h2_ref, z_ref, slope_ref, f_ref, y_ref, h_ref, c0, c1, c2, c3,
    output, expand, shrink, triple, o_hold, c_hold, sems,
):
    copies = fetch(
        [(output_any.at[0], output), (expand_any.at[0], expand), (shrink_any.at[0], shrink), (triple_any.at[1], triple)],
        sems,
    )
    me = scal[0]
    y = mlp_forward(
        0, x_ref[...], mod_ref[0], bias_ref, me, (o0, o1, o2, o3), output, expand, shrink, copies, o_hold, o_ref,
        aout_ref, m_ref, h2_ref, z_ref, slope_ref, f_ref,
    )
    y_ref[...] = y
    copies[3].wait()
    qkv_stage(y, 1, mod_ref[1], bias_ref, triple, cos_ref, sin_ref, me, h_ref, (c0, c1, c2, c3), c_hold)


def peak_kernel(
    scal, x_ref, mod_ref, bias_ref, cotangent, o0, o1, o2, o3, output_any, expand_any, shrink_any,
    out_ref, o_ref, h2_ref, z_ref, dfm, dft, dum, dut, dam, dat, d0, d1, d2, d3, dm_ref, vec_ref,
    output, expand, shrink, o_hold, m_ref, aout_ref, slope_ref, f_ref, df_hold, du_hold, da_hold, sems,
):
    copies = fetch([(output_any.at[1], output), (expand_any.at[1], expand), (shrink_any.at[1], shrink)], sems)
    me, core = scal[0], scal[2]
    y = mlp_forward(
        1, x_ref[...], mod_ref[1], bias_ref, me, (o0, o1, o2, o3), output, expand, shrink, copies, o_hold, o_ref,
        aout_ref, m_ref, h2_ref, z_ref, slope_ref, f_ref,
    )
    out_ref[0] = y.astype(BF)
    mlp_backward(
        cotangent[0].astype(F32), mod_ref[1], me, core, m_ref, f_ref, slope_ref, aout_ref, output, expand, shrink,
        [Done()] * 3, o_hold, (df_hold, du_hold, da_hold), (dfm, dft), (dum, dut), (dam, dat), (d0, d1, d2, d3),
        dm_ref, vec_ref,
    )


def back_kernel(
    scal, x_ref, dm_in, mod_ref, g0, g1, g2, g3, m_ref, f_ref, slope_ref, aout_ref,
    triple_any, output_any, expand_any, shrink_any,
    dqm, dqt, vec_first, dfm, dft, dum, dut, dam, dat, d0, d1, d2, d3, dm_ref, vec_ref,
    triple, output, expand, shrink, g_hold, dq_hold, full, o_hold, df_hold, du_hold, da_hold, sems,
):
    copies = fetch(
        [(triple_any.at[1], triple), (shrink_any.at[0], shrink), (expand_any.at[0], expand), (output_any.at[0], output)],
        sems,
    )
    me, core = scal[0], scal[2]
    dy = qkv_backward(
        x_ref[...], dm_in[...], mod_ref[1], me, core, (g0, g1, g2, g3), triple, copies[0], g_hold, dq_hold, full,
        (dqm, dqt), vec_first,
    )
    mlp_backward(
        dy, mod_ref[0], me, core, m_ref, f_ref, slope_ref, aout_ref, output, expand, shrink,
        [copies[3], copies[2], copies[1]], o_hold, (df_hold, du_hold, da_hold), (dfm, dft), (dum, dut), (dam, dat),
        (d0, d1, d2, d3), dm_ref, vec_ref,
    )


def last_kernel(
    scal, x_ref, dm_in, mod_ref, g0, g1, g2, g3, triple_any,
    dqm, dqt, vec_first, input_grad, mask_ref,
    triple, g_hold, dq_hold, full, sems,
):
    copies = fetch([(triple_any.at[0], triple)], sems)
    me, core = scal[0], scal[2]
    dx = qkv_backward(
        x_ref[...], dm_in[...], mod_ref[0], me, core, (g0, g1, g2, g3), triple, copies[0], g_hold, dq_hold, full,
        (dqm, dqt), vec_first,
    )
    rows = dx.shape[0]
    position = me * rows + lax.broadcasted_iota(jnp.int32, dx.shape, 0)
    masked = position >= scal[3]
    input_grad[0] = jnp.where(masked, 0.0, dx)
    mask_ref[...] = column_sum(jnp.where(masked, dx, 0.0))


BIT = {"x": 4, "y": 8, "a": 1, "b": 2}
ORDERS = ("xyab", "yxab", "abxy")
STEP = {"x": ("blk", 1), "y": ("blk", 2), "a": ("dp", 2), "b": ("dp", 4)}


def place_at(order, index):
    place = 0
    for depth, name in enumerate(order):
        if index & (8 >> depth):
            place |= BIT[name]
    return place


def deliver(result, rows, me16, send_ref, keep_ref, order, row_at, lane_at):
    for index in range(16):
        source = pl.multiple_of((place_at(order, index) ^ me16) * rows, 16)
        block = result[pl.ds(source, rows), lane_at : lane_at + 128]
        if index < 8:
            keep_ref[index, row_at : row_at + rows, :] = block
        else:
            send_ref[index - 8, row_at : row_at + rows, :] = block


def weights_kernel(
    counts, scal, a_own, a_far, b_own, b_far, e_own, e_far, g_own, g_far, *rest
):
    sends, keeps = rest[0:3], rest[3:6]
    first, second = rest[6:8]
    me16 = scal[0] * 4 + scal[1]
    per_first, per_second = counts
    first_rows, second_rows = a_own.shape[1] // 16, e_own.shape[1] // 16
    a = jnp.concatenate([a_own[...], a_far[...]], 0)
    e = jnp.concatenate([e_own[...], e_far[...]], 0)
    for part in range(3):
        order = ORDERS[part]
        width = per_first * 128
        columns = slice(part * width, (part + 1) * width)
        b = jnp.concatenate([b_own[:, columns], b_far[:, columns]], 0)
        first[...] = dot_tn(a, b).astype(BF)
        row = 0
        for number in range(per_first):
            deliver(first, first_rows, me16, sends[part], keeps[part], order, row, number * 128)
            row += first_rows
        width = per_second * 128
        columns = slice(part * width, (part + 1) * width)
        g = jnp.concatenate([g_own[:, columns], g_far[:, columns]], 0)
        second[...] = dot_tn(e, g).astype(BF)
        for number in range(per_second):
            deliver(second, second_rows, me16, sends[part], keeps[part], order, row, number * 128)
            row += second_rows


def shaped(*shape, dtype=F32):
    return jax.ShapeDtypeStruct(shape, dtype)


def call(kernel, specs, outs, scratch, cost, name):
    flops, moved = cost
    return pl.pallas_call(
        kernel,
        in_specs=specs,
        out_specs=[VM] * len(outs),
        out_shape=outs,
        scratch_shapes=scratch,
        compiler_params=pltpu.CompilerParams(vmem_limit_bytes=VMEM_LIMIT),
        cost_estimate=pl.CostEstimate(flops=int(flops), bytes_accessed=int(moved), transcendentals=0),
        name=name,
    )


def swap(values, axis, bit):
    size = 4 if axis == "blk" else 8
    return lax.ppermute(values, axis, [(i, i ^ bit) for i in range(size)])


def swap_chunks(chunks):
    return [chunks[0]] + [swap(chunks[place], "blk", place) for place in (1, 2, 3)]


def scatter_part(keep, send, order):
    held = [keep, swap(send, *STEP[order[0]])]
    for name in order[1:]:
        half = held[0].shape[0] // 2
        out = sum(piece[half:].astype(F32) for piece in held).astype(BF)
        held = [piece[:half] for piece in held]
        held.append(swap(out, *STEP[name]))
    return sum(piece[0].astype(F32) for piece in held)


def settle(units, core):
    rows = units.shape[1] // 2
    mine = lax.dynamic_slice_in_dim(units, core * rows, rows, 1)
    theirs = lax.dynamic_slice_in_dim(units, (1 - core) * rows, rows, 1)
    got = swap(theirs, "dp", 1)
    low = jnp.where(core == 0, mine, got)
    high = jnp.where(core == 0, got, mine)
    both = jnp.concatenate([low, high], 0)
    return jnp.transpose(both, (1, 0, 2)).reshape(rows, both.shape[0] * 128)


def weight_gradients(scal, core, a, b, e, g, counts, name):
    a_width, e_width = a[0].shape[1], e[0].shape[1]
    rows = counts[0] * a_width // 16 + counts[1] * e_width // 16
    shapes = [shaped(8, rows, 128, dtype=BF)] * 6
    flops = 2 * 512 * (a_width * b[0].shape[1] + e_width * g[0].shape[1])
    outs = call(
        functools.partial(weights_kernel, counts),
        [SM] + [VM] * 8,
        shapes,
        [pltpu.VMEM((a_width, counts[0] * 128), BF), pltpu.VMEM((e_width, counts[1] * 128), BF)],
        (flops, 2 * flops // 512),
        name,
    )(scal, *a, *b, *e, *g)
    first, second = [], []
    a_rows, e_rows = a_width // 16, e_width // 16
    for part in range(3):
        total = scatter_part(outs[3 + part], outs[part], ORDERS[part])
        cut = counts[0] * a_rows
        first.append(total[:cut].reshape(counts[0], a_rows, 128))
        second.append(total[cut:].reshape(counts[1], e_rows, 128))
    return settle(jnp.concatenate(first, 0), core), settle(jnp.concatenate(second, 0), core)


def local_fast(
    inputs, condition, prefix, mask_embed, adaptive_weight, adaptive_bias, triple_weight, triple_bias, output_weight,
    output_bias, expand_weight, expand_bias, shrink_weight, shrink_bias, cotangent,
):
    rows = inputs.shape[1]
    hidden = expand_weight.shape[2]
    blk, dp = lax.axis_index("blk"), lax.axis_index("dp")
    core = dp % 2
    scal = jnp.stack([blk, dp // 2, core, prefix[0]]).astype(jnp.int32)
    start = (blk ^ jnp.arange(4, dtype=jnp.int32)) * rows
    position = (start[:, None] + jnp.arange(rows, dtype=jnp.int32)[None, :]).astype(F32)
    lane = jnp.arange(128, dtype=jnp.int32)
    frequency = jnp.exp((lane % 32).astype(F32) * (-2.0 * math.log(10000.0) / HEAD_DIM))
    angles = position[:, :, None] * frequency
    cosine = jnp.cos(angles)
    sine = jnp.sin(angles) * jnp.where(lane % 64 < 32, -1.0, 1.0)
    biases = jnp.concatenate(
        [part.astype(F32) for part in (triple_bias, output_bias, expand_bias, shrink_bias)], 1
    )[:, None, :]
    conditions = lax.all_gather(condition[0], "dp", axis=0)

    f_square = shaped(rows, WIDTH)
    b_square = shaped(rows, WIDTH, dtype=BF)
    b_tall = shaped(rows, hidden, dtype=BF)
    packed = rows + rows // 2
    chunk = shaped(packed, 2 * GROUP, dtype=BF)
    o_chunk = shaped(rows // 2, 2 * GROUP, dtype=BF)
    c_hold = pltpu.VMEM((4, packed, 2 * GROUP), BF)
    o_hold = pltpu.VMEM((4, rows // 2, 2 * GROUP), BF)
    triple_hold = pltpu.VMEM((WIDTH, 3 * WIDTH), BF)
    output_hold = pltpu.VMEM((WIDTH, WIDTH), BF)
    expand_hold = pltpu.VMEM((WIDTH, hidden), BF)
    shrink_hold = pltpu.VMEM((hidden, WIDTH), BF)

    def halved(width):
        return pltpu.VMEM((2, rows, width // 2), BF)

    def half_pair(width):
        return [shaped(rows, width // 2, dtype=BF)] * 2

    product = 2 * rows * WIDTH
    qkv_cost = product * 3 * WIDTH
    mlp_cost = product * (WIDTH + 2 * hidden)

    x0, mod, h0, *chunks = call(
        first_kernel,
        [SM] + [VM] * 8 + [ANY],
        [f_square, shaped(LAYERS, 1, 6 * WIDTH), b_square] + [chunk] * 4,
        [triple_hold, c_hold, pltpu.SemaphoreType.DMA((1,))],
        (qkv_cost, 12e6),
        "qkv_first",
    )(
        scal, inputs, mask_embed[None], condition, adaptive_weight, adaptive_bias[:, None, :], biases, cosine, sine,
        triple_weight,
    )

    def attend(chunks):
        return call(
            attend_kernel,
            [VM] * 4,
            [o_chunk] * 4 + [shaped(4, 8, rows), shaped(4, GROUP, rows)],
            [
                pltpu.VMEM((4, rows, GROUP), BF),
                pltpu.VMEM((4 * rows, GROUP), BF),
                pltpu.VMEM((GROUP, 4 * rows), BF),
            ],
            (6e9, 6e6),
            "attend",
        )(*chunks)

    def attend_back(chunks, given, lse, turned):
        return call(
            attend_back_kernel,
            [VM] * 12,
            [chunk] * 4,
            [
                pltpu.VMEM((3, 4 * rows, GROUP), BF),
                pltpu.VMEM((3, 4 * rows, GROUP), BF),
                pltpu.VMEM((4, rows, GROUP), BF),
                pltpu.VMEM((4, rows, GROUP), BF),
                pltpu.VMEM((4, GROUP, rows), BF),
                pltpu.VMEM((8, 4 * rows), F32),
                pltpu.VMEM((8, 4 * rows), F32),
                pltpu.VMEM((GROUP, 4 * rows), F32),
                pltpu.VMEM((4, rows, GROUP), F32),
                pltpu.VMEM((4, rows, GROUP), F32),
            ],
            (15e9, 10e6),
            "attend_back",
        )(*chunks, *given, lse, turned, cosine, sine)

    chunks0 = swap_chunks(chunks)
    *o_chunks, lse0, turned0 = attend(chunks0)
    o_chunks = swap_chunks(o_chunks)
    o0, aout0, m0, h20, z0, slope0, f0, x1, h1, *chunks = call(
        middle_kernel,
        [SM] + [VM] * 9 + [ANY] * 4,
        [b_square, b_square, f_square, b_square, b_tall, b_tall, b_square, f_square, b_square] + [chunk] * 4,
        [output_hold, expand_hold, shrink_hold, triple_hold, o_hold, c_hold, pltpu.SemaphoreType.DMA((4,))],
        (qkv_cost + mlp_cost, 25e6),
        "mlp_qkv",
    )(scal, x0, mod, biases, cosine, sine, *o_chunks, output_weight, expand_weight, shrink_weight, triple_weight)
    chunks1 = swap_chunks(chunks)
    *o_chunks, lse1, turned1 = attend(chunks1)
    o_chunks = swap_chunks(o_chunks)
    back_outs = half_pair(WIDTH) + half_pair(hidden) + half_pair(WIDTH) + [o_chunk] * 4 + [f_square, shaped(1, 7680)]
    back_holds = [halved(WIDTH), halved(hidden), halved(WIDTH)]
    outputs, o1, h21, z1, dfm1, dft1, dum1, dut1, dam1, dat1, *given, dm1, vec1 = call(
        peak_kernel,
        [SM] + [VM] * 8 + [ANY] * 3,
        [shaped(1, rows, WIDTH, dtype=BF), b_square, b_square, b_tall] + back_outs,
        [output_hold, expand_hold, shrink_hold, o_hold]
        + [
            pltpu.VMEM((rows, WIDTH), F32),
            pltpu.VMEM((rows, WIDTH), BF),
            pltpu.VMEM((rows, hidden), BF),
            pltpu.VMEM((rows, WIDTH), BF),
        ]
        + back_holds
        + [pltpu.SemaphoreType.DMA((3,))],
        (2 * mlp_cost, 25e6),
        "mlp_turn",
    )(scal, x1, mod, biases, cotangent, *o_chunks, output_weight, expand_weight, shrink_weight)

    def far(values):
        return swap(values, "dp", 1)

    given = swap_chunks(given)
    h2_far1, z_far1, h_far1, o_far1 = far(h21), far(z1), far(h1), far(o1)
    h2_far0, z_far0, h_far0, o_far0 = far(h20), far(z0), far(h0), far(o0)
    expand1, shrink1 = weight_gradients(
        scal, core, (h21, h2_far1), (dum1, far(dut1)), (z1, z_far1), (dfm1, far(dft1)), (4, 1), "mlp_weights"
    )
    grads = attend_back(chunks1, given, lse1, turned1)
    grads = swap_chunks(grads)
    dqm1, dqt1, first1, dfm0, dft0, dum0, dut0, dam0, dat0, *given, dm0, vec0 = call(
        back_kernel,
        [SM] + [VM] * 11 + [ANY] * 4,
        half_pair(3 * WIDTH) + [shaped(1, 3840)] + back_outs,
        [triple_hold, output_hold, expand_hold, shrink_hold, c_hold, halved(3 * WIDTH)]
        + [pltpu.VMEM((rows, 3 * WIDTH), BF), o_hold]
        + back_holds
        + [pltpu.SemaphoreType.DMA((4,))],
        (qkv_cost + mlp_cost, 25e6),
        "qkv_mlp_back",
    )(
        scal, x1, dm1, mod, *grads, m0, f0, slope0, aout0, triple_weight, output_weight, expand_weight, shrink_weight
    )
    given = swap_chunks(given)
    triple1, output1 = weight_gradients(
        scal, core, (h1, h_far1), (dqm1, far(dqt1)), (o1, o_far1), (dam1, far(dat1)), (3, 1), "attention_weights"
    )
    expand0, shrink0 = weight_gradients(
        scal, core, (h20, h2_far0), (dum0, far(dut0)), (z0, z_far0), (dfm0, far(dft0)), (4, 1), "mlp_weights"
    )
    grads = attend_back(chunks0, given, lse0, turned0)
    grads = swap_chunks(grads)
    dqm0, dqt0, first0, input_grad, mask_term = call(
        last_kernel,
        [SM] + [VM] * 7 + [ANY],
        half_pair(3 * WIDTH) + [shaped(1, 3840), shaped(1, rows, WIDTH), shaped(1, WIDTH)],
        [triple_hold, c_hold, halved(3 * WIDTH), pltpu.VMEM((rows, 3 * WIDTH), BF), pltpu.SemaphoreType.DMA((1,))],
        (qkv_cost, 10e6),
        "qkv_back",
    )(scal, x0, dm0, mod, *grads, triple_weight)
    triple0, output0 = weight_gradients(
        scal, core, (h0, h_far0), (dqm0, far(dqt0)), (o0, o_far0), (dam0, far(dat0)), (3, 1), "attention_weights"
    )

    small = jnp.concatenate([first0, vec0, first1, vec1, mask_term], 1)
    small = small + swap(small, "blk", 1)
    small = small + swap(small, "blk", 2)
    dmods, sums = [], []
    for layer in range(LAYERS):
        first = small[:, layer * 11520 : layer * 11520 + 3840]
        vec = small[:, layer * 11520 + 3840 : (layer + 1) * 11520]
        dmods += [first[:, 0:1536], vec[:, 2304:3072], vec[:, 768:2304], vec[:, 0:768]]
        sums += [first[:, 1536:3840], vec[:, 6912:7680], vec[:, 3840:6912], vec[:, 3072:3840]]
    dmod = jnp.concatenate(dmods, 1)
    total = jnp.concatenate(sums + [small[:, 2 * 11520 :]], 1)
    condition_grad = sum(
        lax.dot_general(
            dmod[:, layer * 6 * WIDTH : (layer + 1) * 6 * WIDTH],
            adaptive_weight[layer].astype(F32),
            (((1,), (1,)), ((), ())),
            precision=HIGHEST,
        )
        for layer in range(LAYERS)
    )
    gathered = dmod
    for bit in (1, 2, 4):
        gathered = jnp.concatenate([gathered, swap(gathered, "dp", bit)], 0)
        total = total + swap(total, "dp", bit)
    index = blk * 8 + dp
    share_rows = condition.shape[1] // 32
    near = conditions[dp ^ jnp.arange(8, dtype=jnp.int32)]
    near = lax.dynamic_slice_in_dim(near, index * share_rows, share_rows, 1)
    adaptive_w = jnp.sum(near[:, :, None] * gathered[:, None, :], 0)
    adaptive_w = jnp.stack([adaptive_w[:, : 6 * WIDTH], adaptive_w[:, 6 * WIDTH :]], 0)
    adaptive_all = jnp.sum(gathered, 0)

    def cut(values):
        size = values.shape[0] // 32
        return lax.dynamic_slice_in_dim(values, index * size, size, 0)

    adaptive_b = jnp.stack([cut(adaptive_all[: 6 * WIDTH]), cut(adaptive_all[6 * WIDTH :])], 0)
    total = total[0]
    bias_grads = []
    for low, high in BIAS_AT.values():
        bias_grads.append(jnp.stack([cut(total[low:high]), cut(total[6912 + low : 6912 + high])], 0))
    mask_sum = cut(total[2 * 6912 :])
    return (
        outputs,
        input_grad,
        condition_grad,
        mask_sum,
        adaptive_w,
        adaptive_b,
        jnp.stack([triple0, triple1], 0),
        bias_grads[0],
        jnp.stack([output0, output1], 0),
        bias_grads[1],
        jnp.stack([expand0, expand1], 0),
        bias_grads[2],
        jnp.stack([shrink0, shrink1], 0),
        bias_grads[3],
    )


def solution(mesh):
    in_specs = (
        P("dp", "blk", None),
        P("dp", None),
        P("dp"),
        P(),
        P(),
        P(),
        P(),
        P(),
        P(),
        P(),
        P(),
        P(),
        P(),
        P(),
        P("dp", "blk", None),
    )
    out_specs = (
        P("dp", "blk", None),
        P("dp", "blk", None),
        P("dp", None),
        P(("blk", "dp")),
        P(None, ("blk", "dp"), None),
        P(None, ("blk", "dp")),
        P(None, ("blk", "dp"), None),
        P(None, ("blk", "dp")),
        P(None, ("blk", "dp"), None),
        P(None, ("blk", "dp")),
        P(None, ("blk", "dp"), None),
        P(None, ("blk", "dp")),
        P(None, ("blk", "dp"), None),
        P(None, ("blk", "dp")),
    )
    whole = mesh.shape["blk"] == 4 and mesh.shape["dp"] == 8
    body = local_fast if whole else local
    return jax.shard_map(body, mesh=mesh, in_specs=in_specs, out_specs=out_specs, check_vma=False)
```

```python
import functools
import math

import jax
import jax.numpy as jnp
from jax import lax
from jax.experimental import pallas as pl
from jax.experimental.pallas import tpu as pltpu
from jax.sharding import PartitionSpec as P

HEADS = 12
HEAD_DIM = 64
LAYERS = 2


HIGHEST = lax.Precision.HIGHEST
EPSILON = 1e-06


def modulate(residual, shift, scaling):
    average = jnp.mean(residual, -1, keepdims=True)
    centered = residual - average
    variance = jnp.mean(centered * centered, -1, keepdims=True)
    return centered * lax.rsqrt(variance + EPSILON) * (1.0 + scaling) + shift


def gelu_tanh(values):
    return jax.nn.gelu(values, approximate=True)


def tables(offset, row_count, head_dim):
    half_dim = head_dim // 2
    position = (offset + jnp.arange(row_count, dtype=jnp.int32)).astype(jnp.float32)
    frequency = jnp.exp(
        jnp.arange(half_dim, dtype=jnp.float32) * (-2.0 * math.log(10000.0) / head_dim)
    )
    angles = position[:, None] * frequency[None, :]
    return (jnp.cos(angles)[:, None, :], jnp.sin(angles)[:, None, :])


def rotate(vectors, cosine, sine_table):
    half_dim = vectors.shape[-1] // 2
    front_half = vectors[..., :half_dim]
    back_half = vectors[..., half_dim:]
    return jnp.concatenate(
        [
            front_half * cosine - back_half * sine_table,
            back_half * cosine + front_half * sine_table,
        ],
        -1,
    )


def unrotate(gradient, cosine, sine_table):
    half_dim = gradient.shape[-1] // 2
    front_half = gradient[..., :half_dim]
    back_half = gradient[..., half_dim:]
    return jnp.concatenate(
        [
            front_half * cosine + back_half * sine_table,
            back_half * cosine - front_half * sine_table,
        ],
        -1,
    )


def split_einsum(form, float_left, low_right):
    upper = float_left.astype(jnp.bfloat16)
    lower = (float_left - upper.astype(jnp.float32)).astype(jnp.bfloat16)
    first = jnp.einsum(form, upper, low_right, preferred_element_type=jnp.float32)
    return first + jnp.einsum(form, lower, low_right, preferred_element_type=jnp.float32)


def fold_keys(queries, scaling):

    def absorb(carried, key_piece, offset):
        key_flat, value_flat = key_piece
        piece_rows = key_flat.shape[0]
        block_rows = math.gcd(piece_rows, 512)
        key_blocks = key_flat.reshape(piece_rows // block_rows, block_rows, HEADS, HEAD_DIM)
        value_blocks = value_flat.reshape(piece_rows // block_rows, block_rows, HEADS, HEAD_DIM)

        def absorb_inner(running, block_pair):
            running_max, running_sum, weighted = running
            key_block, value_block = block_pair
            scores = (
                jnp.einsum("qhd,khd->hqk", queries, key_block, preferred_element_type=jnp.float32)
                * scaling
            )
            new_max = jnp.maximum(running_max, jnp.max(scores, -1))
            weights = jnp.exp(scores - new_max[..., None])
            factor = jnp.exp(running_max - new_max)
            running_sum = running_sum * factor + jnp.sum(weights, -1)
            weighted = weighted * factor[..., None] + split_einsum(
                "hqk,khd->hqd", weights, value_block
            )
            return ((new_max, running_sum, weighted), None)

        carried, _ = lax.scan(absorb_inner, carried, (key_blocks, value_blocks))
        return carried

    return absorb


def attend_back(queries, key_all, value_all, out_gradient, attended_f, log_total, scaling):
    row_count = queries.shape[0]
    all_rows = key_all.shape[0]
    block_rows = math.gcd(all_rows, 512)
    key_blocks = key_all.reshape(all_rows // block_rows, block_rows, HEADS, HEAD_DIM)
    value_blocks = value_all.reshape(all_rows // block_rows, block_rows, HEADS, HEAD_DIM)
    out_float = out_gradient.astype(jnp.float32)
    row_delta = jnp.transpose(jnp.sum(out_float * attended_f, -1), (1, 0))

    def attend_inner(query_grad, block_pair):
        key_block, value_block = block_pair
        scores = (
            jnp.einsum("qhd,khd->hqk", queries, key_block, preferred_element_type=jnp.float32)
            * scaling
        )
        probs = jnp.exp(scores - log_total[..., None])
        prob_grad = jnp.einsum(
            "qhd,khd->hqk", out_gradient, value_block, preferred_element_type=jnp.float32
        )
        score_grad = (probs * (prob_grad - row_delta[..., None])).astype(jnp.bfloat16)
        query_grad = query_grad + jnp.einsum(
            "hqk,khd->qhd", score_grad, key_block, preferred_element_type=jnp.float32
        )
        key_grad = (
            jnp.einsum("hqk,qhd->khd", score_grad, queries, preferred_element_type=jnp.float32)
            * scaling
        )
        value_grad = split_einsum("hqk,qhd->khd", probs, out_gradient)
        return (query_grad, (key_grad, value_grad))

    start_grad = jnp.zeros((row_count, HEADS, HEAD_DIM), jnp.float32)
    query_grad, (key_grads, value_grads) = lax.scan(
        attend_inner, start_grad, (key_blocks, value_blocks)
    )
    width = HEADS * HEAD_DIM
    return (
        query_grad * scaling,
        key_grads.reshape(all_rows, width),
        value_grads.reshape(all_rows, width),
    )


def forward_layer(residual, modulation, layer_index, weights, cosine, sine_table, scaling):
    (
        adaptive_weight,
        adaptive_bias,
        triple_weight,
        triple_bias,
        output_weight,
        output_bias,
        expand_weight,
        expand_bias,
        shrink_weight,
        shrink_bias,
    ) = weights
    row_count, width = residual.shape
    pieces = [modulation[number * width : (number + 1) * width] for number in range(6)]
    shift_attn, scale_attn, gate_attn, shift_mlp, scale_mlp, gate_mlp = pieces
    normed = modulate(residual, shift_attn, scale_attn).astype(jnp.bfloat16)
    mixed = jnp.dot(
        normed, triple_weight[layer_index], preferred_element_type=jnp.float32
    ) + triple_bias[layer_index].astype(jnp.float32)
    head_shape = (row_count, HEADS, HEAD_DIM)
    queries = rotate(mixed[:, :width].reshape(head_shape), cosine, sine_table).astype(jnp.bfloat16)
    key_flat = (
        rotate(mixed[:, width : 2 * width].reshape(head_shape), cosine, sine_table)
        .astype(jnp.bfloat16)
        .reshape(row_count, width)
    )
    value_flat = mixed[:, 2 * width :].astype(jnp.bfloat16)
    start_state = (
        jnp.full((HEADS, row_count), -1e30, jnp.float32),
        jnp.zeros((HEADS, row_count), jnp.float32),
        jnp.zeros((HEADS, row_count, HEAD_DIM), jnp.float32),
    )
    absorb = fold_keys(queries, scaling)
    final_state = absorb(
        start_state,
        (
            lax.all_gather(key_flat, "blk", axis=0, tiled=True),
            lax.all_gather(value_flat, "blk", axis=0, tiled=True),
        ),
        jnp.int32(0),
    )
    running_max, running_sum, weighted = final_state
    log_total = running_max + jnp.log(running_sum)
    attended_f = jnp.transpose(weighted / running_sum[..., None], (1, 0, 2))
    attended = attended_f.reshape(row_count, width).astype(jnp.bfloat16)
    branch = jnp.dot(
        attended, output_weight[layer_index], preferred_element_type=jnp.float32
    ) + output_bias[layer_index].astype(jnp.float32)
    middle = residual + gate_attn * branch
    normed_mlp = modulate(middle, shift_mlp, scale_mlp).astype(jnp.bfloat16)
    up_proj = jnp.dot(
        normed_mlp, expand_weight[layer_index], preferred_element_type=jnp.float32
    ) + expand_bias[layer_index].astype(jnp.float32)
    active = gelu_tanh(up_proj).astype(jnp.bfloat16)
    lowered = jnp.dot(
        active, shrink_weight[layer_index], preferred_element_type=jnp.float32
    ) + shrink_bias[layer_index].astype(jnp.float32)
    result = middle + gate_mlp * lowered
    saved = (
        residual,
        normed,
        queries,
        key_flat,
        value_flat,
        None,
        attended_f,
        attended,
        log_total,
        branch,
        middle,
        normed_mlp,
        up_proj,
        active,
        lowered,
    )
    return (result, saved)


def backward_layer(
    gradient, modulation, layer_index, weights, saved, cosine, sine_table, scaling, condition
):
    (
        adaptive_weight,
        adaptive_bias,
        triple_weight,
        triple_bias,
        output_weight,
        output_bias,
        expand_weight,
        expand_bias,
        shrink_weight,
        shrink_bias,
    ) = weights
    (
        residual,
        normed,
        queries,
        key_flat,
        value_flat,
        gathered,
        attended_f,
        attended,
        log_total,
        branch,
        middle,
        normed_mlp,
        up_proj,
        active,
        lowered,
    ) = saved
    row_count, width = residual.shape
    pieces = [modulation[number * width : (number + 1) * width] for number in range(6)]
    shift_attn, scale_attn, gate_attn, shift_mlp, scale_mlp, gate_mlp = pieces
    gate_mlp_grad = jnp.sum(gradient * lowered, 0)
    lowered_grad = (gradient * gate_mlp).astype(jnp.bfloat16)
    shrink_w_grad = jnp.einsum(
        "tf,td->fd", active, lowered_grad, preferred_element_type=jnp.float32
    )
    shrink_b_grad = jnp.sum(lowered_grad.astype(jnp.float32), 0)
    active_grad = jnp.einsum(
        "td,fd->tf", lowered_grad, shrink_weight[layer_index], preferred_element_type=jnp.float32
    )
    _, gelu_pull = jax.vjp(gelu_tanh, up_proj)
    up_grad = gelu_pull(active_grad)[0].astype(jnp.bfloat16)
    expand_w_grad = jnp.einsum("td,tf->df", normed_mlp, up_grad, preferred_element_type=jnp.float32)
    expand_b_grad = jnp.sum(up_grad.astype(jnp.float32), 0)
    normed_mlp_grad = jnp.einsum(
        "tf,df->td", up_grad, expand_weight[layer_index], preferred_element_type=jnp.float32
    )
    _, mlp_pull = jax.vjp(modulate, middle, shift_mlp, scale_mlp)
    middle_grad, shift_mlp_grad, scale_mlp_grad = mlp_pull(normed_mlp_grad)
    middle_grad = middle_grad + gradient
    gate_attn_grad = jnp.sum(middle_grad * branch, 0)
    branch_grad = (middle_grad * gate_attn).astype(jnp.bfloat16)
    output_w_grad = jnp.einsum(
        "tc,td->cd", attended, branch_grad, preferred_element_type=jnp.float32
    )
    output_b_grad = jnp.sum(branch_grad.astype(jnp.float32), 0)
    attended_grad = jnp.einsum(
        "td,cd->tc", branch_grad, output_weight[layer_index], preferred_element_type=jnp.float32
    )
    attended_grad = attended_grad.astype(jnp.bfloat16).reshape(row_count, HEADS, HEAD_DIM)
    key_all, value_all = (
        lax.all_gather(key_flat, "blk", axis=0, tiled=True),
        lax.all_gather(value_flat, "blk", axis=0, tiled=True),
    )
    query_grad, key_all_grad, value_all_grad = attend_back(
        queries, key_all, value_all, attended_grad, attended_f, log_total, scaling
    )
    key_grad, value_grad = (
        lax.psum_scatter(
            key_all_grad.astype(jnp.bfloat16), "blk", scatter_dimension=0, tiled=True
        ).astype(jnp.float32),
        lax.psum_scatter(
            value_all_grad.astype(jnp.bfloat16), "blk", scatter_dimension=0, tiled=True
        ).astype(jnp.float32),
    )
    mixed_grad = jnp.concatenate(
        [
            unrotate(query_grad, cosine, sine_table).reshape(row_count, width),
            unrotate(key_grad.reshape(row_count, HEADS, HEAD_DIM), cosine, sine_table).reshape(
                row_count, width
            ),
            value_grad,
        ],
        -1,
    ).astype(jnp.bfloat16)
    triple_w_grad = jnp.einsum("td,tc->dc", normed, mixed_grad, preferred_element_type=jnp.float32)
    triple_b_grad = jnp.sum(mixed_grad.astype(jnp.float32), 0)
    normed_grad = jnp.einsum(
        "tc,dc->td", mixed_grad, triple_weight[layer_index], preferred_element_type=jnp.float32
    )
    _, attn_pull = jax.vjp(modulate, residual, shift_attn, scale_attn)
    residual_grad, shift_attn_grad, scale_attn_grad = attn_pull(normed_grad)
    residual_grad = residual_grad + middle_grad
    modulation_grad = jnp.concatenate(
        [
            shift_attn_grad,
            scale_attn_grad,
            gate_attn_grad,
            shift_mlp_grad,
            scale_mlp_grad,
            gate_mlp_grad,
        ],
        0,
    )
    adaptive_w_grad = condition[0][:, None] * modulation_grad[None, :]
    condition_term = jnp.dot(
        adaptive_weight[layer_index].astype(jnp.float32), modulation_grad, precision=HIGHEST
    )
    grad_terms = (
        adaptive_w_grad,
        modulation_grad,
        triple_w_grad,
        triple_b_grad,
        output_w_grad,
        output_b_grad,
        expand_w_grad,
        expand_b_grad,
        shrink_w_grad,
        shrink_b_grad,
    )
    return (residual_grad, grad_terms, condition_term)


def local(
    inputs,
    condition,
    prefix,
    mask_embed,
    adaptive_weight,
    adaptive_bias,
    triple_weight,
    triple_bias,
    output_weight,
    output_bias,
    expand_weight,
    expand_bias,
    shrink_weight,
    shrink_bias,
    cotangent,
):
    weights = (
        adaptive_weight,
        adaptive_bias,
        triple_weight,
        triple_bias,
        output_weight,
        output_bias,
        expand_weight,
        expand_bias,
        shrink_weight,
        shrink_bias,
    )
    row_count = inputs.shape[1]
    offset = lax.axis_index("blk") * row_count
    position = offset + jnp.arange(row_count, dtype=jnp.int32)
    masked = position >= prefix[0]
    residual = jnp.where(
        masked[:, None], mask_embed.astype(jnp.float32)[None, :], inputs[0].astype(jnp.float32)
    )
    cosine, sine_table = tables(offset, row_count, HEAD_DIM)
    scaling = 1.0 / math.sqrt(HEAD_DIM)
    modulations = []
    saved_layers = []
    for layer_index in range(LAYERS):
        modulation = jnp.dot(
            condition, adaptive_weight[layer_index].astype(jnp.float32), precision=HIGHEST
        )[0] + adaptive_bias[layer_index].astype(jnp.float32)
        residual, saved = forward_layer(
            residual, modulation, layer_index, weights, cosine, sine_table, scaling
        )
        modulations.append(modulation)
        saved_layers.append(saved)
    outputs = residual.astype(jnp.bfloat16)[None]
    gradient = cotangent[0].astype(jnp.float32)
    condition_total = jnp.zeros((condition.shape[1],), jnp.float32)
    collected = [None] * LAYERS
    mask_sum = None
    for layer_index in reversed(range(LAYERS)):
        gradient, grad_terms, condition_term = backward_layer(
            gradient,
            modulations[layer_index],
            layer_index,
            weights,
            saved_layers[layer_index],
            cosine,
            sine_table,
            scaling,
            condition,
        )
        condition_total = condition_total + condition_term
        collected[layer_index] = grad_terms
    mask_term = jnp.sum(jnp.where(masked[:, None], gradient, 0.0), 0)
    flat_terms = ()
    for layer_index in range(LAYERS):
        flat_terms = flat_terms + tuple(collected[layer_index])
    summed = lax.psum_scatter(
        flat_terms + (mask_term,), ("blk", "dp"), scatter_dimension=0, tiled=True
    )
    collected = [summed[layer_index * 10 : (layer_index + 1) * 10] for layer_index in range(LAYERS)]
    mask_sum = summed[LAYERS * 10]
    condition_grad = lax.psum(condition_total, "blk")[None, :]
    input_grad = jnp.where(masked[:, None], 0.0, gradient)[None]
    stacked = [
        jnp.stack([collected[layer_index][number] for layer_index in range(LAYERS)], 0)
        for number in range(10)
    ]
    return (
        outputs,
        input_grad,
        condition_grad,
        mask_sum,
        stacked[0],
        stacked[1],
        stacked[2],
        stacked[3],
        stacked[4],
        stacked[5],
        stacked[6],
        stacked[7],
        stacked[8],
        stacked[9],
    )


BF = jnp.bfloat16
F32 = jnp.float32
WIDTH = HEADS * HEAD_DIM
GROUP = WIDTH // 4
VM = pl.BlockSpec(memory_space=pltpu.VMEM)
ANY = pl.BlockSpec(memory_space=pl.ANY)
HBM = pl.BlockSpec(memory_space=pltpu.HBM)
SM = pl.BlockSpec(memory_space=pltpu.SMEM)
MEBI = 1024 * 1024
ROOT_TWO_PI = math.sqrt(2.0 / math.pi)
CUBIC = 0.044715


def dot_nn(left, right):
    return jnp.dot(left, right, preferred_element_type=F32)


def dot_nt(left, right):
    return lax.dot_general(left, right, (((1,), (1,)), ((), ())), preferred_element_type=F32)


def dot_tn(left, right):
    return lax.dot_general(left, right, (((0,), (0,)), ((), ())), preferred_element_type=F32)


def normalise(values):
    centered = values - jnp.mean(values, -1, keepdims=True)
    rstd = lax.rsqrt(jnp.mean(centered * centered, -1, keepdims=True) + EPSILON)
    return centered * rstd, rstd


def normalise_back(upstream, unit, rstd):
    first = jnp.mean(upstream, -1, keepdims=True)
    second = jnp.mean(upstream * unit, -1, keepdims=True)
    return rstd * (upstream - first - unit * second)


def column_sum(values):
    return jnp.sum(values, 0, keepdims=True)


def turn(values, cosine, signed_sine):
    lane = lax.broadcasted_iota(jnp.int32, (values.shape[0], 128), 1)
    front = (lane % HEAD_DIM) < HEAD_DIM // 2
    pieces = []
    for start in range(0, values.shape[1], 128):
        piece = values[:, start : start + 128]
        swapped = jnp.where(front, pltpu.roll(piece, 96, 1), pltpu.roll(piece, 32, 1))
        pieces.append(piece * cosine + swapped * signed_sine)
    return jnp.concatenate(pieces, 1)


def piece_of(row, number):
    return row[:, number * WIDTH : (number + 1) * WIDTH]


BIAS_AT = {"triple": (0, 2304), "output": (2304, 3072), "expand": (3072, 6144), "shrink": (6144, 6912)}


def bias_of(bias_ref, layer, name):
    low, high = BIAS_AT[name]
    return bias_ref[layer][:, low:high]


def pack_rows(values):
    half = values.shape[0] // 2
    return jnp.concatenate([values[:half], values[half:]], 1)


def qkv_stage(x, layer, mod_row, bias_ref, triple, cos_ref, sin_ref, me, h_ref, chunk_refs, hold):
    unit, _ = normalise(x)
    h = unit * (1.0 + piece_of(mod_row, 1)) + piece_of(mod_row, 0)
    turned = h.T
    h = h.astype(BF)
    each = WIDTH // 32
    for half in range(2):
        picked = [turned[each * (b * 8 + z * 2 + half) :][:each] for z in range(4) for b in range(4)]
        h_ref[half] = jnp.concatenate(picked, 0).astype(BF)
    bias = bias_of(bias_ref, layer, "triple")
    cosine, sine = cos_ref[0], sin_ref[0]
    parts = []
    for number in range(3):
        columns = slice(number * WIDTH, (number + 1) * WIDTH)
        mixed = dot_nn(h, triple[:, columns]) + bias[:, columns]
        if number < 2:
            mixed = turn(mixed, cosine, sine)
        if number == 0:
            mixed = mixed * HEAD_DIM**-0.5
        parts.append(mixed)
    rows = x.shape[0]
    for group in range(4):
        columns = slice(group * GROUP, (group + 1) * GROUP)
        pair = jnp.concatenate([parts[0][:, columns], parts[1][:, columns]], 1)
        hold[group, 0:rows, :] = pair.astype(BF)
        hold[group, rows : rows + rows // 2, :] = pack_rows(parts[2][:, columns]).astype(BF)
    for place in range(4):
        chunk_refs[place][...] = hold[place ^ me]


def first_kernel(
    scal, inputs, mask_embed, condition, adaptive_weight, adaptive_bias, bias_ref, cos_ref, sin_ref, triple_any,
    x_ref, mod_ref, h_ref, c0, c1, c2, c3,
    triple, hold, sems,
):
    copy = pltpu.make_async_copy(triple_any.at[0], triple, sems.at[0])
    copy.start()
    me = scal[0]
    cond = condition[...]
    upper = cond.astype(BF).astype(F32)
    rest = cond - upper
    mid = rest.astype(BF).astype(F32)
    low = rest - mid
    row = lax.broadcasted_iota(jnp.int32, (8, cond.shape[1]), 0)
    stack = jnp.where(row == 0, upper, jnp.where(row == 1, mid, jnp.where(row == 2, low, 0.0))).astype(BF)
    for layer in range(LAYERS):
        total = column_sum(dot_nn(stack, adaptive_weight[layer]))
        mod_ref[layer] = total + adaptive_bias[layer].astype(F32)
    rows = inputs.shape[1]
    position = me * rows + lax.broadcasted_iota(jnp.int32, (rows, WIDTH), 0)
    x = jnp.where(position >= scal[3], mask_embed[...].astype(F32), inputs[0].astype(F32))
    x_ref[...] = x
    copy.wait()
    qkv_stage(
        x, 0, mod_ref[0], bias_ref, triple, cos_ref, sin_ref, me, h_ref, (c0, c1, c2, c3), hold,
    )


def attend_kernel(
    c0, c1, c2, c3,
    o0, o1, o2, o3, lse_ref, ot_ref,
    q_all, k_all, v_turned,
):
    rows = c0.shape[1] * 2 // 3
    rows = 256
    for place, chunk in enumerate((c0, c1, c2, c3)):
        span = slice(place * rows, (place + 1) * rows)
        q_all[place] = chunk[0:rows, 0:GROUP]
        k_all[span, :] = chunk[0:rows, GROUP : 2 * GROUP]
        tail = chunk[rows : rows + rows // 2, :]
        v_block = jnp.concatenate([tail[:, 0:GROUP], tail[:, GROUP : 2 * GROUP]], 0)
        v_turned[:, span] = v_block.T
    head = lax.broadcasted_iota(jnp.int32, (rows, GROUP), 1) // HEAD_DIM

    def step(block, carry):
        q = q_all[block]
        for number in range(3):
            masked = jnp.where(head == number, q, jnp.zeros_like(q))
            scores = dot_nt(k_all[...], masked)
            peak = jnp.max(scores, 0, keepdims=True)
            weights = jnp.exp(scores - peak)
            total = jnp.sum(weights, 0, keepdims=True)
            span = slice(number * HEAD_DIM, (number + 1) * HEAD_DIM)
            ot_ref[block, span, :] = dot_nn(v_turned[span, :], weights.astype(BF)) / total
            lse_ref[block, number : number + 1, :] = peak + jnp.log(total)
        return carry

    lax.fori_loop(0, 4, step, 0)
    for place, out in enumerate((o0, o1, o2, o3)):
        out[...] = pack_rows(ot_ref[place].T).astype(BF)


def gather_chunks(refs, hold):
    for place in range(4):
        hold[place] = refs[place][...]


def mlp_forward(
    layer, x, mod_row, bias_ref, me, o_refs, output, expand, shrink, waits, hold, o_ref, aout_ref, m_ref, turned_ref,
    slope_ref, f_ref,
):
    gather_chunks(o_refs, hold)
    rows = x.shape[0]
    half = rows // 2
    for group in range(4):
        chunk = hold[group ^ me]
        columns = slice(group * GROUP, (group + 1) * GROUP)
        o_ref[0:half, columns] = chunk[:, 0:GROUP]
        o_ref[half:rows, columns] = chunk[:, GROUP : 2 * GROUP]
    o = o_ref[...]
    hidden = expand.shape[1]
    turned_ref[hidden + WIDTH : hidden + 2 * WIDTH, :] = o.T
    waits[0].wait()
    a_out = dot_nn(o, output[...]) + bias_of(bias_ref, layer, "output")
    aout_ref[...] = a_out.astype(BF)
    m = x + piece_of(mod_row, 2) * a_out
    m_ref[...] = m
    unit, _ = normalise(m)
    h2 = (unit * (1.0 + piece_of(mod_row, 4)) + piece_of(mod_row, 3)).astype(BF)
    turned_ref[hidden : hidden + WIDTH, :] = h2.T
    waits[1].wait()
    bias = bias_of(bias_ref, layer, "expand")
    f = bias_of(bias_ref, layer, "shrink")
    for start in range(0, hidden, 768):
        columns = slice(start, start + 768)
        u = dot_nn(h2, expand[:, columns]) + bias[:, columns]
        square = u * u
        gate = 0.5 + 0.5 * jnp.tanh(u * (ROOT_TWO_PI + ROOT_TWO_PI * CUBIC * square))
        active = u * gate
        slope = gate + 2.0 * active * (1.0 - gate) * (ROOT_TWO_PI + 3.0 * ROOT_TWO_PI * CUBIC * square)
        z = active.astype(BF)
        turned_ref[columns, :] = z.T
        slope_ref[:, columns] = slope.astype(BF)
        if start == 0:
            waits[2].wait()
        f = f + dot_nn(z, shrink[columns, :])
    f_ref[...] = f.astype(BF)
    return m + piece_of(mod_row, 5) * f


def share(values, hold, at):
    half = values.shape[1] // 2
    hold[0, :, at : at + half] = values[:, 0:half]
    hold[1, :, at : at + half] = values[:, half : 2 * half]


def mlp_backward(
    dy, mod_row, me, core, m_ref, f_ref, slope_ref, aout_ref, output, expand, shrink, waits, hold, halves,
    do_refs, dm_ref, vec_ref,
):
    def put(place, row):
        vec_ref[:, place : place + row.shape[1]] = row

    put(0, column_sum(dy * f_ref[...].astype(F32)))
    df = (dy * piece_of(mod_row, 5)).astype(BF)
    put(3072, column_sum(df.astype(F32)))
    hidden = expand.shape[1]
    share(df, halves, hidden // 2)
    dh2 = jnp.zeros(dy.shape, F32)
    waits[2].wait()
    for start in range(0, hidden, 768):
        columns = slice(start, start + 768)
        dz = dot_nt(df, shrink[columns, :])
        du = (slope_ref[:, columns].astype(F32) * dz).astype(BF)
        put(3840 + start, column_sum(du.astype(F32)))
        half = hidden // 2
        halves[start // half, :, start % half : start % half + 768] = du
        if start == 0:
            waits[1].wait()
        dh2 = dh2 + dot_nt(du, expand[:, columns])
    unit, rstd = normalise(m_ref[...])
    put(768, column_sum(dh2))
    put(1536, column_sum(dh2 * unit))
    dm = dy + normalise_back(dh2 * (1.0 + piece_of(mod_row, 4)), unit, rstd)
    dm_ref[...] = dm
    put(2304, column_sum(dm * aout_ref[...].astype(F32)))
    da = (dm * piece_of(mod_row, 2)).astype(BF)
    put(6912, column_sum(da.astype(F32)))
    share(da, halves, hidden // 2 + WIDTH // 2)
    waits[0].wait()
    do = dot_nt(da, output[...])
    for group in range(4):
        hold[group] = pack_rows(do[:, group * GROUP : (group + 1) * GROUP]).astype(BF)
    for place in range(4):
        do_refs[place][...] = hold[place ^ me]


def attend_back_kernel(
    c0, c1, c2, c3, d0, d1, d2, d3, lse_ref, ot_ref, cos_ref, sin_ref,
    g0, g1, g2, g3, stacked,
    q_masked, do_masked, k_all, v_all, k_turned, lse_rows, delta_rows, dq_turned, dk_all, dv_all,
):
    rows = 256
    head = lax.broadcasted_iota(jnp.int32, (rows, GROUP), 1) // HEAD_DIM
    for place in range(4):
        chunk = (c0, c1, c2, c3)[place]
        given = (d0, d1, d2, d3)[place][...]
        span = slice(place * rows, (place + 1) * rows)
        q = chunk[0:rows, 0:GROUP]
        k = chunk[0:rows, GROUP : 2 * GROUP]
        tail = chunk[rows : rows + rows // 2, :]
        v_all[place] = jnp.concatenate([tail[:, 0:GROUP], tail[:, GROUP : 2 * GROUP]], 0)
        k_all[place] = k
        k_turned[place] = k.T
        do = jnp.concatenate([given[:, 0:GROUP], given[:, GROUP : 2 * GROUP]], 0)
        product = do.astype(F32).T * ot_ref[place]
        for number in range(3):
            q_masked[number, span, :] = jnp.where(head == number, q, jnp.zeros_like(q))
            do_masked[number, span, :] = jnp.where(head == number, do, jnp.zeros_like(do))
            part = product[number * HEAD_DIM : (number + 1) * HEAD_DIM, :]
            delta_rows[number : number + 1, span] = jnp.sum(part, 0, keepdims=True)
            lse_rows[number : number + 1, span] = lse_ref[place, number : number + 1, :]
    dq_turned[...] = jnp.zeros(dq_turned.shape, F32)

    def step(block, carry):
        k = k_all[block]
        v = v_all[block]
        dk = jnp.zeros((rows, GROUP), F32)
        dv = jnp.zeros((rows, GROUP), F32)
        for number in range(3):
            span = slice(number * HEAD_DIM, (number + 1) * HEAD_DIM)
            scores = dot_nt(k, q_masked[number])
            probs = jnp.exp(scores - lse_rows[number : number + 1, :])
            prob_grad = dot_nt(v, do_masked[number])
            score_grad = (probs * (prob_grad - delta_rows[number : number + 1, :])).astype(BF)
            dv = dv + dot_nn(probs.astype(BF), do_masked[number])
            dk = dk + dot_nn(score_grad, q_masked[number])
            dq_turned[span, :] += dot_nn(k_turned[block, span, :], score_grad)
        dk_all[block] = dk
        dv_all[block] = dv
        return carry

    lax.fori_loop(0, 4, step, 0)
    for place, out in enumerate((g0, g1, g2, g3)):
        span = slice(place * rows, (place + 1) * rows)
        dq = dq_turned[:, span].T * HEAD_DIM**-0.5
        pair = jnp.concatenate([dq, dk_all[place]], 1)
        pair = turn(pair, cos_ref[place], -sin_ref[place]).astype(BF)
        tail = pack_rows(dv_all[place]).astype(BF)
        for target in (out, stacked.at[place]):
            target[0:rows, :] = pair
            target[rows : rows + rows // 2, :] = tail


def qkv_backward(x, dm, mod_row, me, g_refs, triple, wait, hold, full, vec_ref):
    gather_chunks(g_refs, hold)
    rows = x.shape[0]
    half = rows // 2
    for group in range(4):
        chunk = hold[group ^ me]
        low = group * GROUP
        full[:, low : low + GROUP] = chunk[0:rows, 0:GROUP]
        full[:, WIDTH + low : WIDTH + low + GROUP] = chunk[0:rows, GROUP : 2 * GROUP]
        full[0:half, 2 * WIDTH + low : 2 * WIDTH + low + GROUP] = chunk[rows : rows + half, 0:GROUP]
        full[half:rows, 2 * WIDTH + low : 2 * WIDTH + low + GROUP] = chunk[rows : rows + half, GROUP : 2 * GROUP]
    dqkv = full[...]
    vec_ref[:, 1536:3840] = column_sum(dqkv.astype(F32))
    wait.wait()
    dh = dot_nt(dqkv, triple[...])
    unit, rstd = normalise(x)
    vec_ref[:, 0:768] = column_sum(dh)
    vec_ref[:, 768:1536] = column_sum(dh * unit)
    return dm + normalise_back(dh * (1.0 + piece_of(mod_row, 1)), unit, rstd)


def fetch(pairs, sems):
    copies = []
    for number, (source, target) in enumerate(pairs):
        copy = pltpu.make_async_copy(source, target, sems.at[number])
        copy.start()
        copies.append(copy)
    return copies


class Done:
    def wait(self):
        pass


def middle_kernel(
    scal, x_ref, mod_ref, bias_ref, cos_ref, sin_ref, o0, o1, o2, o3, output_any, expand_any, shrink_any, triple_any,
    aout_ref, m_ref, turned_ref, slope_ref, f_ref, y_ref, h_ref, c0, c1, c2, c3,
    output, expand, shrink, triple, o_hold, o_ref, c_hold, sems,
):
    copies = fetch(
        [(output_any.at[0], output), (expand_any.at[0], expand), (shrink_any.at[0], shrink), (triple_any.at[1], triple)],
        sems,
    )
    me = scal[0]
    y = mlp_forward(
        0, x_ref[...], mod_ref[0], bias_ref, me, (o0, o1, o2, o3), output, expand, shrink, copies, o_hold, o_ref,
        aout_ref, m_ref, turned_ref, slope_ref, f_ref,
    )
    y_ref[...] = y
    copies[3].wait()
    qkv_stage(
        y, 1, mod_ref[1], bias_ref, triple, cos_ref, sin_ref, me, h_ref, (c0, c1, c2, c3), c_hold,
    )


def ahead_kernel(
    scal, x_ref, mod_ref, bias_ref, o0, o1, o2, o3, output_any, expand_any, shrink_any,
    out_ref, aout_ref, m_ref, turned_ref, slope_ref, f_ref,
    output, expand, shrink, o_hold, o_ref, sems,
):
    copies = fetch([(output_any.at[1], output), (expand_any.at[1], expand), (shrink_any.at[1], shrink)], sems)
    y = mlp_forward(
        1, x_ref[...], mod_ref[1], bias_ref, scal[0], (o0, o1, o2, o3), output, expand, shrink, copies, o_hold, o_ref,
        aout_ref, m_ref, turned_ref, slope_ref, f_ref,
    )
    out_ref[0] = y.astype(BF)


def turn_kernel(
    scal, cotangent, mod_ref, m_ref, f_ref, slope_ref, aout_ref, output_any, expand_any, shrink_any,
    mine, theirs, d0, d1, d2, d3, dm_ref, vec_ref,
    output, expand, shrink, o_hold, halves, sems,
):
    copies = fetch([(shrink_any.at[1], shrink), (expand_any.at[1], expand), (output_any.at[1], output)], sems)
    me, core = scal[0], scal[2]
    mlp_backward(
        cotangent[0].astype(F32), mod_ref[1], me, core, m_ref, f_ref, slope_ref, aout_ref, output, expand, shrink,
        [copies[2], copies[1], copies[0]], o_hold, halves, (d0, d1, d2, d3), dm_ref, vec_ref,
    )
    mine[...] = halves[core]
    theirs[...] = halves[1 - core]


def back_kernel(
    scal, x_ref, dm_in, mod_ref, g0, g1, g2, g3, m_ref, f_ref, slope_ref, aout_ref,
    triple_any, output_any, expand_any, shrink_any,
    mine, theirs, vec_first, d0, d1, d2, d3, dm_ref, vec_ref,
    triple, output, expand, shrink, g_hold, full, o_hold, halves, sems,
):
    copies = fetch(
        [(triple_any.at[1], triple), (shrink_any.at[0], shrink), (expand_any.at[0], expand), (output_any.at[0], output)],
        sems,
    )
    me, core = scal[0], scal[2]
    dy = qkv_backward(
        x_ref[...], dm_in[...], mod_ref[1], me, (g0, g1, g2, g3), triple, copies[0], g_hold, full, vec_first,
    )
    mlp_backward(
        dy, mod_ref[0], me, core, m_ref, f_ref, slope_ref, aout_ref, output, expand, shrink,
        [copies[3], copies[2], copies[1]], o_hold, halves, (d0, d1, d2, d3), dm_ref, vec_ref,
    )
    mine[...] = halves[core]
    theirs[...] = halves[1 - core]


def last_kernel(
    scal, x_ref, dm_in, mod_ref, g0, g1, g2, g3, triple_any,
    vec_first, input_grad, mask_ref,
    triple, g_hold, full, sems,
):
    copies = fetch([(triple_any.at[0], triple)], sems)
    me = scal[0]
    dx = qkv_backward(
        x_ref[...], dm_in[...], mod_ref[0], me, (g0, g1, g2, g3), triple, copies[0], g_hold, full, vec_first,
    )
    rows = dx.shape[0]
    position = me * rows + lax.broadcasted_iota(jnp.int32, dx.shape, 0)
    masked = position >= scal[3]
    input_grad[0] = jnp.where(masked, 0.0, dx)
    mask_ref[...] = column_sum(jnp.where(masked, dx, 0.0))


def triple_kernel(
    scal, h0, h1, h2, h3, chunks,
    mine, theirs,
    result,
):
    rows = chunks.shape[1] * 2 // 3
    half = rows // 2
    each = WIDTH // 8
    for side in range(2):
        qk = jnp.zeros((WIDTH // 2, 2 * GROUP), F32)
        v = jnp.zeros((WIDTH // 2, GROUP), F32)
        for place, h_ref in enumerate((h0, h1, h2, h3)):
            h = h_ref[side]
            qk = qk + dot_nn(h, chunks[place, 0:rows, :])
            tail = chunks[place, rows : rows + half, :]
            v = v + dot_nn(h, jnp.concatenate([tail[:, 0:GROUP], tail[:, GROUP : 2 * GROUP]], 0))
        for z in range(4):
            span = slice(z * each, (z + 1) * each)
            result[side * 4 + z, 0:each, :] = qk[span].astype(BF)
            result[side * 4 + z, each : each + each // 2, :] = pack_rows(v[span]).astype(BF)
    for place, offset in enumerate((0, 2, 1, 3)):
        at = scal[1] ^ offset
        mine[place] = result[scal[2] * 4 + at]
        theirs[place] = result[(1 - scal[2]) * 4 + at]


def triple_settle_kernel(
    scal, keep, core, first, second,
    b0, b1, b2, b3,
    hold,
):
    each = WIDTH // 8
    total = keep[0].astype(F32) + core[0].astype(F32) + first[0].astype(F32) + second[0].astype(F32)
    v = jnp.concatenate([total[each:, 0:GROUP], total[each:, GROUP : 2 * GROUP]], 0)
    rows = WIDTH // 32
    for b in range(4):
        span = slice(b * rows, (b + 1) * rows)
        hold[b, :, 0 : 2 * GROUP] = total[span]
        hold[b, :, 2 * GROUP : 3 * GROUP] = v[span]
    for place, out in enumerate((b0, b1, b2, b3)):
        out[...] = hold[place ^ scal[0]]


BIT = {"x": 4, "y": 8, "a": 1, "b": 2}
STEP = {"x": ("blk", 1), "y": ("blk", 2), "a": ("dp", 2), "b": ("dp", 4)}


def place_at(order, index):
    place = 0
    for depth, name in enumerate(order):
        if index & (8 >> depth):
            place |= BIT[name]
    return place


def weights_kernel(products, orders, scal, own, far, mine, got, *rest):
    count = len(orders)
    sends, keeps, holds = rest[0:count], rest[count : 2 * count], rest[2 * count :]
    me16 = scal[0] * 4 + scal[1]
    for part, order in enumerate(orders):
        row_at = 0
        for (low, high, at, dealt), hold in zip(products, holds):
            blocks = dealt[part]
            begin = at + sum(dealt[:part]) * 128
            columns = slice(begin, begin + blocks * 128)
            hold[:, 0 : blocks * 128] = (
                dot_nn(own[low:high, :], mine[:, columns]) + dot_nn(far[low:high, :], got[:, columns])
            ).astype(BF)
            rows = (high - low) // 16
            for index in range(16):
                start = pl.multiple_of((place_at(order, index) ^ me16) * rows, 16)
                target = keeps[part] if index < 8 else sends[part]
                for number in range(blocks):
                    lane = number * 128
                    spot = row_at + number * rows
                    target[index % 8, spot : spot + rows, :] = hold[pl.ds(start, rows), lane : lane + 128]
            row_at += blocks * rows


def settle_kernel(spans, scal, *refs):
    pieces, (mine, theirs), (hold, sems) = refs[:-4], refs[-4:-2], refs[-2:]
    sizes = [sum(blocks) for blocks in spans[1]]
    each = (len(pieces) - 1) // len(sizes)
    sources = []
    for part, size in enumerate(sizes):
        sources += [piece.at[0] for piece in pieces[part * each : (part + 1) * each]]
        sources.append(pieces[-1].at[0, sum(sizes[:part]) : sum(sizes[: part + 1]), :])
    each += 1
    copies = []
    for number, source in enumerate(sources):
        copy = pltpu.make_async_copy(source, hold.at[number, 0 : source.shape[0], :], sems.at[number])
        copy.start()
        copies.append(copy)
    for copy in copies:
        copy.wait()
    core = scal[2]
    at = 0
    for part, blocks in enumerate(spans[1]):
        row = 0
        for rows in blocks:
            half = rows // 2
            total = hold[part * each, row : row + rows, :].astype(F32)
            for number in range(1, each):
                total = total + hold[part * each + number, row : row + rows, :].astype(F32)
            low, high = total[0:half], total[half:rows]
            mine[at : at + half, :] = jnp.where(core == 0, low, high)
            theirs[at : at + half, :] = jnp.where(core == 0, high, low)
            row += rows
            at += half


def finish_kernel(plans, scal, *refs):
    pairs = 2 * len(plans)
    groups = refs[pairs : pairs + 4 * LAYERS]
    outs, hold = refs[pairs + 4 * LAYERS : -1], refs[-1]
    core = scal[2]
    for bucket, plan in enumerate(plans):
        mine, got = refs[2 * bucket : 2 * bucket + 2]
        at = 0
        for out, layer, block, rows in plan:
            own, other = mine[at : at + rows, :], got[at : at + rows, :]
            half = outs[out].shape[2] // 2
            low = block * 128
            outs[out][layer, :, low : low + 128] = jnp.where(core == 0, own, other)
            outs[out][layer, :, half + low : half + low + 128] = jnp.where(core == 0, other, own)
            at += rows
    for layer in range(LAYERS):
        for place in range(4):
            hold[place] = groups[layer * 4 + place][...]
        for group in range(4):
            block = hold[group ^ scal[0]]
            for number in range(3):
                low = number * WIDTH + group * GROUP
                outs[0][layer, :, low : low + GROUP] = block[:, number * GROUP : (number + 1) * GROUP]


def shaped(*shape, dtype=F32):
    return jax.ShapeDtypeStruct(shape, dtype)


def call(kernel, specs, outs, scratch, micros, name, limit, after=()):
    count, extra = len(specs), len(after)

    def body(*refs):
        kernel(*refs[:count], *refs[count + extra :])

    made = pl.pallas_call(
        body,
        in_specs=specs + [ANY] * extra,
        out_specs=[VM] * len(outs),
        out_shape=outs,
        scratch_shapes=scratch,
        compiler_params=pltpu.CompilerParams(vmem_limit_bytes=limit * MEBI),
        cost_estimate=pl.CostEstimate(flops=int(micros * 1e9), bytes_accessed=int(micros * 1e6), transcendentals=0),
        name=name,
    )
    return lambda *operands: made(*operands, *after)


def swap(values, axis, bit):
    size = 4 if axis == "blk" else 8
    return lax.ppermute(values, axis, [(i, i ^ bit) for i in range(size)])


def swap_chunks(chunks):
    return [chunks[0]] + [swap(chunks[place], "blk", place) for place in (1, 2, 3)]


class Bucket:
    def __init__(self, sends, keeps, orders):
        self.orders = orders
        self.sent = list(sends)
        self.held = [[keep, swap(send, *STEP[order[0]])] for keep, send, order in zip(keeps, sends, orders)]
        self.depth = 1
        self.size = 8

    def advance(self):
        half = self.size // 2
        self.sent = [
            sum(piece[half : self.size].astype(F32) for piece in held).astype(BF) for held in self.held
        ]
        if half == 1:
            self.sent = [jnp.concatenate(self.sent, 1)]
            self.last = swap(self.sent[0], *STEP[self.orders[0][-1]])
        else:
            for held, out, order in zip(self.held, self.sent, self.orders):
                held.append(swap(out, *STEP[order[self.depth]]))
        self.size = half
        self.depth += 1


def weight_bucket(scal, own, far, mine, got, products, orders, after=()):
    count = len(orders)
    shapes = []
    for part in range(count):
        rows = sum(dealt[part] * (high - low) // 16 for low, high, _, dealt in products)
        shapes.append(shaped(8, rows, 128, dtype=BF))
    outs = call(
        functools.partial(weights_kernel, products, orders),
        [SM] + [VM] * 4,
        shapes * 2,
        [pltpu.VMEM((high - low, max(dealt) * 128), BF) for low, high, _, dealt in products],
        0.1,
        "mlp_weights",
        28,
        after,
    )(scal, own, far, mine, got)
    return Bucket(outs[:count], outs[count:], orders)


def settle(bucket, scal, products):
    count = len(bucket.orders)
    spans = []
    for part in range(count):
        blocks = []
        for low, high, _, dealt in products:
            blocks += [(high - low) // 16] * dealt[part]
        spans.append(blocks)
    rows = sum(sum(blocks) for blocks in spans) // 2
    pieces = [piece for held in bucket.held for piece in held] + [bucket.last]
    number = len(pieces) - 1 + count
    mine, theirs = call(
        functools.partial(settle_kernel, (bucket.orders, spans)),
        [SM] + [ANY] * len(pieces),
        [shaped(rows, 128)] * 2,
        [pltpu.VMEM((number, max(sum(blocks) for blocks in spans), 128), BF), pltpu.SemaphoreType.DMA((number,))],
        0.1,
        "settle",
        10,
    )(scal, *pieces)
    return mine, swap(theirs, "dp", 1)


def plan_of(products, names):
    plan = []
    for part in range(len(products[0][3])):
        for (low, high, _, dealt), (out, layer) in zip(products, names):
            first = sum(dealt[:part])
            plan += [(out, layer, first + number, (high - low) // 32) for number in range(dealt[part])]
    return plan


class Triple:
    def __init__(self, scal, h_rows, stacked, after=()):
        self.scal = scal
        shape = (WIDTH // 8 * 3 // 2, 2 * GROUP)
        keep, theirs = call(
            triple_kernel,
            [SM] + [VM] * 5,
            [shaped(4, *shape, dtype=BF)] * 2,
            [pltpu.VMEM((8, *shape), BF)],
            0.1,
            "triple_weights",
            20,
            after,
        )(scal, *h_rows, stacked)
        self.sent = [theirs]
        self.held = [keep, swap(theirs, "dp", 1)]
        self.steps = [(2, 4, "a"), (1, 2, "b")]

    def advance(self):
        low, high, name = self.steps.pop(0)
        self.sent = [sum(piece[low:high].astype(F32) for piece in self.held).astype(BF)]
        self.held.append(swap(self.sent[0], *STEP[name]))

    def settle(self):
        blocks = call(
            triple_settle_kernel,
            [SM] + [VM] * 4,
            [shaped(WIDTH // 32, 3 * GROUP)] * 4,
            [pltpu.VMEM((4, WIDTH // 32, 3 * GROUP), F32)],
            0.1,
            "triple_settle",
            8,
        )(self.scal, *self.held)
        return swap_chunks(blocks)


def local_fast(
    inputs, condition, prefix, mask_embed, adaptive_weight, adaptive_bias, triple_weight, triple_bias, output_weight,
    output_bias, expand_weight, expand_bias, shrink_weight, shrink_bias, cotangent,
):
    rows = inputs.shape[1]
    hidden = expand_weight.shape[2]
    blk, dp = lax.axis_index("blk"), lax.axis_index("dp")
    core = dp % 2
    scal = jnp.stack([blk, dp // 2, core, prefix[0]]).astype(jnp.int32)
    start = (blk ^ jnp.arange(4, dtype=jnp.int32)) * rows
    position = (start[:, None] + jnp.arange(rows, dtype=jnp.int32)[None, :]).astype(F32)
    lane = jnp.arange(128, dtype=jnp.int32)
    frequency = jnp.exp((lane % 32).astype(F32) * (-2.0 * math.log(10000.0) / HEAD_DIM))
    angles = position[:, :, None] * frequency
    cosine = jnp.cos(angles)
    sine = jnp.sin(angles) * jnp.where(lane % 64 < 32, -1.0, 1.0)
    biases = jnp.concatenate(
        [part.astype(F32) for part in (triple_bias, output_bias, expand_bias, shrink_bias)], 1
    )[:, None, :]
    f_square = shaped(rows, WIDTH)
    b_square = shaped(rows, WIDTH, dtype=BF)
    b_tall = shaped(rows, hidden, dtype=BF)
    packed = rows + rows // 2
    chunk = shaped(packed, 2 * GROUP, dtype=BF)
    o_chunk = shaped(rows // 2, 2 * GROUP, dtype=BF)
    c_hold = pltpu.VMEM((4, packed, 2 * GROUP), BF)
    o_hold = pltpu.VMEM((4, rows // 2, 2 * GROUP), BF)
    triple_hold = pltpu.VMEM((WIDTH, 3 * WIDTH), BF)
    output_hold = pltpu.VMEM((WIDTH, WIDTH), BF)
    expand_hold = pltpu.VMEM((WIDTH, hidden), BF)
    shrink_hold = pltpu.VMEM((hidden, WIDTH), BF)

    h_both = shaped(2, WIDTH // 2, rows, dtype=BF)
    half_width = hidden // 2 + WIDTH
    tall = hidden + 2 * WIDTH

    def far(values):
        return swap(values, "dp", 1)

    x0, mod, h_rows, c0, c1, c2, c3 = call(
        first_kernel,
        [SM] + [VM] * 8 + [HBM],
        [f_square, shaped(LAYERS, 1, 6 * WIDTH), h_both] + [chunk] * 4,
        [triple_hold, c_hold, pltpu.SemaphoreType.DMA((1,))],
        300,
        "qkv_first",
        24,
    )(
        scal, inputs, mask_embed[None], condition, adaptive_weight, adaptive_bias[:, None, :], biases, cosine, sine,
        triple_weight,
    )

    def attend(chunks, after):
        return call(
            attend_kernel,
            [VM] * 4,
            [o_chunk] * 4 + [shaped(4, 8, rows), shaped(4, GROUP, rows)],
            [
                pltpu.VMEM((4, rows, GROUP), BF),
                pltpu.VMEM((4 * rows, GROUP), BF),
                pltpu.VMEM((GROUP, 4 * rows), BF),
            ],
            300,
            "attend",
            20,
            after,
        )(*chunks)

    def attend_back(chunks, given, lse, turned, after):
        return call(
            attend_back_kernel,
            [VM] * 12,
            [chunk] * 4 + [shaped(4, packed, 2 * GROUP, dtype=BF)],
            [
                pltpu.VMEM((3, 4 * rows, GROUP), BF),
                pltpu.VMEM((3, 4 * rows, GROUP), BF),
                pltpu.VMEM((4, rows, GROUP), BF),
                pltpu.VMEM((4, rows, GROUP), BF),
                pltpu.VMEM((4, GROUP, rows), BF),
                pltpu.VMEM((8, 4 * rows), F32),
                pltpu.VMEM((8, 4 * rows), F32),
                pltpu.VMEM((GROUP, 4 * rows), F32),
                pltpu.VMEM((4, rows, GROUP), F32),
                pltpu.VMEM((4, rows, GROUP), F32),
            ],
            300,
            "attend_back",
            24,
            after,
        )(*chunks, *given, lse, turned, cosine, sine)

    def far(values):
        return swap(values, "dp", 1)

    def gather_rows(both):
        near = swap(both, "blk", 1)
        return [both, near, swap(both, "blk", 2), swap(near, "blk", 2)]

    chunks0 = swap_chunks([c0, c1, c2, c3])
    h_rows0 = gather_rows(h_rows)
    *o_chunks, lse0, ot0 = attend(chunks0, ())
    o_chunks = swap_chunks(o_chunks)
    aout0, m0, turned0, slope0, f0, x1, h_rows, c0, c1, c2, c3 = call(
        middle_kernel,
        [SM] + [VM] * 9 + [HBM] * 4,
        [b_square, f_square, shaped(tall, rows, dtype=BF), b_tall, b_square, f_square, h_both] + [chunk] * 4,
        [output_hold, expand_hold, shrink_hold, triple_hold, o_hold, pltpu.VMEM((rows, WIDTH), BF), c_hold]
        + [pltpu.SemaphoreType.DMA((4,))],
        300,
        "mlp_qkv",
        36,
        h_rows0[1:3],
    )(scal, x0, mod, biases, cosine, sine, *o_chunks, output_weight, expand_weight, shrink_weight, triple_weight)
    turned0_far = far(turned0)
    chunks1 = swap_chunks([c0, c1, c2, c3])
    h_rows1 = gather_rows(h_rows)
    *o_chunks, lse1, ot1 = attend(chunks1, h_rows0[3:])
    o_chunks = swap_chunks(o_chunks)
    outputs, aout1, m1, turned1, slope1, f1 = call(
        ahead_kernel,
        [SM] + [VM] * 7 + [HBM] * 3,
        [shaped(1, rows, WIDTH, dtype=BF), b_square, f_square, shaped(tall, rows, dtype=BF), b_tall, b_square],
        [output_hold, expand_hold, shrink_hold, o_hold, pltpu.VMEM((rows, WIDTH), BF), pltpu.SemaphoreType.DMA((3,))],
        300,
        "mlp_ahead",
        32,
        [*h_rows1[1:3], turned0_far],
    )(scal, x1, mod, biases, *o_chunks, output_weight, expand_weight, shrink_weight)
    turned1_far = far(turned1)
    back_outs = [o_chunk] * 4 + [f_square, shaped(1, 7680)]
    mine1, theirs1, *given, dm1, vec1 = call(
        turn_kernel,
        [SM] + [VM] * 6 + [HBM] * 3,
        [shaped(rows, half_width, dtype=BF)] * 2 + back_outs,
        [output_hold, expand_hold, shrink_hold, o_hold, pltpu.VMEM((2, rows, half_width), BF)]
        + [pltpu.SemaphoreType.DMA((3,))],
        300,
        "mlp_turn",
        32,
        h_rows1[3:],
    )(scal, cotangent, mod, m1, f1, slope1, aout1, output_weight, expand_weight, shrink_weight)
    given = swap_chunks(given)
    products = (
        (hidden, hidden + WIDTH, 0, (7, 5)),
        (0, hidden, hidden // 2, (1, 2)),
        (hidden + WIDTH, tall, hidden // 2 + WIDTH // 2, (2, 1)),
    )
    bucket1 = weight_bucket(scal, turned1, turned1_far, mine1, far(theirs1), products, ("axyb", "yaxb"))
    *grads, stacked = attend_back(chunks1, given, lse1, ot1, bucket1.sent[:1])
    grads = swap_chunks(grads)
    triple1 = Triple(scal, h_rows1, stacked)
    bucket1.advance()
    mine0, theirs0, first1, *given, dm0, vec0 = call(
        back_kernel,
        [SM] + [VM] * 11 + [HBM] * 4,
        [shaped(rows, half_width, dtype=BF)] * 2 + [shaped(1, 3840)] + back_outs,
        [triple_hold, output_hold, expand_hold, shrink_hold, c_hold, pltpu.VMEM((rows, 3 * WIDTH), BF), o_hold]
        + [pltpu.VMEM((2, rows, half_width), BF), pltpu.SemaphoreType.DMA((4,))],
        300,
        "qkv_mlp_back",
        36,
        bucket1.sent + triple1.sent,
    )(
        scal, x1, dm1, mod, *grads, m0, f0, slope0, aout0, triple_weight, output_weight, expand_weight, shrink_weight
    )
    given = swap_chunks(given)
    bucket1.advance()
    bucket0 = weight_bucket(
        scal, turned0, turned0_far, mine0, far(theirs0), products, ("ayxb", "xayb")
    )
    *grads, stacked = attend_back(chunks0, given, lse0, ot0, bucket0.sent[:1] + bucket1.sent)
    grads = swap_chunks(grads)
    triple0 = Triple(scal, h_rows0, stacked)
    triple1.advance()
    bucket0.advance()
    bucket1.advance()
    first0, input_grad, mask_term = call(
        last_kernel,
        [SM] + [VM] * 7 + [HBM],
        [shaped(1, 3840), shaped(1, rows, WIDTH), shaped(1, WIDTH)],
        [triple_hold, c_hold, pltpu.VMEM((rows, 3 * WIDTH), BF), pltpu.SemaphoreType.DMA((1,))],
        300,
        "qkv_back",
        24,
        [*triple0.sent, *triple1.sent, *bucket0.sent, *bucket1.sent],
    )(scal, x0, dm0, mod, *grads, triple_weight)
    triple0.advance()
    triple0.advance()
    bucket0.advance()
    bucket0.advance()
    triple1.advance()
    parts = [*settle(bucket1, scal, products), *settle(bucket0, scal, products)]
    plans = (
        plan_of(products, ((2, 1), (3, 1), (1, 1))),
        plan_of(products, ((2, 0), (3, 0), (1, 0))),
    )
    weight_grads = call(
        functools.partial(finish_kernel, plans),
        [SM] + [VM] * 12,
        [
            shaped(LAYERS, WIDTH // 32, 3 * WIDTH),
            shaped(LAYERS, WIDTH // 32, WIDTH),
            shaped(LAYERS, WIDTH // 32, hidden),
            shaped(LAYERS, hidden // 32, WIDTH),
        ],
        [pltpu.VMEM((4, WIDTH // 32, 3 * GROUP), F32)],
        0.1,
        "finish",
        12,
    )(scal, *parts, *triple0.settle(), *triple1.settle())

    small = jnp.concatenate([first0, vec0, first1, vec1, mask_term], 1)
    small = small + swap(small, "blk", 1)
    small = small + swap(small, "blk", 2)
    dmods, sums = [], []
    for layer in range(LAYERS):
        first = small[:, layer * 11520 : layer * 11520 + 3840]
        vec = small[:, layer * 11520 + 3840 : (layer + 1) * 11520]
        dmods += [first[:, 0:1536], vec[:, 2304:3072], vec[:, 768:2304], vec[:, 0:768]]
        sums += [first[:, 1536:3840], vec[:, 6912:7680], vec[:, 3840:6912], vec[:, 3072:3840]]
    dmod = jnp.concatenate(dmods, 1)
    gathered = jnp.concatenate([dmod, condition], 1)
    total = jnp.concatenate(sums + [small[:, 2 * 11520 :]], 1)
    condition_grad = sum(
        lax.dot_general(
            dmod[:, layer * 6 * WIDTH : (layer + 1) * 6 * WIDTH],
            adaptive_weight[layer].astype(F32),
            (((1,), (1,)), ((), ())),
            precision=HIGHEST,
        )
        for layer in range(LAYERS)
    )
    for bit in (1, 2, 4):
        gathered = jnp.concatenate([gathered, swap(gathered, "dp", bit)], 0)
        total = total + swap(total, "dp", bit)
    index = blk * 8 + dp
    share_rows = condition.shape[1] // 32
    near = lax.dynamic_slice_in_dim(gathered[:, 12 * WIDTH :], index * share_rows, share_rows, 1)
    gathered = gathered[:, : 12 * WIDTH]
    adaptive_w = jnp.sum(near[:, :, None] * gathered[:, None, :], 0)
    adaptive_w = jnp.stack([adaptive_w[:, : 6 * WIDTH], adaptive_w[:, 6 * WIDTH :]], 0)
    adaptive_all = jnp.sum(gathered, 0)

    def cut(values):
        size = values.shape[0] // 32
        return lax.dynamic_slice_in_dim(values, index * size, size, 0)

    adaptive_b = jnp.stack([cut(adaptive_all[: 6 * WIDTH]), cut(adaptive_all[6 * WIDTH :])], 0)
    total = total[0]
    bias_grads = []
    for low, high in BIAS_AT.values():
        bias_grads.append(jnp.stack([cut(total[low:high]), cut(total[6912 + low : 6912 + high])], 0))
    mask_sum = cut(total[2 * 6912 :])
    return (
        outputs,
        input_grad,
        condition_grad,
        mask_sum,
        adaptive_w,
        adaptive_b,
        weight_grads[0],
        bias_grads[0],
        weight_grads[1],
        bias_grads[1],
        weight_grads[2],
        bias_grads[2],
        weight_grads[3],
        bias_grads[3],
    )


def solution(mesh):
    in_specs = (
        P("dp", "blk", None),
        P("dp", None),
        P("dp"),
        P(),
        P(),
        P(),
        P(),
        P(),
        P(),
        P(),
        P(),
        P(),
        P(),
        P(),
        P("dp", "blk", None),
    )
    out_specs = (
        P("dp", "blk", None),
        P("dp", "blk", None),
        P("dp", None),
        P(("blk", "dp")),
        P(None, ("blk", "dp"), None),
        P(None, ("blk", "dp")),
        P(None, ("blk", "dp"), None),
        P(None, ("blk", "dp")),
        P(None, ("blk", "dp"), None),
        P(None, ("blk", "dp")),
        P(None, ("blk", "dp"), None),
        P(None, ("blk", "dp")),
        P(None, ("blk", "dp"), None),
        P(None, ("blk", "dp")),
    )
    whole = mesh.shape["blk"] == 4 and mesh.shape["dp"] == 8
    body = local_fast if whole else local
    return jax.shard_map(body, mesh=mesh, in_specs=in_specs, out_specs=out_specs, check_vma=False)
```

```python
import functools
import math

import jax
import jax.numpy as jnp
from jax import lax
from jax.experimental import pallas as pl
from jax.experimental.pallas import tpu as pltpu
from jax.sharding import PartitionSpec as P

HEADS = 12
HEAD_DIM = 64
LAYERS = 2


HIGHEST = lax.Precision.HIGHEST
EPSILON = 1e-06


def modulate(residual, shift, scaling):
    average = jnp.mean(residual, -1, keepdims=True)
    centered = residual - average
    variance = jnp.mean(centered * centered, -1, keepdims=True)
    return centered * lax.rsqrt(variance + EPSILON) * (1.0 + scaling) + shift


def gelu_tanh(values):
    return jax.nn.gelu(values, approximate=True)


def tables(offset, row_count, head_dim):
    half_dim = head_dim // 2
    position = (offset + jnp.arange(row_count, dtype=jnp.int32)).astype(jnp.float32)
    frequency = jnp.exp(
        jnp.arange(half_dim, dtype=jnp.float32) * (-2.0 * math.log(10000.0) / head_dim)
    )
    angles = position[:, None] * frequency[None, :]
    return (jnp.cos(angles)[:, None, :], jnp.sin(angles)[:, None, :])


def rotate(vectors, cosine, sine_table):
    half_dim = vectors.shape[-1] // 2
    front_half = vectors[..., :half_dim]
    back_half = vectors[..., half_dim:]
    return jnp.concatenate(
        [
            front_half * cosine - back_half * sine_table,
            back_half * cosine + front_half * sine_table,
        ],
        -1,
    )


def unrotate(gradient, cosine, sine_table):
    half_dim = gradient.shape[-1] // 2
    front_half = gradient[..., :half_dim]
    back_half = gradient[..., half_dim:]
    return jnp.concatenate(
        [
            front_half * cosine + back_half * sine_table,
            back_half * cosine - front_half * sine_table,
        ],
        -1,
    )


def split_einsum(form, float_left, low_right):
    upper = float_left.astype(jnp.bfloat16)
    lower = (float_left - upper.astype(jnp.float32)).astype(jnp.bfloat16)
    first = jnp.einsum(form, upper, low_right, preferred_element_type=jnp.float32)
    return first + jnp.einsum(form, lower, low_right, preferred_element_type=jnp.float32)


def fold_keys(queries, scaling):

    def absorb(carried, key_piece, offset):
        key_flat, value_flat = key_piece
        piece_rows = key_flat.shape[0]
        block_rows = math.gcd(piece_rows, 512)
        key_blocks = key_flat.reshape(piece_rows // block_rows, block_rows, HEADS, HEAD_DIM)
        value_blocks = value_flat.reshape(piece_rows // block_rows, block_rows, HEADS, HEAD_DIM)

        def absorb_inner(running, block_pair):
            running_max, running_sum, weighted = running
            key_block, value_block = block_pair
            scores = (
                jnp.einsum("qhd,khd->hqk", queries, key_block, preferred_element_type=jnp.float32)
                * scaling
            )
            new_max = jnp.maximum(running_max, jnp.max(scores, -1))
            weights = jnp.exp(scores - new_max[..., None])
            factor = jnp.exp(running_max - new_max)
            running_sum = running_sum * factor + jnp.sum(weights, -1)
            weighted = weighted * factor[..., None] + split_einsum(
                "hqk,khd->hqd", weights, value_block
            )
            return ((new_max, running_sum, weighted), None)

        carried, _ = lax.scan(absorb_inner, carried, (key_blocks, value_blocks))
        return carried

    return absorb


def attend_back(queries, key_all, value_all, out_gradient, attended_f, log_total, scaling):
    row_count = queries.shape[0]
    all_rows = key_all.shape[0]
    block_rows = math.gcd(all_rows, 512)
    key_blocks = key_all.reshape(all_rows // block_rows, block_rows, HEADS, HEAD_DIM)
    value_blocks = value_all.reshape(all_rows // block_rows, block_rows, HEADS, HEAD_DIM)
    out_float = out_gradient.astype(jnp.float32)
    row_delta = jnp.transpose(jnp.sum(out_float * attended_f, -1), (1, 0))

    def attend_inner(query_grad, block_pair):
        key_block, value_block = block_pair
        scores = (
            jnp.einsum("qhd,khd->hqk", queries, key_block, preferred_element_type=jnp.float32)
            * scaling
        )
        probs = jnp.exp(scores - log_total[..., None])
        prob_grad = jnp.einsum(
            "qhd,khd->hqk", out_gradient, value_block, preferred_element_type=jnp.float32
        )
        score_grad = (probs * (prob_grad - row_delta[..., None])).astype(jnp.bfloat16)
        query_grad = query_grad + jnp.einsum(
            "hqk,khd->qhd", score_grad, key_block, preferred_element_type=jnp.float32
        )
        key_grad = (
            jnp.einsum("hqk,qhd->khd", score_grad, queries, preferred_element_type=jnp.float32)
            * scaling
        )
        value_grad = split_einsum("hqk,qhd->khd", probs, out_gradient)
        return (query_grad, (key_grad, value_grad))

    start_grad = jnp.zeros((row_count, HEADS, HEAD_DIM), jnp.float32)
    query_grad, (key_grads, value_grads) = lax.scan(
        attend_inner, start_grad, (key_blocks, value_blocks)
    )
    width = HEADS * HEAD_DIM
    return (
        query_grad * scaling,
        key_grads.reshape(all_rows, width),
        value_grads.reshape(all_rows, width),
    )


def forward_layer(residual, modulation, layer_index, weights, cosine, sine_table, scaling):
    (
        adaptive_weight,
        adaptive_bias,
        triple_weight,
        triple_bias,
        output_weight,
        output_bias,
        expand_weight,
        expand_bias,
        shrink_weight,
        shrink_bias,
    ) = weights
    row_count, width = residual.shape
    pieces = [modulation[number * width : (number + 1) * width] for number in range(6)]
    shift_attn, scale_attn, gate_attn, shift_mlp, scale_mlp, gate_mlp = pieces
    normed = modulate(residual, shift_attn, scale_attn).astype(jnp.bfloat16)
    mixed = jnp.dot(
        normed, triple_weight[layer_index], preferred_element_type=jnp.float32
    ) + triple_bias[layer_index].astype(jnp.float32)
    head_shape = (row_count, HEADS, HEAD_DIM)
    queries = rotate(mixed[:, :width].reshape(head_shape), cosine, sine_table).astype(jnp.bfloat16)
    key_flat = (
        rotate(mixed[:, width : 2 * width].reshape(head_shape), cosine, sine_table)
        .astype(jnp.bfloat16)
        .reshape(row_count, width)
    )
    value_flat = mixed[:, 2 * width :].astype(jnp.bfloat16)
    start_state = (
        jnp.full((HEADS, row_count), -1e30, jnp.float32),
        jnp.zeros((HEADS, row_count), jnp.float32),
        jnp.zeros((HEADS, row_count, HEAD_DIM), jnp.float32),
    )
    absorb = fold_keys(queries, scaling)
    final_state = absorb(
        start_state,
        (
            lax.all_gather(key_flat, "blk", axis=0, tiled=True),
            lax.all_gather(value_flat, "blk", axis=0, tiled=True),
        ),
        jnp.int32(0),
    )
    running_max, running_sum, weighted = final_state
    log_total = running_max + jnp.log(running_sum)
    attended_f = jnp.transpose(weighted / running_sum[..., None], (1, 0, 2))
    attended = attended_f.reshape(row_count, width).astype(jnp.bfloat16)
    branch = jnp.dot(
        attended, output_weight[layer_index], preferred_element_type=jnp.float32
    ) + output_bias[layer_index].astype(jnp.float32)
    middle = residual + gate_attn * branch
    normed_mlp = modulate(middle, shift_mlp, scale_mlp).astype(jnp.bfloat16)
    up_proj = jnp.dot(
        normed_mlp, expand_weight[layer_index], preferred_element_type=jnp.float32
    ) + expand_bias[layer_index].astype(jnp.float32)
    active = gelu_tanh(up_proj).astype(jnp.bfloat16)
    lowered = jnp.dot(
        active, shrink_weight[layer_index], preferred_element_type=jnp.float32
    ) + shrink_bias[layer_index].astype(jnp.float32)
    result = middle + gate_mlp * lowered
    saved = (
        residual,
        normed,
        queries,
        key_flat,
        value_flat,
        None,
        attended_f,
        attended,
        log_total,
        branch,
        middle,
        normed_mlp,
        up_proj,
        active,
        lowered,
    )
    return (result, saved)


def backward_layer(
    gradient, modulation, layer_index, weights, saved, cosine, sine_table, scaling, condition
):
    (
        adaptive_weight,
        adaptive_bias,
        triple_weight,
        triple_bias,
        output_weight,
        output_bias,
        expand_weight,
        expand_bias,
        shrink_weight,
        shrink_bias,
    ) = weights
    (
        residual,
        normed,
        queries,
        key_flat,
        value_flat,
        gathered,
        attended_f,
        attended,
        log_total,
        branch,
        middle,
        normed_mlp,
        up_proj,
        active,
        lowered,
    ) = saved
    row_count, width = residual.shape
    pieces = [modulation[number * width : (number + 1) * width] for number in range(6)]
    shift_attn, scale_attn, gate_attn, shift_mlp, scale_mlp, gate_mlp = pieces
    gate_mlp_grad = jnp.sum(gradient * lowered, 0)
    lowered_grad = (gradient * gate_mlp).astype(jnp.bfloat16)
    shrink_w_grad = jnp.einsum(
        "tf,td->fd", active, lowered_grad, preferred_element_type=jnp.float32
    )
    shrink_b_grad = jnp.sum(lowered_grad.astype(jnp.float32), 0)
    active_grad = jnp.einsum(
        "td,fd->tf", lowered_grad, shrink_weight[layer_index], preferred_element_type=jnp.float32
    )
    _, gelu_pull = jax.vjp(gelu_tanh, up_proj)
    up_grad = gelu_pull(active_grad)[0].astype(jnp.bfloat16)
    expand_w_grad = jnp.einsum("td,tf->df", normed_mlp, up_grad, preferred_element_type=jnp.float32)
    expand_b_grad = jnp.sum(up_grad.astype(jnp.float32), 0)
    normed_mlp_grad = jnp.einsum(
        "tf,df->td", up_grad, expand_weight[layer_index], preferred_element_type=jnp.float32
    )
    _, mlp_pull = jax.vjp(modulate, middle, shift_mlp, scale_mlp)
    middle_grad, shift_mlp_grad, scale_mlp_grad = mlp_pull(normed_mlp_grad)
    middle_grad = middle_grad + gradient
    gate_attn_grad = jnp.sum(middle_grad * branch, 0)
    branch_grad = (middle_grad * gate_attn).astype(jnp.bfloat16)
    output_w_grad = jnp.einsum(
        "tc,td->cd", attended, branch_grad, preferred_element_type=jnp.float32
    )
    output_b_grad = jnp.sum(branch_grad.astype(jnp.float32), 0)
    attended_grad = jnp.einsum(
        "td,cd->tc", branch_grad, output_weight[layer_index], preferred_element_type=jnp.float32
    )
    attended_grad = attended_grad.astype(jnp.bfloat16).reshape(row_count, HEADS, HEAD_DIM)
    key_all, value_all = (
        lax.all_gather(key_flat, "blk", axis=0, tiled=True),
        lax.all_gather(value_flat, "blk", axis=0, tiled=True),
    )
    query_grad, key_all_grad, value_all_grad = attend_back(
        queries, key_all, value_all, attended_grad, attended_f, log_total, scaling
    )
    key_grad, value_grad = (
        lax.psum_scatter(
            key_all_grad.astype(jnp.bfloat16), "blk", scatter_dimension=0, tiled=True
        ).astype(jnp.float32),
        lax.psum_scatter(
            value_all_grad.astype(jnp.bfloat16), "blk", scatter_dimension=0, tiled=True
        ).astype(jnp.float32),
    )
    mixed_grad = jnp.concatenate(
        [
            unrotate(query_grad, cosine, sine_table).reshape(row_count, width),
            unrotate(key_grad.reshape(row_count, HEADS, HEAD_DIM), cosine, sine_table).reshape(
                row_count, width
            ),
            value_grad,
        ],
        -1,
    ).astype(jnp.bfloat16)
    triple_w_grad = jnp.einsum("td,tc->dc", normed, mixed_grad, preferred_element_type=jnp.float32)
    triple_b_grad = jnp.sum(mixed_grad.astype(jnp.float32), 0)
    normed_grad = jnp.einsum(
        "tc,dc->td", mixed_grad, triple_weight[layer_index], preferred_element_type=jnp.float32
    )
    _, attn_pull = jax.vjp(modulate, residual, shift_attn, scale_attn)
    residual_grad, shift_attn_grad, scale_attn_grad = attn_pull(normed_grad)
    residual_grad = residual_grad + middle_grad
    modulation_grad = jnp.concatenate(
        [
            shift_attn_grad,
            scale_attn_grad,
            gate_attn_grad,
            shift_mlp_grad,
            scale_mlp_grad,
            gate_mlp_grad,
        ],
        0,
    )
    adaptive_w_grad = condition[0][:, None] * modulation_grad[None, :]
    condition_term = jnp.dot(
        adaptive_weight[layer_index].astype(jnp.float32), modulation_grad, precision=HIGHEST
    )
    grad_terms = (
        adaptive_w_grad,
        modulation_grad,
        triple_w_grad,
        triple_b_grad,
        output_w_grad,
        output_b_grad,
        expand_w_grad,
        expand_b_grad,
        shrink_w_grad,
        shrink_b_grad,
    )
    return (residual_grad, grad_terms, condition_term)


def local(
    inputs,
    condition,
    prefix,
    mask_embed,
    adaptive_weight,
    adaptive_bias,
    triple_weight,
    triple_bias,
    output_weight,
    output_bias,
    expand_weight,
    expand_bias,
    shrink_weight,
    shrink_bias,
    cotangent,
):
    weights = (
        adaptive_weight,
        adaptive_bias,
        triple_weight,
        triple_bias,
        output_weight,
        output_bias,
        expand_weight,
        expand_bias,
        shrink_weight,
        shrink_bias,
    )
    row_count = inputs.shape[1]
    offset = lax.axis_index("blk") * row_count
    position = offset + jnp.arange(row_count, dtype=jnp.int32)
    masked = position >= prefix[0]
    residual = jnp.where(
        masked[:, None], mask_embed.astype(jnp.float32)[None, :], inputs[0].astype(jnp.float32)
    )
    cosine, sine_table = tables(offset, row_count, HEAD_DIM)
    scaling = 1.0 / math.sqrt(HEAD_DIM)
    modulations = []
    saved_layers = []
    for layer_index in range(LAYERS):
        modulation = jnp.dot(
            condition, adaptive_weight[layer_index].astype(jnp.float32), precision=HIGHEST
        )[0] + adaptive_bias[layer_index].astype(jnp.float32)
        residual, saved = forward_layer(
            residual, modulation, layer_index, weights, cosine, sine_table, scaling
        )
        modulations.append(modulation)
        saved_layers.append(saved)
    outputs = residual.astype(jnp.bfloat16)[None]
    gradient = cotangent[0].astype(jnp.float32)
    condition_total = jnp.zeros((condition.shape[1],), jnp.float32)
    collected = [None] * LAYERS
    mask_sum = None
    for layer_index in reversed(range(LAYERS)):
        gradient, grad_terms, condition_term = backward_layer(
            gradient,
            modulations[layer_index],
            layer_index,
            weights,
            saved_layers[layer_index],
            cosine,
            sine_table,
            scaling,
            condition,
        )
        condition_total = condition_total + condition_term
        collected[layer_index] = grad_terms
    mask_term = jnp.sum(jnp.where(masked[:, None], gradient, 0.0), 0)
    flat_terms = ()
    for layer_index in range(LAYERS):
        flat_terms = flat_terms + tuple(collected[layer_index])
    summed = lax.psum_scatter(
        flat_terms + (mask_term,), ("blk", "dp"), scatter_dimension=0, tiled=True
    )
    collected = [summed[layer_index * 10 : (layer_index + 1) * 10] for layer_index in range(LAYERS)]
    mask_sum = summed[LAYERS * 10]
    condition_grad = lax.psum(condition_total, "blk")[None, :]
    input_grad = jnp.where(masked[:, None], 0.0, gradient)[None]
    stacked = [
        jnp.stack([collected[layer_index][number] for layer_index in range(LAYERS)], 0)
        for number in range(10)
    ]
    return (
        outputs,
        input_grad,
        condition_grad,
        mask_sum,
        stacked[0],
        stacked[1],
        stacked[2],
        stacked[3],
        stacked[4],
        stacked[5],
        stacked[6],
        stacked[7],
        stacked[8],
        stacked[9],
    )


BF = jnp.bfloat16
F32 = jnp.float32
WIDTH = HEADS * HEAD_DIM
GROUP = WIDTH // 4
VM = pl.BlockSpec(memory_space=pltpu.VMEM)
ANY = pl.BlockSpec(memory_space=pl.ANY)
HBM = pl.BlockSpec(memory_space=pltpu.HBM)
HV = pl.BlockSpec(memory_space=pltpu.VMEM)
SM = pl.BlockSpec(memory_space=pltpu.SMEM)
MEBI = 1024 * 1024
ROOT_TWO_PI = math.sqrt(2.0 / math.pi)
CUBIC = 0.044715


def dot_nn(left, right):
    return jnp.dot(left, right, preferred_element_type=F32)


def dot_nt(left, right):
    return lax.dot_general(left, right, (((1,), (1,)), ((), ())), preferred_element_type=F32)


def dot_tn(left, right):
    return lax.dot_general(left, right, (((0,), (0,)), ((), ())), preferred_element_type=F32)


def normalise(values):
    centered = values - jnp.mean(values, -1, keepdims=True)
    rstd = lax.rsqrt(jnp.mean(centered * centered, -1, keepdims=True) + EPSILON)
    return centered * rstd, rstd


def normalise_back(upstream, unit, rstd):
    first = jnp.mean(upstream, -1, keepdims=True)
    second = jnp.mean(upstream * unit, -1, keepdims=True)
    return rstd * (upstream - first - unit * second)


def column_sum(values):
    return jnp.sum(values, 0, keepdims=True)


def turn(values, cosine, signed_sine):
    lane = lax.broadcasted_iota(jnp.int32, (values.shape[0], 128), 1)
    front = (lane % HEAD_DIM) < HEAD_DIM // 2
    pieces = []
    for start in range(0, values.shape[1], 128):
        piece = values[:, start : start + 128]
        swapped = jnp.where(front, pltpu.roll(piece, 96, 1), pltpu.roll(piece, 32, 1))
        pieces.append(piece * cosine + swapped * signed_sine)
    return jnp.concatenate(pieces, 1)


def piece_of(row, number):
    return row[:, number * WIDTH : (number + 1) * WIDTH]


def row_of(ref, layer):
    return ref[...].astype(F32)[layer : layer + 1, :]


def pack_rows(values):
    half = values.shape[0] // 2
    return jnp.concatenate([values[:half], values[half:]], 1)


def qkv_stage(x, layer, mod_row, triple_bias, triple, cos_ref, sin_ref, me, h_ref, chunk_refs, hold):
    unit, _ = normalise(x)
    h = unit * (1.0 + piece_of(mod_row, 1)) + piece_of(mod_row, 0)
    turned = h.T
    h = h.astype(BF)
    each = WIDTH // 32
    for half in range(2):
        picked = [turned[each * (b * 8 + z * 2 + half) :][:each] for z in range(4) for b in range(4)]
        h_ref[half] = jnp.concatenate(picked, 0).astype(BF)
    bias = row_of(triple_bias, layer)
    cosine, sine = cos_ref[0], sin_ref[0]
    parts = []
    for number in range(3):
        columns = slice(number * WIDTH, (number + 1) * WIDTH)
        mixed = dot_nn(h, triple[:, columns]) + bias[:, columns]
        if number < 2:
            mixed = turn(mixed, cosine, sine)
        if number == 0:
            mixed = mixed * HEAD_DIM**-0.5
        parts.append(mixed)
    rows = x.shape[0]
    for group in range(4):
        columns = slice(group * GROUP, (group + 1) * GROUP)
        pair = jnp.concatenate([parts[0][:, columns], parts[1][:, columns]], 1)
        hold[group, 0:rows, :] = pair.astype(BF)
        hold[group, rows : rows + rows // 2, :] = pack_rows(parts[2][:, columns]).astype(BF)
    for place in range(4):
        chunk_refs[place][...] = hold[place ^ me]


def fetch(pairs, sems):
    copies = []
    for number, (source, target) in enumerate(pairs):
        copy = pltpu.make_async_copy(source, target, sems.at[number])
        copy.start()
        copies.append(copy)
    return copies


def three_rows(row):
    upper = row.astype(BF).astype(F32)
    rest = row - upper
    middle = rest.astype(BF).astype(F32)
    low = rest - middle
    number = lax.broadcasted_iota(jnp.int32, (8, row.shape[1]), 0)
    return jnp.where(number == 0, upper, jnp.where(number == 1, middle, jnp.where(number == 2, low, 0.0))).astype(BF)


def modulation(cond, adaptive, adaptive_bias, layer):
    return column_sum(dot_nn(three_rows(cond), adaptive[...])) + row_of(adaptive_bias, layer)


def first_kernel(
    scal, mask_embed, cos_ref, sin_ref, inputs_any, condition_any, adaptive_bias_any, triple_bias_any, adaptive_any,
    triple_any,
    x_ref, mod_ref, h_ref, c0, c1, c2, c3,
    inputs, condition, adaptive_bias, triple_bias, adaptive, triple, hold, sems,
):
    copies = fetch(
        [
            (adaptive_any.at[0], adaptive), (triple_any.at[0], triple), (inputs_any, inputs),
            (condition_any, condition), (adaptive_bias_any, adaptive_bias), (triple_bias_any, triple_bias),
        ],
        sems,
    )
    for copy in copies[2:]:
        copy.wait()
    me = scal[0]
    rows = inputs.shape[1]
    position = me * rows + lax.broadcasted_iota(jnp.int32, (rows, WIDTH), 0)
    x = jnp.where(position >= scal[3], mask_embed[...].astype(F32), inputs[0].astype(F32))
    x_ref[...] = x
    copies[0].wait()
    mod = modulation(condition[...], adaptive, adaptive_bias, 0)
    mod_ref[...] = mod
    copies[1].wait()
    qkv_stage(x, 0, mod, triple_bias, triple, cos_ref, sin_ref, me, h_ref, (c0, c1, c2, c3), hold)


def attend_kernel(
    c0, c1, c2, c3,
    o0, o1, o2, o3, lse_ref, of_ref,
    ot_ref, q_all, k_all, v_turned,
):
    rows = 256
    for place, chunk in enumerate((c0, c1, c2, c3)):
        span = slice(place * rows, (place + 1) * rows)
        q_all[place] = chunk[0:rows, 0:GROUP]
        k_all[span, :] = chunk[0:rows, GROUP : 2 * GROUP]
        tail = chunk[rows : rows + rows // 2, :]
        v_block = jnp.concatenate([tail[:, 0:GROUP], tail[:, GROUP : 2 * GROUP]], 0)
        v_block = v_block.T
        for number in range(3):
            v_turned[number, 0:HEAD_DIM, span] = v_block[number * HEAD_DIM : (number + 1) * HEAD_DIM]
    v_turned[:, HEAD_DIM:, :] = jnp.ones((3, 16, 4 * rows), BF)
    head = lax.broadcasted_iota(jnp.int32, (2 * rows, GROUP), 1) // HEAD_DIM

    for block in range(0, 4, 2):
        q = q_all[block : block + 2].reshape(2 * rows, GROUP)
        for number in range(3):
            masked = jnp.where(head == number, q, jnp.zeros_like(q))
            scores = dot_nt(k_all[...], masked)
            peak = jnp.max(scores, 0, keepdims=True)
            weights = jnp.exp(scores - peak).astype(BF)
            both = dot_nn(v_turned[number], weights)
            total = both[HEAD_DIM : HEAD_DIM + 1]
            span = slice(number * HEAD_DIM, (number + 1) * HEAD_DIM)
            found = both[0:HEAD_DIM] / total
            lse = peak + jnp.log(total)
            for part in range(2):
                columns = slice(part * rows, (part + 1) * rows)
                ot_ref[block + part, span, :] = found[:, columns]
                lse_ref[block + part, number : number + 1, :] = lse[:, columns]
    for place, out in enumerate((o0, o1, o2, o3)):
        found = ot_ref[place].T
        of_ref[place] = found
        out[...] = pack_rows(found).astype(BF)


def gather_chunks(refs, hold):
    for place in range(4):
        hold[place] = refs[place][...]


def mlp_forward(
    layer, x, mod_row, biases, me, o_refs, output, expand, shrink, waits, hold, o_ref, aout_ref, m_ref, turned_ref,
    slope_ref, f_ref,
):
    gather_chunks(o_refs, hold)
    rows = x.shape[0]
    half = rows // 2
    for group in range(4):
        chunk = hold[group ^ me]
        columns = slice(group * GROUP, (group + 1) * GROUP)
        o_ref[0:half, columns] = chunk[:, 0:GROUP]
        o_ref[half:rows, columns] = chunk[:, GROUP : 2 * GROUP]
    o = o_ref[...]
    hidden = expand.shape[1]
    turned_ref[hidden + WIDTH : hidden + 2 * WIDTH, :] = o.T
    waits[0].wait()
    a_out = dot_nn(o, output[...]) + row_of(biases[0], layer)
    aout_ref[...] = a_out.astype(BF)
    m = x + piece_of(mod_row, 2) * a_out
    m_ref[...] = m
    unit, _ = normalise(m)
    h2 = (unit * (1.0 + piece_of(mod_row, 4)) + piece_of(mod_row, 3)).astype(BF)
    turned_ref[hidden : hidden + WIDTH, :] = h2.T
    waits[1].wait()
    bias = row_of(biases[1], layer)
    f = row_of(biases[2], layer)
    for start in range(0, hidden, 768):
        columns = slice(start, start + 768)
        u = dot_nn(h2, expand[:, columns]) + bias[:, columns]
        square = u * u
        gate = 0.5 + 0.5 * jnp.tanh(u * (ROOT_TWO_PI + ROOT_TWO_PI * CUBIC * square))
        active = u * gate
        slope = gate + 2.0 * active * (1.0 - gate) * (ROOT_TWO_PI + 3.0 * ROOT_TWO_PI * CUBIC * square)
        z = active.astype(BF)
        turned_ref[columns, :] = z.T
        slope_ref[:, columns] = slope.astype(BF)
        if start == 0:
            waits[2].wait()
        f = f + dot_nn(z, shrink[columns, :])
    f_ref[...] = f.astype(BF)
    return m + piece_of(mod_row, 5) * f


def share(values, hold, at):
    half = values.shape[1] // 2
    hold[0, :, at : at + half] = values[:, 0:half]
    hold[1, :, at : at + half] = values[:, half : 2 * half]


def mlp_backward(
    dy, mod_row, me, core, m_ref, f_ref, slope_ref, aout_ref, output, expand, shrink, waits, halves,
    do_ref, dm_ref, vec_ref,
):
    def put(place, row):
        vec_ref[:, place : place + row.shape[1]] = row

    put(0, column_sum(dy * f_ref[...].astype(F32)))
    df = (dy * piece_of(mod_row, 5)).astype(BF)
    put(3072, column_sum(df.astype(F32)))
    hidden = expand.shape[1]
    share(df, halves, hidden // 2)
    dh2 = jnp.zeros(dy.shape, F32)
    waits[2].wait()
    for start in range(0, hidden, 768):
        columns = slice(start, start + 768)
        dz = dot_nt(df, shrink[columns, :])
        du = (slope_ref[:, columns].astype(F32) * dz).astype(BF)
        put(3840 + start, column_sum(du.astype(F32)))
        half = hidden // 2
        halves[start // half, :, start % half : start % half + 768] = du
        if start == 0:
            waits[1].wait()
        dh2 = dh2 + dot_nt(du, expand[:, columns])
    unit, rstd = normalise(m_ref[...])
    put(768, column_sum(dh2))
    put(1536, column_sum(dh2 * unit))
    dm = dy + normalise_back(dh2 * (1.0 + piece_of(mod_row, 4)), unit, rstd)
    dm_ref[...] = dm
    put(2304, column_sum(dm * aout_ref[...].astype(F32)))
    da = (dm * piece_of(mod_row, 2)).astype(BF)
    put(6912, column_sum(da.astype(F32)))
    share(da, halves, hidden // 2 + WIDTH // 2)
    waits[0].wait()
    do = dot_nt(da, output[...])
    for group in range(4):
        do_ref[group] = pack_rows(do[:, group * GROUP : (group + 1) * GROUP]).astype(BF)


def attend_back_kernel(
    scal, given_ref, c0, c1, c2, c3, lse_ref, of_ref, cos_any, sin_any, stacked,
    cos_ref, sin_ref, sems, q_masked, do_masked, k_all, v_all, k_turned, lse_rows, delta_rows, dq_turned, dk_all, dv_all,
):
    copies = fetch([(cos_any, cos_ref), (sin_any, sin_ref)], sems)
    rows = 256
    head = lax.broadcasted_iota(jnp.int32, (rows, GROUP), 1) // HEAD_DIM
    of_head = lax.broadcasted_iota(jnp.int32, (8, GROUP), 1) // HEAD_DIM
    pick = jnp.where(of_head == lax.broadcasted_iota(jnp.int32, (8, GROUP), 0), 1.0, 0.0).astype(BF)
    for place in range(4):
        chunk = (c0, c1, c2, c3)[place]
        given = given_ref[place ^ scal[0]]
        span = slice(place * rows, (place + 1) * rows)
        q = chunk[0:rows, 0:GROUP]
        k = chunk[0:rows, GROUP : 2 * GROUP]
        tail = chunk[rows : rows + rows // 2, :]
        v_all[place] = jnp.concatenate([tail[:, 0:GROUP], tail[:, GROUP : 2 * GROUP]], 0)
        k_all[place] = k
        k_turned[place] = k.T
        do = jnp.concatenate([given[:, 0:GROUP], given[:, GROUP : 2 * GROUP]], 0)
        product = do.astype(F32) * of_ref[place]
        upper = product.astype(BF)
        lower = (product - upper.astype(F32)).astype(BF)
        delta_rows[:, span] = dot_nt(pick, upper) + dot_nt(pick, lower)
        for number in range(3):
            q_masked[number, span, :] = jnp.where(head == number, q, jnp.zeros_like(q))
            do_masked[number, span, :] = jnp.where(head == number, do, jnp.zeros_like(do))
            lse_rows[number : number + 1, span] = lse_ref[place, number : number + 1, :]
    dq_turned[...] = jnp.zeros(dq_turned.shape, F32)

    for block in range(4 // 2):
        k = k_all[block * 2 : (block + 1) * 2].reshape(2 * rows, GROUP)
        v = v_all[block * 2 : (block + 1) * 2].reshape(2 * rows, GROUP)
        dk = jnp.zeros((2 * rows, GROUP), F32)
        dv = jnp.zeros((2 * rows, GROUP), F32)
        for number in range(3):
            span = slice(number * HEAD_DIM, (number + 1) * HEAD_DIM)
            scores = dot_nt(k, q_masked[number])
            probs = jnp.exp(scores - lse_rows[number : number + 1, :])
            prob_grad = dot_nt(v, do_masked[number])
            score_grad = (probs * (prob_grad - delta_rows[number : number + 1, :])).astype(BF)
            dv = dv + dot_nn(probs.astype(BF), do_masked[number])
            dk = dk + dot_nn(score_grad, q_masked[number])
            for part in range(2):
                dq_turned[span, :] += dot_nn(k_turned[block * 2 + part, span, :], score_grad[part * rows : (part + 1) * rows])
        dk_all[block * 2 : (block + 1) * 2] = dk.reshape(2, rows, GROUP)
        dv_all[block * 2 : (block + 1) * 2] = dv.reshape(2, rows, GROUP)
    for copy in copies:
        copy.wait()
    for place in range(4):
        span = slice(place * rows, (place + 1) * rows)
        dq = dq_turned[:, span].T * HEAD_DIM**-0.5
        pair = jnp.concatenate([dq, dk_all[place]], 1)
        pair = turn(pair, cos_ref[place], -sin_ref[place]).astype(BF)
        tail = pack_rows(dv_all[place]).astype(BF)
        stacked[place ^ scal[0], 0:rows, :] = pair
        stacked[place ^ scal[0], rows : rows + rows // 2, :] = tail


def qkv_backward(x, dm, mod_row, chunks, triple, wait, full, vec_ref):
    rows = x.shape[0]
    half = rows // 2
    for group in range(4):
        chunk = chunks(group)
        low = group * GROUP
        full[:, low : low + GROUP] = chunk[0:rows, 0:GROUP]
        full[:, WIDTH + low : WIDTH + low + GROUP] = chunk[0:rows, GROUP : 2 * GROUP]
        full[0:half, 2 * WIDTH + low : 2 * WIDTH + low + GROUP] = chunk[rows : rows + half, 0:GROUP]
        full[half:rows, 2 * WIDTH + low : 2 * WIDTH + low + GROUP] = chunk[rows : rows + half, GROUP : 2 * GROUP]
    dqkv = full[...]
    vec_ref[:, 1536:3840] = column_sum(dqkv.astype(F32))
    wait.wait()
    dh = dot_nt(dqkv, triple[...])
    unit, rstd = normalise(x)
    vec_ref[:, 0:768] = column_sum(dh)
    vec_ref[:, 768:1536] = column_sum(dh * unit)
    return dm + normalise_back(dh * (1.0 + piece_of(mod_row, 1)), unit, rstd)


def middle_kernel(
    scal, x_ref, mod_ref, condition, adaptive_bias, output_bias, expand_bias, shrink_bias, triple_bias,
    cos_ref, sin_ref, o0, o1, o2, o3, output_any, expand_any, shrink_any, triple_any, adaptive_any,
    aout_ref, m_ref, turned_ref, slope_ref, f_ref, y_ref, mod_next, h_ref, c0, c1, c2, c3,
    output, expand, shrink, triple, adaptive, o_hold, o_ref, c_hold, sems,
):
    copies = fetch(
        [
            (output_any.at[0], output), (expand_any.at[0], expand), (shrink_any.at[0], shrink),
            (triple_any.at[1], triple), (adaptive_any.at[1], adaptive),
        ],
        sems,
    )
    me = scal[0]
    y = mlp_forward(
        0, x_ref[...], mod_ref[...], (output_bias, expand_bias, shrink_bias), me, (o0, o1, o2, o3), output, expand, shrink, copies, o_hold, o_ref,
        aout_ref, m_ref, turned_ref, slope_ref, f_ref,
    )
    y_ref[...] = y
    copies[3].wait()
    copies[4].wait()
    mod = modulation(condition[...], adaptive, adaptive_bias, 1)
    mod_next[...] = mod
    qkv_stage(
        y, 1, mod, triple_bias, triple, cos_ref, sin_ref, me, h_ref, (c0, c1, c2, c3), c_hold,
    )


def ahead_kernel(
    scal, x_ref, mod_ref, output_bias, expand_bias, shrink_bias, o0, o1, o2, o3, output_any, expand_any, shrink_any,
    out_ref, aout_ref, m_ref, turned_ref, slope_ref, f_ref,
    output, expand, shrink, o_hold, o_ref, sems,
):
    copies = fetch([(output_any.at[1], output), (expand_any.at[1], expand), (shrink_any.at[1], shrink)], sems)
    y = mlp_forward(
        1, x_ref[...], mod_ref[...], (output_bias, expand_bias, shrink_bias), scal[0], (o0, o1, o2, o3), output, expand, shrink, copies, o_hold, o_ref,
        aout_ref, m_ref, turned_ref, slope_ref, f_ref,
    )
    out_ref[0] = y.astype(BF)


def turn_kernel(
    scal, mod_ref, m_ref, f_ref, slope_ref, aout_ref, cotangent_any, output_any, expand_any, shrink_any,
    mine, theirs, do_ref, dm_ref, vec_ref,
    output, expand, shrink, cotangent, halves, sems,
):
    copies = fetch(
        [
            (shrink_any.at[1], shrink), (expand_any.at[1], expand), (output_any.at[1], output),
            (cotangent_any, cotangent),
        ],
        sems,
    )
    copies[3].wait()
    me, core = scal[0], scal[2]
    mlp_backward(
        cotangent[0].astype(F32), mod_ref[...], me, core, m_ref, f_ref, slope_ref, aout_ref, output, expand, shrink,
        [copies[2], copies[1], copies[0]], halves, do_ref, dm_ref, vec_ref,
    )
    mine[...] = halves[core]
    theirs[...] = halves[1 - core]


def back_kernel(
    scal, x_ref, dm_in, mod_ref, mod_low, grads, m_ref, f_ref, slope_ref, aout_ref,
    triple_any, output_any, expand_any, shrink_any,
    mine, theirs, vec_first, do_ref, dm_ref, vec_ref,
    triple, output, expand, shrink, full, halves, sems,
):
    copies = fetch(
        [(triple_any.at[1], triple), (shrink_any.at[0], shrink), (expand_any.at[0], expand), (output_any.at[0], output)],
        sems,
    )
    me, core = scal[0], scal[2]
    dy = qkv_backward(
        x_ref[...], dm_in[...], mod_ref[...], lambda group: grads[group], triple, copies[0], full, vec_first,
    )
    mlp_backward(
        dy, mod_low[...], me, core, m_ref, f_ref, slope_ref, aout_ref, output, expand, shrink,
        [copies[3], copies[2], copies[1]], halves, do_ref, dm_ref, vec_ref,
    )
    mine[...] = halves[core]
    theirs[...] = halves[1 - core]


def last_kernel(
    scal, x_ref, dm_in, mod_ref, grads, triple_any,
    vec_first, input_grad, mask_ref,
    triple, full, sems,
):
    copies = fetch([(triple_any.at[0], triple)], sems)
    me = scal[0]
    dx = qkv_backward(
        x_ref[...], dm_in[...], mod_ref[...], lambda group: grads[group], triple, copies[0], full, vec_first,
    )
    rows = dx.shape[0]
    position = me * rows + lax.broadcasted_iota(jnp.int32, dx.shape, 0)
    masked = position >= scal[3]
    input_grad[0] = jnp.where(masked, 0.0, dx)
    mask_ref[...] = column_sum(jnp.where(masked, dx, 0.0))


def triple_kernel(
    scal, h0, h1, h2, h3, chunks,
    mine, theirs,
    result,
):
    rows = chunks.shape[1] * 2 // 3
    half = rows // 2
    each = WIDTH // 8
    for side in range(2):
        qk = jnp.zeros((WIDTH // 2, 2 * GROUP), F32)
        v = jnp.zeros((WIDTH // 2, GROUP), F32)
        for place, h_ref in enumerate((h0, h1, h2, h3)):
            h = h_ref[side]
            at = place ^ scal[0]
            qk = qk + dot_nn(h, chunks[at, 0:rows, :])
            tail = chunks[at, rows : rows + half, :]
            v = v + dot_nn(h, jnp.concatenate([tail[:, 0:GROUP], tail[:, GROUP : 2 * GROUP]], 0))
        for z in range(4):
            span = slice(z * each, (z + 1) * each)
            block = jnp.concatenate([qk[span], pack_rows(v[span])], 0).astype(BF)
            tall = block.shape[0]
            for number in range(3):
                lanes = slice(number * 128, (number + 1) * 128)
                result[side * 4 + z, number * tall : (number + 1) * tall, :] = block[:, lanes]
    for place, offset in enumerate((0, 2, 1, 3)):
        at = scal[1] ^ offset
        tall = result.shape[1]
        mine[place * tall : (place + 1) * tall, :] = result[scal[2] * 4 + at]
        theirs[place * tall : (place + 1) * tall, :] = result[(1 - scal[2]) * 4 + at]


def bring(layout, pieces, hold, sems):
    copies = []
    for number, (piece, source, slot, target, rows) in enumerate(layout):
        copy = pltpu.make_async_copy(
            pieces[piece].at[source : source + rows, :], hold.at[slot, target : target + rows, :], sems.at[number]
        )
        copy.start()
        copies.append(copy)
    for copy in copies:
        copy.wait()


def triple_settle_kernel(layout, scal, *refs):
    pieces, outs, (hold, blocks, sems) = refs[:-7], refs[-7:-3], refs[-3:]
    bring(layout, pieces, hold, sems)
    each, rows = WIDTH // 8, WIDTH // 32
    tall = each * 3 // 2
    for layer in range(LAYERS):
        lanes = []
        for number in range(3):
            at = (layer * 3 + number) * tall
            lanes.append(sum(hold[slot, at : at + tall, :].astype(F32) for slot in range(hold.shape[0])))
        total = jnp.concatenate(lanes, 1)
        v = jnp.concatenate([total[each:, 0:GROUP], total[each:, GROUP : 2 * GROUP]], 0)
        for b in range(4):
            span = slice(b * rows, (b + 1) * rows)
            blocks[layer, b, :, 0 : 2 * GROUP] = total[span]
            blocks[layer, b, :, 2 * GROUP : 3 * GROUP] = v[span]
    for place, out in enumerate(outs):
        for layer in range(LAYERS):
            out[layer] = blocks[layer, place ^ scal[0]]


BIT = {"x": 4, "y": 8, "a": 1, "b": 2}
STEP = {"x": ("blk", 1), "y": ("blk", 2), "a": ("dp", 2), "b": ("dp", 4)}


def place_at(order, index):
    place = 0
    for depth, name in enumerate(order):
        if index & (8 >> depth):
            place |= BIT[name]
    return place


def weights_kernel(products, orders, scal, own, far, mine, got, *rest):
    count = len(orders)
    sends, keeps, holds = rest[0:count], rest[count : 2 * count], rest[2 * count :]
    me16 = scal[0] * 4 + scal[1]
    for part, order in enumerate(orders):
        row_at = 0
        for (low, high, at, dealt), hold in zip(products, holds):
            blocks = dealt[part]
            begin = at + sum(dealt[:part]) * 128
            columns = slice(begin, begin + blocks * 128)
            hold[:, 0 : blocks * 128] = (
                dot_nn(own[low:high, :], mine[:, columns]) + dot_nn(far[low:high, :], got[:, columns])
            ).astype(BF)
            rows = (high - low) // 16
            for index in range(16):
                start = pl.multiple_of((place_at(order, index) ^ me16) * rows, 16)
                target = keeps[part] if index < 8 else sends[part]
                for number in range(blocks):
                    lane = number * 128
                    spot = row_at + number * rows
                    target[index % 8, spot : spot + rows, :] = hold[pl.ds(start, rows), lane : lane + 128]
            row_at += blocks * rows


def settle_kernel(layout, blocks, scal, *refs):
    pieces, (mine, theirs, hold, sems) = refs[:-4], refs[-4:]
    bring(layout, pieces, hold, sems)
    core = scal[2]
    row = at = 0
    for rows in blocks:
        half = rows // 2
        total = hold[0, row : row + rows, :].astype(F32)
        for slot in range(1, hold.shape[0]):
            total = total + hold[slot, row : row + rows, :].astype(F32)
        low, high = total[0:half], total[half:rows]
        mine[at : at + half, :] = jnp.where(core == 0, low, high)
        theirs[at : at + half, :] = jnp.where(core == 0, high, low)
        row += rows
        at += half


def add_kernel(layout, rows, *refs):
    outs, (hold, sems) = refs[-2 - len(rows) : -2], refs[-2:]
    bring(layout, refs[: -2 - len(rows)], hold, sems)
    depth = {}
    for _, _, slot, target, count in layout:
        depth[target] = (max(slot, depth.get(target, (0, 0))[0]), count)
    at = 0
    for out, size in zip(outs, rows):
        for target in sorted(depth):
            if at <= target < at + size:
                last, count = depth[target]
                total = sum(hold[slot, target : target + count, :].astype(F32) for slot in range(last + 1))
                out[target - at : target - at + count, :] = total.astype(BF)
        at += size


def plain_add_kernel(left, right, out):
    out[...] = left[...] + right[...]


DMOD = 12 * WIDTH
SMALL = 2 * 6912 + WIDTH
SMALL_AT = {"triple": (0, 2304), "output": (2304, 3072), "expand": (3072, 6144), "shrink": (6144, 6912)}


def pack_kernel(first0, vec0, first1, vec1, mask, out):
    for layer, (first, vec) in enumerate(((first0, vec0), (first1, vec1))):
        at = layer * 6 * WIDTH
        out[:, at : at + 1536] = first[:, 0:1536]
        out[:, at + 1536 : at + 2304] = vec[:, 2304:3072]
        out[:, at + 2304 : at + 3840] = vec[:, 768:2304]
        out[:, at + 3840 : at + 4608] = vec[:, 0:768]
        at = DMOD + layer * 6912
        out[:, at : at + 2304] = first[:, 1536:3840]
        out[:, at + 2304 : at + 3072] = vec[:, 6912:7680]
        out[:, at + 3072 : at + 6144] = vec[:, 3840:6912]
        out[:, at + 6144 : at + 6912] = vec[:, 3072:3840]
    out[:, DMOD + 2 * 6912 :] = mask[...]


def join_kernel(own, got, condition, adaptive_any, out, condition_grad, adaptive, sems):
    (copy,) = fetch([(adaptive_any, adaptive)], sems)
    total = own[...] + got[...]
    out[:, 0:DMOD] = total[:, 0:DMOD]
    out[:, DMOD : DMOD + 128] = condition[...]
    out[:, DMOD + 128 :] = total[:, DMOD:]
    copy.wait()
    grad = jnp.zeros((8, 128), F32)
    for layer in range(LAYERS):
        at = layer * 6 * WIDTH
        grad = grad + dot_nt(three_rows(total[:, at : at + 6 * WIDTH]), adaptive[layer])
    condition_grad[...] = column_sum(grad)


def spread_kernel(own, got, out):
    rows = own.shape[1] - SMALL
    out[:, 0:rows] = own[:, 0:rows]
    out[:, rows : 2 * rows] = got[:, 0:rows]
    out[:, 2 * rows :] = own[:, rows:] + got[:, rows:]


def small_kernel(scal, own, got, adaptive_w, adaptive_b, triple_b, output_b, expand_b, shrink_b, mask_sum):
    index = scal[4]
    each = DMOD + 128
    rows = own.shape[1] - SMALL
    share = adaptive_w.shape[1]
    number = lax.broadcasted_iota(jnp.int32, (8, 128), 0)
    lane = lax.broadcasted_iota(jnp.int32, (8, 128), 1)
    pick = (lane == index * share + number) & (number < share)
    totals = [jnp.zeros((8, 6 * WIDTH), F32), jnp.zeros((8, 6 * WIDTH), F32)]
    sums = [jnp.zeros((1, 6 * WIDTH), F32), jnp.zeros((1, 6 * WIDTH), F32)]
    for source in (own, got):
        for at in range(0, rows, each):
            column = jnp.sum(jnp.where(pick, source[:, at + DMOD : at + each], 0.0), 1, keepdims=True)
            for layer in range(LAYERS):
                low = at + layer * 6 * WIDTH
                row = source[:, low : low + 6 * WIDTH]
                totals[layer] = totals[layer] + column * row
                sums[layer] = sums[layer] + row
    summed = own[:, rows:] + got[:, rows:]

    def cut(row):
        size = row.shape[1] // 32
        return pltpu.roll(row, lax.rem(row.shape[1] - index * size, row.shape[1]), 1)[:, 0:size]

    for layer in range(LAYERS):
        adaptive_w[layer] = totals[layer][0:share]
        adaptive_b[layer : layer + 1, :] = cut(sums[layer])
        for out, (low, high) in zip((triple_b, output_b, expand_b, shrink_b), SMALL_AT.values()):
            at = layer * 6912
            out[layer : layer + 1, :] = cut(summed[:, at + low : at + high])
    mask_sum[...] = cut(summed[:, 2 * 6912 :])


def finish_kernel(plans, scal, *refs):
    pairs = 2 * len(plans)
    groups = refs[pairs : pairs + 4]
    outs, hold = refs[pairs + 4 : -1], refs[-1]
    core = scal[2]
    for bucket, plan in enumerate(plans):
        mine, got = refs[2 * bucket : 2 * bucket + 2]
        at = 0
        for out, layer, block, rows in plan:
            own, other = mine[at : at + rows, :], got[at : at + rows, :]
            half = outs[out].shape[2] // 2
            low = block * 128
            outs[out][layer, :, low : low + 128] = jnp.where(core == 0, own, other)
            outs[out][layer, :, half + low : half + low + 128] = jnp.where(core == 0, other, own)
            at += rows
    for layer in range(LAYERS):
        for place in range(4):
            hold[place] = groups[place][layer]
        for group in range(4):
            block = hold[group ^ scal[0]]
            for number in range(3):
                low = number * WIDTH + group * GROUP
                outs[0][layer, :, low : low + GROUP] = block[:, number * GROUP : (number + 1) * GROUP]


def shaped(*shape, dtype=F32):
    return jax.ShapeDtypeStruct(shape, dtype)


class Outs(list):
    token = None


def call(kernel, specs, outs, scratch, micros, name, limit, after=()):
    count, extra = len(specs), len(after)

    def body(*refs):
        mark = refs[count + extra + len(outs)]
        mark[...] = jnp.zeros(mark.shape, F32)
        kernel(*refs[:count], *refs[count + extra : count + extra + len(outs)], *refs[count + extra + len(outs) + 1 :])

    made = pl.pallas_call(
        body,
        in_specs=specs + [ANY] * extra,
        out_specs=[VM] * (len(outs) + 1),
        out_shape=outs + [shaped(8, 128)],
        scratch_shapes=scratch,
        compiler_params=pltpu.CompilerParams(vmem_limit_bytes=limit * MEBI),
        cost_estimate=pl.CostEstimate(flops=int(micros * 1e9), bytes_accessed=int(micros * 1e6), transcendentals=0),
        name=name,
    )

    def run(*operands):
        operands = [
            pltpu.with_memory_space_constraint(operand, pltpu.HBM) if spec is HBM or spec is HV else operand
            for operand, spec in zip(operands, specs)
        ]
        marks = [
            mark if mark.shape == (8, 128) else pltpu.with_memory_space_constraint(mark, pltpu.HBM) for mark in after
        ]
        results = made(*operands, *marks)
        found = Outs(results[:-1])
        found.token = results[-1]
        return found

    return run


def swap(values, axis, bit):
    size = 4 if axis == "blk" else 8
    return lax.ppermute(values, axis, [(i, i ^ bit) for i in range(size)])


def swap_chunks(chunks):
    return [chunks[0]] + [swap(chunks[place], "blk", place) for place in (1, 2, 3)]


def shaped_like(values):
    return shaped(*values.shape, dtype=values.dtype)


class Part:
    def __init__(self, keep, got, rows, order):
        self.views = [(keep, 0), (got, 0)]
        self.rows = rows
        self.order = order

    def halve(self):
        self.rows //= 2


def exchange(parts, cost, after=()):
    groups = {}
    for part in parts:
        groups.setdefault(part.order[0], []).append(part)
        part.order = part.order[1:]
    groups = list(groups.items())
    ordered, rows = [], []
    for _, group in groups:
        for part in group:
            part.halve()
        ordered += group
        rows.append(sum(part.rows for part in group))
    arrays, layout, total = collect(ordered, True)
    slots = max(slot for _, _, slot, _, _ in layout) + 1
    outs = call(
        functools.partial(add_kernel, layout, rows),
        [HBM] * len(arrays),
        [shaped(count, 128, dtype=BF) for count in rows],
        [pltpu.VMEM((slots, total, 128), BF), pltpu.SemaphoreType.DMA((len(layout),))],
        cost,
        "add",
        16,
        after,
    )(*arrays)
    for (axis, group), out in zip(groups, outs):
        got = swap(out, *STEP[axis])
        at = 0
        for part in group:
            part.views.append((got, at))
            at += part.rows
    return [outs.token]


def weight_parts(scal, own, far, mine, got, products, orders, after=()):
    count = len(orders)
    shapes, rows = [], []
    for part in range(count):
        rows.append(sum(dealt[part] * (high - low) // 16 for low, high, _, dealt in products))
        shapes.append(shaped(8, rows[-1], 128, dtype=BF))
    outs = call(
        functools.partial(weights_kernel, products, orders),
        [SM] + [HV] * 4,
        shapes * 2,
        [pltpu.VMEM((high - low, max(dealt) * 128), BF) for low, high, _, dealt in products],
        300,
        "mlp_weights",
        26,
        after,
    )(scal, own, far, mine, got)
    flat = [out.reshape(-1, 128) for out in outs]
    parts = [
        Part(flat[count + number], swap(flat[number], *STEP[order[0]]), 8 * rows[number], order[1:])
        for number, order in enumerate(orders)
    ]
    return parts, [outs.token]


def triple_part(scal, h_rows, stacked, after=()):
    rows = WIDTH // 8 * 3 // 2 * 3
    outs = call(
        triple_kernel,
        [SM] + [HV] * 5,
        [shaped(4 * rows, 128, dtype=BF)] * 2,
        [pltpu.VMEM((8, rows, 128), BF)],
        300,
        "triple_weights",
        20,
        after,
    )(scal, *h_rows, stacked)
    return Part(outs[0], swap(outs[1], "dp", 1), 4 * rows, "ab"), [outs.token]


def collect(parts, upper=False):
    arrays, layout, at = [], [], 0
    for part in parts:
        for slot, (array, first) in enumerate(part.views):
            first = first + part.rows if upper else first
            known = [number for number, other in enumerate(arrays) if other is array]
            if not known:
                arrays.append(array)
                known = [len(arrays) - 1]
            layout.append((known[0], first, slot, at, part.rows))
        at += part.rows
    return arrays, layout, at


def blocks_of(products):
    blocks = []
    for part in range(len(products[0][3])):
        for low, high, _, dealt in products:
            blocks += [(high - low) // 16] * dealt[part]
    return blocks


def settle(parts, scal, products, cost, after=()):
    arrays, layout, rows = collect(parts)
    slots = max(slot for _, _, slot, _, _ in layout) + 1
    outs = call(
        functools.partial(settle_kernel, layout, blocks_of(products)),
        [SM] + [HBM] * len(arrays),
        [shaped(rows // 2, 128)] * 2,
        [pltpu.VMEM((slots, rows, 128), BF), pltpu.SemaphoreType.DMA((len(layout),))],
        cost,
        "settle",
        10,
        after,
    )(scal, *arrays)
    return *outs, outs.token


def triple_settle(parts, scal, after=()):
    arrays, layout, rows = collect(parts)
    slots = max(slot for _, _, slot, _, _ in layout) + 1
    blocks = call(
        functools.partial(triple_settle_kernel, layout),
        [SM] + [HBM] * len(arrays),
        [shaped(LAYERS, WIDTH // 32, 3 * GROUP)] * 4,
        [
            pltpu.VMEM((slots, rows, 128), BF),
            pltpu.VMEM((LAYERS, 4, WIDTH // 32, 3 * GROUP), F32),
            pltpu.SemaphoreType.DMA((len(layout),)),
        ],
        0.1,
        "triple_settle",
        8,
        after,
    )(scal, *arrays)
    return swap_chunks(blocks), [blocks.token]


def plan_of(products, names):
    plan = []
    for part in range(len(products[0][3])):
        for (low, high, _, dealt), (out, layer) in zip(products, names):
            first = sum(dealt[:part])
            plan += [(out, layer, first + number, (high - low) // 32) for number in range(dealt[part])]
    return plan


def rotary_tables(start, rows):
    position = (start[:, None] + jnp.arange(rows, dtype=jnp.int32)[None, :]).astype(F32)
    lane = jnp.arange(128, dtype=jnp.int32)
    frequency = jnp.exp((lane % 32).astype(F32) * (-2.0 * math.log(10000.0) / HEAD_DIM))
    angles = position[:, :, None] * frequency
    return jnp.cos(angles), jnp.sin(angles) * jnp.where(lane % 64 < 32, -1.0, 1.0)


def local_fast(
    inputs, condition, prefix, mask_embed, adaptive_weight, adaptive_bias, triple_weight, triple_bias, output_weight,
    output_bias, expand_weight, expand_bias, shrink_weight, shrink_bias, cotangent,
):
    rows = inputs.shape[1]
    hidden = expand_weight.shape[2]
    blk, dp = lax.axis_index("blk"), lax.axis_index("dp")
    scal = jnp.stack([blk, dp // 2, dp % 2, prefix[0], blk * 8 + dp]).astype(jnp.int32)
    starts = (blk ^ jnp.arange(4, dtype=jnp.int32)) * rows
    cosine, sine = rotary_tables(starts[:1], rows)
    cosines, sines = rotary_tables(starts, rows)

    f_square = shaped(rows, WIDTH)
    b_square = shaped(rows, WIDTH, dtype=BF)
    b_tall = shaped(rows, hidden, dtype=BF)
    packed = rows + rows // 2
    chunk = shaped(packed, 2 * GROUP, dtype=BF)
    o_chunk = shaped(rows // 2, 2 * GROUP, dtype=BF)
    c_hold = pltpu.VMEM((4, packed, 2 * GROUP), BF)
    o_hold = pltpu.VMEM((4, rows // 2, 2 * GROUP), BF)
    adaptive_hold = pltpu.VMEM((condition.shape[1], 6 * WIDTH), BF)
    triple_hold = pltpu.VMEM((WIDTH, 3 * WIDTH), BF)
    output_hold = pltpu.VMEM((WIDTH, WIDTH), BF)
    expand_hold = pltpu.VMEM((WIDTH, hidden), BF)
    shrink_hold = pltpu.VMEM((hidden, WIDTH), BF)
    h_both = shaped(2, WIDTH // 2, rows, dtype=BF)
    half_width = hidden // 2 + WIDTH
    tall = hidden + 2 * WIDTH
    mod_row = shaped(1, 6 * WIDTH)

    x0, mod0, h_rows, *chunks = call(
        first_kernel,
        [SM] + [VM] * 3 + [HBM] * 6,
        [f_square, mod_row, h_both] + [chunk] * 4,
        [
            pltpu.VMEM(inputs.shape, BF), pltpu.VMEM(condition.shape, F32), pltpu.VMEM(adaptive_bias.shape, BF),
            pltpu.VMEM(triple_bias.shape, BF), adaptive_hold, triple_hold, c_hold, pltpu.SemaphoreType.DMA((6,)),
        ],
        300,
        "qkv_first",
        24,
    )(
        scal, mask_embed[None], cosine, sine, inputs, condition, adaptive_bias, triple_bias, adaptive_weight,
        triple_weight,
    )

    def attend(chunks, after):
        return call(
            attend_kernel,
            [VM] * 4,
            [o_chunk] * 4 + [shaped(4, 8, rows), shaped(4, rows, GROUP)],
            [
                pltpu.VMEM((4, GROUP, rows), F32),
                pltpu.VMEM((4, rows, GROUP), BF),
                pltpu.VMEM((4 * rows, GROUP), BF),
                pltpu.VMEM((3, HEAD_DIM + 16, 4 * rows), BF),
            ],
            300,
            "attend",
            20,
            after,
        )(*chunks)

    def attend_back(chunks, given, lse, turned, after):
        stack = shaped(4, packed, 2 * GROUP, dtype=BF)
        return call(
            attend_back_kernel,
            [SM, VM] + [HV] * 6 + [HBM] * 2,
            [stack],
            [
                pltpu.VMEM((4, rows, 128), F32),
                pltpu.VMEM((4, rows, 128), F32),
                pltpu.SemaphoreType.DMA((2,)),
                pltpu.VMEM((3, 4 * rows, GROUP), BF),
                pltpu.VMEM((3, 4 * rows, GROUP), BF),
                pltpu.VMEM((4, rows, GROUP), BF),
                pltpu.VMEM((4, rows, GROUP), BF),
                pltpu.VMEM((4, GROUP, rows), BF),
                pltpu.VMEM((8, 4 * rows), F32),
                pltpu.VMEM((8, 4 * rows), F32),
                pltpu.VMEM((GROUP, 4 * rows), F32),
                pltpu.VMEM((4, rows, GROUP), F32),
                pltpu.VMEM((4, rows, GROUP), F32),
            ],
            300,
            "attend_back",
            24,
            after,
        )(scal, given, *chunks, lse, turned, cosines, sines)

    def far(values):
        return swap(values, "dp", 1)

    def gather_rows(both):
        near = swap(both, "blk", 1)
        return [both, near, swap(both, "blk", 2), swap(near, "blk", 2)]

    chunks0 = swap_chunks(chunks)
    h_rows0 = gather_rows(h_rows)
    *o_chunks, lse0, ot0 = attend(chunks0, ())
    o_chunks = swap_chunks(o_chunks)
    aout0, m0, turned0, slope0, f0, x1, mod1, h_rows, *chunks = call(
        middle_kernel,
        [SM] + [HV] + [VM] * 13 + [HBM] * 5,
        [b_square, f_square, shaped(tall, rows, dtype=BF), b_tall, b_square, f_square, mod_row, h_both] + [chunk] * 4,
        [output_hold, expand_hold, shrink_hold, triple_hold, adaptive_hold, o_hold, pltpu.VMEM((rows, WIDTH), BF)]
        + [c_hold, pltpu.SemaphoreType.DMA((5,))],
        300,
        "mlp_qkv",
        34,
        h_rows0[1:3],
    )(
        scal, x0, mod0, condition, adaptive_bias, output_bias, expand_bias, shrink_bias, triple_bias, cosine, sine,
        *o_chunks, output_weight, expand_weight, shrink_weight, triple_weight, adaptive_weight,
    )
    turned0_far = far(turned0)
    chunks1 = swap_chunks(chunks)
    h_rows1 = gather_rows(h_rows)
    *o_chunks, lse1, ot1 = attend(chunks1, [*h_rows0[3:], cosines, sines])
    o_chunks = swap_chunks(o_chunks)
    outputs, aout1, m1, turned1, slope1, f1 = call(
        ahead_kernel,
        [SM] + [HV] + [VM] * 8 + [HBM] * 3,
        [shaped(1, rows, WIDTH, dtype=BF), b_square, f_square, shaped(tall, rows, dtype=BF), b_tall, b_square],
        [output_hold, expand_hold, shrink_hold, o_hold, pltpu.VMEM((rows, WIDTH), BF), pltpu.SemaphoreType.DMA((3,))],
        300,
        "mlp_ahead",
        28,
        [*h_rows1[1:3], turned0_far],
    )(
        scal, x1, mod1, output_bias, expand_bias, shrink_bias, *o_chunks, output_weight, expand_weight, shrink_weight
    )
    turned1_far = far(turned1)
    back_outs = [shaped(4, rows // 2, 2 * GROUP, dtype=BF), f_square, shaped(1, 7680)]
    mine1, theirs1, given, dm1, vec1 = call(
        turn_kernel,
        [SM] + [VM] * 5 + [HBM] * 4,
        [shaped(rows, half_width, dtype=BF)] * 2 + back_outs,
        [output_hold, expand_hold, shrink_hold, pltpu.VMEM(cotangent.shape, BF)]
        + [pltpu.VMEM((2, rows, half_width), BF), pltpu.SemaphoreType.DMA((4,))],
        300,
        "mlp_turn",
        28,
        h_rows1[3:],
    )(scal, mod1, m1, f1, slope1, aout1, cotangent, output_weight, expand_weight, shrink_weight)

    def exchange_blocks(stack):
        return lax.all_to_all(stack, "blk", 0, 0)

    products = (
        (hidden, hidden + WIDTH, 0, (4, 4, 4)),
        (0, hidden, hidden // 2, (1, 1, 1)),
        (hidden + WIDTH, tall, hidden // 2 + WIDTH // 2, (1, 1, 1)),
    )
    orders = ("axyb", "xyba", "yaxb")
    given = exchange_blocks(given)
    parts1, sent = weight_parts(scal, turned1, turned1_far, mine1, far(theirs1), products, orders)
    outs = attend_back(chunks1, given, lse1, ot1, sent)
    stacked = outs[0]
    grads = exchange_blocks(stacked)
    sent = exchange(parts1, 0.1, [outs.token])
    triple1, sent = triple_part(scal, h_rows1, stacked, sent)
    outs = call(
        back_kernel,
        [SM] + [HV] * 2 + [VM] * 3 + [HV] * 4 + [HBM] * 4,
        [shaped(rows, half_width, dtype=BF)] * 2 + [shaped(1, 3840)] + back_outs,
        [triple_hold, output_hold, expand_hold, shrink_hold, pltpu.VMEM((rows, 3 * WIDTH), BF)]
        + [pltpu.VMEM((2, rows, half_width), BF), pltpu.SemaphoreType.DMA((4,))],
        300,
        "qkv_mlp_back",
        32,
        sent,
    )(
        scal, x1, dm1, mod1, mod0, grads, m0, f0, slope0, aout0, triple_weight, output_weight, expand_weight,
        shrink_weight,
    )
    mine0, theirs0, first1, given, dm0, vec0 = outs
    given = exchange_blocks(given)
    sent = exchange([*parts1, triple1], 300, [outs.token])
    parts0, sent = weight_parts(scal, turned0, turned0_far, mine0, far(theirs0), products, orders, sent)
    sent = exchange([*parts1, triple1], 0.1, sent)
    outs = attend_back(chunks0, given, lse0, ot0, sent)
    stacked = outs[0]
    grads = exchange_blocks(stacked)
    sent = exchange(parts0, 0.1, [outs.token])
    triple0, sent = triple_part(scal, h_rows0, stacked, sent)
    first0, input_grad, mask_term = call(
        last_kernel,
        [SM] + [HV] * 2 + [VM] * 2 + [HBM],
        [shaped(1, 3840), shaped(1, rows, WIDTH), shaped(1, WIDTH)],
        [triple_hold, pltpu.VMEM((rows, 3 * WIDTH), BF), pltpu.SemaphoreType.DMA((1,))],
        300,
        "qkv_back",
        24,
        sent,
    )(scal, x0, dm0, mod0, grads, triple_weight)

    def spread(own, got, cost, after=()):
        wide = shaped(1, 2 * own.shape[1] - SMALL)
        return call(spread_kernel, [VM] * 2, [wide], [], cost, "spread", 8, after)(own, got)

    outs = call(pack_kernel, [VM] * 5, [shaped(1, DMOD + SMALL)], [], 0.1, "pack", 8)(
        first0, vec0, first1, vec1, mask_term
    )
    small = outs[0]
    near = swap(small, "blk", 1)
    sent = exchange([*parts0, triple0], 300, [outs.token])
    (summed,) = call(plain_add_kernel, [VM] * 2, [shaped_like(small)], [], 300, "plain_add", 8, sent)(small, near)
    outs = call(
        join_kernel,
        [VM] * 3 + [HBM],
        [shaped(1, DMOD + 128 + SMALL), shaped(1, 128)],
        [pltpu.VMEM(adaptive_weight.shape, BF), pltpu.SemaphoreType.DMA((1,))],
        0.1,
        "join",
        12,
    )(summed, swap(summed, "blk", 2), condition, adaptive_weight)
    wide, condition_grad = outs
    got = far(wide)
    sent = exchange([*parts0, triple0], 300, [outs.token])
    (wide,) = spread(wide, got, 300, sent)
    outs = spread(wide, swap(wide, *STEP["a"]), 0.1)
    wide = outs[0]
    got = swap(wide, *STEP["b"])
    blocks, cut = triple_settle([triple0, triple1], scal, [outs.token])
    outs = call(
        small_kernel,
        [SM] + [VM] * 2,
        [shaped(LAYERS, condition.shape[1] // 32, 6 * WIDTH), shaped(LAYERS, 6 * WIDTH // 32)]
        + [shaped(LAYERS, (high - low) // 32) for low, high in SMALL_AT.values()]
        + [shaped(1, WIDTH // 32)],
        [],
        300,
        "small",
        10,
        cut,
    )(scal, wide, got)
    small_grads = list(outs)
    own1, theirs1, early = settle(parts1, scal, products, 0.1, cut)
    own0, theirs0, _ = settle(parts0, scal, products, 0.1, [early, outs.token, *blocks[1:]])
    plans = (
        plan_of(products, ((2, 1), (3, 1), (1, 1))),
        plan_of(products, ((2, 0), (3, 0), (1, 0))),
    )
    weight_grads = call(
        functools.partial(finish_kernel, plans),
        [SM] + [VM] * 8,
        [
            shaped(LAYERS, WIDTH // 32, 3 * WIDTH),
            shaped(LAYERS, WIDTH // 32, WIDTH),
            shaped(LAYERS, WIDTH // 32, hidden),
            shaped(LAYERS, hidden // 32, WIDTH),
        ],
        [pltpu.VMEM((4, WIDTH // 32, 3 * GROUP), F32)],
        0.1,
        "finish",
        12,
    )(scal, own1, far(theirs1), own0, far(theirs0), *blocks)
    return (
        outputs,
        input_grad,
        condition_grad,
        small_grads[6][0],
        small_grads[0],
        small_grads[1],
        weight_grads[0],
        small_grads[2],
        weight_grads[1],
        small_grads[3],
        weight_grads[2],
        small_grads[4],
        weight_grads[3],
        small_grads[5],
    )


def solution(mesh):
    in_specs = (
        P("dp", "blk", None),
        P("dp", None),
        P("dp"),
        P(),
        P(),
        P(),
        P(),
        P(),
        P(),
        P(),
        P(),
        P(),
        P(),
        P(),
        P("dp", "blk", None),
    )
    out_specs = (
        P("dp", "blk", None),
        P("dp", "blk", None),
        P("dp", None),
        P(("blk", "dp")),
        P(None, ("blk", "dp"), None),
        P(None, ("blk", "dp")),
        P(None, ("blk", "dp"), None),
        P(None, ("blk", "dp")),
        P(None, ("blk", "dp"), None),
        P(None, ("blk", "dp")),
        P(None, ("blk", "dp"), None),
        P(None, ("blk", "dp")),
        P(None, ("blk", "dp"), None),
        P(None, ("blk", "dp")),
    )
    whole = mesh.shape["blk"] == 4 and mesh.shape["dp"] == 8
    body = local_fast if whole else local
    return jax.shard_map(body, mesh=mesh, in_specs=in_specs, out_specs=out_specs, check_vma=False)
```

```python
import functools
import math

import jax
import jax.numpy as jnp
from jax import lax
from jax.experimental import pallas as pl
from jax.experimental.pallas import tpu as pltpu
from jax.sharding import PartitionSpec as P

HEADS = 12
HEAD_DIM = 64
LAYERS = 2


HIGHEST = lax.Precision.HIGHEST
EPSILON = 1e-06


def modulate(residual, shift, scaling):
    average = jnp.mean(residual, -1, keepdims=True)
    centered = residual - average
    variance = jnp.mean(centered * centered, -1, keepdims=True)
    return centered * lax.rsqrt(variance + EPSILON) * (1.0 + scaling) + shift


def gelu_tanh(values):
    return jax.nn.gelu(values, approximate=True)


def tables(offset, row_count, head_dim):
    half_dim = head_dim // 2
    position = (offset + jnp.arange(row_count, dtype=jnp.int32)).astype(jnp.float32)
    frequency = jnp.exp(
        jnp.arange(half_dim, dtype=jnp.float32) * (-2.0 * math.log(10000.0) / head_dim)
    )
    angles = position[:, None] * frequency[None, :]
    return (jnp.cos(angles)[:, None, :], jnp.sin(angles)[:, None, :])


def rotate(vectors, cosine, sine_table):
    half_dim = vectors.shape[-1] // 2
    front_half = vectors[..., :half_dim]
    back_half = vectors[..., half_dim:]
    return jnp.concatenate(
        [
            front_half * cosine - back_half * sine_table,
            back_half * cosine + front_half * sine_table,
        ],
        -1,
    )


def unrotate(gradient, cosine, sine_table):
    half_dim = gradient.shape[-1] // 2
    front_half = gradient[..., :half_dim]
    back_half = gradient[..., half_dim:]
    return jnp.concatenate(
        [
            front_half * cosine + back_half * sine_table,
            back_half * cosine - front_half * sine_table,
        ],
        -1,
    )


def split_einsum(form, float_left, low_right):
    upper = float_left.astype(jnp.bfloat16)
    lower = (float_left - upper.astype(jnp.float32)).astype(jnp.bfloat16)
    first = jnp.einsum(form, upper, low_right, preferred_element_type=jnp.float32)
    return first + jnp.einsum(form, lower, low_right, preferred_element_type=jnp.float32)


def fold_keys(queries, scaling):

    def absorb(carried, key_piece, offset):
        key_flat, value_flat = key_piece
        piece_rows = key_flat.shape[0]
        block_rows = math.gcd(piece_rows, 512)
        key_blocks = key_flat.reshape(piece_rows // block_rows, block_rows, HEADS, HEAD_DIM)
        value_blocks = value_flat.reshape(piece_rows // block_rows, block_rows, HEADS, HEAD_DIM)

        def absorb_inner(running, block_pair):
            running_max, running_sum, weighted = running
            key_block, value_block = block_pair
            scores = (
                jnp.einsum("qhd,khd->hqk", queries, key_block, preferred_element_type=jnp.float32)
                * scaling
            )
            new_max = jnp.maximum(running_max, jnp.max(scores, -1))
            weights = jnp.exp(scores - new_max[..., None])
            factor = jnp.exp(running_max - new_max)
            running_sum = running_sum * factor + jnp.sum(weights, -1)
            weighted = weighted * factor[..., None] + split_einsum(
                "hqk,khd->hqd", weights, value_block
            )
            return ((new_max, running_sum, weighted), None)

        carried, _ = lax.scan(absorb_inner, carried, (key_blocks, value_blocks))
        return carried

    return absorb


def attend_back(queries, key_all, value_all, out_gradient, attended_f, log_total, scaling):
    row_count = queries.shape[0]
    all_rows = key_all.shape[0]
    block_rows = math.gcd(all_rows, 512)
    key_blocks = key_all.reshape(all_rows // block_rows, block_rows, HEADS, HEAD_DIM)
    value_blocks = value_all.reshape(all_rows // block_rows, block_rows, HEADS, HEAD_DIM)
    out_float = out_gradient.astype(jnp.float32)
    row_delta = jnp.transpose(jnp.sum(out_float * attended_f, -1), (1, 0))

    def attend_inner(query_grad, block_pair):
        key_block, value_block = block_pair
        scores = (
            jnp.einsum("qhd,khd->hqk", queries, key_block, preferred_element_type=jnp.float32)
            * scaling
        )
        probs = jnp.exp(scores - log_total[..., None])
        prob_grad = jnp.einsum(
            "qhd,khd->hqk", out_gradient, value_block, preferred_element_type=jnp.float32
        )
        score_grad = (probs * (prob_grad - row_delta[..., None])).astype(jnp.bfloat16)
        query_grad = query_grad + jnp.einsum(
            "hqk,khd->qhd", score_grad, key_block, preferred_element_type=jnp.float32
        )
        key_grad = (
            jnp.einsum("hqk,qhd->khd", score_grad, queries, preferred_element_type=jnp.float32)
            * scaling
        )
        value_grad = split_einsum("hqk,qhd->khd", probs, out_gradient)
        return (query_grad, (key_grad, value_grad))

    start_grad = jnp.zeros((row_count, HEADS, HEAD_DIM), jnp.float32)
    query_grad, (key_grads, value_grads) = lax.scan(
        attend_inner, start_grad, (key_blocks, value_blocks)
    )
    width = HEADS * HEAD_DIM
    return (
        query_grad * scaling,
        key_grads.reshape(all_rows, width),
        value_grads.reshape(all_rows, width),
    )


def forward_layer(residual, modulation, layer_index, weights, cosine, sine_table, scaling):
    (
        adaptive_weight,
        adaptive_bias,
        triple_weight,
        triple_bias,
        output_weight,
        output_bias,
        expand_weight,
        expand_bias,
        shrink_weight,
        shrink_bias,
    ) = weights
    row_count, width = residual.shape
    pieces = [modulation[number * width : (number + 1) * width] for number in range(6)]
    shift_attn, scale_attn, gate_attn, shift_mlp, scale_mlp, gate_mlp = pieces
    normed = modulate(residual, shift_attn, scale_attn).astype(jnp.bfloat16)
    mixed = jnp.dot(
        normed, triple_weight[layer_index], preferred_element_type=jnp.float32
    ) + triple_bias[layer_index].astype(jnp.float32)
    head_shape = (row_count, HEADS, HEAD_DIM)
    queries = rotate(mixed[:, :width].reshape(head_shape), cosine, sine_table).astype(jnp.bfloat16)
    key_flat = (
        rotate(mixed[:, width : 2 * width].reshape(head_shape), cosine, sine_table)
        .astype(jnp.bfloat16)
        .reshape(row_count, width)
    )
    value_flat = mixed[:, 2 * width :].astype(jnp.bfloat16)
    start_state = (
        jnp.full((HEADS, row_count), -1e30, jnp.float32),
        jnp.zeros((HEADS, row_count), jnp.float32),
        jnp.zeros((HEADS, row_count, HEAD_DIM), jnp.float32),
    )
    absorb = fold_keys(queries, scaling)
    final_state = absorb(
        start_state,
        (
            lax.all_gather(key_flat, "blk", axis=0, tiled=True),
            lax.all_gather(value_flat, "blk", axis=0, tiled=True),
        ),
        jnp.int32(0),
    )
    running_max, running_sum, weighted = final_state
    log_total = running_max + jnp.log(running_sum)
    attended_f = jnp.transpose(weighted / running_sum[..., None], (1, 0, 2))
    attended = attended_f.reshape(row_count, width).astype(jnp.bfloat16)
    branch = jnp.dot(
        attended, output_weight[layer_index], preferred_element_type=jnp.float32
    ) + output_bias[layer_index].astype(jnp.float32)
    middle = residual + gate_attn * branch
    normed_mlp = modulate(middle, shift_mlp, scale_mlp).astype(jnp.bfloat16)
    up_proj = jnp.dot(
        normed_mlp, expand_weight[layer_index], preferred_element_type=jnp.float32
    ) + expand_bias[layer_index].astype(jnp.float32)
    active = gelu_tanh(up_proj).astype(jnp.bfloat16)
    lowered = jnp.dot(
        active, shrink_weight[layer_index], preferred_element_type=jnp.float32
    ) + shrink_bias[layer_index].astype(jnp.float32)
    result = middle + gate_mlp * lowered
    saved = (
        residual,
        normed,
        queries,
        key_flat,
        value_flat,
        None,
        attended_f,
        attended,
        log_total,
        branch,
        middle,
        normed_mlp,
        up_proj,
        active,
        lowered,
    )
    return (result, saved)


def backward_layer(
    gradient, modulation, layer_index, weights, saved, cosine, sine_table, scaling, condition
):
    (
        adaptive_weight,
        adaptive_bias,
        triple_weight,
        triple_bias,
        output_weight,
        output_bias,
        expand_weight,
        expand_bias,
        shrink_weight,
        shrink_bias,
    ) = weights
    (
        residual,
        normed,
        queries,
        key_flat,
        value_flat,
        gathered,
        attended_f,
        attended,
        log_total,
        branch,
        middle,
        normed_mlp,
        up_proj,
        active,
        lowered,
    ) = saved
    row_count, width = residual.shape
    pieces = [modulation[number * width : (number + 1) * width] for number in range(6)]
    shift_attn, scale_attn, gate_attn, shift_mlp, scale_mlp, gate_mlp = pieces
    gate_mlp_grad = jnp.sum(gradient * lowered, 0)
    lowered_grad = (gradient * gate_mlp).astype(jnp.bfloat16)
    shrink_w_grad = jnp.einsum(
        "tf,td->fd", active, lowered_grad, preferred_element_type=jnp.float32
    )
    shrink_b_grad = jnp.sum(lowered_grad.astype(jnp.float32), 0)
    active_grad = jnp.einsum(
        "td,fd->tf", lowered_grad, shrink_weight[layer_index], preferred_element_type=jnp.float32
    )
    _, gelu_pull = jax.vjp(gelu_tanh, up_proj)
    up_grad = gelu_pull(active_grad)[0].astype(jnp.bfloat16)
    expand_w_grad = jnp.einsum("td,tf->df", normed_mlp, up_grad, preferred_element_type=jnp.float32)
    expand_b_grad = jnp.sum(up_grad.astype(jnp.float32), 0)
    normed_mlp_grad = jnp.einsum(
        "tf,df->td", up_grad, expand_weight[layer_index], preferred_element_type=jnp.float32
    )
    _, mlp_pull = jax.vjp(modulate, middle, shift_mlp, scale_mlp)
    middle_grad, shift_mlp_grad, scale_mlp_grad = mlp_pull(normed_mlp_grad)
    middle_grad = middle_grad + gradient
    gate_attn_grad = jnp.sum(middle_grad * branch, 0)
    branch_grad = (middle_grad * gate_attn).astype(jnp.bfloat16)
    output_w_grad = jnp.einsum(
        "tc,td->cd", attended, branch_grad, preferred_element_type=jnp.float32
    )
    output_b_grad = jnp.sum(branch_grad.astype(jnp.float32), 0)
    attended_grad = jnp.einsum(
        "td,cd->tc", branch_grad, output_weight[layer_index], preferred_element_type=jnp.float32
    )
    attended_grad = attended_grad.astype(jnp.bfloat16).reshape(row_count, HEADS, HEAD_DIM)
    key_all, value_all = (
        lax.all_gather(key_flat, "blk", axis=0, tiled=True),
        lax.all_gather(value_flat, "blk", axis=0, tiled=True),
    )
    query_grad, key_all_grad, value_all_grad = attend_back(
        queries, key_all, value_all, attended_grad, attended_f, log_total, scaling
    )
    key_grad, value_grad = (
        lax.psum_scatter(
            key_all_grad.astype(jnp.bfloat16), "blk", scatter_dimension=0, tiled=True
        ).astype(jnp.float32),
        lax.psum_scatter(
            value_all_grad.astype(jnp.bfloat16), "blk", scatter_dimension=0, tiled=True
        ).astype(jnp.float32),
    )
    mixed_grad = jnp.concatenate(
        [
            unrotate(query_grad, cosine, sine_table).reshape(row_count, width),
            unrotate(key_grad.reshape(row_count, HEADS, HEAD_DIM), cosine, sine_table).reshape(
                row_count, width
            ),
            value_grad,
        ],
        -1,
    ).astype(jnp.bfloat16)
    triple_w_grad = jnp.einsum("td,tc->dc", normed, mixed_grad, preferred_element_type=jnp.float32)
    triple_b_grad = jnp.sum(mixed_grad.astype(jnp.float32), 0)
    normed_grad = jnp.einsum(
        "tc,dc->td", mixed_grad, triple_weight[layer_index], preferred_element_type=jnp.float32
    )
    _, attn_pull = jax.vjp(modulate, residual, shift_attn, scale_attn)
    residual_grad, shift_attn_grad, scale_attn_grad = attn_pull(normed_grad)
    residual_grad = residual_grad + middle_grad
    modulation_grad = jnp.concatenate(
        [
            shift_attn_grad,
            scale_attn_grad,
            gate_attn_grad,
            shift_mlp_grad,
            scale_mlp_grad,
            gate_mlp_grad,
        ],
        0,
    )
    adaptive_w_grad = condition[0][:, None] * modulation_grad[None, :]
    condition_term = jnp.dot(
        adaptive_weight[layer_index].astype(jnp.float32), modulation_grad, precision=HIGHEST
    )
    grad_terms = (
        adaptive_w_grad,
        modulation_grad,
        triple_w_grad,
        triple_b_grad,
        output_w_grad,
        output_b_grad,
        expand_w_grad,
        expand_b_grad,
        shrink_w_grad,
        shrink_b_grad,
    )
    return (residual_grad, grad_terms, condition_term)


def local(
    inputs,
    condition,
    prefix,
    mask_embed,
    adaptive_weight,
    adaptive_bias,
    triple_weight,
    triple_bias,
    output_weight,
    output_bias,
    expand_weight,
    expand_bias,
    shrink_weight,
    shrink_bias,
    cotangent,
):
    weights = (
        adaptive_weight,
        adaptive_bias,
        triple_weight,
        triple_bias,
        output_weight,
        output_bias,
        expand_weight,
        expand_bias,
        shrink_weight,
        shrink_bias,
    )
    row_count = inputs.shape[1]
    offset = lax.axis_index("blk") * row_count
    position = offset + jnp.arange(row_count, dtype=jnp.int32)
    masked = position >= prefix[0]
    residual = jnp.where(
        masked[:, None], mask_embed.astype(jnp.float32)[None, :], inputs[0].astype(jnp.float32)
    )
    cosine, sine_table = tables(offset, row_count, HEAD_DIM)
    scaling = 1.0 / math.sqrt(HEAD_DIM)
    modulations = []
    saved_layers = []
    for layer_index in range(LAYERS):
        modulation = jnp.dot(
            condition, adaptive_weight[layer_index].astype(jnp.float32), precision=HIGHEST
        )[0] + adaptive_bias[layer_index].astype(jnp.float32)
        residual, saved = forward_layer(
            residual, modulation, layer_index, weights, cosine, sine_table, scaling
        )
        modulations.append(modulation)
        saved_layers.append(saved)
    outputs = residual.astype(jnp.bfloat16)[None]
    gradient = cotangent[0].astype(jnp.float32)
    condition_total = jnp.zeros((condition.shape[1],), jnp.float32)
    collected = [None] * LAYERS
    mask_sum = None
    for layer_index in reversed(range(LAYERS)):
        gradient, grad_terms, condition_term = backward_layer(
            gradient,
            modulations[layer_index],
            layer_index,
            weights,
            saved_layers[layer_index],
            cosine,
            sine_table,
            scaling,
            condition,
        )
        condition_total = condition_total + condition_term
        collected[layer_index] = grad_terms
    mask_term = jnp.sum(jnp.where(masked[:, None], gradient, 0.0), 0)
    flat_terms = ()
    for layer_index in range(LAYERS):
        flat_terms = flat_terms + tuple(collected[layer_index])
    summed = lax.psum_scatter(
        flat_terms + (mask_term,), ("blk", "dp"), scatter_dimension=0, tiled=True
    )
    collected = [summed[layer_index * 10 : (layer_index + 1) * 10] for layer_index in range(LAYERS)]
    mask_sum = summed[LAYERS * 10]
    condition_grad = lax.psum(condition_total, "blk")[None, :]
    input_grad = jnp.where(masked[:, None], 0.0, gradient)[None]
    stacked = [
        jnp.stack([collected[layer_index][number] for layer_index in range(LAYERS)], 0)
        for number in range(10)
    ]
    return (
        outputs,
        input_grad,
        condition_grad,
        mask_sum,
        stacked[0],
        stacked[1],
        stacked[2],
        stacked[3],
        stacked[4],
        stacked[5],
        stacked[6],
        stacked[7],
        stacked[8],
        stacked[9],
    )


BF = jnp.bfloat16
F32 = jnp.float32
WIDTH = HEADS * HEAD_DIM
GROUP = WIDTH // 4
VM = pl.BlockSpec(memory_space=pltpu.VMEM)
ANY = pl.BlockSpec(memory_space=pl.ANY)
HBM = pl.BlockSpec(memory_space=pltpu.HBM)
HV = pl.BlockSpec(memory_space=pltpu.VMEM)
SM = pl.BlockSpec(memory_space=pltpu.SMEM)
MEBI = 1024 * 1024
ROOT_TWO_PI = math.sqrt(2.0 / math.pi)
CUBIC = 0.044715


def dot_nn(left, right):
    return jnp.dot(left, right, preferred_element_type=F32)


def dot_nt(left, right):
    return lax.dot_general(left, right, (((1,), (1,)), ((), ())), preferred_element_type=F32)


def dot_tn(left, right):
    return lax.dot_general(left, right, (((0,), (0,)), ((), ())), preferred_element_type=F32)


def normalise(values):
    centered = values - jnp.mean(values, -1, keepdims=True)
    rstd = lax.rsqrt(jnp.mean(centered * centered, -1, keepdims=True) + EPSILON)
    return centered * rstd, rstd


def normalise_back(upstream, unit, rstd):
    first = jnp.mean(upstream, -1, keepdims=True)
    second = jnp.mean(upstream * unit, -1, keepdims=True)
    return rstd * (upstream - first - unit * second)


def column_sum(values):
    return jnp.sum(values, 0, keepdims=True)


def turn(values, cosine, signed_sine):
    lane = lax.broadcasted_iota(jnp.int32, (values.shape[0], 128), 1)
    front = (lane % HEAD_DIM) < HEAD_DIM // 2
    pieces = []
    for start in range(0, values.shape[1], 128):
        piece = values[:, start : start + 128]
        swapped = jnp.where(front, pltpu.roll(piece, 96, 1), pltpu.roll(piece, 32, 1))
        pieces.append(piece * cosine + swapped * signed_sine)
    return jnp.concatenate(pieces, 1)


def piece_of(row, number):
    return row[:, number * WIDTH : (number + 1) * WIDTH]


def row_of(ref, layer):
    return ref[...].astype(F32)[layer : layer + 1, :]


def pack_rows(values):
    half = values.shape[0] // 2
    return jnp.concatenate([values[:half], values[half:]], 1)


def qkv_stage(x, layer, mod_row, triple_bias, triple, cos_ref, sin_ref, me, h_ref, chunk_refs, hold):
    unit, _ = normalise(x)
    h = unit * (1.0 + piece_of(mod_row, 1)) + piece_of(mod_row, 0)
    turned = h.T
    h = h.astype(BF)
    each = WIDTH // 32
    for half in range(2):
        picked = [turned[each * (b * 8 + z * 2 + half) :][:each] for z in range(4) for b in range(4)]
        h_ref[half] = jnp.concatenate(picked, 0).astype(BF)
    bias = row_of(triple_bias, layer)
    cosine, sine = cos_ref[0], sin_ref[0]
    parts = []
    for number in range(3):
        columns = slice(number * WIDTH, (number + 1) * WIDTH)
        mixed = dot_nn(h, triple[:, columns]) + bias[:, columns]
        if number < 2:
            mixed = turn(mixed, cosine, sine)
        if number == 0:
            mixed = mixed * HEAD_DIM**-0.5
        parts.append(mixed)
    rows = x.shape[0]
    for group in range(4):
        columns = slice(group * GROUP, (group + 1) * GROUP)
        pair = jnp.concatenate([parts[0][:, columns], parts[1][:, columns]], 1)
        hold[group, 0:rows, :] = pair.astype(BF)
        hold[group, rows : rows + rows // 2, :] = pack_rows(parts[2][:, columns]).astype(BF)
    for place in range(4):
        chunk_refs[place][...] = hold[place ^ me]


def fetch(pairs, sems):
    copies = []
    for number, (source, target) in enumerate(pairs):
        copy = pltpu.make_async_copy(source, target, sems.at[number])
        copy.start()
        copies.append(copy)
    return copies


def wait_all(copies):
    for copy in copies:
        copy.wait()


def three_rows(row):
    upper = row.astype(BF).astype(F32)
    rest = row - upper
    middle = rest.astype(BF).astype(F32)
    low = rest - middle
    number = lax.broadcasted_iota(jnp.int32, (8, row.shape[1]), 0)
    return jnp.where(number == 0, upper, jnp.where(number == 1, middle, jnp.where(number == 2, low, 0.0))).astype(BF)


def modulation(cond, adaptive, adaptive_bias, layer):
    return column_sum(dot_nn(three_rows(cond), adaptive[...])) + row_of(adaptive_bias, layer)


def first_kernel(
    scal, mask_embed, cos_ref, sin_ref, inputs_any, condition_any, adaptive_bias_any, triple_bias_any, adaptive_any,
    triple_any,
    x_ref, mod_ref, h_ref, c0, c1, c2, c3,
    inputs, condition, adaptive_bias, triple_bias, adaptive, triple, hold, sems,
):
    copies = fetch(
        [
            (adaptive_any.at[0], adaptive), (triple_any.at[0], triple), (inputs_any, inputs),
            (condition_any, condition), (adaptive_bias_any, adaptive_bias), (triple_bias_any, triple_bias),
        ],
        sems,
    )
    for copy in copies[2:]:
        copy.wait()
    me = scal[0]
    rows = inputs.shape[1]
    position = me * rows + lax.broadcasted_iota(jnp.int32, (rows, WIDTH), 0)
    x = jnp.where(position >= scal[3], mask_embed[...].astype(F32), inputs[0].astype(F32))
    x_ref[...] = x
    copies[0].wait()
    mod = modulation(condition[...], adaptive, adaptive_bias, 0)
    mod_ref[...] = mod
    copies[1].wait()
    qkv_stage(x, 0, mod, triple_bias, triple, cos_ref, sin_ref, me, h_ref, (c0, c1, c2, c3), hold)


def attend_kernel(
    c0, c1, c2, c3,
    o0, o1, o2, o3, lse_ref, of_ref,
    ot_ref, q_all, k_all, v_turned,
):
    rows = 256
    for place, chunk in enumerate((c0, c1, c2, c3)):
        span = slice(place * rows, (place + 1) * rows)
        q_all[place] = chunk[0:rows, 0:GROUP]
        k_all[span, :] = chunk[0:rows, GROUP : 2 * GROUP]
        tail = chunk[rows : rows + rows // 2, :]
        v_block = jnp.concatenate([tail[:, 0:GROUP], tail[:, GROUP : 2 * GROUP]], 0)
        v_block = v_block.T
        for number in range(3):
            v_turned[number, 0:HEAD_DIM, span] = v_block[number * HEAD_DIM : (number + 1) * HEAD_DIM]
    v_turned[:, HEAD_DIM:, :] = jnp.ones((3, 16, 4 * rows), BF)
    head = lax.broadcasted_iota(jnp.int32, (2 * rows, GROUP), 1) // HEAD_DIM

    for block in range(0, 4, 2):
        q = q_all[block : block + 2].reshape(2 * rows, GROUP)
        for number in range(3):
            masked = jnp.where(head == number, q, jnp.zeros_like(q))
            scores = dot_nt(k_all[...], masked)
            peak = jnp.max(scores, 0, keepdims=True)
            weights = jnp.exp(scores - peak).astype(BF)
            both = dot_nn(v_turned[number], weights)
            total = both[HEAD_DIM : HEAD_DIM + 1]
            span = slice(number * HEAD_DIM, (number + 1) * HEAD_DIM)
            found = both[0:HEAD_DIM] / total
            lse = peak + jnp.log(total)
            for part in range(2):
                columns = slice(part * rows, (part + 1) * rows)
                ot_ref[block + part, span, :] = found[:, columns]
                lse_ref[block + part, number : number + 1, :] = lse[:, columns]
    for place, out in enumerate((o0, o1, o2, o3)):
        found = ot_ref[place].T
        of_ref[place] = found
        out[...] = pack_rows(found).astype(BF)


def gather_chunks(refs, hold):
    for place in range(4):
        hold[place] = refs[place][...]


def place_rows(target, at, values, scal, group=None):
    count = 16 if group is None else 4
    rows = values.shape[0] // count
    me16 = scal[0] * 4 + scal[1]
    for chip in range(count):
        place = (chip if group is None else chip + 4 * group) ^ me16
        start = pl.multiple_of(at + place * rows, 16)
        target[pl.ds(start, rows), :] = values[chip * rows : (chip + 1) * rows]


def mlp_forward(
    layer, x, mod_row, biases, scal, o_refs, output, expand, shrink, waits, hold, o_ref, aout_ref, m_ref, turned_ref,
    slope_ref, f_ref, bias_all,
):
    gather_chunks(o_refs, hold)
    me = scal[0]
    rows = x.shape[0]
    half = rows // 2
    for group in range(4):
        chunk = hold[group ^ me]
        columns = slice(group * GROUP, (group + 1) * GROUP)
        o_ref[0:half, columns] = chunk[:, 0:GROUP]
        o_ref[half:rows, columns] = chunk[:, GROUP : 2 * GROUP]
    o = o_ref[...]
    hidden = expand.shape[1]
    place_rows(turned_ref, hidden + WIDTH, o.T, scal)
    waits[0].wait()
    a_out = dot_nn(o, output[...]) + row_of(biases[0], layer)
    aout_ref[...] = a_out.astype(BF)
    m = x + piece_of(mod_row, 2) * a_out
    m_ref[...] = m
    unit, _ = normalise(m)
    h2 = (unit * (1.0 + piece_of(mod_row, 4)) + piece_of(mod_row, 3)).astype(BF)
    place_rows(turned_ref, hidden, h2.T, scal)
    waits[1].wait()
    waits[2].wait()
    width = 768
    bias_all[...] = row_of(biases[1], layer)

    def hidden_block(number, f):
        start = pl.multiple_of(number * width, width)
        columns = pl.ds(start, width)
        u = dot_nn(h2, expand[:, columns]) + bias_all[:, columns]
        square = u * u
        gate = 0.5 + 0.5 * jnp.tanh(u * (ROOT_TWO_PI + ROOT_TWO_PI * CUBIC * square))
        active = u * gate
        slope = gate + 2.0 * active * (1.0 - gate) * (ROOT_TWO_PI + 3.0 * ROOT_TWO_PI * CUBIC * square)
        z = active.astype(BF)
        place_rows(turned_ref, 0, z.T, scal, number)
        slope_ref[:, columns] = slope.astype(BF)
        return f + dot_nn(z, shrink[columns, :])

    f = lax.fori_loop(0, hidden // width, hidden_block, jnp.zeros(x.shape, F32), unroll=4 if layer else 1) + row_of(biases[2], layer)
    f_ref[...] = f.astype(BF)
    return m + piece_of(mod_row, 5) * f


def share(values, hold, at):
    half = values.shape[1] // 2
    hold[0, :, at : at + half] = values[:, 0:half]
    hold[1, :, at : at + half] = values[:, half : 2 * half]


def mlp_backward(
    dy, mod_row, me, core, m_ref, f_ref, slope_ref, aout_ref, output, expand, shrink, waits, halves,
    do_ref, dm_ref, vec_ref,
):
    def put(place, row):
        vec_ref[:, place : place + row.shape[1]] = row

    put(0, column_sum(dy * f_ref[...].astype(F32)))
    df = (dy * piece_of(mod_row, 5)).astype(BF)
    put(3072, column_sum(df.astype(F32)))
    hidden = expand.shape[1]
    share(df, halves, hidden // 2)
    dh2 = jnp.zeros(dy.shape, F32)
    waits[2].wait()
    for start in range(0, hidden, 768):
        columns = slice(start, start + 768)
        dz = dot_nt(df, shrink[columns, :])
        du = (slope_ref[:, columns].astype(F32) * dz).astype(BF)
        put(3840 + start, column_sum(du.astype(F32)))
        half = hidden // 2
        halves[start // half, :, start % half : start % half + 768] = du
        if start == 0:
            waits[1].wait()
        dh2 = dh2 + dot_nt(du, expand[:, columns])
    unit, rstd = normalise(m_ref[...])
    put(768, column_sum(dh2))
    put(1536, column_sum(dh2 * unit))
    dm = dy + normalise_back(dh2 * (1.0 + piece_of(mod_row, 4)), unit, rstd)
    dm_ref[...] = dm
    put(2304, column_sum(dm * aout_ref[...].astype(F32)))
    da = (dm * piece_of(mod_row, 2)).astype(BF)
    put(6912, column_sum(da.astype(F32)))
    share(da, halves, hidden // 2 + WIDTH // 2)
    waits[0].wait()
    do = dot_nt(da, output[...])
    for group in range(4):
        do_ref[group] = pack_rows(do[:, group * GROUP : (group + 1) * GROUP]).astype(BF)


def attend_back_kernel(
    scal, given_ref, c0, c1, c2, c3, lse_ref, of_ref, cos_any, sin_any, stacked,
    cos_ref, sin_ref, sems, q_masked, do_masked, k_all, v_all, k_turned, lse_rows, delta_rows, dq_turned, dk_all, dv_all,
):
    copies = fetch([(cos_any, cos_ref), (sin_any, sin_ref)], sems)
    rows = 256
    head = lax.broadcasted_iota(jnp.int32, (rows, GROUP), 1) // HEAD_DIM
    of_head = lax.broadcasted_iota(jnp.int32, (8, GROUP), 1) // HEAD_DIM
    pick = jnp.where(of_head == lax.broadcasted_iota(jnp.int32, (8, GROUP), 0), 1.0, 0.0).astype(BF)
    for place in range(4):
        chunk = (c0, c1, c2, c3)[place]
        given = given_ref[place ^ scal[0]]
        span = slice(place * rows, (place + 1) * rows)
        q = chunk[0:rows, 0:GROUP]
        k = chunk[0:rows, GROUP : 2 * GROUP]
        tail = chunk[rows : rows + rows // 2, :]
        v_all[place] = jnp.concatenate([tail[:, 0:GROUP], tail[:, GROUP : 2 * GROUP]], 0)
        k_all[place] = k
        k_turned[place] = k.T
        do = jnp.concatenate([given[:, 0:GROUP], given[:, GROUP : 2 * GROUP]], 0)
        product = do.astype(F32) * of_ref[place]
        upper = product.astype(BF)
        lower = (product - upper.astype(F32)).astype(BF)
        delta_rows[:, span] = dot_nt(pick, upper) + dot_nt(pick, lower)
        for number in range(3):
            q_masked[number, span, :] = jnp.where(head == number, q, jnp.zeros_like(q))
            do_masked[number, span, :] = jnp.where(head == number, do, jnp.zeros_like(do))
            lse_rows[number : number + 1, span] = lse_ref[place, number : number + 1, :]
    dq_turned[...] = jnp.zeros(dq_turned.shape, F32)

    for block in range(4 // 2):
        k = k_all[block * 2 : (block + 1) * 2].reshape(2 * rows, GROUP)
        v = v_all[block * 2 : (block + 1) * 2].reshape(2 * rows, GROUP)
        dk = jnp.zeros((2 * rows, GROUP), F32)
        dv = jnp.zeros((2 * rows, GROUP), F32)
        for number in range(3):
            span = slice(number * HEAD_DIM, (number + 1) * HEAD_DIM)
            scores = dot_nt(k, q_masked[number])
            probs = jnp.exp(scores - lse_rows[number : number + 1, :])
            prob_grad = dot_nt(v, do_masked[number])
            score_grad = (probs * (prob_grad - delta_rows[number : number + 1, :])).astype(BF)
            dv = dv + dot_nn(probs.astype(BF), do_masked[number])
            dk = dk + dot_nn(score_grad, q_masked[number])
            for part in range(2):
                dq_turned[span, :] += dot_nn(k_turned[block * 2 + part, span, :], score_grad[part * rows : (part + 1) * rows])
        dk_all[block * 2 : (block + 1) * 2] = dk.reshape(2, rows, GROUP)
        dv_all[block * 2 : (block + 1) * 2] = dv.reshape(2, rows, GROUP)
    for copy in copies:
        copy.wait()
    for place in range(4):
        span = slice(place * rows, (place + 1) * rows)
        dq = dq_turned[:, span].T * HEAD_DIM**-0.5
        pair = jnp.concatenate([dq, dk_all[place]], 1)
        pair = turn(pair, cos_ref[place], -sin_ref[place]).astype(BF)
        tail = pack_rows(dv_all[place]).astype(BF)
        stacked[place ^ scal[0], 0:rows, :] = pair
        stacked[place ^ scal[0], rows : rows + rows // 2, :] = tail


def qkv_backward(x, dm, mod_row, chunks, triple, wait, full, vec_ref):
    rows = x.shape[0]
    half = rows // 2
    for group in range(4):
        chunk = chunks(group)
        low = group * GROUP
        full[:, low : low + GROUP] = chunk[0:rows, 0:GROUP]
        full[:, WIDTH + low : WIDTH + low + GROUP] = chunk[0:rows, GROUP : 2 * GROUP]
        full[0:half, 2 * WIDTH + low : 2 * WIDTH + low + GROUP] = chunk[rows : rows + half, 0:GROUP]
        full[half:rows, 2 * WIDTH + low : 2 * WIDTH + low + GROUP] = chunk[rows : rows + half, GROUP : 2 * GROUP]
    dqkv = full[...]
    vec_ref[:, 1536:3840] = column_sum(dqkv.astype(F32))
    wait.wait()
    dh = dot_nt(dqkv, triple[...])
    unit, rstd = normalise(x)
    vec_ref[:, 0:768] = column_sum(dh)
    vec_ref[:, 768:1536] = column_sum(dh * unit)
    return dm + normalise_back(dh * (1.0 + piece_of(mod_row, 1)), unit, rstd)


def middle_kernel(
    scal, x_ref, mod_ref, condition, adaptive_bias, output_bias, expand_bias, shrink_bias, triple_bias,
    cos_ref, sin_ref, o0, o1, o2, o3, output_any, expand_any, shrink_any, triple_any, adaptive_any,
    aout_ref, m_ref, turned_ref, slope_ref, f_ref, y_ref, mod_next, h_ref, c0, c1, c2, c3,
    output, expand, shrink, triple, adaptive, bias_all, o_hold, o_ref, c_hold, sems,
):
    copies = fetch(
        [
            (output_any.at[0], output), (expand_any.at[0], expand), (shrink_any.at[0], shrink),
            (triple_any.at[1], triple), (adaptive_any.at[1], adaptive),
        ],
        sems,
    )
    me = scal[0]
    y = mlp_forward(
        0, x_ref[...], mod_ref[...], (output_bias, expand_bias, shrink_bias), scal, (o0, o1, o2, o3), output, expand, shrink, copies, o_hold, o_ref,
        aout_ref, m_ref, turned_ref, slope_ref, f_ref, bias_all,
    )
    y_ref[...] = y
    copies[3].wait()
    copies[4].wait()
    mod = modulation(condition[...], adaptive, adaptive_bias, 1)
    mod_next[...] = mod
    qkv_stage(
        y, 1, mod, triple_bias, triple, cos_ref, sin_ref, me, h_ref, (c0, c1, c2, c3), c_hold,
    )


def ahead_kernel(
    scal, x_ref, mod_ref, output_bias, expand_bias, shrink_bias, o0, o1, o2, o3, output_any, expand_any, shrink_any,
    out_ref, aout_ref, m_ref, turned_ref, slope_ref, f_ref,
    output, expand, shrink, bias_all, o_hold, o_ref, sems,
):
    copies = fetch([(output_any.at[1], output), (expand_any.at[1], expand), (shrink_any.at[1], shrink)], sems)
    y = mlp_forward(
        1, x_ref[...], mod_ref[...], (output_bias, expand_bias, shrink_bias), scal, (o0, o1, o2, o3), output, expand, shrink, copies, o_hold, o_ref,
        aout_ref, m_ref, turned_ref, slope_ref, f_ref, bias_all,
    )
    out_ref[0] = y.astype(BF)


def turn_kernel(
    scal, mod_ref, m_ref, f_ref, slope_ref, aout_ref, cotangent_any, output_any, expand_any, shrink_any,
    mine, theirs, do_ref, dm_ref, vec_ref,
    output, expand, shrink, cotangent, halves, sems,
):
    copies = fetch(
        [
            (shrink_any.at[1], shrink), (expand_any.at[1], expand), (output_any.at[1], output),
            (cotangent_any, cotangent),
        ],
        sems,
    )
    copies[3].wait()
    me, core = scal[0], scal[2]
    mlp_backward(
        cotangent[0].astype(F32), mod_ref[...], me, core, m_ref, f_ref, slope_ref, aout_ref, output, expand, shrink,
        [copies[2], copies[1], copies[0]], halves, do_ref, dm_ref, vec_ref,
    )
    mine[...] = halves[core]
    theirs[...] = halves[1 - core]


def back_kernel(
    scal, x_ref, dm_in, mod_ref, mod_low, grads, m_ref, f_ref, slope_ref, aout_ref,
    triple_any, output_any, expand_any, shrink_any,
    mine, theirs, vec_first, do_ref, dm_ref, vec_ref,
    triple, output, expand, shrink, full, halves, sems,
):
    copies = fetch(
        [(triple_any.at[1], triple), (shrink_any.at[0], shrink), (expand_any.at[0], expand), (output_any.at[0], output)],
        sems,
    )
    me, core = scal[0], scal[2]
    dy = qkv_backward(
        x_ref[...], dm_in[...], mod_ref[...], lambda group: grads[group], triple, copies[0], full, vec_first,
    )
    mlp_backward(
        dy, mod_low[...], me, core, m_ref, f_ref, slope_ref, aout_ref, output, expand, shrink,
        [copies[3], copies[2], copies[1]], halves, do_ref, dm_ref, vec_ref,
    )
    mine[...] = halves[core]
    theirs[...] = halves[1 - core]


def last_kernel(
    scal, x_ref, dm_in, mod_ref, grads, triple_any,
    vec_first, input_grad, mask_ref,
    triple, full, sems,
):
    copies = fetch([(triple_any.at[0], triple)], sems)
    me = scal[0]
    dx = qkv_backward(
        x_ref[...], dm_in[...], mod_ref[...], lambda group: grads[group], triple, copies[0], full, vec_first,
    )
    rows = dx.shape[0]
    position = me * rows + lax.broadcasted_iota(jnp.int32, dx.shape, 0)
    masked = position >= scal[3]
    input_grad[0] = jnp.where(masked, 0.0, dx)
    mask_ref[...] = column_sum(jnp.where(masked, dx, 0.0))


def triple_kernel(
    scal, h0, h1, h2, h3, chunks,
    mine, theirs,
    result,
):
    rows = chunks.shape[1] * 2 // 3
    half = rows // 2
    each = WIDTH // 8
    for side in range(2):
        qk = jnp.zeros((WIDTH // 2, 2 * GROUP), F32)
        v = jnp.zeros((WIDTH // 2, GROUP), F32)
        for place, h_ref in enumerate((h0, h1, h2, h3)):
            h = h_ref[side]
            at = place ^ scal[0]
            qk = qk + dot_nn(h, chunks[at, 0:rows, :])
            tail = chunks[at, rows : rows + half, :]
            v = v + dot_nn(h, jnp.concatenate([tail[:, 0:GROUP], tail[:, GROUP : 2 * GROUP]], 0))
        for z in range(4):
            span = slice(z * each, (z + 1) * each)
            block = jnp.concatenate([qk[span], pack_rows(v[span])], 0).astype(BF)
            tall = block.shape[0]
            for number in range(3):
                lanes = slice(number * 128, (number + 1) * 128)
                result[side * 4 + z, number * tall : (number + 1) * tall, :] = block[:, lanes]
    for place, offset in enumerate((0, 2, 1, 3)):
        at = scal[1] ^ offset
        tall = result.shape[1]
        mine[place * tall : (place + 1) * tall, :] = result[scal[2] * 4 + at]
        theirs[place * tall : (place + 1) * tall, :] = result[(1 - scal[2]) * 4 + at]


def bring_starts(layout, pieces, hold, sems):
    return fetch(
        [
            (pieces[piece].at[source : source + rows, :], hold.at[slot, target : target + rows, :])
            for piece, source, slot, target, rows in layout
        ],
        sems,
    )


def bring(layout, pieces, hold, sems):
    wait_all(bring_starts(layout, pieces, hold, sems))


def triple_settle_kernel(layout, scal, *refs):
    pieces, outs, (hold, blocks, sems) = refs[:-7], refs[-7:-3], refs[-3:]
    bring(layout, pieces, hold, sems)
    each, rows = WIDTH // 8, WIDTH // 32
    tall = each * 3 // 2
    for layer in range(LAYERS):
        lanes = []
        for number in range(3):
            at = (layer * 3 + number) * tall
            lanes.append(sum(hold[slot, at : at + tall, :].astype(F32) for slot in range(hold.shape[0])))
        total = jnp.concatenate(lanes, 1)
        v = jnp.concatenate([total[each:, 0:GROUP], total[each:, GROUP : 2 * GROUP]], 0)
        for b in range(4):
            span = slice(b * rows, (b + 1) * rows)
            blocks[layer, b, :, 0 : 2 * GROUP] = total[span]
            blocks[layer, b, :, 2 * GROUP : 3 * GROUP] = v[span]
    for place, out in enumerate(outs):
        for layer in range(LAYERS):
            out[layer] = blocks[layer, place ^ scal[0]]


BIT = {"x": 4, "y": 8, "a": 1, "b": 2}
STEP = {"x": ("blk", 1), "y": ("blk", 2), "a": ("dp", 2), "b": ("dp", 4)}


def place_at(order, index):
    place = 0
    for depth, name in enumerate(order):
        if index & (8 >> depth):
            place |= BIT[name]
    return place


def weights_kernel(products, orders, scal, own_any, far_any, mine_any, got_any, *rest):
    count = len(orders)
    sends, keeps = rest[0:count], rest[count : 2 * count]
    turned, grads, sems = rest[2 * count :]
    pairs = [(mine_any, grads.at[0:256, :]), (got_any, grads.at[256:512, :])]
    for low, high, _, _ in products:
        pairs += [(own_any.at[low:high, :], turned.at[low:high, 0:256]), (far_any.at[low:high, :], turned.at[low:high, 256:512])]
    copies = fetch(pairs, sems)
    wait_all(copies[0:2])
    row_at = [0] * count
    for step, (low, high, at, dealt) in enumerate(products):
        wait_all(copies[2 + 2 * step : 4 + 2 * step])
        rows = (high - low) // 16
        width = sum(dealt) * 128
        result = dot_nn(turned[low:high, :], grads[:, at : at + width]).astype(BF)
        column = 0
        for part, order in enumerate(orders):
            blocks = dealt[part]
            for index in range(16):
                target = keeps[part] if index < 8 else sends[part]
                place = place_at(order, index)
                for number in range(blocks):
                    spot = row_at[part] + number * rows
                    target[index % 8, spot : spot + rows, :] = result[
                        place * rows : (place + 1) * rows, (column + number) * 128 : (column + number + 1) * 128
                    ]
            row_at[part] += blocks * rows
            column += blocks


def settle_kernel(layout, blocks, scal, *refs):
    pieces, (mine, theirs, hold, sems) = refs[:-4], refs[-4:]
    bring(layout, pieces, hold, sems)
    core = scal[2]
    row = at = 0
    for rows in blocks:
        half = rows // 2
        total = hold[0, row : row + rows, :].astype(F32)
        for slot in range(1, hold.shape[0]):
            total = total + hold[slot, row : row + rows, :].astype(F32)
        low, high = total[0:half], total[half:rows]
        mine[at : at + half, :] = jnp.where(core == 0, low, high)
        theirs[at : at + half, :] = jnp.where(core == 0, high, low)
        row += rows
        at += half


def add_kernel(layout, rows, *refs):
    outs, (hold, sems) = refs[-2 - len(rows) : -2], refs[-2:]
    copies = bring_starts(layout, refs[: -2 - len(rows)], hold, sems)
    depth = {}
    for number, (_, _, slot, target, count) in enumerate(layout):
        depth.setdefault(target, []).append((slot, count, number))
    at = 0
    for out, size in zip(outs, rows):
        for target in sorted(depth):
            if at <= target < at + size:
                for _, _, number in depth[target]:
                    copies[number].wait()
                count = depth[target][0][1]
                total = sum(hold[slot, target : target + count, :].astype(F32) for slot, _, _ in depth[target])
                out[target - at : target - at + count, :] = total.astype(BF)
        at += size


def plain_add_kernel(left, right, out):
    out[...] = left[...] + right[...]


DMOD = 12 * WIDTH
SMALL = 2 * 6912 + WIDTH
SMALL_AT = {"triple": (0, 2304), "output": (2304, 3072), "expand": (3072, 6144), "shrink": (6144, 6912)}


def pack_kernel(first0, vec0, first1, vec1, mask, out):
    for layer, (first, vec) in enumerate(((first0, vec0), (first1, vec1))):
        at = layer * 6 * WIDTH
        out[:, at : at + 1536] = first[:, 0:1536]
        out[:, at + 1536 : at + 2304] = vec[:, 2304:3072]
        out[:, at + 2304 : at + 3840] = vec[:, 768:2304]
        out[:, at + 3840 : at + 4608] = vec[:, 0:768]
        at = DMOD + layer * 6912
        out[:, at : at + 2304] = first[:, 1536:3840]
        out[:, at + 2304 : at + 3072] = vec[:, 6912:7680]
        out[:, at + 3072 : at + 6144] = vec[:, 3840:6912]
        out[:, at + 6144 : at + 6912] = vec[:, 3072:3840]
    out[:, DMOD + 2 * 6912 :] = mask[...]


def join_kernel(own, got, condition, adaptive_any, out, condition_grad, adaptive, sems):
    (copy,) = fetch([(adaptive_any, adaptive)], sems)
    total = own[...] + got[...]
    out[:, 0:DMOD] = total[:, 0:DMOD]
    out[:, DMOD : DMOD + 128] = condition[...]
    out[:, DMOD + 128 :] = total[:, DMOD:]
    copy.wait()
    grad = jnp.zeros((8, 128), F32)
    for layer in range(LAYERS):
        at = layer * 6 * WIDTH
        grad = grad + dot_nt(three_rows(total[:, at : at + 6 * WIDTH]), adaptive[layer])
    condition_grad[...] = column_sum(grad)


def spread_kernel(own, got, out):
    rows = own.shape[1] - SMALL
    out[:, 0:rows] = own[:, 0:rows]
    out[:, rows : 2 * rows] = got[:, 0:rows]
    out[:, 2 * rows :] = own[:, rows:] + got[:, rows:]


def small_kernel(scal, own, got, adaptive_w, adaptive_b, triple_b, output_b, expand_b, shrink_b, mask_sum):
    index = scal[4]
    each = DMOD + 128
    rows = own.shape[1] - SMALL
    share = adaptive_w.shape[1]
    number = lax.broadcasted_iota(jnp.int32, (8, 128), 0)
    lane = lax.broadcasted_iota(jnp.int32, (8, 128), 1)
    pick = (lane == index * share + number) & (number < share)
    totals = [jnp.zeros((8, 6 * WIDTH), F32), jnp.zeros((8, 6 * WIDTH), F32)]
    sums = [jnp.zeros((1, 6 * WIDTH), F32), jnp.zeros((1, 6 * WIDTH), F32)]
    for source in (own, got):
        for at in range(0, rows, each):
            column = jnp.sum(jnp.where(pick, source[:, at + DMOD : at + each], 0.0), 1, keepdims=True)
            for layer in range(LAYERS):
                low = at + layer * 6 * WIDTH
                row = source[:, low : low + 6 * WIDTH]
                totals[layer] = totals[layer] + column * row
                sums[layer] = sums[layer] + row
    summed = own[:, rows:] + got[:, rows:]

    def cut(row):
        size = row.shape[1] // 32
        return pltpu.roll(row, lax.rem(row.shape[1] - index * size, row.shape[1]), 1)[:, 0:size]

    for layer in range(LAYERS):
        adaptive_w[layer] = totals[layer][0:share]
        adaptive_b[layer : layer + 1, :] = cut(sums[layer])
        for out, (low, high) in zip((triple_b, output_b, expand_b, shrink_b), SMALL_AT.values()):
            at = layer * 6912
            out[layer : layer + 1, :] = cut(summed[:, at + low : at + high])
    mask_sum[...] = cut(summed[:, 2 * 6912 :])


def finish_kernel(plans, scal, *refs):
    pairs = 2 * len(plans)
    groups = refs[pairs : pairs + 4]
    outs, hold = refs[pairs + 4 : -1], refs[-1]
    core = scal[2]
    for bucket, plan in enumerate(plans):
        mine, got = refs[2 * bucket : 2 * bucket + 2]
        at = 0
        for out, layer, block, rows in plan:
            own, other = mine[at : at + rows, :], got[at : at + rows, :]
            half = outs[out].shape[2] // 2
            low = block * 128
            outs[out][layer, :, low : low + 128] = jnp.where(core == 0, own, other)
            outs[out][layer, :, half + low : half + low + 128] = jnp.where(core == 0, other, own)
            at += rows
    for layer in range(LAYERS):
        for place in range(4):
            hold[place] = groups[place][layer]
        for group in range(4):
            block = hold[group ^ scal[0]]
            for number in range(3):
                low = number * WIDTH + group * GROUP
                outs[0][layer, :, low : low + GROUP] = block[:, number * GROUP : (number + 1) * GROUP]


def shaped(*shape, dtype=F32):
    return jax.ShapeDtypeStruct(shape, dtype)


class Outs(list):
    token = None


def call(kernel, specs, outs, scratch, micros, name, limit, after=(), away=()):
    count, extra = len(specs), len(after)
    staging = [pltpu.VMEM(outs[number].shape, outs[number].dtype) for number in away]
    if away:
        staging.append(pltpu.SemaphoreType.DMA((len(away),)))

    def body(*refs):
        mark = refs[count + extra + len(outs)]
        mark[...] = jnp.zeros(mark.shape, F32)
        results = list(refs[count + extra : count + extra + len(outs)])
        rest = refs[count + extra + len(outs) + 1 :]
        staged, rest = rest[: len(staging)], rest[len(staging) :]
        targets = [results[number] for number in away]
        for number, stage in zip(away, staged):
            results[number] = stage
        kernel(*refs[:count], *results, *rest)
        if away:
            wait_all(fetch(list(zip(staged, targets)), staged[-1]))

    made = pl.pallas_call(
        body,
        in_specs=specs + [ANY] * extra,
        out_specs=[HBM if number in away else VM for number in range(len(outs))] + [VM],
        out_shape=[
            pltpu.HBM(shape=out.shape, dtype=out.dtype) if number in away else out for number, out in enumerate(outs)
        ]
        + [shaped(8, 128)],
        scratch_shapes=staging + scratch,
        compiler_params=pltpu.CompilerParams(vmem_limit_bytes=limit * MEBI),
        cost_estimate=pl.CostEstimate(flops=int(micros * 1e9), bytes_accessed=int(micros * 1e6), transcendentals=0),
        name=name,
    )

    def run(*operands):
        operands = [
            pltpu.with_memory_space_constraint(operand, pltpu.HBM) if spec is HBM or spec is HV else operand
            for operand, spec in zip(operands, specs)
        ]
        marks = [
            mark if mark.shape == (8, 128) else pltpu.with_memory_space_constraint(mark, pltpu.HBM) for mark in after
        ]
        results = made(*operands, *marks)
        found = Outs(results[:-1])
        found.token = results[-1]
        return found

    return run


def swap(values, axis, bit):
    size = 4 if axis == "blk" else 8
    return lax.ppermute(values, axis, [(i, i ^ bit) for i in range(size)])


def swap_chunks(chunks):
    return [chunks[0]] + [swap(chunks[place], "blk", place) for place in (1, 2, 3)]


def shaped_like(values):
    return shaped(*values.shape, dtype=values.dtype)


class Part:
    def __init__(self, keep, got, rows, order):
        self.views = [(keep, 0), (got, 0)]
        self.rows = rows
        self.order = order

    def halve(self):
        self.rows //= 2


def exchange(parts, cost, after=()):
    groups = {}
    for part in parts:
        groups.setdefault(part.order[0], []).append(part)
        part.order = part.order[1:]
    groups = list(groups.items())
    ordered, rows = [], []
    for _, group in groups:
        for part in group:
            part.halve()
        ordered += group
        rows.append(sum(part.rows for part in group))
    arrays, layout, total = collect(ordered, True)
    slots = max(slot for _, _, slot, _, _ in layout) + 1
    outs = call(
        functools.partial(add_kernel, layout, rows),
        [HBM] * len(arrays),
        [shaped(count, 128, dtype=BF) for count in rows],
        [pltpu.VMEM((slots, total, 128), BF), pltpu.SemaphoreType.DMA((len(layout),))],
        cost,
        "add",
        16,
        after,
    )(*arrays)
    for (axis, group), out in zip(groups, outs):
        got = swap(out, *STEP[axis])
        at = 0
        for part in group:
            part.views.append((got, at))
            at += part.rows
    return [outs.token]


def weight_parts(scal, own, far, mine, got, products, orders, after=()):
    count = len(orders)
    shapes, rows = [], []
    for part in range(count):
        rows.append(sum(dealt[part] * (high - low) // 16 for low, high, _, dealt in products))
        shapes.append(shaped(8, rows[-1], 128, dtype=BF))
    outs = call(
        functools.partial(weights_kernel, products, orders),
        [SM] + [HBM] * 4,
        shapes * 2,
        [
            pltpu.VMEM((own.shape[0], 512), BF),
            pltpu.VMEM((512, mine.shape[1]), BF),
            pltpu.SemaphoreType.DMA((2 + 2 * len(products),)),
        ],
        300,
        "mlp_weights",
        32,
        after,
        tuple(range(count, 2 * count)),
    )(scal, own, far, mine, got)
    flat = [out.reshape(-1, 128) for out in outs]
    parts = [
        Part(flat[count + number], swap(flat[number], *STEP[order[0]]), 8 * rows[number], order[1:])
        for number, order in enumerate(orders)
    ]
    return parts, [outs.token]


def triple_part(scal, h_rows, stacked, after=()):
    rows = WIDTH // 8 * 3 // 2 * 3
    outs = call(
        triple_kernel,
        [SM] + [HV] * 5,
        [shaped(4 * rows, 128, dtype=BF)] * 2,
        [pltpu.VMEM((8, rows, 128), BF)],
        300,
        "triple_weights",
        20,
        after,
    )(scal, *h_rows, stacked)
    return Part(outs[0], swap(outs[1], "dp", 1), 4 * rows, "ab"), [outs.token]


def collect(parts, upper=False):
    arrays, layout, at = [], [], 0
    for part in parts:
        for slot, (array, first) in enumerate(part.views):
            first = first + part.rows if upper else first
            known = [number for number, other in enumerate(arrays) if other is array]
            if not known:
                arrays.append(array)
                known = [len(arrays) - 1]
            layout.append((known[0], first, slot, at, part.rows))
        at += part.rows
    return arrays, layout, at


def blocks_of(products):
    blocks = []
    for part in range(len(products[0][3])):
        for low, high, _, dealt in products:
            blocks += [(high - low) // 16] * dealt[part]
    return blocks


def settle(parts, scal, products, cost, after=()):
    arrays, layout, rows = collect(parts)
    slots = max(slot for _, _, slot, _, _ in layout) + 1
    outs = call(
        functools.partial(settle_kernel, layout, blocks_of(products)),
        [SM] + [HBM] * len(arrays),
        [shaped(rows // 2, 128)] * 2,
        [pltpu.VMEM((slots, rows, 128), BF), pltpu.SemaphoreType.DMA((len(layout),))],
        cost,
        "settle",
        10,
        after,
    )(scal, *arrays)
    return *outs, outs.token


def triple_settle(parts, scal, after=()):
    arrays, layout, rows = collect(parts)
    slots = max(slot for _, _, slot, _, _ in layout) + 1
    blocks = call(
        functools.partial(triple_settle_kernel, layout),
        [SM] + [HBM] * len(arrays),
        [shaped(LAYERS, WIDTH // 32, 3 * GROUP)] * 4,
        [
            pltpu.VMEM((slots, rows, 128), BF),
            pltpu.VMEM((LAYERS, 4, WIDTH // 32, 3 * GROUP), F32),
            pltpu.SemaphoreType.DMA((len(layout),)),
        ],
        0.1,
        "triple_settle",
        8,
        after,
    )(scal, *arrays)
    return swap_chunks(blocks), [blocks.token]


def plan_of(products, names):
    plan = []
    for part in range(len(products[0][3])):
        for (low, high, _, dealt), (out, layer) in zip(products, names):
            first = sum(dealt[:part])
            plan += [(out, layer, first + number, (high - low) // 32) for number in range(dealt[part])]
    return plan


def rotary_tables(start, rows):
    position = (start[:, None] + jnp.arange(rows, dtype=jnp.int32)[None, :]).astype(F32)
    lane = jnp.arange(128, dtype=jnp.int32)
    frequency = jnp.exp((lane % 32).astype(F32) * (-2.0 * math.log(10000.0) / HEAD_DIM))
    angles = position[:, :, None] * frequency
    return jnp.cos(angles), jnp.sin(angles) * jnp.where(lane % 64 < 32, -1.0, 1.0)


def local_fast(
    inputs, condition, prefix, mask_embed, adaptive_weight, adaptive_bias, triple_weight, triple_bias, output_weight,
    output_bias, expand_weight, expand_bias, shrink_weight, shrink_bias, cotangent,
):
    rows = inputs.shape[1]
    hidden = expand_weight.shape[2]
    blk, dp = lax.axis_index("blk"), lax.axis_index("dp")
    scal = jnp.stack([blk, dp // 2, dp % 2, prefix[0], blk * 8 + dp]).astype(jnp.int32)
    starts = (blk ^ jnp.arange(4, dtype=jnp.int32)) * rows
    cosine, sine = rotary_tables(starts[:1], rows)
    cosines, sines = rotary_tables(starts, rows)

    f_square = shaped(rows, WIDTH)
    b_square = shaped(rows, WIDTH, dtype=BF)
    b_tall = shaped(rows, hidden, dtype=BF)
    packed = rows + rows // 2
    chunk = shaped(packed, 2 * GROUP, dtype=BF)
    o_chunk = shaped(rows // 2, 2 * GROUP, dtype=BF)
    c_hold = pltpu.VMEM((4, packed, 2 * GROUP), BF)
    o_hold = pltpu.VMEM((4, rows // 2, 2 * GROUP), BF)
    adaptive_hold = pltpu.VMEM((condition.shape[1], 6 * WIDTH), BF)
    triple_hold = pltpu.VMEM((WIDTH, 3 * WIDTH), BF)
    output_hold = pltpu.VMEM((WIDTH, WIDTH), BF)
    expand_hold = pltpu.VMEM((WIDTH, hidden), BF)
    shrink_hold = pltpu.VMEM((hidden, WIDTH), BF)
    h_both = shaped(2, WIDTH // 2, rows, dtype=BF)
    half_width = hidden // 2 + WIDTH
    tall = hidden + 2 * WIDTH
    mod_row = shaped(1, 6 * WIDTH)

    x0, mod0, h_rows, *chunks = call(
        first_kernel,
        [SM] + [VM] * 3 + [HBM] * 6,
        [f_square, mod_row, h_both] + [chunk] * 4,
        [
            pltpu.VMEM(inputs.shape, BF), pltpu.VMEM(condition.shape, F32), pltpu.VMEM(adaptive_bias.shape, BF),
            pltpu.VMEM(triple_bias.shape, BF), adaptive_hold, triple_hold, c_hold, pltpu.SemaphoreType.DMA((6,)),
        ],
        300,
        "qkv_first",
        24,
    )(
        scal, mask_embed[None], cosine, sine, inputs, condition, adaptive_bias, triple_bias, adaptive_weight,
        triple_weight,
    )

    def attend(chunks, after):
        return call(
            attend_kernel,
            [VM] * 4,
            [o_chunk] * 4 + [shaped(4, 8, rows), shaped(4, rows, GROUP)],
            [
                pltpu.VMEM((4, GROUP, rows), F32),
                pltpu.VMEM((4, rows, GROUP), BF),
                pltpu.VMEM((4 * rows, GROUP), BF),
                pltpu.VMEM((3, HEAD_DIM + 16, 4 * rows), BF),
            ],
            300,
            "attend",
            20,
            after,
        )(*chunks)

    def attend_back(chunks, given, lse, turned, after):
        stack = shaped(4, packed, 2 * GROUP, dtype=BF)
        return call(
            attend_back_kernel,
            [SM, VM] + [HV] * 6 + [HBM] * 2,
            [stack],
            [
                pltpu.VMEM((4, rows, 128), F32),
                pltpu.VMEM((4, rows, 128), F32),
                pltpu.SemaphoreType.DMA((2,)),
                pltpu.VMEM((3, 4 * rows, GROUP), BF),
                pltpu.VMEM((3, 4 * rows, GROUP), BF),
                pltpu.VMEM((4, rows, GROUP), BF),
                pltpu.VMEM((4, rows, GROUP), BF),
                pltpu.VMEM((4, GROUP, rows), BF),
                pltpu.VMEM((8, 4 * rows), F32),
                pltpu.VMEM((8, 4 * rows), F32),
                pltpu.VMEM((GROUP, 4 * rows), F32),
                pltpu.VMEM((4, rows, GROUP), F32),
                pltpu.VMEM((4, rows, GROUP), F32),
            ],
            300,
            "attend_back",
            26,
            after,
            (0,),
        )(scal, given, *chunks, lse, turned, cosines, sines)

    def far(values):
        return swap(values, "dp", 1)

    def gather_rows(both):
        near = swap(both, "blk", 1)
        return [both, near, swap(both, "blk", 2), swap(near, "blk", 2)]

    chunks0 = swap_chunks(chunks)
    h_rows0 = gather_rows(h_rows)
    *o_chunks, lse0, ot0 = attend(chunks0, ())
    o_chunks = swap_chunks(o_chunks)
    aout0, m0, turned0, slope0, f0, x1, mod1, h_rows, *chunks = call(
        middle_kernel,
        [SM] + [HV] + [VM] * 13 + [HBM] * 5,
        [b_square, f_square, shaped(tall, rows, dtype=BF), b_tall, b_square, f_square, mod_row, h_both] + [chunk] * 4,
        [output_hold, expand_hold, shrink_hold, triple_hold, adaptive_hold, pltpu.VMEM((1, hidden), F32), o_hold, pltpu.VMEM((rows, WIDTH), BF)]
        + [c_hold, pltpu.SemaphoreType.DMA((5,))],
        300,
        "mlp_qkv",
        34,
    )(
        scal, x0, mod0, condition, adaptive_bias, output_bias, expand_bias, shrink_bias, triple_bias, cosine, sine,
        *o_chunks, output_weight, expand_weight, shrink_weight, triple_weight, adaptive_weight,
    )
    turned0_far = far(turned0)
    chunks1 = swap_chunks(chunks)
    h_rows1 = gather_rows(h_rows)
    *o_chunks, lse1, ot1 = attend(chunks1, [*h_rows0[1:], cosines, sines])
    o_chunks = swap_chunks(o_chunks)
    outputs, aout1, m1, turned1, slope1, f1 = call(
        ahead_kernel,
        [SM] + [HV] + [VM] * 8 + [HBM] * 3,
        [shaped(1, rows, WIDTH, dtype=BF), b_square, f_square, shaped(tall, rows, dtype=BF), b_tall, b_square],
        [output_hold, expand_hold, shrink_hold, pltpu.VMEM((1, hidden), F32), o_hold, pltpu.VMEM((rows, WIDTH), BF)]
        + [pltpu.SemaphoreType.DMA((3,))],
        300,
        "mlp_ahead",
        28,
        [*h_rows1[1:3], turned0_far],
    )(
        scal, x1, mod1, output_bias, expand_bias, shrink_bias, *o_chunks, output_weight, expand_weight, shrink_weight
    )
    turned1_far = far(turned1)
    back_outs = [shaped(4, rows // 2, 2 * GROUP, dtype=BF), f_square, shaped(1, 7680)]
    mine1, theirs1, given, dm1, vec1 = call(
        turn_kernel,
        [SM] + [VM] * 5 + [HBM] * 4,
        [shaped(rows, half_width, dtype=BF)] * 2 + back_outs,
        [output_hold, expand_hold, shrink_hold, pltpu.VMEM(cotangent.shape, BF)]
        + [pltpu.VMEM((2, rows, half_width), BF), pltpu.SemaphoreType.DMA((4,))],
        300,
        "mlp_turn",
        32,
        h_rows1[3:],
        (0, 3),
    )(scal, mod1, m1, f1, slope1, aout1, cotangent, output_weight, expand_weight, shrink_weight)

    def exchange_blocks(stack):
        return lax.all_to_all(stack, "blk", 0, 0)

    def deal(*dealt):
        return (
            (hidden, hidden + WIDTH, 0, dealt[0]),
            (0, hidden, hidden // 2, dealt[1]),
            (hidden + WIDTH, tall, hidden // 2 + WIDTH // 2, dealt[2]),
        )

    products1 = deal((4, 4, 4), (1, 1, 1), (2, 1, 0))
    products0 = deal((4, 4, 4), (1, 1, 1), (1, 1, 1))
    orders = ("axyb", "xyba", "yaxb")
    given = exchange_blocks(given)
    parts1, sent = weight_parts(scal, turned1, turned1_far, mine1, far(theirs1), products1, orders)
    outs = attend_back(chunks1, given, lse1, ot1, sent)
    stacked = outs[0]
    grads = exchange_blocks(stacked)
    sent = exchange(parts1, 0.1, [outs.token])
    triple1, sent = triple_part(scal, h_rows1, stacked, sent)
    outs = call(
        back_kernel,
        [SM] + [HV] * 2 + [VM] * 3 + [HV] * 4 + [HBM] * 4,
        [shaped(rows, half_width, dtype=BF)] * 2 + [shaped(1, 3840)] + back_outs,
        [triple_hold, output_hold, expand_hold, shrink_hold, pltpu.VMEM((rows, 3 * WIDTH), BF)]
        + [pltpu.VMEM((2, rows, half_width), BF), pltpu.SemaphoreType.DMA((4,))],
        300,
        "qkv_mlp_back",
        32,
        sent,
        (0, 4),
    )(
        scal, x1, dm1, mod1, mod0, grads, m0, f0, slope0, aout0, triple_weight, output_weight, expand_weight,
        shrink_weight,
    )
    mine0, theirs0, first1, given, dm0, vec0 = outs
    given = exchange_blocks(given)
    sent = exchange([*parts1, triple1], 300, [outs.token])
    parts0, sent = weight_parts(scal, turned0, turned0_far, mine0, far(theirs0), products0, orders, sent)
    sent = exchange([*parts1, triple1], 0.1, sent)
    outs = attend_back(chunks0, given, lse0, ot0, sent)
    stacked = outs[0]
    grads = exchange_blocks(stacked)
    sent = exchange(parts0, 0.1, [outs.token])
    triple0, sent = triple_part(scal, h_rows0, stacked, sent)
    sent = [*sent, triple1.views[-1][0]]
    first0, input_grad, mask_term = call(
        last_kernel,
        [SM] + [HV] * 2 + [VM] * 2 + [HBM],
        [shaped(1, 3840), shaped(1, rows, WIDTH), shaped(1, WIDTH)],
        [triple_hold, pltpu.VMEM((rows, 3 * WIDTH), BF), pltpu.SemaphoreType.DMA((1,))],
        300,
        "qkv_back",
        24,
        sent,
    )(scal, x0, dm0, mod0, grads, triple_weight)

    def spread(own, got, cost, after=()):
        wide = shaped(1, 2 * own.shape[1] - SMALL)
        return call(spread_kernel, [VM] * 2, [wide], [], cost, "spread", 8, after)(own, got)

    outs = call(pack_kernel, [VM] * 5, [shaped(1, DMOD + SMALL)], [], 0.1, "pack", 8)(
        first0, vec0, first1, vec1, mask_term
    )
    small = outs[0]
    near = swap(small, "blk", 1)
    sent = exchange([*parts0, triple0], 300, [outs.token])
    (summed,) = call(plain_add_kernel, [VM] * 2, [shaped_like(small)], [], 300, "plain_add", 8, sent)(small, near)
    outs = call(
        join_kernel,
        [VM] * 3 + [HBM],
        [shaped(1, DMOD + 128 + SMALL), shaped(1, 128)],
        [pltpu.VMEM(adaptive_weight.shape, BF), pltpu.SemaphoreType.DMA((1,))],
        0.1,
        "join",
        12,
    )(summed, swap(summed, "blk", 2), condition, adaptive_weight)
    wide, condition_grad = outs
    got = swap(wide, *STEP["b"])
    sent = exchange([*parts0, triple0], 300, [outs.token])
    (wide,) = spread(wide, got, 300, sent)
    outs = spread(wide, swap(wide, *STEP["a"]), 0.1)
    wide = outs[0]
    got = far(wide)
    blocks, cut = triple_settle([triple0, triple1], scal, [outs.token])
    outs = call(
        small_kernel,
        [SM] + [VM] * 2,
        [shaped(LAYERS, condition.shape[1] // 32, 6 * WIDTH), shaped(LAYERS, 6 * WIDTH // 32)]
        + [shaped(LAYERS, (high - low) // 32) for low, high in SMALL_AT.values()]
        + [shaped(1, WIDTH // 32)],
        [],
        300,
        "small",
        10,
        cut,
    )(scal, wide, got)
    small_grads = list(outs)
    own1, theirs1, early = settle(parts1, scal, products1, 0.1, cut)
    own0, theirs0, _ = settle(parts0, scal, products0, 0.1, [early, outs.token, *blocks[1:]])
    plans = (
        plan_of(products1, ((2, 1), (3, 1), (1, 1))),
        plan_of(products0, ((2, 0), (3, 0), (1, 0))),
    )
    weight_grads = call(
        functools.partial(finish_kernel, plans),
        [SM] + [VM] * 8,
        [
            shaped(LAYERS, WIDTH // 32, 3 * WIDTH),
            shaped(LAYERS, WIDTH // 32, WIDTH),
            shaped(LAYERS, WIDTH // 32, hidden),
            shaped(LAYERS, hidden // 32, WIDTH),
        ],
        [pltpu.VMEM((4, WIDTH // 32, 3 * GROUP), F32)],
        0.1,
        "finish",
        12,
    )(scal, own1, far(theirs1), own0, far(theirs0), *blocks)
    return (
        outputs,
        input_grad,
        condition_grad,
        small_grads[6][0],
        small_grads[0],
        small_grads[1],
        weight_grads[0],
        small_grads[2],
        weight_grads[1],
        small_grads[3],
        weight_grads[2],
        small_grads[4],
        weight_grads[3],
        small_grads[5],
    )


def solution(mesh):
    in_specs = (
        P("dp", "blk", None),
        P("dp", None),
        P("dp"),
        P(),
        P(),
        P(),
        P(),
        P(),
        P(),
        P(),
        P(),
        P(),
        P(),
        P(),
        P("dp", "blk", None),
    )
    out_specs = (
        P("dp", "blk", None),
        P("dp", "blk", None),
        P("dp", None),
        P(("blk", "dp")),
        P(None, ("blk", "dp"), None),
        P(None, ("blk", "dp")),
        P(None, ("blk", "dp"), None),
        P(None, ("blk", "dp")),
        P(None, ("blk", "dp"), None),
        P(None, ("blk", "dp")),
        P(None, ("blk", "dp"), None),
        P(None, ("blk", "dp")),
        P(None, ("blk", "dp"), None),
        P(None, ("blk", "dp")),
    )
    whole = mesh.shape["blk"] == 4 and mesh.shape["dp"] == 8
    body = local_fast if whole else local
    return jax.shard_map(body, mesh=mesh, in_specs=in_specs, out_specs=out_specs, check_vma=False)
```

```python
import functools
import math

import jax
import jax.numpy as jnp
from jax import lax
from jax.experimental import pallas as pl
from jax.experimental.pallas import tpu as pltpu
from jax.sharding import PartitionSpec as P

HEADS = 12
HEAD_DIM = 64
LAYERS = 2


HIGHEST = lax.Precision.HIGHEST
EPSILON = 1e-06


def modulate(residual, shift, scaling):
    average = jnp.mean(residual, -1, keepdims=True)
    centered = residual - average
    variance = jnp.mean(centered * centered, -1, keepdims=True)
    return centered * lax.rsqrt(variance + EPSILON) * (1.0 + scaling) + shift


def gelu_tanh(values):
    return jax.nn.gelu(values, approximate=True)


def tables(offset, row_count, head_dim):
    half_dim = head_dim // 2
    position = (offset + jnp.arange(row_count, dtype=jnp.int32)).astype(jnp.float32)
    frequency = jnp.exp(
        jnp.arange(half_dim, dtype=jnp.float32) * (-2.0 * math.log(10000.0) / head_dim)
    )
    angles = position[:, None] * frequency[None, :]
    return (jnp.cos(angles)[:, None, :], jnp.sin(angles)[:, None, :])


def rotate(vectors, cosine, sine_table):
    half_dim = vectors.shape[-1] // 2
    front_half = vectors[..., :half_dim]
    back_half = vectors[..., half_dim:]
    return jnp.concatenate(
        [
            front_half * cosine - back_half * sine_table,
            back_half * cosine + front_half * sine_table,
        ],
        -1,
    )


def unrotate(gradient, cosine, sine_table):
    half_dim = gradient.shape[-1] // 2
    front_half = gradient[..., :half_dim]
    back_half = gradient[..., half_dim:]
    return jnp.concatenate(
        [
            front_half * cosine + back_half * sine_table,
            back_half * cosine - front_half * sine_table,
        ],
        -1,
    )


def split_einsum(form, float_left, low_right):
    upper = float_left.astype(jnp.bfloat16)
    lower = (float_left - upper.astype(jnp.float32)).astype(jnp.bfloat16)
    first = jnp.einsum(form, upper, low_right, preferred_element_type=jnp.float32)
    return first + jnp.einsum(form, lower, low_right, preferred_element_type=jnp.float32)


def fold_keys(queries, scaling):

    def absorb(carried, key_piece, offset):
        key_flat, value_flat = key_piece
        piece_rows = key_flat.shape[0]
        block_rows = math.gcd(piece_rows, 512)
        key_blocks = key_flat.reshape(piece_rows // block_rows, block_rows, HEADS, HEAD_DIM)
        value_blocks = value_flat.reshape(piece_rows // block_rows, block_rows, HEADS, HEAD_DIM)

        def absorb_inner(running, block_pair):
            running_max, running_sum, weighted = running
            key_block, value_block = block_pair
            scores = (
                jnp.einsum("qhd,khd->hqk", queries, key_block, preferred_element_type=jnp.float32)
                * scaling
            )
            new_max = jnp.maximum(running_max, jnp.max(scores, -1))
            weights = jnp.exp(scores - new_max[..., None])
            factor = jnp.exp(running_max - new_max)
            running_sum = running_sum * factor + jnp.sum(weights, -1)
            weighted = weighted * factor[..., None] + split_einsum(
                "hqk,khd->hqd", weights, value_block
            )
            return ((new_max, running_sum, weighted), None)

        carried, _ = lax.scan(absorb_inner, carried, (key_blocks, value_blocks))
        return carried

    return absorb


def attend_back(queries, key_all, value_all, out_gradient, attended_f, log_total, scaling):
    row_count = queries.shape[0]
    all_rows = key_all.shape[0]
    block_rows = math.gcd(all_rows, 512)
    key_blocks = key_all.reshape(all_rows // block_rows, block_rows, HEADS, HEAD_DIM)
    value_blocks = value_all.reshape(all_rows // block_rows, block_rows, HEADS, HEAD_DIM)
    out_float = out_gradient.astype(jnp.float32)
    row_delta = jnp.transpose(jnp.sum(out_float * attended_f, -1), (1, 0))

    def attend_inner(query_grad, block_pair):
        key_block, value_block = block_pair
        scores = (
            jnp.einsum("qhd,khd->hqk", queries, key_block, preferred_element_type=jnp.float32)
            * scaling
        )
        probs = jnp.exp(scores - log_total[..., None])
        prob_grad = jnp.einsum(
            "qhd,khd->hqk", out_gradient, value_block, preferred_element_type=jnp.float32
        )
        score_grad = (probs * (prob_grad - row_delta[..., None])).astype(jnp.bfloat16)
        query_grad = query_grad + jnp.einsum(
            "hqk,khd->qhd", score_grad, key_block, preferred_element_type=jnp.float32
        )
        key_grad = (
            jnp.einsum("hqk,qhd->khd", score_grad, queries, preferred_element_type=jnp.float32)
            * scaling
        )
        value_grad = split_einsum("hqk,qhd->khd", probs, out_gradient)
        return (query_grad, (key_grad, value_grad))

    start_grad = jnp.zeros((row_count, HEADS, HEAD_DIM), jnp.float32)
    query_grad, (key_grads, value_grads) = lax.scan(
        attend_inner, start_grad, (key_blocks, value_blocks)
    )
    width = HEADS * HEAD_DIM
    return (
        query_grad * scaling,
        key_grads.reshape(all_rows, width),
        value_grads.reshape(all_rows, width),
    )


def forward_layer(residual, modulation, layer_index, weights, cosine, sine_table, scaling):
    (
        adaptive_weight,
        adaptive_bias,
        triple_weight,
        triple_bias,
        output_weight,
        output_bias,
        expand_weight,
        expand_bias,
        shrink_weight,
        shrink_bias,
    ) = weights
    row_count, width = residual.shape
    pieces = [modulation[number * width : (number + 1) * width] for number in range(6)]
    shift_attn, scale_attn, gate_attn, shift_mlp, scale_mlp, gate_mlp = pieces
    normed = modulate(residual, shift_attn, scale_attn).astype(jnp.bfloat16)
    mixed = jnp.dot(
        normed, triple_weight[layer_index], preferred_element_type=jnp.float32
    ) + triple_bias[layer_index].astype(jnp.float32)
    head_shape = (row_count, HEADS, HEAD_DIM)
    queries = rotate(mixed[:, :width].reshape(head_shape), cosine, sine_table).astype(jnp.bfloat16)
    key_flat = (
        rotate(mixed[:, width : 2 * width].reshape(head_shape), cosine, sine_table)
        .astype(jnp.bfloat16)
        .reshape(row_count, width)
    )
    value_flat = mixed[:, 2 * width :].astype(jnp.bfloat16)
    start_state = (
        jnp.full((HEADS, row_count), -1e30, jnp.float32),
        jnp.zeros((HEADS, row_count), jnp.float32),
        jnp.zeros((HEADS, row_count, HEAD_DIM), jnp.float32),
    )
    absorb = fold_keys(queries, scaling)
    final_state = absorb(
        start_state,
        (
            lax.all_gather(key_flat, "blk", axis=0, tiled=True),
            lax.all_gather(value_flat, "blk", axis=0, tiled=True),
        ),
        jnp.int32(0),
    )
    running_max, running_sum, weighted = final_state
    log_total = running_max + jnp.log(running_sum)
    attended_f = jnp.transpose(weighted / running_sum[..., None], (1, 0, 2))
    attended = attended_f.reshape(row_count, width).astype(jnp.bfloat16)
    branch = jnp.dot(
        attended, output_weight[layer_index], preferred_element_type=jnp.float32
    ) + output_bias[layer_index].astype(jnp.float32)
    middle = residual + gate_attn * branch
    normed_mlp = modulate(middle, shift_mlp, scale_mlp).astype(jnp.bfloat16)
    up_proj = jnp.dot(
        normed_mlp, expand_weight[layer_index], preferred_element_type=jnp.float32
    ) + expand_bias[layer_index].astype(jnp.float32)
    active = gelu_tanh(up_proj).astype(jnp.bfloat16)
    lowered = jnp.dot(
        active, shrink_weight[layer_index], preferred_element_type=jnp.float32
    ) + shrink_bias[layer_index].astype(jnp.float32)
    result = middle + gate_mlp * lowered
    saved = (
        residual,
        normed,
        queries,
        key_flat,
        value_flat,
        None,
        attended_f,
        attended,
        log_total,
        branch,
        middle,
        normed_mlp,
        up_proj,
        active,
        lowered,
    )
    return (result, saved)


def backward_layer(
    gradient, modulation, layer_index, weights, saved, cosine, sine_table, scaling, condition
):
    (
        adaptive_weight,
        adaptive_bias,
        triple_weight,
        triple_bias,
        output_weight,
        output_bias,
        expand_weight,
        expand_bias,
        shrink_weight,
        shrink_bias,
    ) = weights
    (
        residual,
        normed,
        queries,
        key_flat,
        value_flat,
        gathered,
        attended_f,
        attended,
        log_total,
        branch,
        middle,
        normed_mlp,
        up_proj,
        active,
        lowered,
    ) = saved
    row_count, width = residual.shape
    pieces = [modulation[number * width : (number + 1) * width] for number in range(6)]
    shift_attn, scale_attn, gate_attn, shift_mlp, scale_mlp, gate_mlp = pieces
    gate_mlp_grad = jnp.sum(gradient * lowered, 0)
    lowered_grad = (gradient * gate_mlp).astype(jnp.bfloat16)
    shrink_w_grad = jnp.einsum(
        "tf,td->fd", active, lowered_grad, preferred_element_type=jnp.float32
    )
    shrink_b_grad = jnp.sum(lowered_grad.astype(jnp.float32), 0)
    active_grad = jnp.einsum(
        "td,fd->tf", lowered_grad, shrink_weight[layer_index], preferred_element_type=jnp.float32
    )
    _, gelu_pull = jax.vjp(gelu_tanh, up_proj)
    up_grad = gelu_pull(active_grad)[0].astype(jnp.bfloat16)
    expand_w_grad = jnp.einsum("td,tf->df", normed_mlp, up_grad, preferred_element_type=jnp.float32)
    expand_b_grad = jnp.sum(up_grad.astype(jnp.float32), 0)
    normed_mlp_grad = jnp.einsum(
        "tf,df->td", up_grad, expand_weight[layer_index], preferred_element_type=jnp.float32
    )
    _, mlp_pull = jax.vjp(modulate, middle, shift_mlp, scale_mlp)
    middle_grad, shift_mlp_grad, scale_mlp_grad = mlp_pull(normed_mlp_grad)
    middle_grad = middle_grad + gradient
    gate_attn_grad = jnp.sum(middle_grad * branch, 0)
    branch_grad = (middle_grad * gate_attn).astype(jnp.bfloat16)
    output_w_grad = jnp.einsum(
        "tc,td->cd", attended, branch_grad, preferred_element_type=jnp.float32
    )
    output_b_grad = jnp.sum(branch_grad.astype(jnp.float32), 0)
    attended_grad = jnp.einsum(
        "td,cd->tc", branch_grad, output_weight[layer_index], preferred_element_type=jnp.float32
    )
    attended_grad = attended_grad.astype(jnp.bfloat16).reshape(row_count, HEADS, HEAD_DIM)
    key_all, value_all = (
        lax.all_gather(key_flat, "blk", axis=0, tiled=True),
        lax.all_gather(value_flat, "blk", axis=0, tiled=True),
    )
    query_grad, key_all_grad, value_all_grad = attend_back(
        queries, key_all, value_all, attended_grad, attended_f, log_total, scaling
    )
    key_grad, value_grad = (
        lax.psum_scatter(
            key_all_grad.astype(jnp.bfloat16), "blk", scatter_dimension=0, tiled=True
        ).astype(jnp.float32),
        lax.psum_scatter(
            value_all_grad.astype(jnp.bfloat16), "blk", scatter_dimension=0, tiled=True
        ).astype(jnp.float32),
    )
    mixed_grad = jnp.concatenate(
        [
            unrotate(query_grad, cosine, sine_table).reshape(row_count, width),
            unrotate(key_grad.reshape(row_count, HEADS, HEAD_DIM), cosine, sine_table).reshape(
                row_count, width
            ),
            value_grad,
        ],
        -1,
    ).astype(jnp.bfloat16)
    triple_w_grad = jnp.einsum("td,tc->dc", normed, mixed_grad, preferred_element_type=jnp.float32)
    triple_b_grad = jnp.sum(mixed_grad.astype(jnp.float32), 0)
    normed_grad = jnp.einsum(
        "tc,dc->td", mixed_grad, triple_weight[layer_index], preferred_element_type=jnp.float32
    )
    _, attn_pull = jax.vjp(modulate, residual, shift_attn, scale_attn)
    residual_grad, shift_attn_grad, scale_attn_grad = attn_pull(normed_grad)
    residual_grad = residual_grad + middle_grad
    modulation_grad = jnp.concatenate(
        [
            shift_attn_grad,
            scale_attn_grad,
            gate_attn_grad,
            shift_mlp_grad,
            scale_mlp_grad,
            gate_mlp_grad,
        ],
        0,
    )
    adaptive_w_grad = condition[0][:, None] * modulation_grad[None, :]
    condition_term = jnp.dot(
        adaptive_weight[layer_index].astype(jnp.float32), modulation_grad, precision=HIGHEST
    )
    grad_terms = (
        adaptive_w_grad,
        modulation_grad,
        triple_w_grad,
        triple_b_grad,
        output_w_grad,
        output_b_grad,
        expand_w_grad,
        expand_b_grad,
        shrink_w_grad,
        shrink_b_grad,
    )
    return (residual_grad, grad_terms, condition_term)


def local(
    inputs,
    condition,
    prefix,
    mask_embed,
    adaptive_weight,
    adaptive_bias,
    triple_weight,
    triple_bias,
    output_weight,
    output_bias,
    expand_weight,
    expand_bias,
    shrink_weight,
    shrink_bias,
    cotangent,
):
    weights = (
        adaptive_weight,
        adaptive_bias,
        triple_weight,
        triple_bias,
        output_weight,
        output_bias,
        expand_weight,
        expand_bias,
        shrink_weight,
        shrink_bias,
    )
    row_count = inputs.shape[1]
    offset = lax.axis_index("blk") * row_count
    position = offset + jnp.arange(row_count, dtype=jnp.int32)
    masked = position >= prefix[0]
    residual = jnp.where(
        masked[:, None], mask_embed.astype(jnp.float32)[None, :], inputs[0].astype(jnp.float32)
    )
    cosine, sine_table = tables(offset, row_count, HEAD_DIM)
    scaling = 1.0 / math.sqrt(HEAD_DIM)
    modulations = []
    saved_layers = []
    for layer_index in range(LAYERS):
        modulation = jnp.dot(
            condition, adaptive_weight[layer_index].astype(jnp.float32), precision=HIGHEST
        )[0] + adaptive_bias[layer_index].astype(jnp.float32)
        residual, saved = forward_layer(
            residual, modulation, layer_index, weights, cosine, sine_table, scaling
        )
        modulations.append(modulation)
        saved_layers.append(saved)
    outputs = residual.astype(jnp.bfloat16)[None]
    gradient = cotangent[0].astype(jnp.float32)
    condition_total = jnp.zeros((condition.shape[1],), jnp.float32)
    collected = [None] * LAYERS
    mask_sum = None
    for layer_index in reversed(range(LAYERS)):
        gradient, grad_terms, condition_term = backward_layer(
            gradient,
            modulations[layer_index],
            layer_index,
            weights,
            saved_layers[layer_index],
            cosine,
            sine_table,
            scaling,
            condition,
        )
        condition_total = condition_total + condition_term
        collected[layer_index] = grad_terms
    mask_term = jnp.sum(jnp.where(masked[:, None], gradient, 0.0), 0)
    flat_terms = ()
    for layer_index in range(LAYERS):
        flat_terms = flat_terms + tuple(collected[layer_index])
    summed = lax.psum_scatter(
        flat_terms + (mask_term,), ("blk", "dp"), scatter_dimension=0, tiled=True
    )
    collected = [summed[layer_index * 10 : (layer_index + 1) * 10] for layer_index in range(LAYERS)]
    mask_sum = summed[LAYERS * 10]
    condition_grad = lax.psum(condition_total, "blk")[None, :]
    input_grad = jnp.where(masked[:, None], 0.0, gradient)[None]
    stacked = [
        jnp.stack([collected[layer_index][number] for layer_index in range(LAYERS)], 0)
        for number in range(10)
    ]
    return (
        outputs,
        input_grad,
        condition_grad,
        mask_sum,
        stacked[0],
        stacked[1],
        stacked[2],
        stacked[3],
        stacked[4],
        stacked[5],
        stacked[6],
        stacked[7],
        stacked[8],
        stacked[9],
    )


BF = jnp.bfloat16
F32 = jnp.float32
WIDTH = HEADS * HEAD_DIM
GROUP = WIDTH // 4
VM = pl.BlockSpec(memory_space=pltpu.VMEM)
ANY = pl.BlockSpec(memory_space=pl.ANY)
HBM = pl.BlockSpec(memory_space=pltpu.HBM)
HV = pl.BlockSpec(memory_space=pltpu.VMEM)
SM = pl.BlockSpec(memory_space=pltpu.SMEM)
MEBI = 1024 * 1024
ROOT_TWO_PI = math.sqrt(2.0 / math.pi)
CUBIC = 0.044715


def dot_nn(left, right):
    return jnp.dot(left, right, preferred_element_type=F32)


def dot_nt(left, right):
    return lax.dot_general(left, right, (((1,), (1,)), ((), ())), preferred_element_type=F32)


def dot_tn(left, right):
    return lax.dot_general(left, right, (((0,), (0,)), ((), ())), preferred_element_type=F32)


def normalise(values):
    centered = values - jnp.mean(values, -1, keepdims=True)
    rstd = lax.rsqrt(jnp.mean(centered * centered, -1, keepdims=True) + EPSILON)
    return centered * rstd, rstd


def normalise_back(upstream, unit, rstd):
    first = jnp.mean(upstream, -1, keepdims=True)
    second = jnp.mean(upstream * unit, -1, keepdims=True)
    return rstd * (upstream - first - unit * second)


def column_sum(values):
    return jnp.sum(values, 0, keepdims=True)


def turn(values, cosine, signed_sine):
    lane = lax.broadcasted_iota(jnp.int32, (values.shape[0], 128), 1)
    front = (lane % HEAD_DIM) < HEAD_DIM // 2
    pieces = []
    for start in range(0, values.shape[1], 128):
        piece = values[:, start : start + 128]
        swapped = jnp.where(front, pltpu.roll(piece, 96, 1), pltpu.roll(piece, 32, 1))
        pieces.append(piece * cosine + swapped * signed_sine)
    return jnp.concatenate(pieces, 1)


def piece_of(row, number):
    return row[:, number * WIDTH : (number + 1) * WIDTH]


def row_of(ref, layer):
    return ref[...].astype(F32)[layer : layer + 1, :]


def pack_rows(values):
    half = values.shape[0] // 2
    return jnp.concatenate([values[:half], values[half:]], 1)


def qkv_stage(x, layer, mod_row, triple_bias, triple, cos_ref, sin_ref, me, h_ref, chunk_refs, hold):
    unit, _ = normalise(x)
    h = unit * (1.0 + piece_of(mod_row, 1)) + piece_of(mod_row, 0)
    turned = h.T
    h = h.astype(BF)
    each = WIDTH // 32
    for half in range(2):
        picked = [turned[each * (b * 8 + z * 2 + half) :][:each] for z in range(4) for b in range(4)]
        h_ref[half] = jnp.concatenate(picked, 0).astype(BF)
    bias = row_of(triple_bias, layer)
    cosine, sine = cos_ref[0], sin_ref[0]
    parts = []
    for number in range(3):
        columns = slice(number * WIDTH, (number + 1) * WIDTH)
        mixed = dot_nn(h, triple[:, columns]) + bias[:, columns]
        if number < 2:
            mixed = turn(mixed, cosine, sine)
        if number == 0:
            mixed = mixed * HEAD_DIM**-0.5
        parts.append(mixed)
    rows = x.shape[0]
    for group in range(4):
        columns = slice(group * GROUP, (group + 1) * GROUP)
        pair = jnp.concatenate([parts[0][:, columns], parts[1][:, columns]], 1)
        hold[group, 0:rows, :] = pair.astype(BF)
        hold[group, rows : rows + rows // 2, :] = pack_rows(parts[2][:, columns]).astype(BF)
    for place in range(4):
        chunk_refs[place][...] = hold[place ^ me]


def fetch(pairs, sems):
    copies = []
    for number, (source, target) in enumerate(pairs):
        copy = pltpu.make_async_copy(source, target, sems.at[number])
        copy.start()
        copies.append(copy)
    return copies


def wait_all(copies):
    for copy in copies:
        copy.wait()


def three_rows(row):
    upper = row.astype(BF).astype(F32)
    rest = row - upper
    middle = rest.astype(BF).astype(F32)
    low = rest - middle
    number = lax.broadcasted_iota(jnp.int32, (8, row.shape[1]), 0)
    return jnp.where(number == 0, upper, jnp.where(number == 1, middle, jnp.where(number == 2, low, 0.0))).astype(BF)


def modulation(cond, adaptive, adaptive_bias, layer):
    return column_sum(dot_nn(three_rows(cond), adaptive[...])) + row_of(adaptive_bias, layer)


def first_kernel(
    scal, mask_embed, cos_ref, sin_ref, inputs_any, condition_any, adaptive_bias_any, triple_bias_any, adaptive_any,
    triple_any,
    x_ref, mod_ref, h_ref, c0, c1, c2, c3,
    inputs, condition, adaptive_bias, triple_bias, adaptive, triple, hold, sems,
):
    copies = fetch(
        [
            (adaptive_any.at[0], adaptive), (triple_any.at[0], triple), (inputs_any, inputs),
            (condition_any, condition), (adaptive_bias_any, adaptive_bias), (triple_bias_any, triple_bias),
        ],
        sems,
    )
    for copy in copies[2:]:
        copy.wait()
    me = scal[0]
    rows = inputs.shape[1]
    position = me * rows + lax.broadcasted_iota(jnp.int32, (rows, WIDTH), 0)
    x = jnp.where(position >= scal[3], mask_embed[...].astype(F32), inputs[0].astype(F32))
    x_ref[...] = x
    copies[0].wait()
    mod = modulation(condition[...], adaptive, adaptive_bias, 0)
    mod_ref[...] = mod
    copies[1].wait()
    qkv_stage(x, 0, mod, triple_bias, triple, cos_ref, sin_ref, me, h_ref, (c0, c1, c2, c3), hold)


def attend_kernel(
    c0, c1, c2, c3,
    o0, o1, o2, o3, lse_ref, of_ref,
    ot_ref, q_all, k_all, v_turned,
):
    rows = 256
    for place, chunk in enumerate((c0, c1, c2, c3)):
        span = slice(place * rows, (place + 1) * rows)
        q_all[place] = chunk[0:rows, 0:GROUP]
        k_all[span, :] = chunk[0:rows, GROUP : 2 * GROUP]
        tail = chunk[rows : rows + rows // 2, :]
        v_block = jnp.concatenate([tail[:, 0:GROUP], tail[:, GROUP : 2 * GROUP]], 0)
        v_block = v_block.T
        for number in range(3):
            v_turned[number, 0:HEAD_DIM, span] = v_block[number * HEAD_DIM : (number + 1) * HEAD_DIM]
    v_turned[:, HEAD_DIM:, :] = jnp.ones((3, 16, 4 * rows), BF)
    head = lax.broadcasted_iota(jnp.int32, (2 * rows, GROUP), 1) // HEAD_DIM

    for block in range(0, 4, 2):
        q = q_all[block : block + 2].reshape(2 * rows, GROUP)
        for number in range(3):
            masked = jnp.where(head == number, q, jnp.zeros_like(q))
            scores = dot_nt(k_all[...], masked)
            peak = jnp.max(scores, 0, keepdims=True)
            weights = jnp.exp(scores - peak).astype(BF)
            both = dot_nn(v_turned[number], weights)
            total = both[HEAD_DIM : HEAD_DIM + 1]
            span = slice(number * HEAD_DIM, (number + 1) * HEAD_DIM)
            found = both[0:HEAD_DIM] / total
            lse = peak + jnp.log(total)
            for part in range(2):
                columns = slice(part * rows, (part + 1) * rows)
                ot_ref[block + part, span, :] = found[:, columns]
                lse_ref[block + part, number : number + 1, :] = lse[:, columns]
    for place, out in enumerate((o0, o1, o2, o3)):
        found = ot_ref[place].T
        of_ref[place] = found
        out[...] = pack_rows(found).astype(BF)


def gather_chunks(refs, hold):
    for place in range(4):
        hold[place] = refs[place][...]


def place_rows(target, at, values, scal, group=None):
    count = 16 if group is None else 4
    rows = values.shape[0] // count
    me16 = scal[0] * 4 + scal[1]
    for chip in range(count):
        place = (chip if group is None else chip + 4 * group) ^ me16
        start = pl.multiple_of(at + place * rows, 16)
        target[pl.ds(start, rows), :] = values[chip * rows : (chip + 1) * rows]


def mlp_forward(
    layer, x_ref, mod_row, biases, scal, o_refs, output, expand, shrink, waits, hold, o_ref, aout_ref, m_ref, turned_ref,
    slope_ref, f_ref, bias_all,
):
    gather_chunks(o_refs, hold)
    me = scal[0]
    rows = x_ref.shape[0]
    half = rows // 2
    for group in range(4):
        chunk = hold[group ^ me]
        columns = slice(group * GROUP, (group + 1) * GROUP)
        o_ref[0:half, columns] = chunk[:, 0:GROUP]
        o_ref[half:rows, columns] = chunk[:, GROUP : 2 * GROUP]
    o = o_ref[...]
    hidden = expand.shape[1]
    place_rows(turned_ref, hidden + WIDTH, o.T, scal)
    waits[0].wait()
    a_out = dot_nn(o, output[...]) + row_of(biases[0], layer)
    aout_ref[...] = a_out.astype(BF)
    waits[3].wait()
    m = x_ref[...] + piece_of(mod_row, 2) * a_out
    m_ref[...] = m
    unit, _ = normalise(m)
    h2 = (unit * (1.0 + piece_of(mod_row, 4)) + piece_of(mod_row, 3)).astype(BF)
    place_rows(turned_ref, hidden, h2.T, scal)
    waits[1].wait()
    waits[2].wait()
    width = 768
    bias_all[...] = row_of(biases[1], layer)

    def hidden_block(number, f):
        start = pl.multiple_of(number * width, width)
        columns = pl.ds(start, width)
        u = dot_nn(h2, expand[:, columns]) + bias_all[:, columns]
        square = u * u
        gate = 0.5 + 0.5 * jnp.tanh(u * (ROOT_TWO_PI + ROOT_TWO_PI * CUBIC * square))
        active = u * gate
        slope = gate + 2.0 * active * (1.0 - gate) * (ROOT_TWO_PI + 3.0 * ROOT_TWO_PI * CUBIC * square)
        z = active.astype(BF)
        place_rows(turned_ref, 0, z.T, scal, number)
        slope_ref[:, columns] = slope.astype(BF)
        return f + dot_nn(z, shrink[columns, :])

    f = lax.fori_loop(0, hidden // width, hidden_block, jnp.zeros(x_ref.shape, F32), unroll=4 if layer else 1) + row_of(biases[2], layer)
    f_ref[...] = f.astype(BF)
    return m + piece_of(mod_row, 5) * f


def share(values, hold, at):
    half = values.shape[1] // 2
    hold[0, :, at : at + half] = values[:, 0:half]
    hold[1, :, at : at + half] = values[:, half : 2 * half]


def mlp_backward(
    dy, mod_row, me, core, m_ref, f_ref, slope_ref, aout_ref, output, expand, shrink, waits, halves,
    do_ref, dm_ref, vec_ref,
):
    def put(place, row):
        vec_ref[:, place : place + row.shape[1]] = row

    put(0, column_sum(dy * f_ref[...].astype(F32)))
    df = (dy * piece_of(mod_row, 5)).astype(BF)
    put(3072, column_sum(df.astype(F32)))
    hidden = expand.shape[1]
    share(df, halves, hidden // 2)
    dh2 = jnp.zeros(dy.shape, F32)
    waits[2].wait()
    for start in range(0, hidden, 768):
        columns = slice(start, start + 768)
        dz = dot_nt(df, shrink[columns, :])
        du = (slope_ref[:, columns].astype(F32) * dz).astype(BF)
        put(3840 + start, column_sum(du.astype(F32)))
        half = hidden // 2
        halves[start // half, :, start % half : start % half + 768] = du
        if start == 0:
            waits[1].wait()
        dh2 = dh2 + dot_nt(du, expand[:, columns])
    unit, rstd = normalise(m_ref[...])
    put(768, column_sum(dh2))
    put(1536, column_sum(dh2 * unit))
    dm = dy + normalise_back(dh2 * (1.0 + piece_of(mod_row, 4)), unit, rstd)
    dm_ref[...] = dm
    put(2304, column_sum(dm * aout_ref[...].astype(F32)))
    da = (dm * piece_of(mod_row, 2)).astype(BF)
    put(6912, column_sum(da.astype(F32)))
    share(da, halves, hidden // 2 + WIDTH // 2)
    waits[0].wait()
    do = dot_nt(da, output[...])
    for group in range(4):
        do_ref[group] = pack_rows(do[:, group * GROUP : (group + 1) * GROUP]).astype(BF)


def attend_back_kernel(
    scal, given_ref, c0, c1, c2, c3, lse_ref, of_ref, cos_any, sin_any, stacked,
    cos_ref, sin_ref, sems, q_masked, do_masked, k_all, v_all, k_turned, lse_rows, delta_rows, dq_turned, dk_all, dv_all,
):
    copies = fetch([(cos_any, cos_ref), (sin_any, sin_ref)], sems)
    rows = 256
    head = lax.broadcasted_iota(jnp.int32, (rows, GROUP), 1) // HEAD_DIM
    of_head = lax.broadcasted_iota(jnp.int32, (8, GROUP), 1) // HEAD_DIM
    pick = jnp.where(of_head == lax.broadcasted_iota(jnp.int32, (8, GROUP), 0), 1.0, 0.0).astype(BF)
    for place in range(4):
        chunk = (c0, c1, c2, c3)[place]
        given = given_ref[place ^ scal[0]]
        span = slice(place * rows, (place + 1) * rows)
        q = chunk[0:rows, 0:GROUP]
        k = chunk[0:rows, GROUP : 2 * GROUP]
        tail = chunk[rows : rows + rows // 2, :]
        v_all[place] = jnp.concatenate([tail[:, 0:GROUP], tail[:, GROUP : 2 * GROUP]], 0)
        k_all[place] = k
        k_turned[place] = k.T
        do = jnp.concatenate([given[:, 0:GROUP], given[:, GROUP : 2 * GROUP]], 0)
        product = do.astype(F32) * of_ref[place]
        upper = product.astype(BF)
        lower = (product - upper.astype(F32)).astype(BF)
        delta_rows[:, span] = dot_nt(pick, upper) + dot_nt(pick, lower)
        for number in range(3):
            q_masked[number, span, :] = jnp.where(head == number, q, jnp.zeros_like(q))
            do_masked[number, span, :] = jnp.where(head == number, do, jnp.zeros_like(do))
            lse_rows[number : number + 1, span] = lse_ref[place, number : number + 1, :]
    dq_turned[...] = jnp.zeros(dq_turned.shape, F32)

    for block in range(4 // 2):
        k = k_all[block * 2 : (block + 1) * 2].reshape(2 * rows, GROUP)
        v = v_all[block * 2 : (block + 1) * 2].reshape(2 * rows, GROUP)
        dk = jnp.zeros((2 * rows, GROUP), F32)
        dv = jnp.zeros((2 * rows, GROUP), F32)
        for number in range(3):
            span = slice(number * HEAD_DIM, (number + 1) * HEAD_DIM)
            scores = dot_nt(k, q_masked[number])
            probs = jnp.exp(scores - lse_rows[number : number + 1, :])
            prob_grad = dot_nt(v, do_masked[number])
            score_grad = (probs * (prob_grad - delta_rows[number : number + 1, :])).astype(BF)
            dv = dv + dot_nn(probs.astype(BF), do_masked[number])
            dk = dk + dot_nn(score_grad, q_masked[number])
            for part in range(2):
                dq_turned[span, :] += dot_nn(k_turned[block * 2 + part, span, :], score_grad[part * rows : (part + 1) * rows])
        dk_all[block * 2 : (block + 1) * 2] = dk.reshape(2, rows, GROUP)
        dv_all[block * 2 : (block + 1) * 2] = dv.reshape(2, rows, GROUP)
    for copy in copies:
        copy.wait()
    for place in range(4):
        span = slice(place * rows, (place + 1) * rows)
        dq = dq_turned[:, span].T * HEAD_DIM**-0.5
        pair = jnp.concatenate([dq, dk_all[place]], 1)
        pair = turn(pair, cos_ref[place], -sin_ref[place]).astype(BF)
        tail = pack_rows(dv_all[place]).astype(BF)
        stacked[place ^ scal[0], 0:rows, :] = pair
        stacked[place ^ scal[0], rows : rows + rows // 2, :] = tail


def qkv_backward(x_ref, dm_ref, mod_row, chunks, triple, waits, full, vec_ref):
    rows = full.shape[0]
    half = rows // 2
    for group in range(4):
        chunk = chunks(group)
        low = group * GROUP
        full[:, low : low + GROUP] = chunk[0:rows, 0:GROUP]
        full[:, WIDTH + low : WIDTH + low + GROUP] = chunk[0:rows, GROUP : 2 * GROUP]
        full[0:half, 2 * WIDTH + low : 2 * WIDTH + low + GROUP] = chunk[rows : rows + half, 0:GROUP]
        full[half:rows, 2 * WIDTH + low : 2 * WIDTH + low + GROUP] = chunk[rows : rows + half, GROUP : 2 * GROUP]
    dqkv = full[...]
    vec_ref[:, 1536:3840] = column_sum(dqkv.astype(F32))
    waits[0].wait()
    dh = dot_nt(dqkv, triple[...])
    wait_all(waits[1:3])
    unit, rstd = normalise(x_ref[...])
    vec_ref[:, 0:768] = column_sum(dh)
    vec_ref[:, 768:1536] = column_sum(dh * unit)
    return dm_ref[...] + normalise_back(dh * (1.0 + piece_of(mod_row, 1)), unit, rstd)


def middle_kernel(
    scal, mod_ref, condition, adaptive_bias, output_bias, expand_bias, shrink_bias, triple_bias,
    cos_ref, sin_ref, o0, o1, o2, o3, x_any, output_any, expand_any, shrink_any, triple_any, adaptive_any,
    aout_ref, m_ref, turned_ref, slope_ref, f_ref, y_ref, mod_next, h_ref, c0, c1, c2, c3,
    x_ref, output, expand, shrink, triple, adaptive, bias_all, o_hold, o_ref, c_hold, sems,
):
    copies = fetch(
        [
            (output_any.at[0], output), (x_any, x_ref), (expand_any.at[0], expand), (shrink_any.at[0], shrink),
            (triple_any.at[1], triple), (adaptive_any.at[1], adaptive),
        ],
        sems,
    )
    me = scal[0]
    y = mlp_forward(
        0, x_ref, mod_ref[...], (output_bias, expand_bias, shrink_bias), scal, (o0, o1, o2, o3), output, expand, shrink,
        [copies[0], copies[2], copies[3], copies[1]], o_hold, o_ref,
        aout_ref, m_ref, turned_ref, slope_ref, f_ref, bias_all,
    )
    y_ref[...] = y
    wait_all(copies[4:])
    mod = modulation(condition[...], adaptive, adaptive_bias, 1)
    mod_next[...] = mod
    qkv_stage(
        y, 1, mod, triple_bias, triple, cos_ref, sin_ref, me, h_ref, (c0, c1, c2, c3), c_hold,
    )


def ahead_kernel(
    scal, mod_ref, output_bias, expand_bias, shrink_bias, o0, o1, o2, o3, x_any, output_any, expand_any, shrink_any,
    out_ref, aout_ref, m_ref, turned_ref, slope_ref, f_ref,
    x_ref, output, expand, shrink, bias_all, o_hold, o_ref, sems,
):
    copies = fetch(
        [(output_any.at[1], output), (x_any, x_ref), (expand_any.at[1], expand), (shrink_any.at[1], shrink)], sems
    )
    y = mlp_forward(
        1, x_ref, mod_ref[...], (output_bias, expand_bias, shrink_bias), scal, (o0, o1, o2, o3), output, expand, shrink,
        [copies[0], copies[2], copies[3], copies[1]], o_hold, o_ref,
        aout_ref, m_ref, turned_ref, slope_ref, f_ref, bias_all,
    )
    out_ref[0] = y.astype(BF)


def turn_kernel(
    scal, mod_ref, m_ref, f_ref, slope_ref, aout_ref, cotangent_any, output_any, expand_any, shrink_any,
    mine, theirs, do_ref, dm_ref, vec_ref,
    output, expand, shrink, cotangent, halves, sems,
):
    copies = fetch(
        [
            (shrink_any.at[1], shrink), (expand_any.at[1], expand), (output_any.at[1], output),
            (cotangent_any, cotangent),
        ],
        sems,
    )
    copies[3].wait()
    me, core = scal[0], scal[2]
    mlp_backward(
        cotangent[0].astype(F32), mod_ref[...], me, core, m_ref, f_ref, slope_ref, aout_ref, output, expand, shrink,
        [copies[2], copies[1], copies[0]], halves, do_ref, dm_ref, vec_ref,
    )
    mine[...] = halves[core]
    theirs[...] = halves[1 - core]


def back_kernel(
    scal, mod_ref, mod_low, grads, x_any, dm_any, m_any, f_any, slope_any, aout_any,
    triple_any, output_any, expand_any, shrink_any,
    mine, theirs, vec_first, do_ref, dm_ref, vec_ref,
    triple, output, expand, shrink, full, halves, x_ref, dm_in, m_ref, f_ref, slope_ref, aout_ref, sems,
):
    copies = fetch(
        [
            (triple_any.at[1], triple), (x_any, x_ref), (dm_any, dm_in), (f_any, f_ref), (slope_any, slope_ref),
            (m_any, m_ref), (aout_any, aout_ref), (shrink_any.at[0], shrink), (expand_any.at[0], expand),
            (output_any.at[0], output),
        ],
        sems,
    )
    me, core = scal[0], scal[2]
    dy = qkv_backward(
        x_ref, dm_in, mod_ref[...], lambda group: grads[group], triple, copies[0:3], full, vec_first,
    )
    wait_all(copies[3:7])
    mlp_backward(
        dy, mod_low[...], me, core, m_ref, f_ref, slope_ref, aout_ref, output, expand, shrink,
        [copies[9], copies[8], copies[7]], halves, do_ref, dm_ref, vec_ref,
    )
    mine[...] = halves[core]
    theirs[...] = halves[1 - core]


def last_kernel(
    scal, mod_ref, grads, x_any, dm_any, triple_any,
    vec_first, input_grad, mask_ref,
    triple, full, x_ref, dm_in, sems,
):
    copies = fetch([(triple_any.at[0], triple), (x_any, x_ref), (dm_any, dm_in)], sems)
    me = scal[0]
    dx = qkv_backward(
        x_ref, dm_in, mod_ref[...], lambda group: grads[group], triple, copies, full, vec_first,
    )
    rows = dx.shape[0]
    position = me * rows + lax.broadcasted_iota(jnp.int32, dx.shape, 0)
    masked = position >= scal[3]
    input_grad[0] = jnp.where(masked, 0.0, dx)
    mask_ref[...] = column_sum(jnp.where(masked, dx, 0.0))


def triple_kernel(
    scal, h0, h1, h2, h3, chunks,
    mine, theirs,
    result,
):
    rows = chunks.shape[1] * 2 // 3
    half = rows // 2
    each = WIDTH // 8
    for side in range(2):
        qk = jnp.zeros((WIDTH // 2, 2 * GROUP), F32)
        v = jnp.zeros((WIDTH // 2, GROUP), F32)
        for place, h_ref in enumerate((h0, h1, h2, h3)):
            h = h_ref[side]
            at = place ^ scal[0]
            qk = qk + dot_nn(h, chunks[at, 0:rows, :])
            tail = chunks[at, rows : rows + half, :]
            v = v + dot_nn(h, jnp.concatenate([tail[:, 0:GROUP], tail[:, GROUP : 2 * GROUP]], 0))
        for z in range(4):
            span = slice(z * each, (z + 1) * each)
            block = jnp.concatenate([qk[span], pack_rows(v[span])], 0).astype(BF)
            tall = block.shape[0]
            for number in range(3):
                lanes = slice(number * 128, (number + 1) * 128)
                result[side * 4 + z, number * tall : (number + 1) * tall, :] = block[:, lanes]
    for place, offset in enumerate((0, 2, 1, 3)):
        at = scal[1] ^ offset
        tall = result.shape[1]
        mine[place * tall : (place + 1) * tall, :] = result[scal[2] * 4 + at]
        theirs[place * tall : (place + 1) * tall, :] = result[(1 - scal[2]) * 4 + at]


def bring_starts(layout, pieces, hold, sems):
    return fetch(
        [
            (pieces[piece].at[source : source + rows, :], hold.at[slot, target : target + rows, :])
            for piece, source, slot, target, rows in layout
        ],
        sems,
    )


def bring(layout, pieces, hold, sems):
    wait_all(bring_starts(layout, pieces, hold, sems))


def triple_settle_kernel(layout, scal, *refs):
    pieces, outs, (hold, blocks, sems) = refs[:-7], refs[-7:-3], refs[-3:]
    bring(layout, pieces, hold, sems)
    each, rows = WIDTH // 8, WIDTH // 32
    tall = each * 3 // 2
    for layer in range(LAYERS):
        lanes = []
        for number in range(3):
            at = (layer * 3 + number) * tall
            lanes.append(sum(hold[slot, at : at + tall, :].astype(F32) for slot in range(hold.shape[0])))
        total = jnp.concatenate(lanes, 1)
        v = jnp.concatenate([total[each:, 0:GROUP], total[each:, GROUP : 2 * GROUP]], 0)
        for b in range(4):
            span = slice(b * rows, (b + 1) * rows)
            blocks[layer, b, :, 0 : 2 * GROUP] = total[span]
            blocks[layer, b, :, 2 * GROUP : 3 * GROUP] = v[span]
    for place, out in enumerate(outs):
        for layer in range(LAYERS):
            out[layer] = blocks[layer, place ^ scal[0]]


BIT = {"x": 4, "y": 8, "a": 1, "b": 2}
STEP = {"x": ("blk", 1), "y": ("blk", 2), "a": ("dp", 2), "b": ("dp", 4)}


def place_at(order, index):
    place = 0
    for depth, name in enumerate(order):
        if index & (8 >> depth):
            place |= BIT[name]
    return place


def weights_kernel(products, orders, scal, own_any, far_any, mine_any, got_any, *rest):
    count = len(orders)
    sends, keeps = rest[0:count], rest[count : 2 * count]
    turned, grads, sems = rest[2 * count :]
    pairs = [(mine_any, grads.at[0:256, :]), (got_any, grads.at[256:512, :])]
    for low, high, _, _ in products:
        pairs += [(own_any.at[low:high, :], turned.at[low:high, 0:256]), (far_any.at[low:high, :], turned.at[low:high, 256:512])]
    copies = fetch(pairs, sems)
    wait_all(copies[0:2])
    row_at = [0] * count
    for step, (low, high, at, dealt) in enumerate(products):
        wait_all(copies[2 + 2 * step : 4 + 2 * step])
        rows = (high - low) // 16
        width = sum(dealt) * 128
        result = dot_nn(turned[low:high, :], grads[:, at : at + width]).astype(BF)
        column = 0
        for part, order in enumerate(orders):
            blocks = dealt[part]
            for index in range(16):
                target = keeps[part] if index < 8 else sends[part]
                place = place_at(order, index)
                for number in range(blocks):
                    spot = row_at[part] + number * rows
                    target[index % 8, spot : spot + rows, :] = result[
                        place * rows : (place + 1) * rows, (column + number) * 128 : (column + number + 1) * 128
                    ]
            row_at[part] += blocks * rows
            column += blocks


def settle_kernel(layout, blocks, scal, *refs):
    pieces, (mine, theirs, hold, sems) = refs[:-4], refs[-4:]
    bring(layout, pieces, hold, sems)
    core = scal[2]
    row = at = 0
    for rows in blocks:
        half = rows // 2
        total = hold[0, row : row + rows, :].astype(F32)
        for slot in range(1, hold.shape[0]):
            total = total + hold[slot, row : row + rows, :].astype(F32)
        low, high = total[0:half], total[half:rows]
        mine[at : at + half, :] = jnp.where(core == 0, low, high)
        theirs[at : at + half, :] = jnp.where(core == 0, high, low)
        row += rows
        at += half


def add_kernel(layout, rows, *refs):
    outs, (hold, sems) = refs[-2 - len(rows) : -2], refs[-2:]
    copies = bring_starts(layout, refs[: -2 - len(rows)], hold, sems)
    depth = {}
    for number, (_, _, slot, target, count) in enumerate(layout):
        depth.setdefault(target, []).append((slot, count, number))
    at = 0
    for out, size in zip(outs, rows):
        for target in sorted(depth):
            if at <= target < at + size:
                for _, _, number in depth[target]:
                    copies[number].wait()
                count = depth[target][0][1]
                total = sum(hold[slot, target : target + count, :].astype(F32) for slot, _, _ in depth[target])
                out[target - at : target - at + count, :] = total.astype(BF)
        at += size


def plain_add_kernel(left, right, out):
    out[...] = left[...] + right[...]


DMOD = 12 * WIDTH
SMALL = 2 * 6912 + WIDTH
SMALL_AT = {"triple": (0, 2304), "output": (2304, 3072), "expand": (3072, 6144), "shrink": (6144, 6912)}


def pack_kernel(first0, vec0, first1, vec1, mask, out):
    for layer, (first, vec) in enumerate(((first0, vec0), (first1, vec1))):
        at = layer * 6 * WIDTH
        out[:, at : at + 1536] = first[:, 0:1536]
        out[:, at + 1536 : at + 2304] = vec[:, 2304:3072]
        out[:, at + 2304 : at + 3840] = vec[:, 768:2304]
        out[:, at + 3840 : at + 4608] = vec[:, 0:768]
        at = DMOD + layer * 6912
        out[:, at : at + 2304] = first[:, 1536:3840]
        out[:, at + 2304 : at + 3072] = vec[:, 6912:7680]
        out[:, at + 3072 : at + 6144] = vec[:, 3840:6912]
        out[:, at + 6144 : at + 6912] = vec[:, 3072:3840]
    out[:, DMOD + 2 * 6912 :] = mask[...]


def join_kernel(own, got, condition, adaptive_any, out, condition_grad, adaptive, sems):
    (copy,) = fetch([(adaptive_any, adaptive)], sems)
    total = own[...] + got[...]
    out[:, 0:DMOD] = total[:, 0:DMOD]
    out[:, DMOD : DMOD + 128] = condition[...]
    out[:, DMOD + 128 :] = total[:, DMOD:]
    copy.wait()
    grad = jnp.zeros((8, 128), F32)
    for layer in range(LAYERS):
        at = layer * 6 * WIDTH
        grad = grad + dot_nt(three_rows(total[:, at : at + 6 * WIDTH]), adaptive[layer])
    condition_grad[...] = column_sum(grad)


def spread_kernel(own, got, out):
    rows = own.shape[1] - SMALL
    out[:, 0:rows] = own[:, 0:rows]
    out[:, rows : 2 * rows] = got[:, 0:rows]
    out[:, 2 * rows :] = own[:, rows:] + got[:, rows:]


def small_kernel(scal, own, got, adaptive_w, adaptive_b, triple_b, output_b, expand_b, shrink_b, mask_sum):
    index = scal[4]
    each = DMOD + 128
    rows = own.shape[1] - SMALL
    share = adaptive_w.shape[1]
    number = lax.broadcasted_iota(jnp.int32, (8, 128), 0)
    lane = lax.broadcasted_iota(jnp.int32, (8, 128), 1)
    pick = (lane == index * share + number) & (number < share)
    totals = [jnp.zeros((8, 6 * WIDTH), F32), jnp.zeros((8, 6 * WIDTH), F32)]
    sums = [jnp.zeros((1, 6 * WIDTH), F32), jnp.zeros((1, 6 * WIDTH), F32)]
    for source in (own, got):
        for at in range(0, rows, each):
            column = jnp.sum(jnp.where(pick, source[:, at + DMOD : at + each], 0.0), 1, keepdims=True)
            for layer in range(LAYERS):
                low = at + layer * 6 * WIDTH
                row = source[:, low : low + 6 * WIDTH]
                totals[layer] = totals[layer] + column * row
                sums[layer] = sums[layer] + row
    summed = own[:, rows:] + got[:, rows:]

    def cut(row):
        size = row.shape[1] // 32
        return pltpu.roll(row, lax.rem(row.shape[1] - index * size, row.shape[1]), 1)[:, 0:size]

    for layer in range(LAYERS):
        adaptive_w[layer] = totals[layer][0:share]
        adaptive_b[layer : layer + 1, :] = cut(sums[layer])
        for out, (low, high) in zip((triple_b, output_b, expand_b, shrink_b), SMALL_AT.values()):
            at = layer * 6912
            out[layer : layer + 1, :] = cut(summed[:, at + low : at + high])
    mask_sum[...] = cut(summed[:, 2 * 6912 :])


def finish_kernel(plans, scal, *refs):
    pairs = 2 * len(plans)
    groups = refs[pairs : pairs + 4]
    outs, hold = refs[pairs + 4 : -1], refs[-1]
    core = scal[2]
    for bucket, plan in enumerate(plans):
        mine, got = refs[2 * bucket : 2 * bucket + 2]
        at = 0
        for out, layer, block, rows in plan:
            own, other = mine[at : at + rows, :], got[at : at + rows, :]
            half = outs[out].shape[2] // 2
            low = block * 128
            outs[out][layer, :, low : low + 128] = jnp.where(core == 0, own, other)
            outs[out][layer, :, half + low : half + low + 128] = jnp.where(core == 0, other, own)
            at += rows
    for layer in range(LAYERS):
        for place in range(4):
            hold[place] = groups[place][layer]
        for group in range(4):
            block = hold[group ^ scal[0]]
            for number in range(3):
                low = number * WIDTH + group * GROUP
                outs[0][layer, :, low : low + GROUP] = block[:, number * GROUP : (number + 1) * GROUP]


def shaped(*shape, dtype=F32):
    return jax.ShapeDtypeStruct(shape, dtype)


class Outs(list):
    token = None


def call(kernel, specs, outs, scratch, micros, name, limit, after=(), away=()):
    count, extra = len(specs), len(after)
    staging = [pltpu.VMEM(outs[number].shape, outs[number].dtype) for number in away]
    if away:
        staging.append(pltpu.SemaphoreType.DMA((len(away),)))

    def body(*refs):
        mark = refs[count + extra + len(outs)]
        mark[...] = jnp.zeros(mark.shape, F32)
        results = list(refs[count + extra : count + extra + len(outs)])
        rest = refs[count + extra + len(outs) + 1 :]
        staged, rest = rest[: len(staging)], rest[len(staging) :]
        targets = [results[number] for number in away]
        for number, stage in zip(away, staged):
            results[number] = stage
        kernel(*refs[:count], *results, *rest)
        if away:
            wait_all(fetch(list(zip(staged, targets)), staged[-1]))

    made = pl.pallas_call(
        body,
        in_specs=specs + [ANY] * extra,
        out_specs=[HBM if number in away else VM for number in range(len(outs))] + [VM],
        out_shape=[
            pltpu.HBM(shape=out.shape, dtype=out.dtype) if number in away else out for number, out in enumerate(outs)
        ]
        + [shaped(8, 128)],
        scratch_shapes=staging + scratch,
        compiler_params=pltpu.CompilerParams(vmem_limit_bytes=limit * MEBI),
        cost_estimate=pl.CostEstimate(flops=int(micros * 1e9), bytes_accessed=int(micros * 1e6), transcendentals=0),
        name=name,
    )

    def run(*operands):
        operands = [
            pltpu.with_memory_space_constraint(operand, pltpu.HBM) if spec is HBM or spec is HV else operand
            for operand, spec in zip(operands, specs)
        ]
        marks = [
            mark if mark.shape == (8, 128) else pltpu.with_memory_space_constraint(mark, pltpu.HBM) for mark in after
        ]
        results = made(*operands, *marks)
        found = Outs(results[:-1])
        found.token = results[-1]
        return found

    return run


def swap(values, axis, bit):
    size = 4 if axis == "blk" else 8
    return lax.ppermute(values, axis, [(i, i ^ bit) for i in range(size)])


def swap_chunks(chunks):
    return [chunks[0]] + [swap(chunks[place], "blk", place) for place in (1, 2, 3)]


def shaped_like(values):
    return shaped(*values.shape, dtype=values.dtype)


class Part:
    def __init__(self, keep, got, rows, order):
        self.views = [(keep, 0), (got, 0)]
        self.rows = rows
        self.order = order

    def halve(self):
        self.rows //= 2


def exchange(parts, cost, after=()):
    groups = {}
    for part in parts:
        groups.setdefault(part.order[0], []).append(part)
        part.order = part.order[1:]
    groups = list(groups.items())
    ordered, rows = [], []
    for _, group in groups:
        for part in group:
            part.halve()
        ordered += group
        rows.append(sum(part.rows for part in group))
    arrays, layout, total = collect(ordered, True)
    slots = max(slot for _, _, slot, _, _ in layout) + 1
    outs = call(
        functools.partial(add_kernel, layout, rows),
        [HBM] * len(arrays),
        [shaped(count, 128, dtype=BF) for count in rows],
        [pltpu.VMEM((slots, total, 128), BF), pltpu.SemaphoreType.DMA((len(layout),))],
        cost,
        "add",
        16,
        after,
    )(*arrays)
    for (axis, group), out in zip(groups, outs):
        got = swap(out, *STEP[axis])
        at = 0
        for part in group:
            part.views.append((got, at))
            at += part.rows
    return [outs.token]


def weight_parts(scal, own, far, mine, got, products, orders, after=()):
    count = len(orders)
    shapes, rows = [], []
    for part in range(count):
        rows.append(sum(dealt[part] * (high - low) // 16 for low, high, _, dealt in products))
        shapes.append(shaped(8, rows[-1], 128, dtype=BF))
    outs = call(
        functools.partial(weights_kernel, products, orders),
        [SM] + [HBM] * 4,
        shapes * 2,
        [
            pltpu.VMEM((own.shape[0], 512), BF),
            pltpu.VMEM((512, mine.shape[1]), BF),
            pltpu.SemaphoreType.DMA((2 + 2 * len(products),)),
        ],
        300,
        "mlp_weights",
        32,
        after,
        tuple(range(count, 2 * count)),
    )(scal, own, far, mine, got)
    flat = [out.reshape(-1, 128) for out in outs]
    parts = [
        Part(flat[count + number], swap(flat[number], *STEP[order[0]]), 8 * rows[number], order[1:])
        for number, order in enumerate(orders)
    ]
    return parts, [outs.token]


def triple_part(scal, h_rows, stacked, after=()):
    rows = WIDTH // 8 * 3 // 2 * 3
    outs = call(
        triple_kernel,
        [SM] + [HV] * 5,
        [shaped(4 * rows, 128, dtype=BF)] * 2,
        [pltpu.VMEM((8, rows, 128), BF)],
        300,
        "triple_weights",
        20,
        after,
    )(scal, *h_rows, stacked)
    return Part(outs[0], swap(outs[1], "dp", 1), 4 * rows, "ab"), [outs.token]


def collect(parts, upper=False):
    arrays, layout, at = [], [], 0
    for part in parts:
        for slot, (array, first) in enumerate(part.views):
            first = first + part.rows if upper else first
            known = [number for number, other in enumerate(arrays) if other is array]
            if not known:
                arrays.append(array)
                known = [len(arrays) - 1]
            layout.append((known[0], first, slot, at, part.rows))
        at += part.rows
    return arrays, layout, at


def blocks_of(products):
    blocks = []
    for part in range(len(products[0][3])):
        for low, high, _, dealt in products:
            blocks += [(high - low) // 16] * dealt[part]
    return blocks


def settle(parts, scal, products, cost, after=()):
    arrays, layout, rows = collect(parts)
    slots = max(slot for _, _, slot, _, _ in layout) + 1
    outs = call(
        functools.partial(settle_kernel, layout, blocks_of(products)),
        [SM] + [HBM] * len(arrays),
        [shaped(rows // 2, 128)] * 2,
        [pltpu.VMEM((slots, rows, 128), BF), pltpu.SemaphoreType.DMA((len(layout),))],
        cost,
        "settle",
        10,
        after,
    )(scal, *arrays)
    return *outs, outs.token


def triple_settle(parts, scal, after=()):
    arrays, layout, rows = collect(parts)
    slots = max(slot for _, _, slot, _, _ in layout) + 1
    blocks = call(
        functools.partial(triple_settle_kernel, layout),
        [SM] + [HBM] * len(arrays),
        [shaped(LAYERS, WIDTH // 32, 3 * GROUP)] * 4,
        [
            pltpu.VMEM((slots, rows, 128), BF),
            pltpu.VMEM((LAYERS, 4, WIDTH // 32, 3 * GROUP), F32),
            pltpu.SemaphoreType.DMA((len(layout),)),
        ],
        0.1,
        "triple_settle",
        8,
        after,
    )(scal, *arrays)
    return swap_chunks(blocks), [blocks.token]


def plan_of(products, names):
    plan = []
    for part in range(len(products[0][3])):
        for (low, high, _, dealt), (out, layer) in zip(products, names):
            first = sum(dealt[:part])
            plan += [(out, layer, first + number, (high - low) // 32) for number in range(dealt[part])]
    return plan


def rotary_tables(start, rows):
    position = (start[:, None] + jnp.arange(rows, dtype=jnp.int32)[None, :]).astype(F32)
    lane = jnp.arange(128, dtype=jnp.int32)
    frequency = jnp.exp((lane % 32).astype(F32) * (-2.0 * math.log(10000.0) / HEAD_DIM))
    angles = position[:, :, None] * frequency
    return jnp.cos(angles), jnp.sin(angles) * jnp.where(lane % 64 < 32, -1.0, 1.0)


def local_fast(
    inputs, condition, prefix, mask_embed, adaptive_weight, adaptive_bias, triple_weight, triple_bias, output_weight,
    output_bias, expand_weight, expand_bias, shrink_weight, shrink_bias, cotangent,
):
    rows = inputs.shape[1]
    hidden = expand_weight.shape[2]
    blk, dp = lax.axis_index("blk"), lax.axis_index("dp")
    scal = jnp.stack([blk, dp // 2, dp % 2, prefix[0], blk * 8 + dp]).astype(jnp.int32)
    starts = (blk ^ jnp.arange(4, dtype=jnp.int32)) * rows
    cosine, sine = rotary_tables(starts[:1], rows)
    cosines, sines = rotary_tables(starts, rows)

    f_square = shaped(rows, WIDTH)
    x_hold = pltpu.VMEM((rows, WIDTH), F32)
    b_square = shaped(rows, WIDTH, dtype=BF)
    b_tall = shaped(rows, hidden, dtype=BF)
    packed = rows + rows // 2
    chunk = shaped(packed, 2 * GROUP, dtype=BF)
    o_chunk = shaped(rows // 2, 2 * GROUP, dtype=BF)
    c_hold = pltpu.VMEM((4, packed, 2 * GROUP), BF)
    o_hold = pltpu.VMEM((4, rows // 2, 2 * GROUP), BF)
    adaptive_hold = pltpu.VMEM((condition.shape[1], 6 * WIDTH), BF)
    triple_hold = pltpu.VMEM((WIDTH, 3 * WIDTH), BF)
    output_hold = pltpu.VMEM((WIDTH, WIDTH), BF)
    expand_hold = pltpu.VMEM((WIDTH, hidden), BF)
    shrink_hold = pltpu.VMEM((hidden, WIDTH), BF)
    h_both = shaped(2, WIDTH // 2, rows, dtype=BF)
    half_width = hidden // 2 + WIDTH
    tall = hidden + 2 * WIDTH
    mod_row = shaped(1, 6 * WIDTH)

    x0, mod0, h_rows, *chunks = call(
        first_kernel,
        [SM] + [VM] * 3 + [HBM] * 6,
        [f_square, mod_row, h_both] + [chunk] * 4,
        [
            pltpu.VMEM(inputs.shape, BF), pltpu.VMEM(condition.shape, F32), pltpu.VMEM(adaptive_bias.shape, BF),
            pltpu.VMEM(triple_bias.shape, BF), adaptive_hold, triple_hold, c_hold, pltpu.SemaphoreType.DMA((6,)),
        ],
        300,
        "qkv_first",
        24,
    )(
        scal, mask_embed[None], cosine, sine, inputs, condition, adaptive_bias, triple_bias, adaptive_weight,
        triple_weight,
    )

    def attend(chunks, after):
        return call(
            attend_kernel,
            [VM] * 4,
            [o_chunk] * 4 + [shaped(4, 8, rows), shaped(4, rows, GROUP)],
            [
                pltpu.VMEM((4, GROUP, rows), F32),
                pltpu.VMEM((4, rows, GROUP), BF),
                pltpu.VMEM((4 * rows, GROUP), BF),
                pltpu.VMEM((3, HEAD_DIM + 16, 4 * rows), BF),
            ],
            300,
            "attend",
            20,
            after,
        )(*chunks)

    def attend_back(chunks, given, lse, turned, after):
        stack = shaped(4, packed, 2 * GROUP, dtype=BF)
        return call(
            attend_back_kernel,
            [SM, VM] + [HV] * 6 + [HBM] * 2,
            [stack],
            [
                pltpu.VMEM((4, rows, 128), F32),
                pltpu.VMEM((4, rows, 128), F32),
                pltpu.SemaphoreType.DMA((2,)),
                pltpu.VMEM((3, 4 * rows, GROUP), BF),
                pltpu.VMEM((3, 4 * rows, GROUP), BF),
                pltpu.VMEM((4, rows, GROUP), BF),
                pltpu.VMEM((4, rows, GROUP), BF),
                pltpu.VMEM((4, GROUP, rows), BF),
                pltpu.VMEM((8, 4 * rows), F32),
                pltpu.VMEM((8, 4 * rows), F32),
                pltpu.VMEM((GROUP, 4 * rows), F32),
                pltpu.VMEM((4, rows, GROUP), F32),
                pltpu.VMEM((4, rows, GROUP), F32),
            ],
            300,
            "attend_back",
            26,
            after,
            (0,),
        )(scal, given, *chunks, lse, turned, cosines, sines)

    def far(values):
        return swap(values, "dp", 1)

    def gather_rows(both, first, second):
        near = [swap(both, "blk", bit) for bit in (1, 2)]
        return [both, *near, swap(near[first - 1], "blk", second)]

    chunks0 = swap_chunks(chunks)
    h_rows0 = gather_rows(h_rows, 2, 1)
    *o_chunks, lse0, ot0 = attend(chunks0, ())
    o_chunks = swap_chunks(o_chunks)
    aout0, m0, turned0, slope0, f0, x1, mod1, h_rows, *chunks = call(
        middle_kernel,
        [SM] + [VM] * 13 + [HBM] * 6,
        [b_square, f_square, shaped(tall, rows, dtype=BF), b_tall, b_square, f_square, mod_row, h_both] + [chunk] * 4,
        [x_hold, output_hold, expand_hold, shrink_hold, triple_hold, adaptive_hold, pltpu.VMEM((1, hidden), F32), o_hold, pltpu.VMEM((rows, WIDTH), BF)]
        + [c_hold, pltpu.SemaphoreType.DMA((6,))],
        300,
        "mlp_qkv",
        34,
        h_rows0[1:3],
    )(
        scal, mod0, condition, adaptive_bias, output_bias, expand_bias, shrink_bias, triple_bias, cosine, sine,
        *o_chunks, x0, output_weight, expand_weight, shrink_weight, triple_weight, adaptive_weight,
    )
    turned0_far = far(turned0)
    chunks1 = swap_chunks(chunks)
    h_rows1 = gather_rows(h_rows, 1, 2)
    *o_chunks, lse1, ot1 = attend(chunks1, [cosines, sines])
    o_chunks = swap_chunks(o_chunks)
    outputs, aout1, m1, turned1, slope1, f1 = call(
        ahead_kernel,
        [SM] + [VM] * 8 + [HBM] * 4,
        [shaped(1, rows, WIDTH, dtype=BF), b_square, f_square, shaped(tall, rows, dtype=BF), b_tall, b_square],
        [x_hold, output_hold, expand_hold, shrink_hold, pltpu.VMEM((1, hidden), F32), o_hold]
        + [pltpu.VMEM((rows, WIDTH), BF), pltpu.SemaphoreType.DMA((4,))],
        300,
        "mlp_ahead",
        28,
        [*h_rows1[1:3], turned0_far],
    )(
        scal, mod1, output_bias, expand_bias, shrink_bias, *o_chunks, x1, output_weight, expand_weight, shrink_weight
    )
    turned1_far = far(turned1)
    back_outs = [shaped(4, rows // 2, 2 * GROUP, dtype=BF), f_square, shaped(1, 7680)]
    mine1, theirs1, given, dm1, vec1 = call(
        turn_kernel,
        [SM] + [VM] * 5 + [HBM] * 4,
        [shaped(rows, half_width, dtype=BF)] * 2 + back_outs,
        [output_hold, expand_hold, shrink_hold, pltpu.VMEM(cotangent.shape, BF)]
        + [pltpu.VMEM((2, rows, half_width), BF), pltpu.SemaphoreType.DMA((4,))],
        300,
        "mlp_turn",
        32,
        [h_rows0[3], h_rows1[3]],
        (0, 3),
    )(scal, mod1, m1, f1, slope1, aout1, cotangent, output_weight, expand_weight, shrink_weight)

    def exchange_blocks(stack):
        return lax.all_to_all(stack, "blk", 0, 0)

    def deal(*dealt):
        return (
            (hidden, hidden + WIDTH, 0, dealt[0]),
            (0, hidden, hidden // 2, dealt[1]),
            (hidden + WIDTH, tall, hidden // 2 + WIDTH // 2, dealt[2]),
        )

    products1 = deal((4, 4, 4), (1, 1, 1), (2, 1, 0))
    products0 = deal((4, 4, 4), (1, 1, 1), (1, 1, 1))
    orders = ("axyb", "xyba", "yaxb")
    given = exchange_blocks(given)
    parts1, sent = weight_parts(scal, turned1, turned1_far, mine1, far(theirs1), products1, orders)
    outs = attend_back(chunks1, given, lse1, ot1, sent)
    stacked = outs[0]
    grads = exchange_blocks(stacked)
    sent = exchange(parts1, 0.1, [outs.token])
    triple1, sent = triple_part(scal, h_rows1, stacked, sent)
    outs = call(
        back_kernel,
        [SM] + [VM] * 3 + [HBM] * 10,
        [shaped(rows, half_width, dtype=BF)] * 2 + [shaped(1, 3840)] + back_outs,
        [triple_hold, output_hold, expand_hold, shrink_hold, pltpu.VMEM((rows, 3 * WIDTH), BF)]
        + [pltpu.VMEM((2, rows, half_width), BF), x_hold, x_hold, x_hold, pltpu.VMEM((rows, WIDTH), BF)]
        + [pltpu.VMEM((rows, hidden), BF), pltpu.VMEM((rows, WIDTH), BF), pltpu.SemaphoreType.DMA((10,))],
        300,
        "qkv_mlp_back",
        32,
        sent,
        (0, 4),
    )(
        scal, mod1, mod0, grads, x1, dm1, m0, f0, slope0, aout0, triple_weight, output_weight, expand_weight,
        shrink_weight,
    )
    mine0, theirs0, first1, given, dm0, vec0 = outs
    given = exchange_blocks(given)
    sent = exchange([*parts1, triple1], 300, [outs.token])
    parts0, sent = weight_parts(scal, turned0, turned0_far, mine0, far(theirs0), products0, orders, sent)
    sent = exchange([*parts1, triple1], 0.1, sent)
    outs = attend_back(chunks0, given, lse0, ot0, sent)
    stacked = outs[0]
    grads = exchange_blocks(stacked)
    sent = exchange(parts0, 0.1, [outs.token])
    triple0, sent = triple_part(scal, h_rows0, stacked, sent)
    sent = [*sent, triple1.views[-1][0]]
    first0, input_grad, mask_term = call(
        last_kernel,
        [SM] + [VM] * 2 + [HBM] * 3,
        [shaped(1, 3840), shaped(1, rows, WIDTH), shaped(1, WIDTH)],
        [triple_hold, pltpu.VMEM((rows, 3 * WIDTH), BF), x_hold, x_hold, pltpu.SemaphoreType.DMA((3,))],
        300,
        "qkv_back",
        24,
        sent,
    )(scal, mod0, grads, x0, dm0, triple_weight)

    def spread(own, got, cost, after=()):
        wide = shaped(1, 2 * own.shape[1] - SMALL)
        return call(spread_kernel, [VM] * 2, [wide], [], cost, "spread", 8, after)(own, got)

    outs = call(pack_kernel, [VM] * 5, [shaped(1, DMOD + SMALL)], [], 0.1, "pack", 8)(
        first0, vec0, first1, vec1, mask_term
    )
    small = outs[0]
    near = swap(small, "blk", 1)
    sent = exchange([*parts0, triple0], 300, [outs.token])
    (summed,) = call(plain_add_kernel, [VM] * 2, [shaped_like(small)], [], 300, "plain_add", 8, sent)(small, near)
    outs = call(
        join_kernel,
        [VM] * 3 + [HBM],
        [shaped(1, DMOD + 128 + SMALL), shaped(1, 128)],
        [pltpu.VMEM(adaptive_weight.shape, BF), pltpu.SemaphoreType.DMA((1,))],
        0.1,
        "join",
        12,
    )(summed, swap(summed, "blk", 2), condition, adaptive_weight)
    wide, condition_grad = outs
    got = swap(wide, *STEP["b"])
    sent = exchange([*parts0, triple0], 300, [outs.token])
    own1, theirs1, early = settle(parts1, scal, products1, 0.1, sent)
    outs = spread(wide, got, 300, [early])
    wide = outs[0]
    outs = spread(wide, swap(wide, *STEP["a"]), 0.1)
    wide = outs[0]
    outs = call(
        small_kernel,
        [SM] + [VM] * 2,
        [shaped(LAYERS, condition.shape[1] // 32, 6 * WIDTH), shaped(LAYERS, 6 * WIDTH // 32)]
        + [shaped(LAYERS, (high - low) // 32) for low, high in SMALL_AT.values()]
        + [shaped(1, WIDTH // 32)],
        [],
        0.1,
        "small",
        10,
    )(scal, wide, far(wide))
    small_grads = list(outs)
    blocks, cut = triple_settle([triple0, triple1], scal, [outs.token])
    own0, theirs0, _ = settle(parts0, scal, products0, 0.1, [*cut, *blocks[1:]])
    plans = (
        plan_of(products1, ((2, 1), (3, 1), (1, 1))),
        plan_of(products0, ((2, 0), (3, 0), (1, 0))),
    )
    weight_grads = call(
        functools.partial(finish_kernel, plans),
        [SM] + [VM] * 8,
        [
            shaped(LAYERS, WIDTH // 32, 3 * WIDTH),
            shaped(LAYERS, WIDTH // 32, WIDTH),
            shaped(LAYERS, WIDTH // 32, hidden),
            shaped(LAYERS, hidden // 32, WIDTH),
        ],
        [pltpu.VMEM((4, WIDTH // 32, 3 * GROUP), F32)],
        0.1,
        "finish",
        12,
    )(scal, own1, far(theirs1), own0, far(theirs0), *blocks)
    return (
        outputs,
        input_grad,
        condition_grad,
        small_grads[6][0],
        small_grads[0],
        small_grads[1],
        weight_grads[0],
        small_grads[2],
        weight_grads[1],
        small_grads[3],
        weight_grads[2],
        small_grads[4],
        weight_grads[3],
        small_grads[5],
    )


def solution(mesh):
    in_specs = (
        P("dp", "blk", None),
        P("dp", None),
        P("dp"),
        P(),
        P(),
        P(),
        P(),
        P(),
        P(),
        P(),
        P(),
        P(),
        P(),
        P(),
        P("dp", "blk", None),
    )
    out_specs = (
        P("dp", "blk", None),
        P("dp", "blk", None),
        P("dp", None),
        P(("blk", "dp")),
        P(None, ("blk", "dp"), None),
        P(None, ("blk", "dp")),
        P(None, ("blk", "dp"), None),
        P(None, ("blk", "dp")),
        P(None, ("blk", "dp"), None),
        P(None, ("blk", "dp")),
        P(None, ("blk", "dp"), None),
        P(None, ("blk", "dp")),
        P(None, ("blk", "dp"), None),
        P(None, ("blk", "dp")),
    )
    whole = mesh.shape["blk"] == 4 and mesh.shape["dp"] == 8
    body = local_fast if whole else local
    return jax.shard_map(body, mesh=mesh, in_specs=in_specs, out_specs=out_specs, check_vma=False)
```

```python
import functools
import math

import jax
import jax.numpy as jnp
from jax import lax
from jax.experimental import pallas as pl
from jax.experimental.pallas import tpu as pltpu
from jax.sharding import PartitionSpec as P

HEADS = 12
HEAD_DIM = 64
LAYERS = 2


HIGHEST = lax.Precision.HIGHEST
EPSILON = 1e-06


def modulate(residual, shift, scaling):
    average = jnp.mean(residual, -1, keepdims=True)
    centered = residual - average
    variance = jnp.mean(centered * centered, -1, keepdims=True)
    return centered * lax.rsqrt(variance + EPSILON) * (1.0 + scaling) + shift


def gelu_tanh(values):
    return jax.nn.gelu(values, approximate=True)


def tables(offset, row_count, head_dim):
    half_dim = head_dim // 2
    position = (offset + jnp.arange(row_count, dtype=jnp.int32)).astype(jnp.float32)
    frequency = jnp.exp(
        jnp.arange(half_dim, dtype=jnp.float32) * (-2.0 * math.log(10000.0) / head_dim)
    )
    angles = position[:, None] * frequency[None, :]
    return (jnp.cos(angles)[:, None, :], jnp.sin(angles)[:, None, :])


def rotate(vectors, cosine, sine_table):
    half_dim = vectors.shape[-1] // 2
    front_half = vectors[..., :half_dim]
    back_half = vectors[..., half_dim:]
    return jnp.concatenate(
        [
            front_half * cosine - back_half * sine_table,
            back_half * cosine + front_half * sine_table,
        ],
        -1,
    )


def unrotate(gradient, cosine, sine_table):
    half_dim = gradient.shape[-1] // 2
    front_half = gradient[..., :half_dim]
    back_half = gradient[..., half_dim:]
    return jnp.concatenate(
        [
            front_half * cosine + back_half * sine_table,
            back_half * cosine - front_half * sine_table,
        ],
        -1,
    )


def split_einsum(form, float_left, low_right):
    upper = float_left.astype(jnp.bfloat16)
    lower = (float_left - upper.astype(jnp.float32)).astype(jnp.bfloat16)
    first = jnp.einsum(form, upper, low_right, preferred_element_type=jnp.float32)
    return first + jnp.einsum(form, lower, low_right, preferred_element_type=jnp.float32)


def fold_keys(queries, scaling):

    def absorb(carried, key_piece, offset):
        key_flat, value_flat = key_piece
        piece_rows = key_flat.shape[0]
        block_rows = math.gcd(piece_rows, 512)
        key_blocks = key_flat.reshape(piece_rows // block_rows, block_rows, HEADS, HEAD_DIM)
        value_blocks = value_flat.reshape(piece_rows // block_rows, block_rows, HEADS, HEAD_DIM)

        def absorb_inner(running, block_pair):
            running_max, running_sum, weighted = running
            key_block, value_block = block_pair
            scores = (
                jnp.einsum("qhd,khd->hqk", queries, key_block, preferred_element_type=jnp.float32)
                * scaling
            )
            new_max = jnp.maximum(running_max, jnp.max(scores, -1))
            weights = jnp.exp(scores - new_max[..., None])
            factor = jnp.exp(running_max - new_max)
            running_sum = running_sum * factor + jnp.sum(weights, -1)
            weighted = weighted * factor[..., None] + split_einsum(
                "hqk,khd->hqd", weights, value_block
            )
            return ((new_max, running_sum, weighted), None)

        carried, _ = lax.scan(absorb_inner, carried, (key_blocks, value_blocks))
        return carried

    return absorb


def attend_back(queries, key_all, value_all, out_gradient, attended_f, log_total, scaling):
    row_count = queries.shape[0]
    all_rows = key_all.shape[0]
    block_rows = math.gcd(all_rows, 512)
    key_blocks = key_all.reshape(all_rows // block_rows, block_rows, HEADS, HEAD_DIM)
    value_blocks = value_all.reshape(all_rows // block_rows, block_rows, HEADS, HEAD_DIM)
    out_float = out_gradient.astype(jnp.float32)
    row_delta = jnp.transpose(jnp.sum(out_float * attended_f, -1), (1, 0))

    def attend_inner(query_grad, block_pair):
        key_block, value_block = block_pair
        scores = (
            jnp.einsum("qhd,khd->hqk", queries, key_block, preferred_element_type=jnp.float32)
            * scaling
        )
        probs = jnp.exp(scores - log_total[..., None])
        prob_grad = jnp.einsum(
            "qhd,khd->hqk", out_gradient, value_block, preferred_element_type=jnp.float32
        )
        score_grad = (probs * (prob_grad - row_delta[..., None])).astype(jnp.bfloat16)
        query_grad = query_grad + jnp.einsum(
            "hqk,khd->qhd", score_grad, key_block, preferred_element_type=jnp.float32
        )
        key_grad = (
            jnp.einsum("hqk,qhd->khd", score_grad, queries, preferred_element_type=jnp.float32)
            * scaling
        )
        value_grad = split_einsum("hqk,qhd->khd", probs, out_gradient)
        return (query_grad, (key_grad, value_grad))

    start_grad = jnp.zeros((row_count, HEADS, HEAD_DIM), jnp.float32)
    query_grad, (key_grads, value_grads) = lax.scan(
        attend_inner, start_grad, (key_blocks, value_blocks)
    )
    width = HEADS * HEAD_DIM
    return (
        query_grad * scaling,
        key_grads.reshape(all_rows, width),
        value_grads.reshape(all_rows, width),
    )


def forward_layer(residual, modulation, layer_index, weights, cosine, sine_table, scaling):
    (
        adaptive_weight,
        adaptive_bias,
        triple_weight,
        triple_bias,
        output_weight,
        output_bias,
        expand_weight,
        expand_bias,
        shrink_weight,
        shrink_bias,
    ) = weights
    row_count, width = residual.shape
    pieces = [modulation[number * width : (number + 1) * width] for number in range(6)]
    shift_attn, scale_attn, gate_attn, shift_mlp, scale_mlp, gate_mlp = pieces
    normed = modulate(residual, shift_attn, scale_attn).astype(jnp.bfloat16)
    mixed = jnp.dot(
        normed, triple_weight[layer_index], preferred_element_type=jnp.float32
    ) + triple_bias[layer_index].astype(jnp.float32)
    head_shape = (row_count, HEADS, HEAD_DIM)
    queries = rotate(mixed[:, :width].reshape(head_shape), cosine, sine_table).astype(jnp.bfloat16)
    key_flat = (
        rotate(mixed[:, width : 2 * width].reshape(head_shape), cosine, sine_table)
        .astype(jnp.bfloat16)
        .reshape(row_count, width)
    )
    value_flat = mixed[:, 2 * width :].astype(jnp.bfloat16)
    start_state = (
        jnp.full((HEADS, row_count), -1e30, jnp.float32),
        jnp.zeros((HEADS, row_count), jnp.float32),
        jnp.zeros((HEADS, row_count, HEAD_DIM), jnp.float32),
    )
    absorb = fold_keys(queries, scaling)
    final_state = absorb(
        start_state,
        (
            lax.all_gather(key_flat, "blk", axis=0, tiled=True),
            lax.all_gather(value_flat, "blk", axis=0, tiled=True),
        ),
        jnp.int32(0),
    )
    running_max, running_sum, weighted = final_state
    log_total = running_max + jnp.log(running_sum)
    attended_f = jnp.transpose(weighted / running_sum[..., None], (1, 0, 2))
    attended = attended_f.reshape(row_count, width).astype(jnp.bfloat16)
    branch = jnp.dot(
        attended, output_weight[layer_index], preferred_element_type=jnp.float32
    ) + output_bias[layer_index].astype(jnp.float32)
    middle = residual + gate_attn * branch
    normed_mlp = modulate(middle, shift_mlp, scale_mlp).astype(jnp.bfloat16)
    up_proj = jnp.dot(
        normed_mlp, expand_weight[layer_index], preferred_element_type=jnp.float32
    ) + expand_bias[layer_index].astype(jnp.float32)
    active = gelu_tanh(up_proj).astype(jnp.bfloat16)
    lowered = jnp.dot(
        active, shrink_weight[layer_index], preferred_element_type=jnp.float32
    ) + shrink_bias[layer_index].astype(jnp.float32)
    result = middle + gate_mlp * lowered
    saved = (
        residual,
        normed,
        queries,
        key_flat,
        value_flat,
        None,
        attended_f,
        attended,
        log_total,
        branch,
        middle,
        normed_mlp,
        up_proj,
        active,
        lowered,
    )
    return (result, saved)


def backward_layer(
    gradient, modulation, layer_index, weights, saved, cosine, sine_table, scaling, condition
):
    (
        adaptive_weight,
        adaptive_bias,
        triple_weight,
        triple_bias,
        output_weight,
        output_bias,
        expand_weight,
        expand_bias,
        shrink_weight,
        shrink_bias,
    ) = weights
    (
        residual,
        normed,
        queries,
        key_flat,
        value_flat,
        gathered,
        attended_f,
        attended,
        log_total,
        branch,
        middle,
        normed_mlp,
        up_proj,
        active,
        lowered,
    ) = saved
    row_count, width = residual.shape
    pieces = [modulation[number * width : (number + 1) * width] for number in range(6)]
    shift_attn, scale_attn, gate_attn, shift_mlp, scale_mlp, gate_mlp = pieces
    gate_mlp_grad = jnp.sum(gradient * lowered, 0)
    lowered_grad = (gradient * gate_mlp).astype(jnp.bfloat16)
    shrink_w_grad = jnp.einsum(
        "tf,td->fd", active, lowered_grad, preferred_element_type=jnp.float32
    )
    shrink_b_grad = jnp.sum(lowered_grad.astype(jnp.float32), 0)
    active_grad = jnp.einsum(
        "td,fd->tf", lowered_grad, shrink_weight[layer_index], preferred_element_type=jnp.float32
    )
    _, gelu_pull = jax.vjp(gelu_tanh, up_proj)
    up_grad = gelu_pull(active_grad)[0].astype(jnp.bfloat16)
    expand_w_grad = jnp.einsum("td,tf->df", normed_mlp, up_grad, preferred_element_type=jnp.float32)
    expand_b_grad = jnp.sum(up_grad.astype(jnp.float32), 0)
    normed_mlp_grad = jnp.einsum(
        "tf,df->td", up_grad, expand_weight[layer_index], preferred_element_type=jnp.float32
    )
    _, mlp_pull = jax.vjp(modulate, middle, shift_mlp, scale_mlp)
    middle_grad, shift_mlp_grad, scale_mlp_grad = mlp_pull(normed_mlp_grad)
    middle_grad = middle_grad + gradient
    gate_attn_grad = jnp.sum(middle_grad * branch, 0)
    branch_grad = (middle_grad * gate_attn).astype(jnp.bfloat16)
    output_w_grad = jnp.einsum(
        "tc,td->cd", attended, branch_grad, preferred_element_type=jnp.float32
    )
    output_b_grad = jnp.sum(branch_grad.astype(jnp.float32), 0)
    attended_grad = jnp.einsum(
        "td,cd->tc", branch_grad, output_weight[layer_index], preferred_element_type=jnp.float32
    )
    attended_grad = attended_grad.astype(jnp.bfloat16).reshape(row_count, HEADS, HEAD_DIM)
    key_all, value_all = (
        lax.all_gather(key_flat, "blk", axis=0, tiled=True),
        lax.all_gather(value_flat, "blk", axis=0, tiled=True),
    )
    query_grad, key_all_grad, value_all_grad = attend_back(
        queries, key_all, value_all, attended_grad, attended_f, log_total, scaling
    )
    key_grad, value_grad = (
        lax.psum_scatter(
            key_all_grad.astype(jnp.bfloat16), "blk", scatter_dimension=0, tiled=True
        ).astype(jnp.float32),
        lax.psum_scatter(
            value_all_grad.astype(jnp.bfloat16), "blk", scatter_dimension=0, tiled=True
        ).astype(jnp.float32),
    )
    mixed_grad = jnp.concatenate(
        [
            unrotate(query_grad, cosine, sine_table).reshape(row_count, width),
            unrotate(key_grad.reshape(row_count, HEADS, HEAD_DIM), cosine, sine_table).reshape(
                row_count, width
            ),
            value_grad,
        ],
        -1,
    ).astype(jnp.bfloat16)
    triple_w_grad = jnp.einsum("td,tc->dc", normed, mixed_grad, preferred_element_type=jnp.float32)
    triple_b_grad = jnp.sum(mixed_grad.astype(jnp.float32), 0)
    normed_grad = jnp.einsum(
        "tc,dc->td", mixed_grad, triple_weight[layer_index], preferred_element_type=jnp.float32
    )
    _, attn_pull = jax.vjp(modulate, residual, shift_attn, scale_attn)
    residual_grad, shift_attn_grad, scale_attn_grad = attn_pull(normed_grad)
    residual_grad = residual_grad + middle_grad
    modulation_grad = jnp.concatenate(
        [
            shift_attn_grad,
            scale_attn_grad,
            gate_attn_grad,
            shift_mlp_grad,
            scale_mlp_grad,
            gate_mlp_grad,
        ],
        0,
    )
    adaptive_w_grad = condition[0][:, None] * modulation_grad[None, :]
    condition_term = jnp.dot(
        adaptive_weight[layer_index].astype(jnp.float32), modulation_grad, precision=HIGHEST
    )
    grad_terms = (
        adaptive_w_grad,
        modulation_grad,
        triple_w_grad,
        triple_b_grad,
        output_w_grad,
        output_b_grad,
        expand_w_grad,
        expand_b_grad,
        shrink_w_grad,
        shrink_b_grad,
    )
    return (residual_grad, grad_terms, condition_term)


def local(
    inputs,
    condition,
    prefix,
    mask_embed,
    adaptive_weight,
    adaptive_bias,
    triple_weight,
    triple_bias,
    output_weight,
    output_bias,
    expand_weight,
    expand_bias,
    shrink_weight,
    shrink_bias,
    cotangent,
):
    weights = (
        adaptive_weight,
        adaptive_bias,
        triple_weight,
        triple_bias,
        output_weight,
        output_bias,
        expand_weight,
        expand_bias,
        shrink_weight,
        shrink_bias,
    )
    row_count = inputs.shape[1]
    offset = lax.axis_index("blk") * row_count
    position = offset + jnp.arange(row_count, dtype=jnp.int32)
    masked = position >= prefix[0]
    residual = jnp.where(
        masked[:, None], mask_embed.astype(jnp.float32)[None, :], inputs[0].astype(jnp.float32)
    )
    cosine, sine_table = tables(offset, row_count, HEAD_DIM)
    scaling = 1.0 / math.sqrt(HEAD_DIM)
    modulations = []
    saved_layers = []
    for layer_index in range(LAYERS):
        modulation = jnp.dot(
            condition, adaptive_weight[layer_index].astype(jnp.float32), precision=HIGHEST
        )[0] + adaptive_bias[layer_index].astype(jnp.float32)
        residual, saved = forward_layer(
            residual, modulation, layer_index, weights, cosine, sine_table, scaling
        )
        modulations.append(modulation)
        saved_layers.append(saved)
    outputs = residual.astype(jnp.bfloat16)[None]
    gradient = cotangent[0].astype(jnp.float32)
    condition_total = jnp.zeros((condition.shape[1],), jnp.float32)
    collected = [None] * LAYERS
    mask_sum = None
    for layer_index in reversed(range(LAYERS)):
        gradient, grad_terms, condition_term = backward_layer(
            gradient,
            modulations[layer_index],
            layer_index,
            weights,
            saved_layers[layer_index],
            cosine,
            sine_table,
            scaling,
            condition,
        )
        condition_total = condition_total + condition_term
        collected[layer_index] = grad_terms
    mask_term = jnp.sum(jnp.where(masked[:, None], gradient, 0.0), 0)
    flat_terms = ()
    for layer_index in range(LAYERS):
        flat_terms = flat_terms + tuple(collected[layer_index])
    summed = lax.psum_scatter(
        flat_terms + (mask_term,), ("blk", "dp"), scatter_dimension=0, tiled=True
    )
    collected = [summed[layer_index * 10 : (layer_index + 1) * 10] for layer_index in range(LAYERS)]
    mask_sum = summed[LAYERS * 10]
    condition_grad = lax.psum(condition_total, "blk")[None, :]
    input_grad = jnp.where(masked[:, None], 0.0, gradient)[None]
    stacked = [
        jnp.stack([collected[layer_index][number] for layer_index in range(LAYERS)], 0)
        for number in range(10)
    ]
    return (
        outputs,
        input_grad,
        condition_grad,
        mask_sum,
        stacked[0],
        stacked[1],
        stacked[2],
        stacked[3],
        stacked[4],
        stacked[5],
        stacked[6],
        stacked[7],
        stacked[8],
        stacked[9],
    )


BF = jnp.bfloat16
F32 = jnp.float32
WIDTH = HEADS * HEAD_DIM
GROUP = WIDTH // 4
VM = pl.BlockSpec(memory_space=pltpu.VMEM)
ANY = pl.BlockSpec(memory_space=pl.ANY)
HBM = pl.BlockSpec(memory_space=pltpu.HBM)
HV = pl.BlockSpec(memory_space=pltpu.VMEM)
SM = pl.BlockSpec(memory_space=pltpu.SMEM)
MEBI = 1024 * 1024
ROOT_TWO_PI = math.sqrt(2.0 / math.pi)
CUBIC = 0.044715


def dot_nn(left, right):
    return jnp.dot(left, right, preferred_element_type=F32)


def dot_nt(left, right):
    return lax.dot_general(left, right, (((1,), (1,)), ((), ())), preferred_element_type=F32)


def dot_tn(left, right):
    return lax.dot_general(left, right, (((0,), (0,)), ((), ())), preferred_element_type=F32)


def normalise(values):
    centered = values - jnp.mean(values, -1, keepdims=True)
    rstd = lax.rsqrt(jnp.mean(centered * centered, -1, keepdims=True) + EPSILON)
    return centered * rstd, rstd


def normalise_back(upstream, unit, rstd):
    first = jnp.mean(upstream, -1, keepdims=True)
    second = jnp.mean(upstream * unit, -1, keepdims=True)
    return rstd * (upstream - first - unit * second)


def column_sum(values):
    return jnp.sum(values, 0, keepdims=True)


def turn(values, cosine, signed_sine):
    lane = lax.broadcasted_iota(jnp.int32, (values.shape[0], 128), 1)
    front = (lane % HEAD_DIM) < HEAD_DIM // 2
    pieces = []
    for start in range(0, values.shape[1], 128):
        piece = values[:, start : start + 128]
        swapped = jnp.where(front, pltpu.roll(piece, 96, 1), pltpu.roll(piece, 32, 1))
        pieces.append(piece * cosine + swapped * signed_sine)
    return jnp.concatenate(pieces, 1)


def piece_of(row, number):
    return row[:, number * WIDTH : (number + 1) * WIDTH]


def row_of(ref, layer):
    return ref[...].astype(F32)[layer : layer + 1, :]


def pack_rows(values):
    half = values.shape[0] // 2
    return jnp.concatenate([values[:half], values[half:]], 1)


def qkv_stage(x, layer, mod_row, triple_bias, triple, cos_ref, sin_ref, me, h_ref, chunk_refs, hold):
    unit, _ = normalise(x)
    h = unit * (1.0 + piece_of(mod_row, 1)) + piece_of(mod_row, 0)
    turned = h.T
    h = h.astype(BF)
    each = WIDTH // 32
    for half in range(2):
        picked = [turned[each * (b * 8 + z * 2 + half) :][:each] for z in range(4) for b in range(4)]
        h_ref[half] = jnp.concatenate(picked, 0).astype(BF)
    bias = row_of(triple_bias, layer)
    cosine, sine = cos_ref[0], sin_ref[0]
    parts = []
    for number in range(3):
        columns = slice(number * WIDTH, (number + 1) * WIDTH)
        mixed = dot_nn(h, triple[:, columns]) + bias[:, columns]
        if number < 2:
            mixed = turn(mixed, cosine, sine)
        if number == 0:
            mixed = mixed * HEAD_DIM**-0.5
        parts.append(mixed)
    rows = x.shape[0]
    for group in range(4):
        columns = slice(group * GROUP, (group + 1) * GROUP)
        pair = jnp.concatenate([parts[0][:, columns], parts[1][:, columns]], 1)
        hold[group, 0:rows, :] = pair.astype(BF)
        hold[group, rows : rows + rows // 2, :] = pack_rows(parts[2][:, columns]).astype(BF)
    for place in range(4):
        chunk_refs[place][...] = hold[place ^ me]


def fetch(pairs, sems):
    copies = []
    for number, (source, target) in enumerate(pairs):
        copy = pltpu.make_async_copy(source, target, sems.at[number])
        copy.start()
        copies.append(copy)
    return copies


def wait_all(copies):
    for copy in copies:
        copy.wait()


def three_rows(row):
    upper = row.astype(BF).astype(F32)
    rest = row - upper
    middle = rest.astype(BF).astype(F32)
    low = rest - middle
    number = lax.broadcasted_iota(jnp.int32, (8, row.shape[1]), 0)
    return jnp.where(number == 0, upper, jnp.where(number == 1, middle, jnp.where(number == 2, low, 0.0))).astype(BF)


def modulation(cond, adaptive, adaptive_bias, layer):
    return column_sum(dot_nn(three_rows(cond), adaptive[...])) + row_of(adaptive_bias, layer)


def first_kernel(
    scal, mask_embed, cos_ref, sin_ref, inputs_any, condition_any, adaptive_bias_any, triple_bias_any, adaptive_any,
    triple_any,
    x_ref, mod_ref, h_ref, c0, c1, c2, c3,
    inputs, condition, adaptive_bias, triple_bias, adaptive, triple, hold, sems,
):
    copies = fetch(
        [
            (adaptive_any.at[0], adaptive), (triple_any.at[0], triple), (inputs_any, inputs),
            (condition_any, condition), (adaptive_bias_any, adaptive_bias), (triple_bias_any, triple_bias),
        ],
        sems,
    )
    for copy in copies[2:]:
        copy.wait()
    me = scal[0]
    rows = inputs.shape[1]
    position = me * rows + lax.broadcasted_iota(jnp.int32, (rows, WIDTH), 0)
    x = jnp.where(position >= scal[3], mask_embed[...].astype(F32), inputs[0].astype(F32))
    x_ref[...] = x
    copies[0].wait()
    mod = modulation(condition[...], adaptive, adaptive_bias, 0)
    mod_ref[...] = mod
    copies[1].wait()
    qkv_stage(x, 0, mod, triple_bias, triple, cos_ref, sin_ref, me, h_ref, (c0, c1, c2, c3), hold)


def attend_kernel(
    c0, c1, c2, c3,
    o0, o1, o2, o3, lse_ref, of_ref,
    ot_ref, q_all, k_all, v_turned,
):
    rows = 256
    for place, chunk in enumerate((c0, c1, c2, c3)):
        span = slice(place * rows, (place + 1) * rows)
        q_all[place] = chunk[0:rows, 0:GROUP]
        k_all[span, :] = chunk[0:rows, GROUP : 2 * GROUP]
        tail = chunk[rows : rows + rows // 2, :]
        v_block = jnp.concatenate([tail[:, 0:GROUP], tail[:, GROUP : 2 * GROUP]], 0)
        v_block = v_block.T
        for number in range(3):
            v_turned[number, 0:HEAD_DIM, span] = v_block[number * HEAD_DIM : (number + 1) * HEAD_DIM]
    v_turned[:, HEAD_DIM:, :] = jnp.ones((3, 16, 4 * rows), BF)
    head = lax.broadcasted_iota(jnp.int32, (2 * rows, GROUP), 1) // HEAD_DIM

    for block in range(0, 4, 2):
        q = q_all[block : block + 2].reshape(2 * rows, GROUP)
        for number in range(3):
            masked = jnp.where(head == number, q, jnp.zeros_like(q))
            scores = dot_nt(k_all[...], masked)
            peak = jnp.max(scores, 0, keepdims=True)
            weights = jnp.exp(scores - peak).astype(BF)
            both = dot_nn(v_turned[number], weights)
            total = both[HEAD_DIM : HEAD_DIM + 1]
            span = slice(number * HEAD_DIM, (number + 1) * HEAD_DIM)
            found = both[0:HEAD_DIM] / total
            lse = peak + jnp.log(total)
            for part in range(2):
                columns = slice(part * rows, (part + 1) * rows)
                ot_ref[block + part, span, :] = found[:, columns]
                lse_ref[block + part, number : number + 1, :] = lse[:, columns]
    for place, out in enumerate((o0, o1, o2, o3)):
        found = ot_ref[place].T
        of_ref[place] = found
        out[...] = pack_rows(found).astype(BF)


def gather_chunks(refs, hold):
    for place in range(4):
        hold[place] = refs[place][...]


def place_rows(target, at, values, scal, group=None):
    count = 16 if group is None else 4
    rows = values.shape[0] // count
    me16 = scal[0] * 4 + scal[1]
    for chip in range(count):
        place = (chip if group is None else chip + 4 * group) ^ me16
        start = pl.multiple_of(at + place * rows, 16)
        target[pl.ds(start, rows), :] = values[chip * rows : (chip + 1) * rows]


def mlp_forward(
    layer, x_ref, mod_row, biases, scal, o_refs, output, expand, shrink, waits, hold, o_ref, aout_ref, m_ref, turned_ref,
    slope_ref, f_ref, bias_all,
):
    gather_chunks(o_refs, hold)
    me = scal[0]
    rows = x_ref.shape[0]
    half = rows // 2
    for group in range(4):
        chunk = hold[group ^ me]
        columns = slice(group * GROUP, (group + 1) * GROUP)
        o_ref[0:half, columns] = chunk[:, 0:GROUP]
        o_ref[half:rows, columns] = chunk[:, GROUP : 2 * GROUP]
    o = o_ref[...]
    hidden = expand.shape[1]
    place_rows(turned_ref, hidden + WIDTH, o.T, scal)
    waits[0].wait()
    a_out = dot_nn(o, output[...]) + row_of(biases[0], layer)
    aout_ref[...] = a_out.astype(BF)
    waits[3].wait()
    m = x_ref[...] + piece_of(mod_row, 2) * a_out
    m_ref[...] = m
    unit, _ = normalise(m)
    h2 = (unit * (1.0 + piece_of(mod_row, 4)) + piece_of(mod_row, 3)).astype(BF)
    place_rows(turned_ref, hidden, h2.T, scal)
    waits[1].wait()
    waits[2].wait()
    width = 768
    bias_all[...] = row_of(biases[1], layer)

    def hidden_block(number, f):
        start = pl.multiple_of(number * width, width)
        columns = pl.ds(start, width)
        u = dot_nn(h2, expand[:, columns]) + bias_all[:, columns]
        square = u * u
        gate = 0.5 + 0.5 * jnp.tanh(u * (ROOT_TWO_PI + ROOT_TWO_PI * CUBIC * square))
        active = u * gate
        slope = gate + 2.0 * active * (1.0 - gate) * (ROOT_TWO_PI + 3.0 * ROOT_TWO_PI * CUBIC * square)
        z = active.astype(BF)
        place_rows(turned_ref, 0, z.T, scal, number)
        slope_ref[:, columns] = slope.astype(BF)
        return f + dot_nn(z, shrink[columns, :])

    f = lax.fori_loop(0, hidden // width, hidden_block, jnp.zeros(x_ref.shape, F32), unroll=4 if layer else 1) + row_of(biases[2], layer)
    f_ref[...] = f.astype(BF)
    return m + piece_of(mod_row, 5) * f


def share(values, hold, at):
    half = values.shape[1] // 2
    hold[0, :, at : at + half] = values[:, 0:half]
    hold[1, :, at : at + half] = values[:, half : 2 * half]


def mlp_backward(
    dy, mod_row, me, core, m_ref, f_ref, slope_ref, aout_ref, output, expand, shrink, waits, halves,
    do_ref, dm_ref, vec_ref,
):
    def put(place, row):
        vec_ref[:, place : place + row.shape[1]] = row

    put(0, column_sum(dy * f_ref[...].astype(F32)))
    df = (dy * piece_of(mod_row, 5)).astype(BF)
    put(3072, column_sum(df.astype(F32)))
    hidden = expand.shape[1]
    share(df, halves, hidden // 2)
    dh2 = jnp.zeros(dy.shape, F32)
    waits[2].wait()
    for start in range(0, hidden, 768):
        columns = slice(start, start + 768)
        dz = dot_nt(df, shrink[columns, :])
        du = (slope_ref[:, columns].astype(F32) * dz).astype(BF)
        put(3840 + start, column_sum(du.astype(F32)))
        half = hidden // 2
        halves[start // half, :, start % half : start % half + 768] = du
        if start == 0:
            waits[1].wait()
        dh2 = dh2 + dot_nt(du, expand[:, columns])
    unit, rstd = normalise(m_ref[...])
    put(768, column_sum(dh2))
    put(1536, column_sum(dh2 * unit))
    dm = dy + normalise_back(dh2 * (1.0 + piece_of(mod_row, 4)), unit, rstd)
    dm_ref[...] = dm
    put(2304, column_sum(dm * aout_ref[...].astype(F32)))
    da = (dm * piece_of(mod_row, 2)).astype(BF)
    put(6912, column_sum(da.astype(F32)))
    share(da, halves, hidden // 2 + WIDTH // 2)
    waits[0].wait()
    do = dot_nt(da, output[...])
    for group in range(4):
        do_ref[group] = pack_rows(do[:, group * GROUP : (group + 1) * GROUP]).astype(BF)


def attend_back_kernel(
    scal, given_ref, c0, c1, c2, c3, lse_ref, of_ref, cos_any, sin_any, stacked,
    cos_ref, sin_ref, sems, q_masked, do_masked, k_all, v_all, k_turned, lse_rows, delta_rows, dq_turned, dk_all, dv_all,
):
    copies = fetch([(cos_any, cos_ref), (sin_any, sin_ref)], sems)
    rows = 256
    head = lax.broadcasted_iota(jnp.int32, (rows, GROUP), 1) // HEAD_DIM
    of_head = lax.broadcasted_iota(jnp.int32, (8, GROUP), 1) // HEAD_DIM
    pick = jnp.where(of_head == lax.broadcasted_iota(jnp.int32, (8, GROUP), 0), 1.0, 0.0).astype(BF)
    for place in range(4):
        chunk = (c0, c1, c2, c3)[place]
        given = given_ref[place ^ scal[0]]
        span = slice(place * rows, (place + 1) * rows)
        q = chunk[0:rows, 0:GROUP]
        k = chunk[0:rows, GROUP : 2 * GROUP]
        tail = chunk[rows : rows + rows // 2, :]
        v_all[place] = jnp.concatenate([tail[:, 0:GROUP], tail[:, GROUP : 2 * GROUP]], 0)
        k_all[place] = k
        k_turned[place] = k.T
        do = jnp.concatenate([given[:, 0:GROUP], given[:, GROUP : 2 * GROUP]], 0)
        product = do.astype(F32) * of_ref[place]
        upper = product.astype(BF)
        lower = (product - upper.astype(F32)).astype(BF)
        delta_rows[:, span] = dot_nt(pick, upper) + dot_nt(pick, lower)
        for number in range(3):
            q_masked[number, span, :] = jnp.where(head == number, q, jnp.zeros_like(q))
            do_masked[number, span, :] = jnp.where(head == number, do, jnp.zeros_like(do))
            lse_rows[number : number + 1, span] = lse_ref[place, number : number + 1, :]
    dq_turned[...] = jnp.zeros(dq_turned.shape, F32)

    for block in range(4 // 2):
        k = k_all[block * 2 : (block + 1) * 2].reshape(2 * rows, GROUP)
        v = v_all[block * 2 : (block + 1) * 2].reshape(2 * rows, GROUP)
        dk = jnp.zeros((2 * rows, GROUP), F32)
        dv = jnp.zeros((2 * rows, GROUP), F32)
        for number in range(3):
            span = slice(number * HEAD_DIM, (number + 1) * HEAD_DIM)
            scores = dot_nt(k, q_masked[number])
            probs = jnp.exp(scores - lse_rows[number : number + 1, :])
            prob_grad = dot_nt(v, do_masked[number])
            score_grad = (probs * (prob_grad - delta_rows[number : number + 1, :])).astype(BF)
            dv = dv + dot_nn(probs.astype(BF), do_masked[number])
            dk = dk + dot_nn(score_grad, q_masked[number])
            for part in range(2):
                dq_turned[span, :] += dot_nn(k_turned[block * 2 + part, span, :], score_grad[part * rows : (part + 1) * rows])
        dk_all[block * 2 : (block + 1) * 2] = dk.reshape(2, rows, GROUP)
        dv_all[block * 2 : (block + 1) * 2] = dv.reshape(2, rows, GROUP)
    for copy in copies:
        copy.wait()
    for place in range(4):
        span = slice(place * rows, (place + 1) * rows)
        dq = dq_turned[:, span].T * HEAD_DIM**-0.5
        pair = jnp.concatenate([dq, dk_all[place]], 1)
        pair = turn(pair, cos_ref[place], -sin_ref[place]).astype(BF)
        tail = pack_rows(dv_all[place]).astype(BF)
        stacked[place ^ scal[0], 0:rows, :] = pair
        stacked[place ^ scal[0], rows : rows + rows // 2, :] = tail


def qkv_backward(x_ref, dm_ref, mod_row, chunks, triple, waits, full, vec_ref):
    rows = full.shape[0]
    half = rows // 2
    for group in range(4):
        chunk = chunks(group)
        low = group * GROUP
        full[:, low : low + GROUP] = chunk[0:rows, 0:GROUP]
        full[:, WIDTH + low : WIDTH + low + GROUP] = chunk[0:rows, GROUP : 2 * GROUP]
        full[0:half, 2 * WIDTH + low : 2 * WIDTH + low + GROUP] = chunk[rows : rows + half, 0:GROUP]
        full[half:rows, 2 * WIDTH + low : 2 * WIDTH + low + GROUP] = chunk[rows : rows + half, GROUP : 2 * GROUP]
    dqkv = full[...]
    vec_ref[:, 1536:3840] = column_sum(dqkv.astype(F32))
    waits[0].wait()
    dh = dot_nt(dqkv, triple[...])
    wait_all(waits[1:3])
    unit, rstd = normalise(x_ref[...])
    vec_ref[:, 0:768] = column_sum(dh)
    vec_ref[:, 768:1536] = column_sum(dh * unit)
    return dm_ref[...] + normalise_back(dh * (1.0 + piece_of(mod_row, 1)), unit, rstd)


def middle_kernel(
    scal, mod_ref, condition, adaptive_bias, output_bias, expand_bias, shrink_bias, triple_bias,
    cos_ref, sin_ref, o0, o1, o2, o3, x_any, output_any, expand_any, shrink_any, triple_any, adaptive_any,
    aout_ref, m_ref, turned_ref, slope_ref, f_ref, y_ref, mod_next, h_ref, c0, c1, c2, c3,
    x_ref, output, expand, shrink, triple, adaptive, bias_all, o_hold, o_ref, c_hold, sems,
):
    copies = fetch(
        [
            (output_any.at[0], output), (x_any, x_ref), (expand_any.at[0], expand), (shrink_any.at[0], shrink),
            (triple_any.at[1], triple), (adaptive_any.at[1], adaptive),
        ],
        sems,
    )
    me = scal[0]
    y = mlp_forward(
        0, x_ref, mod_ref[...], (output_bias, expand_bias, shrink_bias), scal, (o0, o1, o2, o3), output, expand, shrink,
        [copies[0], copies[2], copies[3], copies[1]], o_hold, o_ref,
        aout_ref, m_ref, turned_ref, slope_ref, f_ref, bias_all,
    )
    y_ref[...] = y
    wait_all(copies[4:])
    mod = modulation(condition[...], adaptive, adaptive_bias, 1)
    mod_next[...] = mod
    qkv_stage(
        y, 1, mod, triple_bias, triple, cos_ref, sin_ref, me, h_ref, (c0, c1, c2, c3), c_hold,
    )


def ahead_kernel(
    scal, mod_ref, output_bias, expand_bias, shrink_bias, o0, o1, o2, o3, x_any, output_any, expand_any, shrink_any,
    out_ref, aout_ref, m_ref, turned_ref, slope_ref, f_ref,
    x_ref, output, expand, shrink, bias_all, o_hold, o_ref, sems,
):
    copies = fetch(
        [(output_any.at[1], output), (x_any, x_ref), (expand_any.at[1], expand), (shrink_any.at[1], shrink)], sems
    )
    y = mlp_forward(
        1, x_ref, mod_ref[...], (output_bias, expand_bias, shrink_bias), scal, (o0, o1, o2, o3), output, expand, shrink,
        [copies[0], copies[2], copies[3], copies[1]], o_hold, o_ref,
        aout_ref, m_ref, turned_ref, slope_ref, f_ref, bias_all,
    )
    out_ref[0] = y.astype(BF)


def turn_kernel(
    scal, mod_ref, m_ref, f_ref, slope_ref, aout_ref, cotangent_any, output_any, expand_any, shrink_any,
    mine, theirs, do_ref, dm_ref, vec_ref,
    output, expand, shrink, cotangent, halves, sems,
):
    copies = fetch(
        [
            (shrink_any.at[1], shrink), (expand_any.at[1], expand), (output_any.at[1], output),
            (cotangent_any, cotangent),
        ],
        sems,
    )
    copies[3].wait()
    me, core = scal[0], scal[2]
    mlp_backward(
        cotangent[0].astype(F32), mod_ref[...], me, core, m_ref, f_ref, slope_ref, aout_ref, output, expand, shrink,
        [copies[2], copies[1], copies[0]], halves, do_ref, dm_ref, vec_ref,
    )
    mine[...] = halves[core]
    theirs[...] = halves[1 - core]


def back_kernel(
    scal, mod_ref, mod_low, grads, x_any, dm_any, m_any, f_any, slope_any, aout_any,
    triple_any, output_any, expand_any, shrink_any,
    mine, theirs, vec_first, do_ref, dm_ref, vec_ref,
    triple, output, expand, shrink, full, halves, x_ref, dm_in, m_ref, f_ref, slope_ref, aout_ref, sems,
):
    copies = fetch(
        [
            (triple_any.at[1], triple), (x_any, x_ref), (dm_any, dm_in), (f_any, f_ref), (slope_any, slope_ref),
            (m_any, m_ref), (aout_any, aout_ref), (shrink_any.at[0], shrink), (expand_any.at[0], expand),
            (output_any.at[0], output),
        ],
        sems,
    )
    me, core = scal[0], scal[2]
    dy = qkv_backward(
        x_ref, dm_in, mod_ref[...], lambda group: grads[group], triple, copies[0:3], full, vec_first,
    )
    wait_all(copies[3:7])
    mlp_backward(
        dy, mod_low[...], me, core, m_ref, f_ref, slope_ref, aout_ref, output, expand, shrink,
        [copies[9], copies[8], copies[7]], halves, do_ref, dm_ref, vec_ref,
    )
    mine[...] = halves[core]
    theirs[...] = halves[1 - core]


def last_kernel(
    scal, mod_ref, grads, vec0, first1, vec1, x_any, dm_any, triple_any,
    input_grad, small,
    triple, full, x_ref, dm_in, vec_first, mask_ref, sems,
):
    copies = fetch([(triple_any.at[0], triple), (x_any, x_ref), (dm_any, dm_in)], sems)
    me = scal[0]
    dx = qkv_backward(
        x_ref, dm_in, mod_ref[...], lambda group: grads[group], triple, copies, full, vec_first,
    )
    rows = dx.shape[0]
    position = me * rows + lax.broadcasted_iota(jnp.int32, dx.shape, 0)
    masked = position >= scal[3]
    input_grad[0] = jnp.where(masked, 0.0, dx)
    mask_ref[...] = column_sum(jnp.where(masked, dx, 0.0))
    pack(vec_first, vec0, first1, vec1, mask_ref, small)


def triple_kernel(
    scal, h0, h1, h2, h3, chunks,
    mine, theirs,
    result,
):
    rows = chunks.shape[1] * 2 // 3
    half = rows // 2
    each = WIDTH // 8
    for side in range(2):
        qk = jnp.zeros((WIDTH // 2, 2 * GROUP), F32)
        v = jnp.zeros((WIDTH // 2, GROUP), F32)
        for place, h_ref in enumerate((h0, h1, h2, h3)):
            h = h_ref[side]
            at = place ^ scal[0]
            qk = qk + dot_nn(h, chunks[at, 0:rows, :])
            tail = chunks[at, rows : rows + half, :]
            v = v + dot_nn(h, jnp.concatenate([tail[:, 0:GROUP], tail[:, GROUP : 2 * GROUP]], 0))
        for z in range(4):
            span = slice(z * each, (z + 1) * each)
            block = jnp.concatenate([qk[span], pack_rows(v[span])], 0).astype(BF)
            tall = block.shape[0]
            for number in range(3):
                lanes = slice(number * 128, (number + 1) * 128)
                result[side * 4 + z, number * tall : (number + 1) * tall, :] = block[:, lanes]
    for place, offset in enumerate((0, 2, 1, 3)):
        at = scal[1] ^ offset
        tall = result.shape[1]
        mine[place * tall : (place + 1) * tall, :] = result[scal[2] * 4 + at]
        theirs[place * tall : (place + 1) * tall, :] = result[(1 - scal[2]) * 4 + at]


def bring_starts(layout, pieces, hold, sems):
    return fetch(
        [
            (pieces[piece].at[source : source + rows, :], hold.at[slot, target : target + rows, :])
            for piece, source, slot, target, rows in layout
        ],
        sems,
    )


def bring(layout, pieces, hold, sems):
    wait_all(bring_starts(layout, pieces, hold, sems))


def triple_settle_kernel(layout, scal, *refs):
    pieces, outs, (hold, blocks, sems) = refs[:-7], refs[-7:-3], refs[-3:]
    bring(layout, pieces, hold, sems)
    each, rows = WIDTH // 8, WIDTH // 32
    tall = each * 3 // 2
    for layer in range(LAYERS):
        lanes = []
        for number in range(3):
            at = (layer * 3 + number) * tall
            lanes.append(sum(hold[slot, at : at + tall, :].astype(F32) for slot in range(hold.shape[0])))
        total = jnp.concatenate(lanes, 1)
        v = jnp.concatenate([total[each:, 0:GROUP], total[each:, GROUP : 2 * GROUP]], 0)
        for b in range(4):
            span = slice(b * rows, (b + 1) * rows)
            blocks[layer, b, :, 0 : 2 * GROUP] = total[span]
            blocks[layer, b, :, 2 * GROUP : 3 * GROUP] = v[span]
    for place, out in enumerate(outs):
        for layer in range(LAYERS):
            out[layer] = blocks[layer, place ^ scal[0]]


BIT = {"x": 4, "y": 8, "a": 1, "b": 2}
STEP = {"x": ("blk", 1), "y": ("blk", 2), "a": ("dp", 2), "b": ("dp", 4)}


def place_at(order, index):
    place = 0
    for depth, name in enumerate(order):
        if index & (8 >> depth):
            place |= BIT[name]
    return place


def weights_kernel(products, orders, scal, own_any, far_any, mine_any, got_any, *rest):
    count = len(orders)
    sends, keeps = rest[0:count], rest[count : 2 * count]
    turned, grads, sems = rest[2 * count :]
    pairs = [(mine_any, grads.at[0:256, :]), (got_any, grads.at[256:512, :])]
    for low, high, _, _ in products:
        pairs += [(own_any.at[low:high, :], turned.at[low:high, 0:256]), (far_any.at[low:high, :], turned.at[low:high, 256:512])]
    copies = fetch(pairs, sems)
    wait_all(copies[0:2])
    row_at = [0] * count
    for step, (low, high, at, dealt) in enumerate(products):
        wait_all(copies[2 + 2 * step : 4 + 2 * step])
        rows = (high - low) // 16
        width = sum(dealt) * 128
        result = dot_nn(turned[low:high, :], grads[:, at : at + width]).astype(BF)
        column = 0
        for part, order in enumerate(orders):
            blocks = dealt[part]
            for index in range(16):
                target = keeps[part] if index < 8 else sends[part]
                place = place_at(order, index)
                for number in range(blocks):
                    spot = row_at[part] + number * rows
                    target[index % 8, spot : spot + rows, :] = result[
                        place * rows : (place + 1) * rows, (column + number) * 128 : (column + number + 1) * 128
                    ]
            row_at[part] += blocks * rows
            column += blocks


def settle_kernel(layout, blocks, scal, *refs):
    pieces, (mine, theirs, hold, sems) = refs[:-4], refs[-4:]
    bring(layout, pieces, hold, sems)
    core = scal[2]
    row = at = 0
    for rows in blocks:
        half = rows // 2
        total = hold[0, row : row + rows, :].astype(F32)
        for slot in range(1, hold.shape[0]):
            total = total + hold[slot, row : row + rows, :].astype(F32)
        low, high = total[0:half], total[half:rows]
        mine[at : at + half, :] = jnp.where(core == 0, low, high)
        theirs[at : at + half, :] = jnp.where(core == 0, high, low)
        row += rows
        at += half


def add_kernel(layout, rows, *refs):
    outs, (hold, sems) = refs[-2 - len(rows) : -2], refs[-2:]
    copies = bring_starts(layout, refs[: -2 - len(rows)], hold, sems)
    depth = {}
    for number, (_, _, slot, target, count) in enumerate(layout):
        depth.setdefault(target, []).append((slot, count, number))
    at = 0
    for out, size in zip(outs, rows):
        for target in sorted(depth):
            if at <= target < at + size:
                for _, _, number in depth[target]:
                    copies[number].wait()
                count = depth[target][0][1]
                total = sum(hold[slot, target : target + count, :].astype(F32) for slot, _, _ in depth[target])
                out[target - at : target - at + count, :] = total.astype(BF)
        at += size


def plain_add_kernel(left, right, out):
    out[...] = left[...] + right[...]


DMOD = 12 * WIDTH
SMALL = 2 * 6912 + WIDTH
SMALL_AT = {"triple": (0, 2304), "output": (2304, 3072), "expand": (3072, 6144), "shrink": (6144, 6912)}


def pack(first0, vec0, first1, vec1, mask, out):
    for layer, (first, vec) in enumerate(((first0, vec0), (first1, vec1))):
        at = layer * 6 * WIDTH
        out[:, at : at + 1536] = first[:, 0:1536]
        out[:, at + 1536 : at + 2304] = vec[:, 2304:3072]
        out[:, at + 2304 : at + 3840] = vec[:, 768:2304]
        out[:, at + 3840 : at + 4608] = vec[:, 0:768]
        at = DMOD + layer * 6912
        out[:, at : at + 2304] = first[:, 1536:3840]
        out[:, at + 2304 : at + 3072] = vec[:, 6912:7680]
        out[:, at + 3072 : at + 6144] = vec[:, 3840:6912]
        out[:, at + 6144 : at + 6912] = vec[:, 3072:3840]
    out[:, DMOD + 2 * 6912 :] = mask[...]


def join_kernel(own, got, condition, out):
    total = own[...] + got[...]
    out[:, 0:DMOD] = total[:, 0:DMOD]
    out[:, DMOD : DMOD + 128] = condition[...]
    out[:, DMOD + 128 :] = total[:, DMOD:]


def spread_kernel(own, got, out):
    rows = own.shape[1] - SMALL
    out[:, 0:rows] = own[:, 0:rows]
    out[:, rows : 2 * rows] = got[:, 0:rows]
    out[:, 2 * rows :] = own[:, rows:] + got[:, rows:]


def small_kernel(
    scal, own, got, adaptive_any, adaptive_w, adaptive_b, triple_b, output_b, expand_b, shrink_b, mask_sum,
    condition_grad, adaptive, sems,
):
    (copy,) = fetch([(adaptive_any, adaptive)], sems)
    index = scal[4]
    each = DMOD + 128
    rows = own.shape[1] - SMALL
    share = adaptive_w.shape[1]
    number = lax.broadcasted_iota(jnp.int32, (8, 128), 0)
    lane = lax.broadcasted_iota(jnp.int32, (8, 128), 1)
    pick = (lane == index * share + number) & (number < share)
    totals = [jnp.zeros((8, 6 * WIDTH), F32), jnp.zeros((8, 6 * WIDTH), F32)]
    sums = [jnp.zeros((1, 6 * WIDTH), F32), jnp.zeros((1, 6 * WIDTH), F32)]
    for source in (own, got):
        for at in range(0, rows, each):
            column = jnp.sum(jnp.where(pick, source[:, at + DMOD : at + each], 0.0), 1, keepdims=True)
            for layer in range(LAYERS):
                low = at + layer * 6 * WIDTH
                row = source[:, low : low + 6 * WIDTH]
                totals[layer] = totals[layer] + column * row
                sums[layer] = sums[layer] + row
    summed = own[:, rows:] + got[:, rows:]

    def cut(row):
        size = row.shape[1] // 32
        return pltpu.roll(row, lax.rem(row.shape[1] - index * size, row.shape[1]), 1)[:, 0:size]

    for layer in range(LAYERS):
        adaptive_w[layer] = totals[layer][0:share]
        adaptive_b[layer : layer + 1, :] = cut(sums[layer])
        for out, (low, high) in zip((triple_b, output_b, expand_b, shrink_b), SMALL_AT.values()):
            at = layer * 6912
            out[layer : layer + 1, :] = cut(summed[:, at + low : at + high])
    mask_sum[...] = cut(summed[:, 2 * 6912 :])
    copy.wait()
    grad = jnp.zeros((8, 128), F32)
    for layer in range(LAYERS):
        at = layer * 6 * WIDTH
        grad = grad + dot_nt(three_rows(own[:, at : at + 6 * WIDTH]), adaptive[layer])
    condition_grad[...] = column_sum(grad)


def finish_kernel(plans, scal, *refs):
    pairs = 2 * len(plans)
    groups = refs[pairs : pairs + 4]
    outs, hold = refs[pairs + 4 : -1], refs[-1]
    core = scal[2]
    for bucket, plan in enumerate(plans):
        mine, got = refs[2 * bucket : 2 * bucket + 2]
        at = 0
        for out, layer, block, rows in plan:
            own, other = mine[at : at + rows, :], got[at : at + rows, :]
            half = outs[out].shape[2] // 2
            low = block * 128
            outs[out][layer, :, low : low + 128] = jnp.where(core == 0, own, other)
            outs[out][layer, :, half + low : half + low + 128] = jnp.where(core == 0, other, own)
            at += rows
    for layer in range(LAYERS):
        for place in range(4):
            hold[place] = groups[place][layer]
        for group in range(4):
            block = hold[group ^ scal[0]]
            for number in range(3):
                low = number * WIDTH + group * GROUP
                outs[0][layer, :, low : low + GROUP] = block[:, number * GROUP : (number + 1) * GROUP]


def shaped(*shape, dtype=F32):
    return jax.ShapeDtypeStruct(shape, dtype)


class Outs(list):
    token = None


def call(kernel, specs, outs, scratch, micros, name, limit, after=(), away=()):
    count, extra = len(specs), len(after)
    staging = [pltpu.VMEM(outs[number].shape, outs[number].dtype) for number in away]
    if away:
        staging.append(pltpu.SemaphoreType.DMA((len(away),)))

    def body(*refs):
        mark = refs[count + extra + len(outs)]
        mark[...] = jnp.zeros(mark.shape, F32)
        results = list(refs[count + extra : count + extra + len(outs)])
        rest = refs[count + extra + len(outs) + 1 :]
        staged, rest = rest[: len(staging)], rest[len(staging) :]
        targets = [results[number] for number in away]
        for number, stage in zip(away, staged):
            results[number] = stage
        kernel(*refs[:count], *results, *rest)
        if away:
            wait_all(fetch(list(zip(staged, targets)), staged[-1]))

    made = pl.pallas_call(
        body,
        in_specs=specs + [ANY] * extra,
        out_specs=[HBM if number in away else VM for number in range(len(outs))] + [VM],
        out_shape=[
            pltpu.HBM(shape=out.shape, dtype=out.dtype) if number in away else out for number, out in enumerate(outs)
        ]
        + [shaped(8, 128)],
        scratch_shapes=staging + scratch,
        compiler_params=pltpu.CompilerParams(vmem_limit_bytes=limit * MEBI),
        cost_estimate=pl.CostEstimate(flops=int(micros * 1e9), bytes_accessed=int(micros * 1e6), transcendentals=0),
        name=name,
    )

    def run(*operands):
        operands = [
            pltpu.with_memory_space_constraint(operand, pltpu.HBM) if spec is HBM or spec is HV else operand
            for operand, spec in zip(operands, specs)
        ]
        marks = [
            mark if mark.size * mark.dtype.itemsize < 200000 else pltpu.with_memory_space_constraint(mark, pltpu.HBM)
            for mark in after
        ]
        results = made(*operands, *marks)
        found = Outs(results[:-1])
        found.token = results[-1]
        return found

    return run


def swap(values, axis, bit):
    size = 4 if axis == "blk" else 8
    return lax.ppermute(values, axis, [(i, i ^ bit) for i in range(size)])


def swap_chunks(chunks):
    return [chunks[0]] + [swap(chunks[place], "blk", place) for place in (1, 2, 3)]


def shaped_like(values):
    return shaped(*values.shape, dtype=values.dtype)


class Part:
    def __init__(self, keep, got, rows, order):
        self.views = [(keep, 0), (got, 0)]
        self.rows = rows
        self.order = order

    def halve(self):
        self.rows //= 2


def exchange(parts, cost, after=()):
    groups = {}
    for part in parts:
        groups.setdefault(part.order[0], []).append(part)
        part.order = part.order[1:]
    groups = list(groups.items())
    ordered, rows = [], []
    for _, group in groups:
        for part in group:
            part.halve()
        ordered += group
        rows.append(sum(part.rows for part in group))
    arrays, layout, total = collect(ordered, True)
    slots = max(slot for _, _, slot, _, _ in layout) + 1
    outs = call(
        functools.partial(add_kernel, layout, rows),
        [HBM] * len(arrays),
        [shaped(count, 128, dtype=BF) for count in rows],
        [pltpu.VMEM((slots, total, 128), BF), pltpu.SemaphoreType.DMA((len(layout),))],
        cost,
        "add",
        16,
        after,
    )(*arrays)
    for (axis, group), out in zip(groups, outs):
        got = swap(out, *STEP[axis])
        at = 0
        for part in group:
            part.views.append((got, at))
            at += part.rows
    return [outs.token]


def weight_parts(scal, own, far, mine, got, products, orders, after=()):
    count = len(orders)
    shapes, rows = [], []
    for part in range(count):
        rows.append(sum(dealt[part] * (high - low) // 16 for low, high, _, dealt in products))
        shapes.append(shaped(8, rows[-1], 128, dtype=BF))
    outs = call(
        functools.partial(weights_kernel, products, orders),
        [SM] + [HBM] * 3 + [ANY],
        shapes * 2,
        [
            pltpu.VMEM((own.shape[0], 512), BF),
            pltpu.VMEM((512, mine.shape[1]), BF),
            pltpu.SemaphoreType.DMA((2 + 2 * len(products),)),
        ],
        300,
        "mlp_weights",
        32,
        after,
        tuple(range(count, 2 * count)),
    )(scal, own, far, mine, got)
    flat = [out.reshape(-1, 128) for out in outs]
    parts = [
        Part(flat[count + number], swap(flat[number], *STEP[order[0]]), 8 * rows[number], order[1:])
        for number, order in enumerate(orders)
    ]
    return parts, [outs.token]


def triple_part(scal, h_rows, stacked, after=()):
    rows = WIDTH // 8 * 3 // 2 * 3
    outs = call(
        triple_kernel,
        [SM] + [HV] * 5,
        [shaped(4 * rows, 128, dtype=BF)] * 2,
        [pltpu.VMEM((8, rows, 128), BF)],
        300,
        "triple_weights",
        20,
        after,
    )(scal, *h_rows, stacked)
    return Part(outs[0], swap(outs[1], "dp", 1), 4 * rows, "ab"), [outs.token]


def collect(parts, upper=False):
    arrays, layout, at = [], [], 0
    for part in parts:
        for slot, (array, first) in enumerate(part.views):
            first = first + part.rows if upper else first
            known = [number for number, other in enumerate(arrays) if other is array]
            if not known:
                arrays.append(array)
                known = [len(arrays) - 1]
            layout.append((known[0], first, slot, at, part.rows))
        at += part.rows
    return arrays, layout, at


def blocks_of(products):
    blocks = []
    for part in range(len(products[0][3])):
        for low, high, _, dealt in products:
            blocks += [(high - low) // 16] * dealt[part]
    return blocks


def settle(parts, scal, products, cost, after=()):
    arrays, layout, rows = collect(parts)
    slots = max(slot for _, _, slot, _, _ in layout) + 1
    outs = call(
        functools.partial(settle_kernel, layout, blocks_of(products)),
        [SM] + [HBM] * len(arrays),
        [shaped(rows // 2, 128)] * 2,
        [pltpu.VMEM((slots, rows, 128), BF), pltpu.SemaphoreType.DMA((len(layout),))],
        cost,
        "settle",
        10,
        after,
    )(scal, *arrays)
    return *outs, outs.token


def triple_settle(parts, scal, after=()):
    arrays, layout, rows = collect(parts)
    slots = max(slot for _, _, slot, _, _ in layout) + 1
    blocks = call(
        functools.partial(triple_settle_kernel, layout),
        [SM] + [HBM] * len(arrays),
        [shaped(LAYERS, WIDTH // 32, 3 * GROUP)] * 4,
        [
            pltpu.VMEM((slots, rows, 128), BF),
            pltpu.VMEM((LAYERS, 4, WIDTH // 32, 3 * GROUP), F32),
            pltpu.SemaphoreType.DMA((len(layout),)),
        ],
        0.1,
        "triple_settle",
        8,
        after,
    )(scal, *arrays)
    return swap_chunks(blocks), [blocks.token]


def plan_of(products, names):
    plan = []
    for part in range(len(products[0][3])):
        for (low, high, _, dealt), (out, layer) in zip(products, names):
            first = sum(dealt[:part])
            plan += [(out, layer, first + number, (high - low) // 32) for number in range(dealt[part])]
    return plan


def rotary_tables(start, rows):
    position = (start[:, None] + jnp.arange(rows, dtype=jnp.int32)[None, :]).astype(F32)
    lane = jnp.arange(128, dtype=jnp.int32)
    frequency = jnp.exp((lane % 32).astype(F32) * (-2.0 * math.log(10000.0) / HEAD_DIM))
    angles = position[:, :, None] * frequency
    return jnp.cos(angles), jnp.sin(angles) * jnp.where(lane % 64 < 32, -1.0, 1.0)


def local_fast(
    inputs, condition, prefix, mask_embed, adaptive_weight, adaptive_bias, triple_weight, triple_bias, output_weight,
    output_bias, expand_weight, expand_bias, shrink_weight, shrink_bias, cotangent,
):
    rows = inputs.shape[1]
    hidden = expand_weight.shape[2]
    blk, dp = lax.axis_index("blk"), lax.axis_index("dp")
    scal = jnp.stack([blk, dp // 2, dp % 2, prefix[0], blk * 8 + dp]).astype(jnp.int32)
    starts = (blk ^ jnp.arange(4, dtype=jnp.int32)) * rows
    cosine, sine = rotary_tables(starts[:1], rows)
    cosines, sines = rotary_tables(starts, rows)

    f_square = shaped(rows, WIDTH)
    x_hold = pltpu.VMEM((rows, WIDTH), F32)
    b_square = shaped(rows, WIDTH, dtype=BF)
    b_tall = shaped(rows, hidden, dtype=BF)
    packed = rows + rows // 2
    chunk = shaped(packed, 2 * GROUP, dtype=BF)
    o_chunk = shaped(rows // 2, 2 * GROUP, dtype=BF)
    c_hold = pltpu.VMEM((4, packed, 2 * GROUP), BF)
    o_hold = pltpu.VMEM((4, rows // 2, 2 * GROUP), BF)
    adaptive_hold = pltpu.VMEM((condition.shape[1], 6 * WIDTH), BF)
    triple_hold = pltpu.VMEM((WIDTH, 3 * WIDTH), BF)
    output_hold = pltpu.VMEM((WIDTH, WIDTH), BF)
    expand_hold = pltpu.VMEM((WIDTH, hidden), BF)
    shrink_hold = pltpu.VMEM((hidden, WIDTH), BF)
    h_both = shaped(2, WIDTH // 2, rows, dtype=BF)
    half_width = hidden // 2 + WIDTH
    tall = hidden + 2 * WIDTH
    mod_row = shaped(1, 6 * WIDTH)

    x0, mod0, h_rows, *chunks = call(
        first_kernel,
        [SM] + [VM] * 3 + [HBM] * 6,
        [f_square, mod_row, h_both] + [chunk] * 4,
        [
            pltpu.VMEM(inputs.shape, BF), pltpu.VMEM(condition.shape, F32), pltpu.VMEM(adaptive_bias.shape, BF),
            pltpu.VMEM(triple_bias.shape, BF), adaptive_hold, triple_hold, c_hold, pltpu.SemaphoreType.DMA((6,)),
        ],
        300,
        "qkv_first",
        24,
    )(
        scal, mask_embed[None], cosine, sine, inputs, condition, adaptive_bias, triple_bias, adaptive_weight,
        triple_weight,
    )

    def attend(chunks, after):
        return call(
            attend_kernel,
            [VM] * 4,
            [o_chunk] * 4 + [shaped(4, 8, rows), shaped(4, rows, GROUP)],
            [
                pltpu.VMEM((4, GROUP, rows), F32),
                pltpu.VMEM((4, rows, GROUP), BF),
                pltpu.VMEM((4 * rows, GROUP), BF),
                pltpu.VMEM((3, HEAD_DIM + 16, 4 * rows), BF),
            ],
            300,
            "attend",
            20,
            after,
        )(*chunks)

    def attend_back(chunks, given, lse, turned, after):
        stack = shaped(4, packed, 2 * GROUP, dtype=BF)
        return call(
            attend_back_kernel,
            [SM, VM] + [HV] * 6 + [HBM] * 2,
            [stack],
            [
                pltpu.VMEM((4, rows, 128), F32),
                pltpu.VMEM((4, rows, 128), F32),
                pltpu.SemaphoreType.DMA((2,)),
                pltpu.VMEM((3, 4 * rows, GROUP), BF),
                pltpu.VMEM((3, 4 * rows, GROUP), BF),
                pltpu.VMEM((4, rows, GROUP), BF),
                pltpu.VMEM((4, rows, GROUP), BF),
                pltpu.VMEM((4, GROUP, rows), BF),
                pltpu.VMEM((8, 4 * rows), F32),
                pltpu.VMEM((8, 4 * rows), F32),
                pltpu.VMEM((GROUP, 4 * rows), F32),
                pltpu.VMEM((4, rows, GROUP), F32),
                pltpu.VMEM((4, rows, GROUP), F32),
            ],
            300,
            "attend_back",
            26,
            after,
            (0,),
        )(scal, given, *chunks, lse, turned, cosines, sines)

    def far(values):
        return swap(values, "dp", 1)

    def gather_rows(both, first, second):
        near = [swap(both, "blk", bit) for bit in (1, 2)]
        return [both, *near, swap(near[first - 1], "blk", second)]

    chunks0 = swap_chunks(chunks)
    h_rows0 = gather_rows(h_rows, 2, 1)
    *o_chunks, lse0, ot0 = attend(chunks0, ())
    o_chunks = swap_chunks(o_chunks)
    aout0, m0, turned0, slope0, f0, x1, mod1, h_rows, *chunks = call(
        middle_kernel,
        [SM] + [VM] * 13 + [HBM] * 6,
        [b_square, f_square, shaped(tall, rows, dtype=BF), b_tall, b_square, f_square, mod_row, h_both] + [chunk] * 4,
        [x_hold, output_hold, expand_hold, shrink_hold, triple_hold, adaptive_hold, pltpu.VMEM((1, hidden), F32), o_hold, pltpu.VMEM((rows, WIDTH), BF)]
        + [c_hold, pltpu.SemaphoreType.DMA((6,))],
        300,
        "mlp_qkv",
        34,
    )(
        scal, mod0, condition, adaptive_bias, output_bias, expand_bias, shrink_bias, triple_bias, cosine, sine,
        *o_chunks, x0, output_weight, expand_weight, shrink_weight, triple_weight, adaptive_weight,
    )
    turned0_far = far(turned0)
    chunks1 = swap_chunks(chunks)
    h_rows1 = gather_rows(h_rows, 1, 2)
    *o_chunks, lse1, ot1 = attend(chunks1, [*h_rows0[1:3], cosines, sines])
    o_chunks = swap_chunks(o_chunks)
    outputs, aout1, m1, turned1, slope1, f1 = call(
        ahead_kernel,
        [SM] + [VM] * 8 + [HBM] * 4,
        [shaped(1, rows, WIDTH, dtype=BF), b_square, f_square, shaped(tall, rows, dtype=BF), b_tall, b_square],
        [x_hold, output_hold, expand_hold, shrink_hold, pltpu.VMEM((1, hidden), F32), o_hold]
        + [pltpu.VMEM((rows, WIDTH), BF), pltpu.SemaphoreType.DMA((4,))],
        300,
        "mlp_ahead",
        28,
        [*h_rows1[1:3], turned0_far],
    )(
        scal, mod1, output_bias, expand_bias, shrink_bias, *o_chunks, x1, output_weight, expand_weight, shrink_weight
    )
    turned1_far = far(turned1)
    back_outs = [shaped(4, rows // 2, 2 * GROUP, dtype=BF), f_square, shaped(1, 7680)]
    mine1, theirs1, given, dm1, vec1 = call(
        turn_kernel,
        [SM] + [VM] * 5 + [HBM] * 4,
        [shaped(rows, half_width, dtype=BF)] * 2 + back_outs,
        [output_hold, expand_hold, shrink_hold, pltpu.VMEM(cotangent.shape, BF)]
        + [pltpu.VMEM((2, rows, half_width), BF), pltpu.SemaphoreType.DMA((4,))],
        300,
        "mlp_turn",
        32,
        [h_rows0[3], h_rows1[3]],
        (0, 3),
    )(scal, mod1, m1, f1, slope1, aout1, cotangent, output_weight, expand_weight, shrink_weight)

    def exchange_blocks(stack):
        return lax.all_to_all(stack, "blk", 0, 0)

    def deal(*dealt):
        return (
            (hidden, hidden + WIDTH, 0, dealt[0]),
            (0, hidden, hidden // 2, dealt[1]),
            (hidden + WIDTH, tall, hidden // 2 + WIDTH // 2, dealt[2]),
        )

    products1 = deal((4, 4, 4), (1, 1, 1), (2, 1, 0))
    products0 = deal((4, 4, 4), (1, 1, 1), (1, 1, 1))
    orders = ("axyb", "xyba", "yaxb")
    given = exchange_blocks(given)
    parts1, sent = weight_parts(scal, turned1, turned1_far, mine1, far(theirs1), products1, orders)
    outs = attend_back(chunks1, given, lse1, ot1, sent)
    stacked = outs[0]
    grads = exchange_blocks(stacked)
    sent = exchange(parts1, 0.1, [outs.token])
    triple1, sent = triple_part(scal, h_rows1, stacked, sent)
    outs = call(
        back_kernel,
        [SM] + [VM] * 3 + [HBM] * 10,
        [shaped(rows, half_width, dtype=BF)] * 2 + [shaped(1, 3840)] + back_outs,
        [triple_hold, output_hold, expand_hold, shrink_hold, pltpu.VMEM((rows, 3 * WIDTH), BF)]
        + [pltpu.VMEM((2, rows, half_width), BF), x_hold, x_hold, x_hold, pltpu.VMEM((rows, WIDTH), BF)]
        + [pltpu.VMEM((rows, hidden), BF), pltpu.VMEM((rows, WIDTH), BF), pltpu.SemaphoreType.DMA((10,))],
        300,
        "qkv_mlp_back",
        32,
        sent,
        (0, 4),
    )(
        scal, mod1, mod0, grads, x1, dm1, m0, f0, slope0, aout0, triple_weight, output_weight, expand_weight,
        shrink_weight,
    )
    mine0, theirs0, first1, given, dm0, vec0 = outs
    given = exchange_blocks(given)
    sent = exchange([*parts1, triple1], 300, [outs.token])
    parts0, sent = weight_parts(scal, turned0, turned0_far, mine0, far(theirs0), products0, orders, sent)
    sent = exchange([*parts1, triple1], 0.1, sent)
    outs = attend_back(chunks0, given, lse0, ot0, sent)
    stacked = outs[0]
    grads = exchange_blocks(stacked)
    sent = exchange(parts0, 0.1, [outs.token])
    triple0, sent = triple_part(scal, h_rows0, stacked, sent)
    sent = [*sent, triple1.views[-1][0]]
    outs = call(
        last_kernel,
        [SM] + [VM] * 5 + [HBM] * 3,
        [shaped(1, rows, WIDTH), shaped(1, DMOD + SMALL)],
        [triple_hold, pltpu.VMEM((rows, 3 * WIDTH), BF), x_hold, x_hold]
        + [pltpu.VMEM((1, 3840), F32), pltpu.VMEM((1, WIDTH), F32), pltpu.SemaphoreType.DMA((3,))],
        300,
        "qkv_back",
        24,
        sent,
    )(scal, mod0, grads, vec0, first1, vec1, x0, dm0, triple_weight)

    def spread(own, got, cost, after=()):
        wide = shaped(1, 2 * own.shape[1] - SMALL)
        return call(spread_kernel, [VM] * 2, [wide], [], cost, "spread", 8, after)(own, got)

    input_grad, small = outs
    near = swap(small, "blk", 1)
    sent = exchange([*parts0, triple0], 300, [outs.token])
    (summed,) = call(plain_add_kernel, [VM] * 2, [shaped_like(small)], [], 300, "plain_add", 8, sent)(small, near)
    outs = call(
        join_kernel,
        [VM] * 3,
        [shaped(1, DMOD + 128 + SMALL)],
        [],
        0.1,
        "join",
        8,
    )(summed, swap(summed, "blk", 2), condition)
    wide = outs[0]
    got = swap(wide, *STEP["b"])
    sent = exchange([*parts0, triple0], 300, [outs.token])
    own1, theirs1, early = settle(parts1, scal, products1, 0.1, sent)
    outs = spread(wide, got, 300, [early])
    wide = outs[0]
    outs = spread(wide, swap(wide, *STEP["a"]), 0.1)
    wide = outs[0]
    outs = call(
        small_kernel,
        [SM] + [VM] * 2 + [HBM],
        [shaped(LAYERS, condition.shape[1] // 32, 6 * WIDTH), shaped(LAYERS, 6 * WIDTH // 32)]
        + [shaped(LAYERS, (high - low) // 32) for low, high in SMALL_AT.values()]
        + [shaped(1, WIDTH // 32), shaped(1, 128)],
        [pltpu.VMEM(adaptive_weight.shape, BF), pltpu.SemaphoreType.DMA((1,))],
        0.1,
        "small",
        14,
    )(scal, wide, far(wide), adaptive_weight)
    small_grads = list(outs)
    blocks, cut = triple_settle([triple0, triple1], scal, [outs.token])
    own0, theirs0, _ = settle(parts0, scal, products0, 0.1, [*cut, *blocks[1:]])
    plans = (
        plan_of(products1, ((2, 1), (3, 1), (1, 1))),
        plan_of(products0, ((2, 0), (3, 0), (1, 0))),
    )
    weight_grads = call(
        functools.partial(finish_kernel, plans),
        [SM] + [VM] * 8,
        [
            shaped(LAYERS, WIDTH // 32, 3 * WIDTH),
            shaped(LAYERS, WIDTH // 32, WIDTH),
            shaped(LAYERS, WIDTH // 32, hidden),
            shaped(LAYERS, hidden // 32, WIDTH),
        ],
        [pltpu.VMEM((4, WIDTH // 32, 3 * GROUP), F32)],
        0.1,
        "finish",
        12,
    )(scal, own1, far(theirs1), own0, far(theirs0), *blocks)
    return (
        outputs,
        input_grad,
        small_grads[7],
        small_grads[6][0],
        small_grads[0],
        small_grads[1],
        weight_grads[0],
        small_grads[2],
        weight_grads[1],
        small_grads[3],
        weight_grads[2],
        small_grads[4],
        weight_grads[3],
        small_grads[5],
    )


def solution(mesh):
    in_specs = (
        P("dp", "blk", None),
        P("dp", None),
        P("dp"),
        P(),
        P(),
        P(),
        P(),
        P(),
        P(),
        P(),
        P(),
        P(),
        P(),
        P(),
        P("dp", "blk", None),
    )
    out_specs = (
        P("dp", "blk", None),
        P("dp", "blk", None),
        P("dp", None),
        P(("blk", "dp")),
        P(None, ("blk", "dp"), None),
        P(None, ("blk", "dp")),
        P(None, ("blk", "dp"), None),
        P(None, ("blk", "dp")),
        P(None, ("blk", "dp"), None),
        P(None, ("blk", "dp")),
        P(None, ("blk", "dp"), None),
        P(None, ("blk", "dp")),
        P(None, ("blk", "dp"), None),
        P(None, ("blk", "dp")),
    )
    whole = mesh.shape["blk"] == 4 and mesh.shape["dp"] == 8
    body = local_fast if whole else local
    return jax.shard_map(body, mesh=mesh, in_specs=in_specs, out_specs=out_specs, check_vma=False)
```

```python
import functools
import math

import jax
import jax.numpy as jnp
from jax import lax
from jax.experimental import pallas as pl
from jax.experimental.pallas import tpu as pltpu
from jax.sharding import PartitionSpec as P

HEADS = 12
HEAD_DIM = 64
LAYERS = 2


HIGHEST = lax.Precision.HIGHEST
EPSILON = 1e-06


def modulate(residual, shift, scaling):
    average = jnp.mean(residual, -1, keepdims=True)
    centered = residual - average
    variance = jnp.mean(centered * centered, -1, keepdims=True)
    return centered * lax.rsqrt(variance + EPSILON) * (1.0 + scaling) + shift


def gelu_tanh(values):
    return jax.nn.gelu(values, approximate=True)


def tables(offset, row_count, head_dim):
    half_dim = head_dim // 2
    position = (offset + jnp.arange(row_count, dtype=jnp.int32)).astype(jnp.float32)
    frequency = jnp.exp(
        jnp.arange(half_dim, dtype=jnp.float32) * (-2.0 * math.log(10000.0) / head_dim)
    )
    angles = position[:, None] * frequency[None, :]
    return (jnp.cos(angles)[:, None, :], jnp.sin(angles)[:, None, :])


def rotate(vectors, cosine, sine_table):
    half_dim = vectors.shape[-1] // 2
    front_half = vectors[..., :half_dim]
    back_half = vectors[..., half_dim:]
    return jnp.concatenate(
        [
            front_half * cosine - back_half * sine_table,
            back_half * cosine + front_half * sine_table,
        ],
        -1,
    )


def unrotate(gradient, cosine, sine_table):
    half_dim = gradient.shape[-1] // 2
    front_half = gradient[..., :half_dim]
    back_half = gradient[..., half_dim:]
    return jnp.concatenate(
        [
            front_half * cosine + back_half * sine_table,
            back_half * cosine - front_half * sine_table,
        ],
        -1,
    )


def split_einsum(form, float_left, low_right):
    upper = float_left.astype(jnp.bfloat16)
    lower = (float_left - upper.astype(jnp.float32)).astype(jnp.bfloat16)
    first = jnp.einsum(form, upper, low_right, preferred_element_type=jnp.float32)
    return first + jnp.einsum(form, lower, low_right, preferred_element_type=jnp.float32)


def fold_keys(queries, scaling):

    def absorb(carried, key_piece, offset):
        key_flat, value_flat = key_piece
        piece_rows = key_flat.shape[0]
        block_rows = math.gcd(piece_rows, 512)
        key_blocks = key_flat.reshape(piece_rows // block_rows, block_rows, HEADS, HEAD_DIM)
        value_blocks = value_flat.reshape(piece_rows // block_rows, block_rows, HEADS, HEAD_DIM)

        def absorb_inner(running, block_pair):
            running_max, running_sum, weighted = running
            key_block, value_block = block_pair
            scores = (
                jnp.einsum("qhd,khd->hqk", queries, key_block, preferred_element_type=jnp.float32)
                * scaling
            )
            new_max = jnp.maximum(running_max, jnp.max(scores, -1))
            weights = jnp.exp(scores - new_max[..., None])
            factor = jnp.exp(running_max - new_max)
            running_sum = running_sum * factor + jnp.sum(weights, -1)
            weighted = weighted * factor[..., None] + split_einsum(
                "hqk,khd->hqd", weights, value_block
            )
            return ((new_max, running_sum, weighted), None)

        carried, _ = lax.scan(absorb_inner, carried, (key_blocks, value_blocks))
        return carried

    return absorb


def attend_back(queries, key_all, value_all, out_gradient, attended_f, log_total, scaling):
    row_count = queries.shape[0]
    all_rows = key_all.shape[0]
    block_rows = math.gcd(all_rows, 512)
    key_blocks = key_all.reshape(all_rows // block_rows, block_rows, HEADS, HEAD_DIM)
    value_blocks = value_all.reshape(all_rows // block_rows, block_rows, HEADS, HEAD_DIM)
    out_float = out_gradient.astype(jnp.float32)
    row_delta = jnp.transpose(jnp.sum(out_float * attended_f, -1), (1, 0))

    def attend_inner(query_grad, block_pair):
        key_block, value_block = block_pair
        scores = (
            jnp.einsum("qhd,khd->hqk", queries, key_block, preferred_element_type=jnp.float32)
            * scaling
        )
        probs = jnp.exp(scores - log_total[..., None])
        prob_grad = jnp.einsum(
            "qhd,khd->hqk", out_gradient, value_block, preferred_element_type=jnp.float32
        )
        score_grad = (probs * (prob_grad - row_delta[..., None])).astype(jnp.bfloat16)
        query_grad = query_grad + jnp.einsum(
            "hqk,khd->qhd", score_grad, key_block, preferred_element_type=jnp.float32
        )
        key_grad = (
            jnp.einsum("hqk,qhd->khd", score_grad, queries, preferred_element_type=jnp.float32)
            * scaling
        )
        value_grad = split_einsum("hqk,qhd->khd", probs, out_gradient)
        return (query_grad, (key_grad, value_grad))

    start_grad = jnp.zeros((row_count, HEADS, HEAD_DIM), jnp.float32)
    query_grad, (key_grads, value_grads) = lax.scan(
        attend_inner, start_grad, (key_blocks, value_blocks)
    )
    width = HEADS * HEAD_DIM
    return (
        query_grad * scaling,
        key_grads.reshape(all_rows, width),
        value_grads.reshape(all_rows, width),
    )


def forward_layer(residual, modulation, layer_index, weights, cosine, sine_table, scaling):
    (
        adaptive_weight,
        adaptive_bias,
        triple_weight,
        triple_bias,
        output_weight,
        output_bias,
        expand_weight,
        expand_bias,
        shrink_weight,
        shrink_bias,
    ) = weights
    row_count, width = residual.shape
    pieces = [modulation[number * width : (number + 1) * width] for number in range(6)]
    shift_attn, scale_attn, gate_attn, shift_mlp, scale_mlp, gate_mlp = pieces
    normed = modulate(residual, shift_attn, scale_attn).astype(jnp.bfloat16)
    mixed = jnp.dot(
        normed, triple_weight[layer_index], preferred_element_type=jnp.float32
    ) + triple_bias[layer_index].astype(jnp.float32)
    head_shape = (row_count, HEADS, HEAD_DIM)
    queries = rotate(mixed[:, :width].reshape(head_shape), cosine, sine_table).astype(jnp.bfloat16)
    key_flat = (
        rotate(mixed[:, width : 2 * width].reshape(head_shape), cosine, sine_table)
        .astype(jnp.bfloat16)
        .reshape(row_count, width)
    )
    value_flat = mixed[:, 2 * width :].astype(jnp.bfloat16)
    start_state = (
        jnp.full((HEADS, row_count), -1e30, jnp.float32),
        jnp.zeros((HEADS, row_count), jnp.float32),
        jnp.zeros((HEADS, row_count, HEAD_DIM), jnp.float32),
    )
    absorb = fold_keys(queries, scaling)
    final_state = absorb(
        start_state,
        (
            lax.all_gather(key_flat, "blk", axis=0, tiled=True),
            lax.all_gather(value_flat, "blk", axis=0, tiled=True),
        ),
        jnp.int32(0),
    )
    running_max, running_sum, weighted = final_state
    log_total = running_max + jnp.log(running_sum)
    attended_f = jnp.transpose(weighted / running_sum[..., None], (1, 0, 2))
    attended = attended_f.reshape(row_count, width).astype(jnp.bfloat16)
    branch = jnp.dot(
        attended, output_weight[layer_index], preferred_element_type=jnp.float32
    ) + output_bias[layer_index].astype(jnp.float32)
    middle = residual + gate_attn * branch
    normed_mlp = modulate(middle, shift_mlp, scale_mlp).astype(jnp.bfloat16)
    up_proj = jnp.dot(
        normed_mlp, expand_weight[layer_index], preferred_element_type=jnp.float32
    ) + expand_bias[layer_index].astype(jnp.float32)
    active = gelu_tanh(up_proj).astype(jnp.bfloat16)
    lowered = jnp.dot(
        active, shrink_weight[layer_index], preferred_element_type=jnp.float32
    ) + shrink_bias[layer_index].astype(jnp.float32)
    result = middle + gate_mlp * lowered
    saved = (
        residual,
        normed,
        queries,
        key_flat,
        value_flat,
        None,
        attended_f,
        attended,
        log_total,
        branch,
        middle,
        normed_mlp,
        up_proj,
        active,
        lowered,
    )
    return (result, saved)


def backward_layer(
    gradient, modulation, layer_index, weights, saved, cosine, sine_table, scaling, condition
):
    (
        adaptive_weight,
        adaptive_bias,
        triple_weight,
        triple_bias,
        output_weight,
        output_bias,
        expand_weight,
        expand_bias,
        shrink_weight,
        shrink_bias,
    ) = weights
    (
        residual,
        normed,
        queries,
        key_flat,
        value_flat,
        gathered,
        attended_f,
        attended,
        log_total,
        branch,
        middle,
        normed_mlp,
        up_proj,
        active,
        lowered,
    ) = saved
    row_count, width = residual.shape
    pieces = [modulation[number * width : (number + 1) * width] for number in range(6)]
    shift_attn, scale_attn, gate_attn, shift_mlp, scale_mlp, gate_mlp = pieces
    gate_mlp_grad = jnp.sum(gradient * lowered, 0)
    lowered_grad = (gradient * gate_mlp).astype(jnp.bfloat16)
    shrink_w_grad = jnp.einsum(
        "tf,td->fd", active, lowered_grad, preferred_element_type=jnp.float32
    )
    shrink_b_grad = jnp.sum(lowered_grad.astype(jnp.float32), 0)
    active_grad = jnp.einsum(
        "td,fd->tf", lowered_grad, shrink_weight[layer_index], preferred_element_type=jnp.float32
    )
    _, gelu_pull = jax.vjp(gelu_tanh, up_proj)
    up_grad = gelu_pull(active_grad)[0].astype(jnp.bfloat16)
    expand_w_grad = jnp.einsum("td,tf->df", normed_mlp, up_grad, preferred_element_type=jnp.float32)
    expand_b_grad = jnp.sum(up_grad.astype(jnp.float32), 0)
    normed_mlp_grad = jnp.einsum(
        "tf,df->td", up_grad, expand_weight[layer_index], preferred_element_type=jnp.float32
    )
    _, mlp_pull = jax.vjp(modulate, middle, shift_mlp, scale_mlp)
    middle_grad, shift_mlp_grad, scale_mlp_grad = mlp_pull(normed_mlp_grad)
    middle_grad = middle_grad + gradient
    gate_attn_grad = jnp.sum(middle_grad * branch, 0)
    branch_grad = (middle_grad * gate_attn).astype(jnp.bfloat16)
    output_w_grad = jnp.einsum(
        "tc,td->cd", attended, branch_grad, preferred_element_type=jnp.float32
    )
    output_b_grad = jnp.sum(branch_grad.astype(jnp.float32), 0)
    attended_grad = jnp.einsum(
        "td,cd->tc", branch_grad, output_weight[layer_index], preferred_element_type=jnp.float32
    )
    attended_grad = attended_grad.astype(jnp.bfloat16).reshape(row_count, HEADS, HEAD_DIM)
    key_all, value_all = (
        lax.all_gather(key_flat, "blk", axis=0, tiled=True),
        lax.all_gather(value_flat, "blk", axis=0, tiled=True),
    )
    query_grad, key_all_grad, value_all_grad = attend_back(
        queries, key_all, value_all, attended_grad, attended_f, log_total, scaling
    )
    key_grad, value_grad = (
        lax.psum_scatter(
            key_all_grad.astype(jnp.bfloat16), "blk", scatter_dimension=0, tiled=True
        ).astype(jnp.float32),
        lax.psum_scatter(
            value_all_grad.astype(jnp.bfloat16), "blk", scatter_dimension=0, tiled=True
        ).astype(jnp.float32),
    )
    mixed_grad = jnp.concatenate(
        [
            unrotate(query_grad, cosine, sine_table).reshape(row_count, width),
            unrotate(key_grad.reshape(row_count, HEADS, HEAD_DIM), cosine, sine_table).reshape(
                row_count, width
            ),
            value_grad,
        ],
        -1,
    ).astype(jnp.bfloat16)
    triple_w_grad = jnp.einsum("td,tc->dc", normed, mixed_grad, preferred_element_type=jnp.float32)
    triple_b_grad = jnp.sum(mixed_grad.astype(jnp.float32), 0)
    normed_grad = jnp.einsum(
        "tc,dc->td", mixed_grad, triple_weight[layer_index], preferred_element_type=jnp.float32
    )
    _, attn_pull = jax.vjp(modulate, residual, shift_attn, scale_attn)
    residual_grad, shift_attn_grad, scale_attn_grad = attn_pull(normed_grad)
    residual_grad = residual_grad + middle_grad
    modulation_grad = jnp.concatenate(
        [
            shift_attn_grad,
            scale_attn_grad,
            gate_attn_grad,
            shift_mlp_grad,
            scale_mlp_grad,
            gate_mlp_grad,
        ],
        0,
    )
    adaptive_w_grad = condition[0][:, None] * modulation_grad[None, :]
    condition_term = jnp.dot(
        adaptive_weight[layer_index].astype(jnp.float32), modulation_grad, precision=HIGHEST
    )
    grad_terms = (
        adaptive_w_grad,
        modulation_grad,
        triple_w_grad,
        triple_b_grad,
        output_w_grad,
        output_b_grad,
        expand_w_grad,
        expand_b_grad,
        shrink_w_grad,
        shrink_b_grad,
    )
    return (residual_grad, grad_terms, condition_term)


def local(
    inputs,
    condition,
    prefix,
    mask_embed,
    adaptive_weight,
    adaptive_bias,
    triple_weight,
    triple_bias,
    output_weight,
    output_bias,
    expand_weight,
    expand_bias,
    shrink_weight,
    shrink_bias,
    cotangent,
):
    weights = (
        adaptive_weight,
        adaptive_bias,
        triple_weight,
        triple_bias,
        output_weight,
        output_bias,
        expand_weight,
        expand_bias,
        shrink_weight,
        shrink_bias,
    )
    row_count = inputs.shape[1]
    offset = lax.axis_index("blk") * row_count
    position = offset + jnp.arange(row_count, dtype=jnp.int32)
    masked = position >= prefix[0]
    residual = jnp.where(
        masked[:, None], mask_embed.astype(jnp.float32)[None, :], inputs[0].astype(jnp.float32)
    )
    cosine, sine_table = tables(offset, row_count, HEAD_DIM)
    scaling = 1.0 / math.sqrt(HEAD_DIM)
    modulations = []
    saved_layers = []
    for layer_index in range(LAYERS):
        modulation = jnp.dot(
            condition, adaptive_weight[layer_index].astype(jnp.float32), precision=HIGHEST
        )[0] + adaptive_bias[layer_index].astype(jnp.float32)
        residual, saved = forward_layer(
            residual, modulation, layer_index, weights, cosine, sine_table, scaling
        )
        modulations.append(modulation)
        saved_layers.append(saved)
    outputs = residual.astype(jnp.bfloat16)[None]
    gradient = cotangent[0].astype(jnp.float32)
    condition_total = jnp.zeros((condition.shape[1],), jnp.float32)
    collected = [None] * LAYERS
    mask_sum = None
    for layer_index in reversed(range(LAYERS)):
        gradient, grad_terms, condition_term = backward_layer(
            gradient,
            modulations[layer_index],
            layer_index,
            weights,
            saved_layers[layer_index],
            cosine,
            sine_table,
            scaling,
            condition,
        )
        condition_total = condition_total + condition_term
        collected[layer_index] = grad_terms
    mask_term = jnp.sum(jnp.where(masked[:, None], gradient, 0.0), 0)
    flat_terms = ()
    for layer_index in range(LAYERS):
        flat_terms = flat_terms + tuple(collected[layer_index])
    summed = lax.psum_scatter(
        flat_terms + (mask_term,), ("blk", "dp"), scatter_dimension=0, tiled=True
    )
    collected = [summed[layer_index * 10 : (layer_index + 1) * 10] for layer_index in range(LAYERS)]
    mask_sum = summed[LAYERS * 10]
    condition_grad = lax.psum(condition_total, "blk")[None, :]
    input_grad = jnp.where(masked[:, None], 0.0, gradient)[None]
    stacked = [
        jnp.stack([collected[layer_index][number] for layer_index in range(LAYERS)], 0)
        for number in range(10)
    ]
    return (
        outputs,
        input_grad,
        condition_grad,
        mask_sum,
        stacked[0],
        stacked[1],
        stacked[2],
        stacked[3],
        stacked[4],
        stacked[5],
        stacked[6],
        stacked[7],
        stacked[8],
        stacked[9],
    )


BF = jnp.bfloat16
F32 = jnp.float32
WIDTH = HEADS * HEAD_DIM
GROUP = WIDTH // 4
VM = pl.BlockSpec(memory_space=pltpu.VMEM)
ANY = pl.BlockSpec(memory_space=pl.ANY)
HBM = pl.BlockSpec(memory_space=pltpu.HBM)
HV = pl.BlockSpec(memory_space=pltpu.VMEM)
SM = pl.BlockSpec(memory_space=pltpu.SMEM)
MEBI = 1024 * 1024
ROOT_TWO_PI = math.sqrt(2.0 / math.pi)
CUBIC = 0.044715


def dot_nn(left, right):
    return jnp.dot(left, right, preferred_element_type=F32)


def dot_nt(left, right):
    return lax.dot_general(left, right, (((1,), (1,)), ((), ())), preferred_element_type=F32)


def dot_tn(left, right):
    return lax.dot_general(left, right, (((0,), (0,)), ((), ())), preferred_element_type=F32)


def normalise(values):
    centered = values - jnp.mean(values, -1, keepdims=True)
    rstd = lax.rsqrt(jnp.mean(centered * centered, -1, keepdims=True) + EPSILON)
    return centered * rstd, rstd


def normalise_back(upstream, unit, rstd):
    first = jnp.mean(upstream, -1, keepdims=True)
    second = jnp.mean(upstream * unit, -1, keepdims=True)
    return rstd * (upstream - first - unit * second)


def column_sum(values):
    return jnp.sum(values, 0, keepdims=True)


def turn(values, cosine, signed_sine):
    lane = lax.broadcasted_iota(jnp.int32, (values.shape[0], 128), 1)
    front = (lane % HEAD_DIM) < HEAD_DIM // 2
    pieces = []
    for start in range(0, values.shape[1], 128):
        piece = values[:, start : start + 128]
        swapped = jnp.where(front, pltpu.roll(piece, 96, 1), pltpu.roll(piece, 32, 1))
        pieces.append(piece * cosine + swapped * signed_sine)
    return jnp.concatenate(pieces, 1)


def piece_of(row, number):
    return row[:, number * WIDTH : (number + 1) * WIDTH]


def row_of(ref, layer):
    return ref[...].astype(F32)[layer : layer + 1, :]


def pack_rows(values):
    half = values.shape[0] // 2
    return jnp.concatenate([values[:half], values[half:]], 1)


def qkv_stage(x, layer, mod_row, triple_bias, triple, cos_ref, sin_ref, me, h_ref, chunk_refs, hold):
    unit, _ = normalise(x)
    h = unit * (1.0 + piece_of(mod_row, 1)) + piece_of(mod_row, 0)
    turned = h.T
    h = h.astype(BF)
    each = WIDTH // 32
    for half in range(2):
        picked = [turned[each * (b * 8 + z * 2 + half) :][:each] for z in range(4) for b in range(4)]
        h_ref[half] = jnp.concatenate(picked, 0).astype(BF)
    bias = row_of(triple_bias, layer)
    cosine, sine = cos_ref[0], sin_ref[0]
    parts = []
    for number in range(3):
        columns = slice(number * WIDTH, (number + 1) * WIDTH)
        mixed = dot_nn(h, triple[:, columns]) + bias[:, columns]
        if number < 2:
            mixed = turn(mixed, cosine, sine)
        if number == 0:
            mixed = mixed * HEAD_DIM**-0.5
        parts.append(mixed)
    rows = x.shape[0]
    for group in range(4):
        columns = slice(group * GROUP, (group + 1) * GROUP)
        pair = jnp.concatenate([parts[0][:, columns], parts[1][:, columns]], 1)
        hold[group, 0:rows, :] = pair.astype(BF)
        hold[group, rows : rows + rows // 2, :] = pack_rows(parts[2][:, columns]).astype(BF)
    for place in range(4):
        chunk_refs[place][...] = hold[place ^ me]


def fetch(pairs, sems):
    copies = []
    for number, (source, target) in enumerate(pairs):
        copy = pltpu.make_async_copy(source, target, sems.at[number])
        copy.start()
        copies.append(copy)
    return copies


def wait_all(copies):
    for copy in copies:
        copy.wait()


def three_rows(row):
    upper = row.astype(BF).astype(F32)
    rest = row - upper
    middle = rest.astype(BF).astype(F32)
    low = rest - middle
    number = lax.broadcasted_iota(jnp.int32, (8, row.shape[1]), 0)
    return jnp.where(number == 0, upper, jnp.where(number == 1, middle, jnp.where(number == 2, low, 0.0))).astype(BF)


def modulation(cond, adaptive, adaptive_bias, layer):
    return column_sum(dot_nn(three_rows(cond), adaptive[...])) + row_of(adaptive_bias, layer)


def first_kernel(
    scal, mask_embed, cos_ref, sin_ref, inputs_any, condition_any, adaptive_bias_any, triple_bias_any, adaptive_any,
    triple_any,
    x_ref, mod_ref, h_ref, c0, c1, c2, c3,
    inputs, condition, adaptive_bias, triple_bias, adaptive, triple, hold, sems,
):
    copies = fetch(
        [
            (adaptive_any.at[0], adaptive), (triple_any.at[0], triple), (inputs_any, inputs),
            (condition_any, condition), (adaptive_bias_any, adaptive_bias), (triple_bias_any, triple_bias),
        ],
        sems,
    )
    for copy in copies[2:]:
        copy.wait()
    me = scal[0]
    rows = inputs.shape[1]
    position = me * rows + lax.broadcasted_iota(jnp.int32, (rows, WIDTH), 0)
    x = jnp.where(position >= scal[3], mask_embed[...].astype(F32), inputs[0].astype(F32))
    x_ref[...] = x
    copies[0].wait()
    mod = modulation(condition[...], adaptive, adaptive_bias, 0)
    mod_ref[...] = mod
    copies[1].wait()
    qkv_stage(x, 0, mod, triple_bias, triple, cos_ref, sin_ref, me, h_ref, (c0, c1, c2, c3), hold)


def attend_kernel(
    c0, c1, c2, c3,
    o0, o1, o2, o3, lse_ref, of_ref,
    ot_ref, q_all, k_all, v_turned,
):
    rows = 256
    for place, chunk in enumerate((c0, c1, c2, c3)):
        span = slice(place * rows, (place + 1) * rows)
        q_all[place] = chunk[0:rows, 0:GROUP]
        k_all[span, :] = chunk[0:rows, GROUP : 2 * GROUP]
        tail = chunk[rows : rows + rows // 2, :]
        v_block = jnp.concatenate([tail[:, 0:GROUP], tail[:, GROUP : 2 * GROUP]], 0)
        v_block = v_block.T
        for number in range(3):
            v_turned[number, 0:HEAD_DIM, span] = v_block[number * HEAD_DIM : (number + 1) * HEAD_DIM]
    v_turned[:, HEAD_DIM:, :] = jnp.ones((3, 16, 4 * rows), BF)
    head = lax.broadcasted_iota(jnp.int32, (2 * rows, GROUP), 1) // HEAD_DIM

    for block in range(0, 4, 2):
        q = q_all[block : block + 2].reshape(2 * rows, GROUP)
        for number in range(3):
            masked = jnp.where(head == number, q, jnp.zeros_like(q))
            scores = dot_nt(k_all[...], masked)
            peak = jnp.max(scores, 0, keepdims=True)
            weights = jnp.exp(scores - peak).astype(BF)
            both = dot_nn(v_turned[number], weights)
            total = both[HEAD_DIM : HEAD_DIM + 1]
            span = slice(number * HEAD_DIM, (number + 1) * HEAD_DIM)
            found = both[0:HEAD_DIM] / total
            lse = peak + jnp.log(total)
            for part in range(2):
                columns = slice(part * rows, (part + 1) * rows)
                ot_ref[block + part, span, :] = found[:, columns]
                lse_ref[block + part, number : number + 1, :] = lse[:, columns]
    for place, out in enumerate((o0, o1, o2, o3)):
        found = ot_ref[place].T
        of_ref[place] = found
        out[...] = pack_rows(found).astype(BF)


def gather_chunks(refs, hold):
    for place in range(4):
        hold[place] = refs[place][...]


def place_rows(target, at, values, scal, group=None):
    count = 16 if group is None else 4
    rows = values.shape[0] // count
    me16 = scal[0] * 4 + scal[1]
    for chip in range(count):
        place = (chip if group is None else chip + 4 * group) ^ me16
        start = pl.multiple_of(at + place * rows, 16)
        target[pl.ds(start, rows), :] = values[chip * rows : (chip + 1) * rows]


def mlp_forward(
    layer, x_ref, mod_row, biases, scal, o_refs, output, expand, shrink, waits, hold, o_ref, aout_ref, m_ref, turned_ref,
    slope_ref, f_ref, bias_all,
):
    gather_chunks(o_refs, hold)
    me = scal[0]
    rows = x_ref.shape[0]
    half = rows // 2
    for group in range(4):
        chunk = hold[group ^ me]
        columns = slice(group * GROUP, (group + 1) * GROUP)
        o_ref[0:half, columns] = chunk[:, 0:GROUP]
        o_ref[half:rows, columns] = chunk[:, GROUP : 2 * GROUP]
    o = o_ref[...]
    hidden = expand.shape[1]
    place_rows(turned_ref, hidden + WIDTH, o.T, scal)
    waits[0].wait()
    a_out = dot_nn(o, output[...]) + row_of(biases[0], layer)
    aout_ref[...] = a_out.astype(BF)
    waits[3].wait()
    m = x_ref[...] + piece_of(mod_row, 2) * a_out
    m_ref[...] = m
    unit, _ = normalise(m)
    h2 = (unit * (1.0 + piece_of(mod_row, 4)) + piece_of(mod_row, 3)).astype(BF)
    place_rows(turned_ref, hidden, h2.T, scal)
    waits[1].wait()
    waits[2].wait()
    width = 768
    bias_all[...] = row_of(biases[1], layer)

    def hidden_block(number, f):
        start = pl.multiple_of(number * width, width)
        columns = pl.ds(start, width)
        u = dot_nn(h2, expand[:, columns]) + bias_all[:, columns]
        square = u * u
        gate = 0.5 + 0.5 * jnp.tanh(u * (ROOT_TWO_PI + ROOT_TWO_PI * CUBIC * square))
        active = u * gate
        slope = gate + 2.0 * active * (1.0 - gate) * (ROOT_TWO_PI + 3.0 * ROOT_TWO_PI * CUBIC * square)
        z = active.astype(BF)
        place_rows(turned_ref, 0, z.T, scal, number)
        slope_ref[:, columns] = slope.astype(BF)
        return f + dot_nn(z, shrink[columns, :])

    f = lax.fori_loop(0, hidden // width, hidden_block, jnp.zeros(x_ref.shape, F32), unroll=4 if layer else 1) + row_of(biases[2], layer)
    f_ref[...] = f.astype(BF)
    return m + piece_of(mod_row, 5) * f


def share(values, hold, at):
    half = values.shape[1] // 2
    hold[0, :, at : at + half] = values[:, 0:half]
    hold[1, :, at : at + half] = values[:, half : 2 * half]


def mlp_backward(
    dy, mod_row, me, core, m_ref, f_ref, slope_ref, aout_ref, output, expand, shrink, waits, halves,
    do_ref, dm_ref, vec_ref,
):
    def put(place, row):
        vec_ref[:, place : place + row.shape[1]] = row

    put(0, column_sum(dy * f_ref[...].astype(F32)))
    df = (dy * piece_of(mod_row, 5)).astype(BF)
    put(3072, column_sum(df.astype(F32)))
    hidden = expand.shape[1]
    share(df, halves, hidden // 2)
    dh2 = jnp.zeros(dy.shape, F32)
    waits[2].wait()
    for start in range(0, hidden, 768):
        columns = slice(start, start + 768)
        dz = dot_nt(df, shrink[columns, :])
        du = (slope_ref[:, columns].astype(F32) * dz).astype(BF)
        put(3840 + start, column_sum(du.astype(F32)))
        half = hidden // 2
        halves[start // half, :, start % half : start % half + 768] = du
        if start == 0:
            waits[1].wait()
        dh2 = dh2 + dot_nt(du, expand[:, columns])
    unit, rstd = normalise(m_ref[...])
    put(768, column_sum(dh2))
    put(1536, column_sum(dh2 * unit))
    dm = dy + normalise_back(dh2 * (1.0 + piece_of(mod_row, 4)), unit, rstd)
    dm_ref[...] = dm
    put(2304, column_sum(dm * aout_ref[...].astype(F32)))
    da = (dm * piece_of(mod_row, 2)).astype(BF)
    put(6912, column_sum(da.astype(F32)))
    share(da, halves, hidden // 2 + WIDTH // 2)
    waits[0].wait()
    do = dot_nt(da, output[...])
    for group in range(4):
        do_ref[group] = pack_rows(do[:, group * GROUP : (group + 1) * GROUP]).astype(BF)


def attend_back_kernel(
    scal, given_ref, c0, c1, c2, c3, lse_ref, of_ref, cos_any, sin_any, stacked,
    cos_ref, sin_ref, sems, q_masked, do_masked, k_all, v_all, k_turned, lse_rows, delta_rows, dq_turned, dk_all, dv_all,
):
    copies = fetch([(cos_any, cos_ref), (sin_any, sin_ref)], sems)
    rows = 256
    head = lax.broadcasted_iota(jnp.int32, (rows, GROUP), 1) // HEAD_DIM
    of_head = lax.broadcasted_iota(jnp.int32, (8, GROUP), 1) // HEAD_DIM
    pick = jnp.where(of_head == lax.broadcasted_iota(jnp.int32, (8, GROUP), 0), 1.0, 0.0).astype(BF)
    for place in range(4):
        chunk = (c0, c1, c2, c3)[place]
        given = given_ref[place ^ scal[0]]
        span = slice(place * rows, (place + 1) * rows)
        q = chunk[0:rows, 0:GROUP]
        k = chunk[0:rows, GROUP : 2 * GROUP]
        tail = chunk[rows : rows + rows // 2, :]
        v_all[place] = jnp.concatenate([tail[:, 0:GROUP], tail[:, GROUP : 2 * GROUP]], 0)
        k_all[place] = k
        k_turned[place] = k.T
        do = jnp.concatenate([given[:, 0:GROUP], given[:, GROUP : 2 * GROUP]], 0)
        product = do.astype(F32) * of_ref[place]
        upper = product.astype(BF)
        lower = (product - upper.astype(F32)).astype(BF)
        delta_rows[:, span] = dot_nt(pick, upper) + dot_nt(pick, lower)
        for number in range(3):
            q_masked[number, span, :] = jnp.where(head == number, q, jnp.zeros_like(q))
            do_masked[number, span, :] = jnp.where(head == number, do, jnp.zeros_like(do))
            lse_rows[number : number + 1, span] = lse_ref[place, number : number + 1, :]
    dq_turned[...] = jnp.zeros(dq_turned.shape, F32)

    for block in range(4 // 2):
        k = k_all[block * 2 : (block + 1) * 2].reshape(2 * rows, GROUP)
        v = v_all[block * 2 : (block + 1) * 2].reshape(2 * rows, GROUP)
        dk = jnp.zeros((2 * rows, GROUP), F32)
        dv = jnp.zeros((2 * rows, GROUP), F32)
        for number in range(3):
            span = slice(number * HEAD_DIM, (number + 1) * HEAD_DIM)
            scores = dot_nt(k, q_masked[number])
            probs = jnp.exp(scores - lse_rows[number : number + 1, :])
            prob_grad = dot_nt(v, do_masked[number])
            score_grad = (probs * (prob_grad - delta_rows[number : number + 1, :])).astype(BF)
            dv = dv + dot_nn(probs.astype(BF), do_masked[number])
            dk = dk + dot_nn(score_grad, q_masked[number])
            for part in range(2):
                dq_turned[span, :] += dot_nn(k_turned[block * 2 + part, span, :], score_grad[part * rows : (part + 1) * rows])
        dk_all[block * 2 : (block + 1) * 2] = dk.reshape(2, rows, GROUP)
        dv_all[block * 2 : (block + 1) * 2] = dv.reshape(2, rows, GROUP)
    for copy in copies:
        copy.wait()
    for place in range(4):
        span = slice(place * rows, (place + 1) * rows)
        dq = dq_turned[:, span].T * HEAD_DIM**-0.5
        pair = jnp.concatenate([dq, dk_all[place]], 1)
        pair = turn(pair, cos_ref[place], -sin_ref[place]).astype(BF)
        tail = pack_rows(dv_all[place]).astype(BF)
        stacked[place ^ scal[0], 0:rows, :] = pair
        stacked[place ^ scal[0], rows : rows + rows // 2, :] = tail


def qkv_backward(x_ref, dm_ref, mod_row, chunks, triple, waits, full, vec_ref):
    rows = full.shape[0]
    half = rows // 2
    for group in range(4):
        chunk = chunks(group)
        low = group * GROUP
        full[:, low : low + GROUP] = chunk[0:rows, 0:GROUP]
        full[:, WIDTH + low : WIDTH + low + GROUP] = chunk[0:rows, GROUP : 2 * GROUP]
        full[0:half, 2 * WIDTH + low : 2 * WIDTH + low + GROUP] = chunk[rows : rows + half, 0:GROUP]
        full[half:rows, 2 * WIDTH + low : 2 * WIDTH + low + GROUP] = chunk[rows : rows + half, GROUP : 2 * GROUP]
    dqkv = full[...]
    vec_ref[:, 1536:3840] = column_sum(dqkv.astype(F32))
    waits[0].wait()
    dh = dot_nt(dqkv, triple[...])
    wait_all(waits[1:3])
    unit, rstd = normalise(x_ref[...])
    vec_ref[:, 0:768] = column_sum(dh)
    vec_ref[:, 768:1536] = column_sum(dh * unit)
    return dm_ref[...] + normalise_back(dh * (1.0 + piece_of(mod_row, 1)), unit, rstd)


def middle_kernel(
    scal, mod_ref, condition, adaptive_bias, output_bias, expand_bias, shrink_bias, triple_bias,
    cos_ref, sin_ref, o0, o1, o2, o3, x_any, output_any, expand_any, shrink_any, triple_any, adaptive_any,
    aout_ref, m_ref, turned_ref, slope_ref, f_ref, y_ref, mod_next, h_ref, c0, c1, c2, c3,
    x_ref, output, expand, shrink, triple, adaptive, bias_all, o_hold, o_ref, c_hold, sems,
):
    copies = fetch(
        [
            (output_any.at[0], output), (x_any, x_ref), (expand_any.at[0], expand), (shrink_any.at[0], shrink),
            (triple_any.at[1], triple), (adaptive_any.at[1], adaptive),
        ],
        sems,
    )
    me = scal[0]
    y = mlp_forward(
        0, x_ref, mod_ref[...], (output_bias, expand_bias, shrink_bias), scal, (o0, o1, o2, o3), output, expand, shrink,
        [copies[0], copies[2], copies[3], copies[1]], o_hold, o_ref,
        aout_ref, m_ref, turned_ref, slope_ref, f_ref, bias_all,
    )
    y_ref[...] = y
    wait_all(copies[4:])
    mod = modulation(condition[...], adaptive, adaptive_bias, 1)
    mod_next[...] = mod
    qkv_stage(
        y, 1, mod, triple_bias, triple, cos_ref, sin_ref, me, h_ref, (c0, c1, c2, c3), c_hold,
    )


def ahead_kernel(
    scal, mod_ref, output_bias, expand_bias, shrink_bias, o0, o1, o2, o3, x_any, output_any, expand_any, shrink_any,
    out_ref, aout_ref, m_ref, turned_ref, slope_ref, f_ref,
    x_ref, output, expand, shrink, bias_all, o_hold, o_ref, sems,
):
    copies = fetch(
        [(output_any.at[1], output), (x_any, x_ref), (expand_any.at[1], expand), (shrink_any.at[1], shrink)], sems
    )
    y = mlp_forward(
        1, x_ref, mod_ref[...], (output_bias, expand_bias, shrink_bias), scal, (o0, o1, o2, o3), output, expand, shrink,
        [copies[0], copies[2], copies[3], copies[1]], o_hold, o_ref,
        aout_ref, m_ref, turned_ref, slope_ref, f_ref, bias_all,
    )
    out_ref[0] = y.astype(BF)


def turn_kernel(
    scal, mod_ref, m_ref, f_ref, slope_ref, aout_ref, cotangent_any, output_any, expand_any, shrink_any,
    mine, theirs, do_ref, dm_ref, vec_ref,
    output, expand, shrink, cotangent, halves, sems,
):
    copies = fetch(
        [
            (shrink_any.at[1], shrink), (expand_any.at[1], expand), (output_any.at[1], output),
            (cotangent_any, cotangent),
        ],
        sems,
    )
    copies[3].wait()
    me, core = scal[0], scal[2]
    mlp_backward(
        cotangent[0].astype(F32), mod_ref[...], me, core, m_ref, f_ref, slope_ref, aout_ref, output, expand, shrink,
        [copies[2], copies[1], copies[0]], halves, do_ref, dm_ref, vec_ref,
    )
    mine[...] = halves[core]
    theirs[...] = halves[1 - core]


def back_kernel(
    scal, mod_ref, mod_low, grads, x_any, dm_any, m_any, f_any, slope_any, aout_any,
    triple_any, output_any, expand_any, shrink_any,
    mine, theirs, vec_first, do_ref, dm_ref, vec_ref,
    triple, output, expand, shrink, full, halves, x_ref, dm_in, m_ref, f_ref, slope_ref, aout_ref, sems,
):
    copies = fetch(
        [
            (triple_any.at[1], triple), (x_any, x_ref), (dm_any, dm_in), (f_any, f_ref), (slope_any, slope_ref),
            (m_any, m_ref), (aout_any, aout_ref), (shrink_any.at[0], shrink), (expand_any.at[0], expand),
            (output_any.at[0], output),
        ],
        sems,
    )
    me, core = scal[0], scal[2]
    dy = qkv_backward(
        x_ref, dm_in, mod_ref[...], lambda group: grads[group], triple, copies[0:3], full, vec_first,
    )
    wait_all(copies[3:7])
    mlp_backward(
        dy, mod_low[...], me, core, m_ref, f_ref, slope_ref, aout_ref, output, expand, shrink,
        [copies[9], copies[8], copies[7]], halves, do_ref, dm_ref, vec_ref,
    )
    mine[...] = halves[core]
    theirs[...] = halves[1 - core]


def last_kernel(
    scal, mod_ref, grads, vec0, first1, vec1, x_any, dm_any, triple_any,
    input_grad, small,
    triple, full, x_ref, dm_in, vec_first, mask_ref, sems,
):
    copies = fetch([(triple_any.at[0], triple), (x_any, x_ref), (dm_any, dm_in)], sems)
    me = scal[0]
    dx = qkv_backward(
        x_ref, dm_in, mod_ref[...], lambda group: grads[group], triple, copies, full, vec_first,
    )
    rows = dx.shape[0]
    position = me * rows + lax.broadcasted_iota(jnp.int32, dx.shape, 0)
    masked = position >= scal[3]
    input_grad[0] = jnp.where(masked, 0.0, dx)
    mask_ref[...] = column_sum(jnp.where(masked, dx, 0.0))
    pack(vec_first, vec0, first1, vec1, mask_ref, small)


def triple_kernel(
    scal, h0, h1, h2, h3, chunks,
    mine, theirs,
    result,
):
    rows = chunks.shape[1] * 2 // 3
    half = rows // 2
    each = WIDTH // 8
    for side in range(2):
        qk = jnp.zeros((WIDTH // 2, 2 * GROUP), F32)
        v = jnp.zeros((WIDTH // 2, GROUP), F32)
        for place, h_ref in enumerate((h0, h1, h2, h3)):
            h = h_ref[side]
            at = place ^ scal[0]
            qk = qk + dot_nn(h, chunks[at, 0:rows, :])
            tail = chunks[at, rows : rows + half, :]
            v = v + dot_nn(h, jnp.concatenate([tail[:, 0:GROUP], tail[:, GROUP : 2 * GROUP]], 0))
        for z in range(4):
            span = slice(z * each, (z + 1) * each)
            block = jnp.concatenate([qk[span], pack_rows(v[span])], 0).astype(BF)
            tall = block.shape[0]
            for number in range(3):
                lanes = slice(number * 128, (number + 1) * 128)
                result[side * 4 + z, number * tall : (number + 1) * tall, :] = block[:, lanes]
    for place, offset in enumerate((0, 2, 1, 3)):
        at = scal[1] ^ offset
        tall = result.shape[1]
        mine[place * tall : (place + 1) * tall, :] = result[scal[2] * 4 + at]
        theirs[place * tall : (place + 1) * tall, :] = result[(1 - scal[2]) * 4 + at]


def bring_starts(layout, pieces, hold, sems):
    return fetch(
        [
            (pieces[piece].at[source : source + rows, :], hold.at[slot, target : target + rows, :])
            for piece, source, slot, target, rows in layout
        ],
        sems,
    )


def bring(layout, pieces, hold, sems):
    wait_all(bring_starts(layout, pieces, hold, sems))


def triple_settle_kernel(layout, scal, *refs):
    pieces, outs, (hold, blocks, sems) = refs[:-7], refs[-7:-3], refs[-3:]
    bring(layout, pieces, hold, sems)
    each, rows = WIDTH // 8, WIDTH // 32
    tall = each * 3 // 2
    for layer in range(LAYERS):
        lanes = []
        for number in range(3):
            at = (layer * 3 + number) * tall
            lanes.append(sum(hold[slot, at : at + tall, :].astype(F32) for slot in range(hold.shape[0])))
        total = jnp.concatenate(lanes, 1)
        v = jnp.concatenate([total[each:, 0:GROUP], total[each:, GROUP : 2 * GROUP]], 0)
        for b in range(4):
            span = slice(b * rows, (b + 1) * rows)
            blocks[layer, b, :, 0 : 2 * GROUP] = total[span]
            blocks[layer, b, :, 2 * GROUP : 3 * GROUP] = v[span]
    for place, out in enumerate(outs):
        for layer in range(LAYERS):
            out[layer] = blocks[layer, place ^ scal[0]]


BIT = {"x": 4, "y": 8, "a": 1, "b": 2}
STEP = {"x": ("blk", 1), "y": ("blk", 2), "a": ("dp", 2), "b": ("dp", 4)}


def place_at(order, index):
    place = 0
    for depth, name in enumerate(order):
        if index & (8 >> depth):
            place |= BIT[name]
    return place


def weights_kernel(products, orders, scal, own_any, far_any, mine_any, got_any, *rest):
    count = len(orders)
    sends, keeps = rest[0:count], rest[count : 2 * count]
    turned, grads, sems = rest[2 * count :]
    pairs = [(mine_any, grads.at[0:256, :]), (got_any, grads.at[256:512, :])]
    for low, high, _, _ in products:
        pairs += [(own_any.at[low:high, :], turned.at[low:high, 0:256]), (far_any.at[low:high, :], turned.at[low:high, 256:512])]
    copies = fetch(pairs, sems)
    wait_all(copies[0:2])
    row_at = [0] * count
    for step, (low, high, at, dealt) in enumerate(products):
        wait_all(copies[2 + 2 * step : 4 + 2 * step])
        rows = (high - low) // 16
        width = sum(dealt) * 128
        result = dot_nn(turned[low:high, :], grads[:, at : at + width]).astype(BF)
        column = 0
        for part, order in enumerate(orders):
            blocks = dealt[part]
            for index in range(16):
                target = keeps[part] if index < 8 else sends[part]
                place = place_at(order, index)
                for number in range(blocks):
                    spot = row_at[part] + number * rows
                    target[index % 8, spot : spot + rows, :] = result[
                        place * rows : (place + 1) * rows, (column + number) * 128 : (column + number + 1) * 128
                    ]
            row_at[part] += blocks * rows
            column += blocks


def settle_kernel(layout, blocks, scal, *refs):
    pieces, (mine, theirs, hold, sems) = refs[:-4], refs[-4:]
    bring(layout, pieces, hold, sems)
    core = scal[2]
    row = at = 0
    for rows in blocks:
        half = rows // 2
        total = hold[0, row : row + rows, :].astype(F32)
        for slot in range(1, hold.shape[0]):
            total = total + hold[slot, row : row + rows, :].astype(F32)
        low, high = total[0:half], total[half:rows]
        mine[at : at + half, :] = jnp.where(core == 0, low, high)
        theirs[at : at + half, :] = jnp.where(core == 0, high, low)
        row += rows
        at += half


def add_kernel(layout, rows, *refs):
    outs, (hold, sems) = refs[-2 - len(rows) : -2], refs[-2:]
    copies = bring_starts(layout, refs[: -2 - len(rows)], hold, sems)
    depth = {}
    for number, (_, _, slot, target, count) in enumerate(layout):
        depth.setdefault(target, []).append((slot, count, number))
    at = 0
    for out, size in zip(outs, rows):
        for target in sorted(depth):
            if at <= target < at + size:
                for _, _, number in depth[target]:
                    copies[number].wait()
                count = depth[target][0][1]
                total = sum(hold[slot, target : target + count, :].astype(F32) for slot, _, _ in depth[target])
                out[target - at : target - at + count, :] = total.astype(BF)
        at += size


def plain_add_kernel(left, right, out):
    out[...] = left[...] + right[...]


DMOD = 12 * WIDTH
SMALL = 2 * 6912 + WIDTH
SMALL_AT = {"triple": (0, 2304), "output": (2304, 3072), "expand": (3072, 6144), "shrink": (6144, 6912)}


def pack(first0, vec0, first1, vec1, mask, out):
    for layer, (first, vec) in enumerate(((first0, vec0), (first1, vec1))):
        at = layer * 6 * WIDTH
        out[:, at : at + 1536] = first[:, 0:1536]
        out[:, at + 1536 : at + 2304] = vec[:, 2304:3072]
        out[:, at + 2304 : at + 3840] = vec[:, 768:2304]
        out[:, at + 3840 : at + 4608] = vec[:, 0:768]
        at = DMOD + layer * 6912
        out[:, at : at + 2304] = first[:, 1536:3840]
        out[:, at + 2304 : at + 3072] = vec[:, 6912:7680]
        out[:, at + 3072 : at + 6144] = vec[:, 3840:6912]
        out[:, at + 6144 : at + 6912] = vec[:, 3072:3840]
    out[:, DMOD + 2 * 6912 :] = mask[...]


def join_kernel(own, got, condition, out):
    total = own[...] + got[...]
    out[:, 0:DMOD] = total[:, 0:DMOD]
    out[:, DMOD : DMOD + 128] = condition[...]
    out[:, DMOD + 128 :] = total[:, DMOD:]


def spread_kernel(own, got, out):
    rows = own.shape[1] - SMALL
    out[:, 0:rows] = own[:, 0:rows]
    out[:, rows : 2 * rows] = got[:, 0:rows]
    out[:, 2 * rows :] = own[:, rows:] + got[:, rows:]


def small_kernel(
    scal, own, got, adaptive_any, adaptive_w, adaptive_b, triple_b, output_b, expand_b, shrink_b, mask_sum,
    condition_grad, adaptive, sems,
):
    (copy,) = fetch([(adaptive_any, adaptive)], sems)
    index = scal[4]
    each = DMOD + 128
    rows = own.shape[1] - SMALL
    share = adaptive_w.shape[1]
    number = lax.broadcasted_iota(jnp.int32, (8, 128), 0)
    lane = lax.broadcasted_iota(jnp.int32, (8, 128), 1)
    pick = (lane == index * share + number) & (number < share)
    totals = [jnp.zeros((8, 6 * WIDTH), F32), jnp.zeros((8, 6 * WIDTH), F32)]
    sums = [jnp.zeros((1, 6 * WIDTH), F32), jnp.zeros((1, 6 * WIDTH), F32)]
    for source in (own, got):
        for at in range(0, rows, each):
            column = jnp.sum(jnp.where(pick, source[:, at + DMOD : at + each], 0.0), 1, keepdims=True)
            for layer in range(LAYERS):
                low = at + layer * 6 * WIDTH
                row = source[:, low : low + 6 * WIDTH]
                totals[layer] = totals[layer] + column * row
                sums[layer] = sums[layer] + row
    summed = own[:, rows:] + got[:, rows:]

    def cut(row):
        size = row.shape[1] // 32
        return pltpu.roll(row, lax.rem(row.shape[1] - index * size, row.shape[1]), 1)[:, 0:size]

    for layer in range(LAYERS):
        adaptive_w[layer] = totals[layer][0:share]
        adaptive_b[layer : layer + 1, :] = cut(sums[layer])
        for out, (low, high) in zip((triple_b, output_b, expand_b, shrink_b), SMALL_AT.values()):
            at = layer * 6912
            out[layer : layer + 1, :] = cut(summed[:, at + low : at + high])
    mask_sum[...] = cut(summed[:, 2 * 6912 :])
    copy.wait()
    grad = jnp.zeros((8, 128), F32)
    for layer in range(LAYERS):
        at = layer * 6 * WIDTH
        grad = grad + dot_nt(three_rows(own[:, at : at + 6 * WIDTH]), adaptive[layer])
    condition_grad[...] = column_sum(grad)


def finish_kernel(plans, scal, *refs):
    pairs = 2 * len(plans)
    groups = refs[pairs : pairs + 4]
    outs, hold = refs[pairs + 4 : -1], refs[-1]
    core = scal[2]
    for bucket, plan in enumerate(plans):
        mine, got = refs[2 * bucket : 2 * bucket + 2]
        at = 0
        for out, layer, block, rows in plan:
            own, other = mine[at : at + rows, :], got[at : at + rows, :]
            half = outs[out].shape[2] // 2
            low = block * 128
            outs[out][layer, :, low : low + 128] = jnp.where(core == 0, own, other)
            outs[out][layer, :, half + low : half + low + 128] = jnp.where(core == 0, other, own)
            at += rows
    for layer in range(LAYERS):
        for place in range(4):
            hold[place] = groups[place][layer]
        for group in range(4):
            block = hold[group ^ scal[0]]
            for number in range(3):
                low = number * WIDTH + group * GROUP
                outs[0][layer, :, low : low + GROUP] = block[:, number * GROUP : (number + 1) * GROUP]


def shaped(*shape, dtype=F32):
    return jax.ShapeDtypeStruct(shape, dtype)


class Outs(list):
    token = None


def call(kernel, specs, outs, scratch, micros, name, limit, after=(), away=()):
    count, extra = len(specs), len(after)
    staging = [pltpu.VMEM(outs[number].shape, outs[number].dtype) for number in away]
    if away:
        staging.append(pltpu.SemaphoreType.DMA((len(away),)))

    def body(*refs):
        mark = refs[count + extra + len(outs)]
        mark[...] = jnp.zeros(mark.shape, F32)
        results = list(refs[count + extra : count + extra + len(outs)])
        rest = refs[count + extra + len(outs) + 1 :]
        staged, rest = rest[: len(staging)], rest[len(staging) :]
        targets = [results[number] for number in away]
        for number, stage in zip(away, staged):
            results[number] = stage
        kernel(*refs[:count], *results, *rest)
        if away:
            wait_all(fetch(list(zip(staged, targets)), staged[-1]))

    made = pl.pallas_call(
        body,
        in_specs=specs + [ANY] * extra,
        out_specs=[HBM if number in away else VM for number in range(len(outs))] + [VM],
        out_shape=[
            pltpu.HBM(shape=out.shape, dtype=out.dtype) if number in away else out for number, out in enumerate(outs)
        ]
        + [shaped(8, 128)],
        scratch_shapes=staging + scratch,
        compiler_params=pltpu.CompilerParams(vmem_limit_bytes=limit * MEBI),
        cost_estimate=pl.CostEstimate(flops=int(micros * 1e9), bytes_accessed=int(micros * 1e6), transcendentals=0),
        name=name,
    )

    def run(*operands):
        operands = [
            pltpu.with_memory_space_constraint(operand, pltpu.HBM) if spec is HBM or spec is HV else operand
            for operand, spec in zip(operands, specs)
        ]
        marks = [
            mark if mark.size * mark.dtype.itemsize < 200000 else pltpu.with_memory_space_constraint(mark, pltpu.HBM)
            for mark in after
        ]
        results = made(*operands, *marks)
        found = Outs(results[:-1])
        found.token = results[-1]
        return found

    return run


def swap(values, axis, bit):
    size = 4 if axis == "blk" else 8
    return lax.ppermute(values, axis, [(i, i ^ bit) for i in range(size)])


def swap_chunks(chunks):
    return [chunks[0]] + [swap(chunks[place], "blk", place) for place in (1, 2, 3)]


def shaped_like(values):
    return shaped(*values.shape, dtype=values.dtype)


class Part:
    def __init__(self, keep, got, rows, order):
        self.views = [(keep, 0), (got, 0)]
        self.rows = rows
        self.order = order

    def halve(self):
        self.rows //= 2


def exchange(parts, cost, after=()):
    groups = {}
    for part in parts:
        groups.setdefault(part.order[0], []).append(part)
        part.order = part.order[1:]
    groups = list(groups.items())
    ordered, rows = [], []
    for _, group in groups:
        for part in group:
            part.halve()
        ordered += group
        rows.append(sum(part.rows for part in group))
    arrays, layout, total = collect(ordered, True)
    slots = max(slot for _, _, slot, _, _ in layout) + 1
    outs = call(
        functools.partial(add_kernel, layout, rows),
        [HBM] * len(arrays),
        [shaped(count, 128, dtype=BF) for count in rows],
        [pltpu.VMEM((slots, total, 128), BF), pltpu.SemaphoreType.DMA((len(layout),))],
        cost,
        "add",
        16,
        after,
    )(*arrays)
    for (axis, group), out in zip(groups, outs):
        got = swap(out, *STEP[axis])
        at = 0
        for part in group:
            part.views.append((got, at))
            at += part.rows
    return [outs.token]


def weight_parts(scal, own, far, mine, got, products, orders, after=()):
    count = len(orders)
    shapes, rows = [], []
    for part in range(count):
        rows.append(sum(dealt[part] * (high - low) // 16 for low, high, _, dealt in products))
        shapes.append(shaped(8, rows[-1], 128, dtype=BF))
    outs = call(
        functools.partial(weights_kernel, products, orders),
        [SM] + [HBM] * 3 + [ANY],
        shapes * 2,
        [
            pltpu.VMEM((own.shape[0], 512), BF),
            pltpu.VMEM((512, mine.shape[1]), BF),
            pltpu.SemaphoreType.DMA((2 + 2 * len(products),)),
        ],
        300,
        "mlp_weights",
        32,
        after,
        tuple(range(count, 2 * count)),
    )(scal, own, far, mine, got)
    flat = [out.reshape(-1, 128) for out in outs]
    parts = [
        Part(flat[count + number], swap(flat[number], *STEP[order[0]]), 8 * rows[number], order[1:])
        for number, order in enumerate(orders)
    ]
    return parts, [outs.token]


def triple_part(scal, h_rows, stacked, after=()):
    rows = WIDTH // 8 * 3 // 2 * 3
    outs = call(
        triple_kernel,
        [SM] + [HV] * 5,
        [shaped(4 * rows, 128, dtype=BF)] * 2,
        [pltpu.VMEM((8, rows, 128), BF)],
        300,
        "triple_weights",
        20,
        after,
    )(scal, *h_rows, stacked)
    return Part(outs[0], swap(outs[1], "dp", 1), 4 * rows, "ab"), [outs.token]


def collect(parts, upper=False):
    arrays, layout, at = [], [], 0
    for part in parts:
        for slot, (array, first) in enumerate(part.views):
            first = first + part.rows if upper else first
            known = [number for number, other in enumerate(arrays) if other is array]
            if not known:
                arrays.append(array)
                known = [len(arrays) - 1]
            layout.append((known[0], first, slot, at, part.rows))
        at += part.rows
    return arrays, layout, at


def blocks_of(products):
    blocks = []
    for part in range(len(products[0][3])):
        for low, high, _, dealt in products:
            blocks += [(high - low) // 16] * dealt[part]
    return blocks


def settle(parts, scal, products, cost, after=()):
    arrays, layout, rows = collect(parts)
    slots = max(slot for _, _, slot, _, _ in layout) + 1
    outs = call(
        functools.partial(settle_kernel, layout, blocks_of(products)),
        [SM] + [HBM] * len(arrays),
        [shaped(rows // 2, 128)] * 2,
        [pltpu.VMEM((slots, rows, 128), BF), pltpu.SemaphoreType.DMA((len(layout),))],
        cost,
        "settle",
        10,
        after,
    )(scal, *arrays)
    return *outs, outs.token


def triple_settle(parts, scal, after=()):
    arrays, layout, rows = collect(parts)
    slots = max(slot for _, _, slot, _, _ in layout) + 1
    blocks = call(
        functools.partial(triple_settle_kernel, layout),
        [SM] + [HBM] * len(arrays),
        [shaped(LAYERS, WIDTH // 32, 3 * GROUP)] * 4,
        [
            pltpu.VMEM((slots, rows, 128), BF),
            pltpu.VMEM((LAYERS, 4, WIDTH // 32, 3 * GROUP), F32),
            pltpu.SemaphoreType.DMA((len(layout),)),
        ],
        0.1,
        "triple_settle",
        8,
        after,
    )(scal, *arrays)
    return swap_chunks(blocks), [blocks.token]


def plan_of(products, names):
    plan = []
    for part in range(len(products[0][3])):
        for (low, high, _, dealt), (out, layer) in zip(products, names):
            first = sum(dealt[:part])
            plan += [(out, layer, first + number, (high - low) // 32) for number in range(dealt[part])]
    return plan


def rotary_tables(start, rows):
    position = (start[:, None] + jnp.arange(rows, dtype=jnp.int32)[None, :]).astype(F32)
    lane = jnp.arange(128, dtype=jnp.int32)
    frequency = jnp.exp((lane % 32).astype(F32) * (-2.0 * math.log(10000.0) / HEAD_DIM))
    angles = position[:, :, None] * frequency
    return jnp.cos(angles), jnp.sin(angles) * jnp.where(lane % 64 < 32, -1.0, 1.0)


def local_fast(
    inputs, condition, prefix, mask_embed, adaptive_weight, adaptive_bias, triple_weight, triple_bias, output_weight,
    output_bias, expand_weight, expand_bias, shrink_weight, shrink_bias, cotangent,
):
    rows = inputs.shape[1]
    hidden = expand_weight.shape[2]
    blk, dp = lax.axis_index("blk"), lax.axis_index("dp")
    scal = jnp.stack([blk, dp // 2, dp % 2, prefix[0], blk * 8 + dp]).astype(jnp.int32)
    starts = (blk ^ jnp.arange(4, dtype=jnp.int32)) * rows
    cosine, sine = rotary_tables(starts[:1], rows)
    cosines, sines = rotary_tables(starts, rows)

    f_square = shaped(rows, WIDTH)
    x_hold = pltpu.VMEM((rows, WIDTH), F32)
    b_square = shaped(rows, WIDTH, dtype=BF)
    b_tall = shaped(rows, hidden, dtype=BF)
    packed = rows + rows // 2
    chunk = shaped(packed, 2 * GROUP, dtype=BF)
    o_chunk = shaped(rows // 2, 2 * GROUP, dtype=BF)
    c_hold = pltpu.VMEM((4, packed, 2 * GROUP), BF)
    o_hold = pltpu.VMEM((4, rows // 2, 2 * GROUP), BF)
    adaptive_hold = pltpu.VMEM((condition.shape[1], 6 * WIDTH), BF)
    triple_hold = pltpu.VMEM((WIDTH, 3 * WIDTH), BF)
    output_hold = pltpu.VMEM((WIDTH, WIDTH), BF)
    expand_hold = pltpu.VMEM((WIDTH, hidden), BF)
    shrink_hold = pltpu.VMEM((hidden, WIDTH), BF)
    h_both = shaped(2, WIDTH // 2, rows, dtype=BF)
    half_width = hidden // 2 + WIDTH
    tall = hidden + 2 * WIDTH
    mod_row = shaped(1, 6 * WIDTH)

    x0, mod0, h_rows, *chunks = call(
        first_kernel,
        [SM] + [VM] * 3 + [HBM] * 6,
        [f_square, mod_row, h_both] + [chunk] * 4,
        [
            pltpu.VMEM(inputs.shape, BF), pltpu.VMEM(condition.shape, F32), pltpu.VMEM(adaptive_bias.shape, BF),
            pltpu.VMEM(triple_bias.shape, BF), adaptive_hold, triple_hold, c_hold, pltpu.SemaphoreType.DMA((6,)),
        ],
        300,
        "qkv_first",
        24,
    )(
        scal, mask_embed[None], cosine, sine, inputs, condition, adaptive_bias, triple_bias, adaptive_weight,
        triple_weight,
    )

    def attend(chunks, after):
        return call(
            attend_kernel,
            [VM] * 4,
            [o_chunk] * 4 + [shaped(4, 8, rows), shaped(4, rows, GROUP)],
            [
                pltpu.VMEM((4, GROUP, rows), F32),
                pltpu.VMEM((4, rows, GROUP), BF),
                pltpu.VMEM((4 * rows, GROUP), BF),
                pltpu.VMEM((3, HEAD_DIM + 16, 4 * rows), BF),
            ],
            300,
            "attend",
            20,
            after,
        )(*chunks)

    def attend_back(chunks, given, lse, turned, after):
        stack = shaped(4, packed, 2 * GROUP, dtype=BF)
        return call(
            attend_back_kernel,
            [SM, VM] + [VM] * 5 + [HV] + [HBM] * 2,
            [stack],
            [
                pltpu.VMEM((4, rows, 128), F32),
                pltpu.VMEM((4, rows, 128), F32),
                pltpu.SemaphoreType.DMA((2,)),
                pltpu.VMEM((3, 4 * rows, GROUP), BF),
                pltpu.VMEM((3, 4 * rows, GROUP), BF),
                pltpu.VMEM((4, rows, GROUP), BF),
                pltpu.VMEM((4, rows, GROUP), BF),
                pltpu.VMEM((4, GROUP, rows), BF),
                pltpu.VMEM((8, 4 * rows), F32),
                pltpu.VMEM((8, 4 * rows), F32),
                pltpu.VMEM((GROUP, 4 * rows), F32),
                pltpu.VMEM((4, rows, GROUP), F32),
                pltpu.VMEM((4, rows, GROUP), F32),
            ],
            300,
            "attend_back",
            26,
            after,
            (0,),
        )(scal, given, *chunks, lse, turned, cosines, sines)

    def far(values):
        return swap(values, "dp", 1)

    def gather_rows(both, first, second):
        near = [swap(both, "blk", bit) for bit in (1, 2)]
        return [both, *near, swap(near[first - 1], "blk", second)]

    chunks0 = swap_chunks(chunks)
    h_rows0 = gather_rows(h_rows, 2, 1)
    *o_chunks, lse0, ot0 = attend(chunks0, ())
    o_chunks = swap_chunks(o_chunks)
    aout0, m0, turned0, slope0, f0, x1, mod1, h_rows, *chunks = call(
        middle_kernel,
        [SM] + [VM] * 13 + [HBM] * 6,
        [b_square, f_square, shaped(tall, rows, dtype=BF), b_tall, b_square, f_square, mod_row, h_both] + [chunk] * 4,
        [x_hold, output_hold, expand_hold, shrink_hold, triple_hold, adaptive_hold, pltpu.VMEM((1, hidden), F32), o_hold, pltpu.VMEM((rows, WIDTH), BF)]
        + [c_hold, pltpu.SemaphoreType.DMA((6,))],
        300,
        "mlp_qkv",
        34,
    )(
        scal, mod0, condition, adaptive_bias, output_bias, expand_bias, shrink_bias, triple_bias, cosine, sine,
        *o_chunks, x0, output_weight, expand_weight, shrink_weight, triple_weight, adaptive_weight,
    )
    turned0_far = far(turned0)
    chunks1 = swap_chunks(chunks)
    h_rows1 = gather_rows(h_rows, 1, 2)
    *o_chunks, lse1, ot1 = attend(chunks1, [*h_rows0[1:3], cosines, sines])
    o_chunks = swap_chunks(o_chunks)
    outputs, aout1, m1, turned1, slope1, f1 = call(
        ahead_kernel,
        [SM] + [VM] * 8 + [HBM] * 4,
        [shaped(1, rows, WIDTH, dtype=BF), b_square, f_square, shaped(tall, rows, dtype=BF), b_tall, b_square],
        [x_hold, output_hold, expand_hold, shrink_hold, pltpu.VMEM((1, hidden), F32), o_hold]
        + [pltpu.VMEM((rows, WIDTH), BF), pltpu.SemaphoreType.DMA((4,))],
        300,
        "mlp_ahead",
        28,
        [*h_rows1[1:3], turned0_far],
    )(
        scal, mod1, output_bias, expand_bias, shrink_bias, *o_chunks, x1, output_weight, expand_weight, shrink_weight
    )
    turned1_far = far(turned1)
    back_outs = [shaped(4, rows // 2, 2 * GROUP, dtype=BF), f_square, shaped(1, 7680)]
    mine1, theirs1, given, dm1, vec1 = call(
        turn_kernel,
        [SM] + [VM] * 5 + [HBM] * 4,
        [shaped(rows, half_width, dtype=BF)] * 2 + back_outs,
        [output_hold, expand_hold, shrink_hold, pltpu.VMEM(cotangent.shape, BF)]
        + [pltpu.VMEM((2, rows, half_width), BF), pltpu.SemaphoreType.DMA((4,))],
        300,
        "mlp_turn",
        32,
        [h_rows0[3], h_rows1[3]],
        (0, 3),
    )(scal, mod1, m1, f1, slope1, aout1, cotangent, output_weight, expand_weight, shrink_weight)

    def exchange_blocks(stack):
        return lax.all_to_all(stack, "blk", 0, 0)

    def deal(*dealt):
        return (
            (hidden, hidden + WIDTH, 0, dealt[0]),
            (0, hidden, hidden // 2, dealt[1]),
            (hidden + WIDTH, tall, hidden // 2 + WIDTH // 2, dealt[2]),
        )

    products1 = deal((4, 4, 4), (1, 1, 1), (2, 1, 0))
    products0 = deal((4, 4, 4), (1, 1, 1), (1, 1, 1))
    orders = ("axyb", "xyba", "yaxb")
    given = exchange_blocks(given)
    parts1, sent = weight_parts(scal, turned1, turned1_far, mine1, far(theirs1), products1, orders)
    outs = attend_back(chunks1, given, lse1, ot1, sent)
    stacked = outs[0]
    grads = exchange_blocks(stacked)
    sent = exchange(parts1, 0.1, [outs.token])
    triple1, sent = triple_part(scal, h_rows1, stacked, sent)
    outs = call(
        back_kernel,
        [SM] + [VM] * 3 + [HBM] * 10,
        [shaped(rows, half_width, dtype=BF)] * 2 + [shaped(1, 3840)] + back_outs,
        [triple_hold, output_hold, expand_hold, shrink_hold, pltpu.VMEM((rows, 3 * WIDTH), BF)]
        + [pltpu.VMEM((2, rows, half_width), BF), x_hold, x_hold, x_hold, pltpu.VMEM((rows, WIDTH), BF)]
        + [pltpu.VMEM((rows, hidden), BF), pltpu.VMEM((rows, WIDTH), BF), pltpu.SemaphoreType.DMA((10,))],
        300,
        "qkv_mlp_back",
        32,
        sent,
        (0, 4),
    )(
        scal, mod1, mod0, grads, x1, dm1, m0, f0, slope0, aout0, triple_weight, output_weight, expand_weight,
        shrink_weight,
    )
    mine0, theirs0, first1, given, dm0, vec0 = outs
    given = exchange_blocks(given)
    sent = exchange([*parts1, triple1], 300, [outs.token])
    parts0, sent = weight_parts(scal, turned0, turned0_far, mine0, far(theirs0), products0, orders, sent)
    sent = exchange([*parts1, triple1], 0.1, sent)
    outs = attend_back(chunks0, given, lse0, ot0, sent)
    stacked = outs[0]
    grads = exchange_blocks(stacked)
    sent = exchange(parts0, 0.1, [outs.token])
    triple0, sent = triple_part(scal, h_rows0, stacked, sent)
    sent = [*sent, triple1.views[-1][0]]
    outs = call(
        last_kernel,
        [SM] + [VM] * 5 + [HBM] * 3,
        [shaped(1, rows, WIDTH), shaped(1, DMOD + SMALL)],
        [triple_hold, pltpu.VMEM((rows, 3 * WIDTH), BF), x_hold, x_hold]
        + [pltpu.VMEM((1, 3840), F32), pltpu.VMEM((1, WIDTH), F32), pltpu.SemaphoreType.DMA((3,))],
        300,
        "qkv_back",
        24,
        sent,
    )(scal, mod0, grads, vec0, first1, vec1, x0, dm0, triple_weight)

    def spread(own, got, cost, after=()):
        wide = shaped(1, 2 * own.shape[1] - SMALL)
        return call(spread_kernel, [VM] * 2, [wide], [], cost, "spread", 8, after)(own, got)

    input_grad, small = outs
    near = swap(small, "blk", 1)
    sent = exchange([*parts0, triple0], 300, [outs.token])
    (summed,) = call(plain_add_kernel, [VM] * 2, [shaped_like(small)], [], 300, "plain_add", 8, sent)(small, near)
    outs = call(
        join_kernel,
        [VM] * 3,
        [shaped(1, DMOD + 128 + SMALL)],
        [],
        0.1,
        "join",
        8,
    )(summed, swap(summed, "blk", 2), condition)
    wide = outs[0]
    got = swap(wide, *STEP["b"])
    sent = exchange([*parts0, triple0], 300, [outs.token])
    own1, theirs1, early = settle(parts1, scal, products1, 0.1, sent)
    outs = spread(wide, got, 300, [early])
    wide = outs[0]
    outs = spread(wide, swap(wide, *STEP["a"]), 0.1)
    wide = outs[0]
    outs = call(
        small_kernel,
        [SM] + [VM] * 2 + [HBM],
        [shaped(LAYERS, condition.shape[1] // 32, 6 * WIDTH), shaped(LAYERS, 6 * WIDTH // 32)]
        + [shaped(LAYERS, (high - low) // 32) for low, high in SMALL_AT.values()]
        + [shaped(1, WIDTH // 32), shaped(1, 128)],
        [pltpu.VMEM(adaptive_weight.shape, BF), pltpu.SemaphoreType.DMA((1,))],
        0.1,
        "small",
        14,
    )(scal, wide, far(wide), adaptive_weight)
    small_grads = list(outs)
    blocks, cut = triple_settle([triple0, triple1], scal, [outs.token])
    own0, theirs0, _ = settle(parts0, scal, products0, 0.1, [*cut, *blocks[1:]])
    plans = (
        plan_of(products1, ((2, 1), (3, 1), (1, 1))),
        plan_of(products0, ((2, 0), (3, 0), (1, 0))),
    )
    weight_grads = call(
        functools.partial(finish_kernel, plans),
        [SM] + [VM] * 8,
        [
            shaped(LAYERS, WIDTH // 32, 3 * WIDTH),
            shaped(LAYERS, WIDTH // 32, WIDTH),
            shaped(LAYERS, WIDTH // 32, hidden),
            shaped(LAYERS, hidden // 32, WIDTH),
        ],
        [pltpu.VMEM((4, WIDTH // 32, 3 * GROUP), F32)],
        0.1,
        "finish",
        12,
    )(scal, own1, far(theirs1), own0, far(theirs0), *blocks)
    return (
        outputs,
        input_grad,
        small_grads[7],
        small_grads[6][0],
        small_grads[0],
        small_grads[1],
        weight_grads[0],
        small_grads[2],
        weight_grads[1],
        small_grads[3],
        weight_grads[2],
        small_grads[4],
        weight_grads[3],
        small_grads[5],
    )


def solution(mesh):
    in_specs = (
        P("dp", "blk", None),
        P("dp", None),
        P("dp"),
        P(),
        P(),
        P(),
        P(),
        P(),
        P(),
        P(),
        P(),
        P(),
        P(),
        P(),
        P("dp", "blk", None),
    )
    out_specs = (
        P("dp", "blk", None),
        P("dp", "blk", None),
        P("dp", None),
        P(("blk", "dp")),
        P(None, ("blk", "dp"), None),
        P(None, ("blk", "dp")),
        P(None, ("blk", "dp"), None),
        P(None, ("blk", "dp")),
        P(None, ("blk", "dp"), None),
        P(None, ("blk", "dp")),
        P(None, ("blk", "dp"), None),
        P(None, ("blk", "dp")),
        P(None, ("blk", "dp"), None),
        P(None, ("blk", "dp")),
    )
    whole = mesh.shape["blk"] == 4 and mesh.shape["dp"] == 8
    body = local_fast if whole else local
    return jax.shard_map(body, mesh=mesh, in_specs=in_specs, out_specs=out_specs, check_vma=False)
```
